32 devices in a mesh: span: 2 (over y), stream: 16 (over z, x, core).
Axes of the slice: x: 2, y: 2, z: 4, core: 2. Of those that a mesh axis runs over, the one named last changes fastest.
Arguments:
- velocity: float32 [3, 8, 128, 256], P(None, 'span', 'stream'), may hold values from -32 to 32
- strain: float32 [6, 8, 128, 256], P(None, 'span', 'stream'), may hold values from -4 to 4
- row_bins: int32 [128], P('stream'), may hold values from 0 to 63, never falling along the last dimension, each value on 1 to 4 neighbouring positions
- cotangent: float32 [6, 8, 128, 256], P(None, 'span', 'stream'), may hold values from -6 to 6
Outputs:
- model_residual: float32 [6, 8, 128, 256], P(None, 'span', 'stream')
- velocity_grad: float32 [3, 8, 128, 256], P(None, 'span', 'stream')
The draws below stay inside these ranges and needn't reach their ends.
Inputs may be any that keep to these rules, and one draw needn't show every extreme that they name: `row_bins`: bins never fall along the rows, and every bin holds 1 to 4 rows.
All inputs are finite; a program needn't handle non-finite values.
Results may differ from the reference program's by a relative error of at most 0.0003.
Values sent between devices are 32-bit elements; how exact they have to be, the bound alone decides.
No kernel may reach another device: no remote copies, remote signals or barrier semaphores. Data moves between devices by JAX's collectives and lax.ppermute only.
A program may use at most 64 MiB of HBM per device.

```python
import math
import jax
import jax.numpy as jnp
import numpy as np
from jax import lax

PX = 256
NBINS = 64
NZ = 8
NY = 128


def draw_velocity(key, part):
    key_base, key_span, key_plane = jax.random.split(key, 3)
    span_scale = jnp.exp(jax.random.uniform(key_span, (1, NZ, 1, 1), minval=-0.7, maxval=0.7))
    plane_scale = jnp.exp(jax.random.uniform(key_plane, (1, 1, 1, PX), minval=-0.7, maxval=0.7))
    row_positions = jnp.arange(NY, dtype=jnp.float32)
    row_scale = (0.6 * jnp.exp(jnp.log(3.0) * row_positions / NY))[None, None, :, None]
    base_draw = jnp.clip(jax.random.normal(key_base, (3, NZ, NY, PX)), -4.0, 4.0)
    return (base_draw * span_scale * plane_scale * row_scale).astype(jnp.float32)


def steps_of(key, dims, cuts, smallest, high):
    def one(dim, shards_of):
        heights = jax.random.uniform(jax.random.fold_in(jax.random.fold_in(key, 6), dim), (shards_of,), jnp.float32, smallest / len(cuts), high / len(cuts))
        return jnp.repeat(jnp.exp(heights), dims[dim] // shards_of).reshape((-1,) + (1,) * (len(dims) - dim - 1))

    gain = one(*cuts[0])
    for cut in cuts[1:]:
        gain = gain * one(*cut)
    return gain


def length_profile(number_of, total, limit, slope):
    loads = [(1 << 20) // math.isqrt(grade ** slope) + 1 for grade in range(2, number_of + 1)]
    surplus, holding = total - limit - (number_of - 1), [1] * (number_of - 1)
    while surplus > 0:
        free = [i for i in range(number_of - 1) if holding[i] < limit]
        mass, remaining = sum([loads[i] for i in free]), surplus
        for i in free:
            addition = min(limit - holding[i], max(1, remaining * loads[i] // mass), surplus)
            holding[i] = holding[i] + addition
            surplus = surplus - addition
    return np.array([limit] + holding)


def ragged(stream_key, number_of, total, most, lean):
    if number_of == 2:
        one = jax.random.randint(stream_key, (), max(1, total - most), min(most, total - 1) + 1)
        return jnp.stack([one, total - one])
    sizes = jnp.asarray(length_profile(number_of, total, most, lean), jnp.int32)
    couples = (number_of - 1) // 2
    giver, taker = sizes[1:1 + 2 * couples:2], sizes[2:2 + 2 * couples:2]
    room = jnp.minimum(giver - 1, most - taker)
    shifted = jax.random.randint(jax.random.fold_in(stream_key, 1), (couples,), 0, 1 << 20) % (room + 1)
    sizes = sizes.at[1:1 + 2 * couples:2].set(giver - shifted).at[2:2 + 2 * couples:2].set(taker + shifted)
    return sizes[jax.random.permutation(jax.random.fold_in(stream_key, 2), number_of)]


def noise(stream_key, dims, scale, most, pieces=(), held_as=jnp.bfloat16):
    factor_of = steps_of(stream_key, dims, pieces, -0.22, 0.18) if pieces else 1.0
    entries = jax.random.normal(stream_key, dims, jnp.float32) * scale * factor_of
    return jnp.minimum(jnp.maximum(entries, -most), most).astype(held_as)


def setup_inputs(seed: int = 0) -> dict:
    arg_keys = jax.random.split(jax.random.key(seed), 5)
    return {
        "velocity": draw_velocity(jax.random.fold_in(arg_keys[4], 71), 0),
        "strain": noise(arg_keys[1], (6, NZ, NY, PX), 0.3, 4.0, ((1, 2), (2, 16)), jnp.float32),
        "row_bins": jnp.searchsorted(jnp.cumsum(ragged(arg_keys[2], NBINS, NY, 2 * NY // NBINS, 0)), jnp.arange(NY), side="right").astype(jnp.int32),
        "cotangent": noise(arg_keys[3], (6, NZ, NY, PX), 1.0, 6.0, ((1, 2), (2, 16)), jnp.float32),
    }


FILTER_ALPHA = 0.45
CENTER_WEIGHT = 0.95
SIDE_WEIGHT = 0.475
STRAIN_FLOOR = 0.25
EPSILON = 1e-06
INDEX_PAIRS = ((0, 0), (0, 1), (0, 2), (1, 1), (1, 2), (2, 2))
PAIR_WEIGHTS = (1.0, 2.0, 2.0, 1.0, 2.0, 1.0)
HIGHEST = lax.Precision.HIGHEST

def explicit_side(values):
    return CENTER_WEIGHT * values + SIDE_WEIGHT * (jnp.roll(values, 1, axis=1) + jnp.roll(values, -1, axis=1))

def implicit_inverse(cell_count):
    identity = jnp.eye(cell_count, dtype=jnp.float32)
    system = identity + FILTER_ALPHA * (jnp.roll(identity, 1, axis=1) + jnp.roll(identity, -1, axis=1))
    return jnp.linalg.inv(system)

def test_filter(values, inverse):
    return jnp.einsum('zw,fwyx->fzyx', inverse, explicit_side(values), precision=HIGHEST)

def germano(velocity, strain, row_bins):
    inverse = implicit_inverse(velocity.shape[1])
    onehot = (row_bins[:, None] == jnp.arange(NBINS, dtype=jnp.int32)[None, :]).astype(jnp.float32)
    weights = jnp.asarray(PAIR_WEIGHTS, jnp.float32)[:, None, None, None]
    products = jnp.stack([velocity[former] * velocity[latter] for former, latter in INDEX_PAIRS])
    size_field = jnp.sqrt(jnp.maximum(2.0 * lax.optimization_barrier(jnp.sum(weights * strain * strain, axis=0)), STRAIN_FLOOR))
    fields = jnp.concatenate([velocity, products, size_field[None]], axis=0)
    filtered = test_filter(fields, inverse)
    coarse = jnp.stack([filtered[former] * filtered[latter] for former, latter in INDEX_PAIRS])
    leonard = filtered[3:9] - coarse
    model_term = products - coarse + 2.0 * (4.0 * filtered[9] - size_field)[None] * strain
    cross_rows = lax.optimization_barrier(jnp.sum(weights * leonard * model_term, axis=(0, 1, 3)))
    square_rows = lax.optimization_barrier(jnp.sum(weights * model_term * model_term, axis=(0, 1, 3)))
    numerator = jnp.dot(cross_rows, onehot, precision=HIGHEST)
    denominator = jnp.dot(square_rows, onehot, precision=HIGHEST) + EPSILON
    coefficient = numerator / denominator
    row_coefficient = jnp.dot(onehot, coefficient, precision=HIGHEST)
    return leonard - row_coefficient[None, None, :, None] * model_term

def reference(velocity, strain, row_bins, cotangent):
    residual, pullback = jax.vjp(lambda moving: germano(moving, strain, row_bins), velocity)
    return (residual, pullback(cotangent)[0])
```

```python
import functools

import jax
import jax.numpy as jnp
import numpy as np
from jax import lax
from jax.experimental import pallas as pl
from jax.experimental.pallas import tpu as pltpu
from jax.sharding import PartitionSpec as P

NBINS = 64
FILTER_ALPHA = 0.45
CENTER_WEIGHT = 0.95
SIDE_WEIGHT = 0.475
STRAIN_FLOOR = 0.25
EPSILON = 1e-06
INDEX_PAIRS = ((0, 0), (0, 1), (0, 2), (1, 1), (1, 2), (2, 2))
PAIR_WEIGHTS = (1.0, 2.0, 2.0, 1.0, 2.0, 1.0)
PAIR_OF = ((0, 1, 2), (1, 3, 4), (2, 4, 5))
LANES = 128


def filter_row(extent):
    eye = np.eye(extent)
    ring = np.roll(eye, 1, axis=1) + np.roll(eye, -1, axis=1)
    system = eye + FILTER_ALPHA * ring
    side = CENTER_WEIGHT * eye + SIDE_WEIGHT * ring
    return np.linalg.solve(system, side)[0]


def end_weights(cells):
    weights = np.zeros((2, cells))
    weights[0, 0] = 1.0
    weights[1, cells - 1] = 1.0
    inner = cells - 2
    if inner > 0:
        system = np.eye(inner) + FILTER_ALPHA * (np.eye(inner, k=1) + np.eye(inner, k=-1))
        right = np.zeros((inner, 2))
        right[0, 0] = -FILTER_ALPHA
        right[inner - 1, 1] = -FILTER_ALPHA
        weights[:, 1:-1] = np.linalg.solve(system, right).T
    return weights


class Tables:
    def __init__(self, cells, devices):
        row = filter_row(cells * devices)
        extent = cells * devices
        self.cells = cells
        self.devices = devices
        self.own = [[float(row[(z - w) % extent]) for w in range(cells)] for z in range(cells)]
        self.ends = [[float(x) for x in line] for line in end_weights(cells)]
        self.couple = [
            [[float(row[(z - shift * cells - w) % extent]) for w in (0, cells - 1)] for z in range(cells)]
            for shift in range(devices)
        ]

    def project(self, values):
        return [weighted(line, values) for line in self.ends]

    def inside(self, values):
        return [weighted(line, values) for line in self.own]

    def outside(self, shift, ends):
        return [weighted(line, ends) for line in self.couple[shift]]


def weighted(weights, values):
    total = None
    for weight, value in zip(weights, values):
        if weight == 0.0:
            continue
        term = value if weight == 1.0 else value * weight
        total = term if total is None else total + term
    return total


def add_lists(left, right):
    return [x + y for x, y in zip(left, right)]


def halves(width):
    return [pl.ds(start, LANES) for start in range(0, width, LANES)]


def prepare_kernel(tables, strain_ref, cot_ref, size_ref, size_ends_ref, cot_ends_ref):
    cells = tables.cells
    for lanes in halves(strain_ref.shape[-1]):
        size = []
        for z in range(cells):
            total = None
            for k, weight in enumerate(PAIR_WEIGHTS):
                value = strain_ref[k, z, :, lanes]
                term = weight * (value * value)
                total = term if total is None else total + term
            size.append(jnp.sqrt(jnp.maximum(2.0 * total, STRAIN_FLOOR)))
            size_ref[z, :, lanes] = size[z]
        for end, value in enumerate(tables.project(size)):
            size_ends_ref[end, :, lanes] = value
        for k in range(6):
            cells_of = [cot_ref[k, z, :, lanes] for z in range(cells)]
            for end, value in enumerate(tables.project(cells_of)):
                cot_ends_ref[2 * k + end, :, lanes] = value


def forward_kernel(tables, *refs):
    peers = tables.devices - 1
    cells = tables.cells
    v_ref, strain_ref, cot_ref, size_ref, bins_ref = refs[:5]
    far_v_refs = refs[5 : 5 + peers]
    far_size_refs = refs[5 + peers : 5 + 2 * peers]
    leonard_ref, model_ref, duals_ref, message_ref, sums_ref = refs[5 + 2 * peers :]
    cross = square = blame = None
    for lanes in halves(v_ref.shape[-1]):
        v = [[v_ref[a, z, :, lanes] for z in range(cells)] for a in range(3)]
        size = [size_ref[z, :, lanes] for z in range(cells)]
        products = [[v[a][z] * v[b][z] for z in range(cells)] for a, b in INDEX_PAIRS]
        filtered = [tables.inside(field) for field in v + products + [size]]
        for shift in range(1, tables.devices):
            far_v_ref = far_v_refs[shift - 1]
            far = [[far_v_ref[a, z, :, lanes] for z in range(cells)] for a in range(3)]
            far_products = [[far[a][z] * far[b][z] for z in range(cells)] for a, b in INDEX_PAIRS]
            ends = [tables.project(field) for field in far + far_products]
            ends.append([far_size_refs[shift - 1][end, :, lanes] for end in range(2)])
            filtered = [add_lists(near, tables.outside(shift, pair)) for near, pair in zip(filtered, ends)]
        smooth_v = filtered[:3]
        factor = [2.0 * (4.0 * filtered[9][z] - size[z]) for z in range(cells)]
        model, leonard = [], []
        for k, (a, b) in enumerate(INDEX_PAIRS):
            model.append([])
            leonard.append([])
            for z in range(cells):
                coarse = smooth_v[a][z] * smooth_v[b][z]
                big = filtered[3 + k][z] - coarse
                term = products[k][z] - coarse + factor[z] * strain_ref[k, z, :, lanes]
                leonard[k].append(big)
                model[k].append(term)
                leonard_ref[k, z, :, lanes] = big
                model_ref[k, z, :, lanes] = term
                scaled = PAIR_WEIGHTS[k] * term
                parts = (scaled * big, scaled * term, term * cot_ref[k, z, :, lanes])
                if cross is None:
                    cross, square, blame = parts
                else:
                    cross, square, blame = cross + parts[0], square + parts[1], blame + parts[2]
            for end, value in enumerate(tables.project(model[k])):
                message_ref[2 * k + end, :, lanes] = value
        for a in range(3):
            of_cot, of_both, of_model = [], [], []
            for z in range(cells):
                first = second = third = None
                for b in range(3):
                    k = PAIR_OF[a][b]
                    value = cot_ref[k, z, :, lanes] * smooth_v[b][z]
                    if a == b:
                        value = 2.0 * value
                    other = model[k][z] * smooth_v[b][z]
                    both = leonard[k][z] * smooth_v[b][z] + other
                    first = value if first is None else first + value
                    second = both if second is None else second + both
                    third = other if third is None else third + other
                of_cot.append(first)
                of_both.append(2.0 * second)
                of_model.append(2.0 * third)
            for kind, dual in enumerate((of_cot, of_both, of_model)):
                place = 3 * kind + a
                for z in range(cells):
                    duals_ref[place, z, :, lanes] = dual[z]
                for end, value in enumerate(tables.project(dual)):
                    message_ref[12 + 2 * place + end, :, lanes] = value
    rows = cross.shape[0]
    lane = lax.broadcasted_iota(jnp.int32, (rows, LANES), 1)
    mine = bins_ref[...] == lane
    place = lax.broadcasted_iota(jnp.int32, (8, LANES), 0)
    table = jnp.zeros((8, LANES), jnp.float32)
    for index, sums in enumerate((cross, square, blame)):
        per_row = jnp.sum(sums, axis=1, keepdims=True)
        per_bin = jnp.sum(jnp.where(mine, per_row, 0.0), axis=0, keepdims=True)
        table = jnp.where(place == index, per_bin, table)
    sums_ref[...] = table


def local_kernel(tables, v_ref, cot_ref, leonard_ref, model_ref, duals_ref, parts_ref):
    cells = tables.cells
    for lanes in halves(v_ref.shape[-1]):
        v = [[v_ref[a, z, :, lanes] for z in range(cells)] for a in range(3)]
        cot = [[cot_ref[k, z, :, lanes] for z in range(cells)] for k in range(6)]
        model = [[model_ref[k, z, :, lanes] for z in range(cells)] for k in range(6)]
        smooth_cot = [tables.inside(field) for field in cot]
        inner = [
            add_lists(tables.inside(model[k]), [leonard_ref[k, z, :, lanes] for z in range(cells)]) for k in range(6)
        ]
        for a in range(3):
            smooth_duals = [
                tables.inside([duals_ref[3 * kind + a, z, :, lanes] for z in range(cells)]) for kind in range(3)
            ]
            for z in range(cells):
                first = second = third = fourth = None
                for b in range(3):
                    k = PAIR_OF[a][b]
                    twice = 2.0 * v[b][z]
                    single = twice if a == b else v[b][z]
                    terms = (
                        smooth_cot[k][z] * single,
                        cot[k][z] * single,
                        inner[k][z] * twice,
                        model[k][z] * twice,
                    )
                    if first is None:
                        first, second, third, fourth = terms
                    else:
                        first, second = first + terms[0], second + terms[1]
                        third, fourth = third + terms[2], fourth + terms[3]
                parts_ref[a, z, :, lanes] = first - smooth_duals[0][z]
                parts_ref[3 + a, z, :, lanes] = smooth_duals[0][z] - second
                parts_ref[6 + a, z, :, lanes] = third - smooth_duals[1][z]
                parts_ref[9 + a, z, :, lanes] = 2.0 * (smooth_duals[2][z] - fourth)


def finish_kernel(tables, count, *refs):
    peers = tables.devices - 1
    cells = tables.cells
    v_ref, leonard_ref, model_ref, parts_ref, bins_ref = refs[:5]
    sums_refs = refs[5 : 5 + count]
    far_cot_refs = refs[5 + count : 5 + count + peers]
    far_message_refs = refs[5 + count + peers : 5 + count + 2 * peers]
    residual_ref, grad_ref = refs[5 + count + 2 * peers :]
    total = sums_refs[0][...]
    for ref in sums_refs[1:]:
        total = total + ref[...]
    inverse = 1.0 / (total[1:2] + EPSILON)
    rows = v_ref.shape[2]
    lane = lax.broadcasted_iota(jnp.int32, (rows, LANES), 1)
    mine = bins_ref[...] == lane

    def of_rows(per_bin):
        column = jnp.sum(jnp.where(mine, per_bin, 0.0), axis=1, keepdims=True)
        return jnp.broadcast_to(column, (rows, LANES))

    coefficient = of_rows(total[0:1] * inverse)
    pull = of_rows(-(total[2:3] * inverse))
    both = pull * coefficient
    for lanes in halves(v_ref.shape[-1]):
        for k in range(6):
            for z in range(cells):
                residual_ref[k, z, :, lanes] = (
                    leonard_ref[k, z, :, lanes] - coefficient * model_ref[k, z, :, lanes]
                )
        v = [[v_ref[a, z, :, lanes] for z in range(cells)] for a in range(3)]
        from_products = [None] * 6
        from_velocity = [None] * 3
        for shift in range(1, tables.devices):
            cot_ends = far_cot_refs[shift - 1]
            ends = far_message_refs[shift - 1]
            for k in range(6):
                pair = [
                    cot_ends[2 * k + end, :, lanes] + (PAIR_WEIGHTS[k] * pull) * ends[2 * k + end, :, lanes]
                    for end in range(2)
                ]
                far = tables.outside(shift, pair)
                from_products[k] = far if from_products[k] is None else add_lists(from_products[k], far)
            for a in range(3):
                pair = [
                    (coefficient - 1.0) * ends[12 + 2 * a + end, :, lanes]
                    - pull * ends[18 + 2 * a + end, :, lanes]
                    + (2.0 * both) * ends[24 + 2 * a + end, :, lanes]
                    for end in range(2)
                ]
                far = tables.outside(shift, pair)
                from_velocity[a] = far if from_velocity[a] is None else add_lists(from_velocity[a], far)
        for a in range(3):
            for z in range(cells):
                value = (
                    parts_ref[a, z, :, lanes]
                    + coefficient * parts_ref[3 + a, z, :, lanes]
                    + pull * parts_ref[6 + a, z, :, lanes]
                    + both * parts_ref[9 + a, z, :, lanes]
                )
                if peers:
                    value = value + from_velocity[a][z]
                    for b in range(3):
                        term = from_products[PAIR_OF[a][b]][z] * v[b][z]
                        value = value + (2.0 * term if a == b else term)
                grad_ref[a, z, :, lanes] = value


def call(kernel, outs, operations, *operands):
    nbytes = sum(4 * int(np.prod(x.shape)) for x in (*operands, *outs))
    whole = pl.BlockSpec(memory_space=pltpu.VMEM)
    return pl.pallas_call(
        kernel,
        out_shape=outs,
        in_specs=[whole] * len(operands),
        out_specs=[whole] * len(outs),
        compiler_params=pltpu.CompilerParams(vmem_limit_bytes=32 * 1024 * 1024),
        cost_estimate=pl.CostEstimate(flops=operations, bytes_accessed=nbytes, transcendentals=0),
    )(*operands)


def from_ahead(values, shift):
    peers = lax.axis_size("span")
    return lax.ppermute(values, "span", [((i + shift) % peers, i) for i in range(peers)])


def from_place(values, span_shift, stream_shift):
    span, stream = lax.axis_size("span"), lax.axis_size("stream")
    pairs = []
    for i in range(span):
        for j in range(stream):
            source = ((i + span_shift) % span) * stream + (j + stream_shift) % stream
            pairs.append((source, i * stream + j))
    return lax.ppermute(values, ("span", "stream"), pairs)


def on_device(velocity, strain, row_bins, cotangent):
    span, stream = lax.axis_size("span"), lax.axis_size("stream")
    cells, rows, width = velocity.shape[1:]
    tables = Tables(cells, span)
    slab = (rows, width)

    def shaped(*leading):
        return jax.ShapeDtypeStruct(leading + slab, jnp.float32)

    bins = jnp.broadcast_to(row_bins[:, None], (rows, LANES))
    far_v = [from_ahead(velocity, shift) for shift in range(1, span)]
    work = cells * rows * width
    size, size_ends, cot_ends = call(
        functools.partial(prepare_kernel, tables),
        [shaped(cells), shaped(2), shaped(12)],
        60 * work,
        strain,
        cotangent,
    )
    far_size = [from_ahead(size_ends, shift) for shift in range(1, span)]
    far_cot = [from_ahead(cot_ends, shift) for shift in range(1, span)]
    leonard, model, duals, message, sums = call(
        functools.partial(forward_kernel, tables),
        [shaped(6, cells), shaped(6, cells), shaped(9, cells), shaped(30), jax.ShapeDtypeStruct((8, LANES), jnp.float32)],
        400 * work,
        velocity,
        strain,
        cotangent,
        size,
        bins,
        *far_v,
        *far_size,
    )
    most_rows = 2 * rows * stream // NBINS
    reach = min(-(-(most_rows - 1) // rows), (stream - 1) // 2)
    all_sums = [sums]
    for span_shift in range(span):
        for stream_shift in range(-reach, reach + 1):
            if span_shift or stream_shift:
                all_sums.append(from_place(sums, span_shift, stream_shift))
    far_message = [from_ahead(message, shift) for shift in range(1, span)]
    (parts,) = call(
        functools.partial(local_kernel, tables), [shaped(12, cells)], 300 * work, velocity, cotangent, leonard, model, duals
    )
    return tuple(
        call(
            functools.partial(finish_kernel, tables, len(all_sums)),
            [shaped(6, cells), shaped(3, cells)],
            200 * work,
            velocity,
            leonard,
            model,
            parts,
            bins,
            *all_sums,
            *far_cot,
            *far_message,
        )
    )


def solution(mesh):
    fields = P(None, "span", "stream", None)
    return jax.shard_map(
        on_device,
        mesh=mesh,
        in_specs=(fields, fields, P("stream"), fields),
        out_specs=(fields, fields),
        check_vma=False,
    )
```

```python
import functools

import jax
import jax.numpy as jnp
import numpy as np
from jax import lax
from jax.experimental import pallas as pl
from jax.experimental.pallas import tpu as pltpu
from jax.sharding import PartitionSpec as P

NBINS = 64
FILTER_ALPHA = 0.45
CENTER_WEIGHT = 0.95
SIDE_WEIGHT = 0.475
STRAIN_FLOOR = 0.25
EPSILON = 1e-06
INDEX_PAIRS = ((0, 0), (0, 1), (0, 2), (1, 1), (1, 2), (2, 2))
PAIR_WEIGHTS = (1.0, 2.0, 2.0, 1.0, 2.0, 1.0)
PAIR_OF = ((0, 1, 2), (1, 3, 4), (2, 4, 5))
LANES = 128


def filter_row(extent):
    eye = np.eye(extent)
    ring = np.roll(eye, 1, axis=1) + np.roll(eye, -1, axis=1)
    system = eye + FILTER_ALPHA * ring
    side = CENTER_WEIGHT * eye + SIDE_WEIGHT * ring
    return np.linalg.solve(system, side)[0]


def end_weights(cells):
    weights = np.zeros((2, cells))
    weights[0, 0] = 1.0
    weights[1, cells - 1] = 1.0
    inner = cells - 2
    if inner > 0:
        system = np.eye(inner) + FILTER_ALPHA * (np.eye(inner, k=1) + np.eye(inner, k=-1))
        right = np.zeros((inner, 2))
        right[0, 0] = -FILTER_ALPHA
        right[inner - 1, 1] = -FILTER_ALPHA
        weights[:, 1:-1] = np.linalg.solve(system, right).T
    return weights


class Tables:
    def __init__(self, cells, devices):
        row = filter_row(cells * devices)
        extent = cells * devices
        self.cells = cells
        self.devices = devices
        self.own = [[float(row[(z - w) % extent]) for w in range(cells)] for z in range(cells)]
        self.ends = [[float(x) for x in line] for line in end_weights(cells)]
        self.couple = [
            [[float(row[(z - shift * cells - w) % extent]) for w in (0, cells - 1)] for z in range(cells)]
            for shift in range(devices)
        ]

    def project(self, values):
        return [weighted(line, values) for line in self.ends]

    def inside(self, values):
        return [weighted(line, values) for line in self.own]

    def outside(self, shift, ends):
        return [weighted(line, ends) for line in self.couple[shift]]


def weighted(weights, values):
    total = None
    for weight, value in zip(weights, values):
        if weight == 0.0:
            continue
        term = value if weight == 1.0 else value * weight
        total = term if total is None else total + term
    return total


def add_lists(left, right):
    return [x + y for x, y in zip(left, right)]


def halves(width):
    return [pl.ds(start, LANES) for start in range(0, width, LANES)]


def sum_up(terms):
    total = terms[0]
    for term in terms[1:]:
        total = total + term
    return total


def prepare_kernel(tables, strain_ref, size_ref, size_ends_ref):
    cells = tables.cells
    for lanes in halves(strain_ref.shape[-1]):
        size = []
        for z in range(cells):
            values = [strain_ref[k, z, :, lanes] for k in range(6)]
            total = sum_up([weight * (value * value) for weight, value in zip(PAIR_WEIGHTS, values)])
            size.append(jnp.sqrt(jnp.maximum(2.0 * total, STRAIN_FLOOR)))
            size_ref[z, :, lanes] = size[z]
        for end, value in enumerate(tables.project(size)):
            size_ends_ref[end, :, lanes] = value


def products_of(v):
    return [[x * y for x, y in zip(v[a], v[b])] for a, b in INDEX_PAIRS]


def filtered_block(tables, place, fields, ends):
    filtered = [tables.inside(field) for field in fields]
    for other in range(tables.devices):
        if other != place:
            shift = (other - place) % tables.devices
            filtered = [add_lists(near, tables.outside(shift, far)) for near, far in zip(filtered, ends[other])]
    return filtered


def plain_dual(tensor, vector, a, cells):
    return [sum_up([tensor[PAIR_OF[a][b]][z] * vector[b][z] for b in range(3)]) for z in range(cells)]


def weighted_dual(tensor, vector, a, cells):
    plain = plain_dual(tensor, vector, a, cells)
    return [plain[z] + tensor[PAIR_OF[a][a]][z] * vector[a][z] for z in range(cells)]


def forward_kernel(tables, *refs):
    peers = tables.devices - 1
    cells = tables.cells
    v_ref, strain_ref, cot_ref, size_ref, bins_ref = refs[:5]
    far_v_refs = refs[5 : 5 + peers]
    far_size_refs = refs[5 + peers : 5 + 2 * peers]
    smooth_ref, leonard_ref, model_ref, dual_ref, message_ref, sums_ref = refs[5 + 2 * peers :]
    cross, square, blame = [], [], []
    for lanes in halves(v_ref.shape[-1]):
        v = [[v_ref[a, z, :, lanes] for z in range(cells)] for a in range(3)]
        size = [size_ref[z, :, lanes] for z in range(cells)]
        products = products_of(v)
        ends = [None]
        for far_v_ref, far_size_ref in zip(far_v_refs, far_size_refs):
            far = [[far_v_ref[a, z, :, lanes] for z in range(cells)] for a in range(3)]
            ends.append([tables.project(field) for field in far + products_of(far)])
            ends[-1].append([far_size_ref[end, :, lanes] for end in range(2)])
        filtered = filtered_block(tables, 0, v + products + [size], ends)
        smooth_v = filtered[:3]
        factor = [2.0 * (4.0 * filtered[9][z] - size[z]) for z in range(cells)]
        model = []
        for k, (a, b) in enumerate(INDEX_PAIRS):
            model.append([])
            for z in range(cells):
                coarse = smooth_v[a][z] * smooth_v[b][z]
                leonard = filtered[3 + k][z] - coarse
                term = products[k][z] - coarse + factor[z] * strain_ref[k, z, :, lanes]
                model[k].append(term)
                leonard_ref[k, z, :, lanes] = leonard
                model_ref[k, z, :, lanes] = term
                scaled = PAIR_WEIGHTS[k] * term
                cross.append(scaled * leonard)
                square.append(scaled * term)
                blame.append(term * cot_ref[k, z, :, lanes])
            cross, square, blame = [sum_up(cross)], [sum_up(square)], [sum_up(blame)]
            for end, value in enumerate(tables.project(model[k])):
                message_ref[2 * k + end, :, lanes] = value
        for a in range(3):
            dual = [2.0 * x for x in plain_dual(model, smooth_v, a, cells)]
            for z in range(cells):
                smooth_ref[a, z, :, lanes] = smooth_v[a][z]
                dual_ref[a, z, :, lanes] = dual[z]
            for end, value in enumerate(tables.project(dual)):
                message_ref[12 + 2 * a + end, :, lanes] = value
    lane = lax.broadcasted_iota(jnp.int32, bins_ref.shape, 1)
    mine = bins_ref[...] == lane
    place = lax.broadcasted_iota(jnp.int32, (8, LANES), 0)
    table = jnp.zeros((8, LANES), jnp.float32)
    for index, sums in enumerate((cross, square, blame)):
        per_row = jnp.sum(sums[0], axis=1, keepdims=True)
        per_bin = jnp.sum(jnp.where(mine, per_row, 0.0), axis=0, keepdims=True)
        table = jnp.where(place == index, per_bin, table)
    sums_ref[...] = table
    message_ref[18, 0:8, 0:LANES] = table


def local_kernel(tables, *refs):
    peers = tables.devices - 1
    cells = tables.cells
    v_ref, cot_ref, smooth_ref, leonard_ref, model_ref, dual_ref = refs[:6]
    far_v_refs = refs[6 : 6 + peers]
    far_cot_refs = refs[6 + peers : 6 + 2 * peers]
    parts_ref = refs[-1]
    for lanes in halves(v_ref.shape[-1]):

        def load(ref, count):
            return [[ref[f, z, :, lanes] for z in range(cells)] for f in range(count)]

        fields, ends = [], []
        for ref in (v_ref, *far_v_refs):
            v = load(ref, 3)
            fields.append(v + products_of(v))
            ends.append([tables.project(field) for field in fields[-1]])
        v = fields[0][:3]
        cot, model, leonard, smooth_v = load(cot_ref, 6), load(model_ref, 6), load(leonard_ref, 6), load(smooth_ref, 3)
        smooth_cot = [tables.inside(field) for field in cot]
        duals = [weighted_dual(cot, smooth_v, a, cells) for a in range(3)]
        others = [plain_dual(leonard, smooth_v, a, cells) for a in range(3)]
        smooth_duals = [tables.inside(field) for field in duals]
        smooth_others = [tables.inside(field) for field in others]
        for place in range(1, tables.devices):
            far_cot = load(far_cot_refs[place - 1], 6)
            filtered = filtered_block(tables, place, fields[place], ends)
            far_smooth = filtered[:3]
            far_leonard = [
                [filtered[3 + k][z] - far_smooth[a][z] * far_smooth[b][z] for z in range(cells)]
                for k, (a, b) in enumerate(INDEX_PAIRS)
            ]
            for k in range(6):
                far = tables.outside(place, tables.project(far_cot[k]))
                smooth_cot[k] = add_lists(smooth_cot[k], far)
            for a in range(3):
                far = tables.outside(place, tables.project(weighted_dual(far_cot, far_smooth, a, cells)))
                smooth_duals[a] = add_lists(smooth_duals[a], far)
                far = tables.outside(place, tables.project(plain_dual(far_leonard, far_smooth, a, cells)))
                smooth_others[a] = add_lists(smooth_others[a], far)
        inner = [add_lists(tables.inside(model[k]), leonard[k]) for k in range(6)]
        for a in range(3):
            first = weighted_dual(smooth_cot, v, a, cells)
            second = weighted_dual(cot, v, a, cells)
            dual = tables.inside([dual_ref[a, z, :, lanes] for z in range(cells)])
            third = plain_dual(inner, v, a, cells)
            fourth = plain_dual(model, v, a, cells)
            for z in range(cells):
                parts_ref[a, z, :, lanes] = first[z] - smooth_duals[a][z]
                parts_ref[3 + a, z, :, lanes] = smooth_duals[a][z] - second[z]
                parts_ref[6 + a, z, :, lanes] = 2.0 * (third[z] - smooth_others[a][z]) - dual[z]
                parts_ref[9 + a, z, :, lanes] = 2.0 * dual[z] - 4.0 * fourth[z]


def finish_kernel(tables, count, *refs):
    peers = tables.devices - 1
    cells = tables.cells
    v_ref, leonard_ref, model_ref, parts_ref, bins_ref = refs[:5]
    sums_refs = refs[5 : 5 + count]
    far_message_refs = refs[5 + count : 5 + count + peers]
    residual_hbm, grad_hbm, residual_ref, grad_ref, left = refs[5 + count + peers :]
    total = sum_up([ref[...] for ref in sums_refs] + [ref[18, 0:8, 0:LANES] for ref in far_message_refs])
    inverse = 1.0 / (total[1:2] + EPSILON)
    rows = v_ref.shape[2]
    lane = lax.broadcasted_iota(jnp.int32, bins_ref.shape, 1)
    mine = bins_ref[...] == lane

    def of_rows(per_bin):
        column = jnp.sum(jnp.where(mine, per_bin, 0.0), axis=1, keepdims=True)
        return jnp.broadcast_to(column, (rows, LANES))

    coefficient = of_rows(total[0:1] * inverse)
    pull = of_rows(-(total[2:3] * inverse))
    copies = []
    for k in range(6):
        for lanes in halves(v_ref.shape[-1]):
            for z in range(cells):
                residual_ref[k, z, :, lanes] = (
                    leonard_ref[k, z, :, lanes] - coefficient * model_ref[k, z, :, lanes]
                )
        copies.append(pltpu.make_async_copy(residual_ref.at[k], residual_hbm.at[k], left.at[k]))
        copies[k].start()
    for lanes in halves(v_ref.shape[-1]):
        v = [[v_ref[a, z, :, lanes] for z in range(cells)] for a in range(3)]
        from_model = [[] for _ in range(6)]
        from_dual = [[] for _ in range(3)]
        for place, ends in enumerate(far_message_refs, start=1):
            for k in range(6):
                from_model[k].append(tables.outside(place, [2.0 * ends[2 * k + end, :, lanes] for end in range(2)]))
            for a in range(3):
                pair = [(2.0 * coefficient - 1.0) * ends[12 + 2 * a + end, :, lanes] for end in range(2)]
                from_dual[a].append(tables.outside(place, pair))
        from_model = [functools.reduce(add_lists, lists) if lists else None for lists in from_model]
        from_dual = [functools.reduce(add_lists, lists) if lists else None for lists in from_dual]
        for a in range(3):
            for z in range(cells):
                pulled = parts_ref[6 + a, z, :, lanes] + coefficient * parts_ref[9 + a, z, :, lanes]
                if peers:
                    terms = [from_model[PAIR_OF[a][b]][z] * v[b][z] for b in range(3)]
                    pulled = pulled + from_dual[a][z] + sum_up(terms)
                grad_ref[a, z, :, lanes] = (
                    parts_ref[a, z, :, lanes] + coefficient * parts_ref[3 + a, z, :, lanes] + pull * pulled
                )
    for a in range(3):
        copies.append(pltpu.make_async_copy(grad_ref.at[a], grad_hbm.at[a], left.at[6 + a]))
        copies[6 + a].start()
    for copy in copies:
        copy.wait()


WHOLE = pl.BlockSpec(memory_space=pltpu.VMEM)
REMAIN = pl.BlockSpec(memory_space=pltpu.HBM)


def call(kernel, outs, operations, *operands, in_specs=None, out_specs=None, scratch=()):
    nbytes = sum(4 * int(np.prod(x.shape)) for x in (*operands, *outs))
    return pl.pallas_call(
        kernel,
        out_shape=outs,
        in_specs=in_specs or [WHOLE] * len(operands),
        out_specs=out_specs or [WHOLE] * len(outs),
        scratch_shapes=list(scratch),
        compiler_params=pltpu.CompilerParams(vmem_limit_bytes=32 * 1024 * 1024),
        cost_estimate=pl.CostEstimate(flops=operations, bytes_accessed=nbytes, transcendentals=0),
    )(*operands)


def from_ahead(values, shift):
    peers = lax.axis_size("span")
    return lax.ppermute(values, "span", [((i + shift) % peers, i) for i in range(peers)])


def swapped(values, span_shift, distance, parity):
    span, stream = lax.axis_size("span"), lax.axis_size("stream")
    pairs = []
    for i in range(span):
        row = ((i + span_shift) % span) * stream
        for j in range(stream - distance):
            if (j // distance) % 2 == parity:
                pairs.append((row + j, i * stream + j + distance))
                pairs.append((row + j + distance, i * stream + j))
    return lax.ppermute(values, ("span", "stream"), pairs)


def on_device(velocity, strain, row_bins, cotangent):
    span, stream = lax.axis_size("span"), lax.axis_size("stream")
    cells, rows, width = velocity.shape[1:]
    tables = Tables(cells, span)
    slab = (rows, width)

    def shaped(*leading):
        return jax.ShapeDtypeStruct(leading + slab, jnp.float32)

    bins = jnp.broadcast_to(row_bins[:, None], (rows, LANES))
    far_v = [from_ahead(velocity, shift) for shift in range(1, span)]
    far_cot = [from_ahead(cotangent, shift) for shift in range(1, span)]
    work = cells * rows * width
    size, size_ends = call(functools.partial(prepare_kernel, tables), [shaped(cells), shaped(2)], 40 * work, strain)
    far_size = [from_ahead(size_ends, shift) for shift in range(1, span)]
    smooth, leonard, model, dual, message, sums = call(
        functools.partial(forward_kernel, tables),
        [
            shaped(3, cells),
            shaped(6, cells),
            shaped(6, cells),
            shaped(3, cells),
            shaped(19),
            jax.ShapeDtypeStruct((8, LANES), jnp.float32),
        ],
        300 * work,
        velocity,
        strain,
        cotangent,
        size,
        bins,
        *far_v,
        *far_size,
    )
    far_message = [from_ahead(message, shift) for shift in range(1, span)]
    most_rows = 2 * rows * stream // NBINS
    reach = min(-(-(most_rows - 1) // rows), stream - 1)
    all_sums = [sums]
    for span_shift in range(span):
        for distance in range(1, reach + 1):
            for parity in range(2):
                all_sums.append(swapped(sums, span_shift, distance, parity))
    (parts,) = call(
        functools.partial(local_kernel, tables),
        [shaped(12, cells)],
        500 * work,
        velocity,
        cotangent,
        smooth,
        leonard,
        model,
        dual,
        *far_v,
        *far_cot,
    )
    outs = [shaped(6, cells), shaped(3, cells)]
    return tuple(
        call(
            functools.partial(finish_kernel, tables, len(all_sums)),
            outs,
            200 * work,
            velocity,
            leonard,
            model,
            parts,
            bins,
            *all_sums,
            *far_message,
            out_specs=[REMAIN] * 2,
            scratch=[pltpu.VMEM(x.shape, x.dtype) for x in outs] + [pltpu.SemaphoreType.DMA((9,))],
        )
    )


def solution(mesh):
    fields = P(None, "span", "stream", None)
    return jax.shard_map(
        on_device,
        mesh=mesh,
        in_specs=(fields, fields, P("stream"), fields),
        out_specs=(fields, fields),
        check_vma=False,
    )
```

```python
import functools

import jax
import jax.numpy as jnp
import numpy as np
from jax import lax
from jax.experimental import pallas as pl
from jax.experimental.pallas import tpu as pltpu
from jax.sharding import PartitionSpec as P

NBINS = 64
FILTER_ALPHA = 0.45
CENTER_WEIGHT = 0.95
SIDE_WEIGHT = 0.475
STRAIN_FLOOR = 0.25
EPSILON = 1e-06
INDEX_PAIRS = ((0, 0), (0, 1), (0, 2), (1, 1), (1, 2), (2, 2))
PAIR_WEIGHTS = (1.0, 2.0, 2.0, 1.0, 2.0, 1.0)
PAIR_OF = ((0, 1, 2), (1, 3, 4), (2, 4, 5))
LANES = 128


def filter_row(extent):
    eye = np.eye(extent)
    ring = np.roll(eye, 1, axis=1) + np.roll(eye, -1, axis=1)
    system = eye + FILTER_ALPHA * ring
    side = CENTER_WEIGHT * eye + SIDE_WEIGHT * ring
    return np.linalg.solve(system, side)[0]


def end_weights(cells):
    weights = np.zeros((2, cells))
    weights[0, 0] = 1.0
    weights[1, cells - 1] = 1.0
    inner = cells - 2
    if inner > 0:
        system = np.eye(inner) + FILTER_ALPHA * (np.eye(inner, k=1) + np.eye(inner, k=-1))
        right = np.zeros((inner, 2))
        right[0, 0] = -FILTER_ALPHA
        right[inner - 1, 1] = -FILTER_ALPHA
        weights[:, 1:-1] = np.linalg.solve(system, right).T
    return weights


class Tables:
    def __init__(self, cells, devices):
        row = filter_row(cells * devices)
        extent = cells * devices
        self.cells = cells
        self.devices = devices
        self.own = [[float(row[(z - w) % extent]) for w in range(cells)] for z in range(cells)]
        self.ends = [[float(x) for x in line] for line in end_weights(cells)]
        self.couple = [
            [[float(row[(z - shift * cells - w) % extent]) for w in (0, cells - 1)] for z in range(cells)]
            for shift in range(devices)
        ]

    def project(self, values):
        return [weighted(line, values) for line in self.ends]

    def inside(self, values):
        return [weighted(line, values) for line in self.own]

    def outside(self, shift, ends):
        return [weighted(line, ends) for line in self.couple[shift]]


def weighted(weights, values):
    total = None
    for weight, value in zip(weights, values):
        if weight == 0.0:
            continue
        term = value if weight == 1.0 else value * weight
        total = term if total is None else total + term
    return total


def add_lists(left, right):
    return [x + y for x, y in zip(left, right)]


def halves(width):
    return [pl.ds(start, LANES) for start in range(0, width, LANES)]


def sum_up(terms):
    total = terms[0]
    for term in terms[1:]:
        total = total + term
    return total


def fetch(source, target, arrived):
    copies = [pltpu.make_async_copy(source.at[k], target.at[k], arrived.at[k]) for k in range(source.shape[0])]
    for copy in copies:
        copy.start()
    return copies


def prepare_kernel(tables, strain_hbm, strain_ref, size_ref, size_ends_ref, arrived):
    cells = tables.cells
    for copy in fetch(strain_hbm, strain_ref, arrived):
        copy.wait()
    for lanes in halves(strain_ref.shape[-1]):
        size = []
        for z in range(cells):
            values = [strain_ref[k, z, :, lanes] for k in range(6)]
            total = sum_up([weight * (value * value) for weight, value in zip(PAIR_WEIGHTS, values)])
            size.append(jnp.sqrt(jnp.maximum(2.0 * total, STRAIN_FLOOR)))
            size_ref[z, :, lanes] = size[z]
        for end, value in enumerate(tables.project(size)):
            size_ends_ref[end, :, lanes] = value


def fetch_kernel(cot_hbm, cot_ref, arrived):
    for copy in fetch(cot_hbm, cot_ref, arrived):
        copy.wait()


def products_of(v):
    return [[x * y for x, y in zip(v[a], v[b])] for a, b in INDEX_PAIRS]


def filtered_block(tables, place, fields, ends):
    filtered = [tables.inside(field) for field in fields]
    for other in range(tables.devices):
        if other != place:
            shift = (other - place) % tables.devices
            filtered = [add_lists(near, tables.outside(shift, far)) for near, far in zip(filtered, ends[other])]
    return filtered


def plain_dual(tensor, vector, a, cells):
    return [sum_up([tensor[PAIR_OF[a][b]][z] * vector[b][z] for b in range(3)]) for z in range(cells)]


def weighted_dual(tensor, vector, a, cells):
    plain = plain_dual(tensor, vector, a, cells)
    return [plain[z] + tensor[PAIR_OF[a][a]][z] * vector[a][z] for z in range(cells)]


def forward_kernel(tables, *refs):
    peers = tables.devices - 1
    cells = tables.cells
    v_ref, strain_ref, cot_ref, size_ref, bins_ref = refs[:5]
    far_v_refs = refs[5 : 5 + peers]
    far_size_refs = refs[5 + peers : 5 + 2 * peers]
    smooth_ref, leonard_ref, model_ref, dual_ref, message_ref, sums_ref = refs[5 + 2 * peers :]
    cross, square, blame = [], [], []
    for lanes in halves(v_ref.shape[-1]):
        v = [[v_ref[a, z, :, lanes] for z in range(cells)] for a in range(3)]
        size = [size_ref[z, :, lanes] for z in range(cells)]
        products = products_of(v)
        ends = [None]
        for far_v_ref, far_size_ref in zip(far_v_refs, far_size_refs):
            far = [[far_v_ref[a, z, :, lanes] for z in range(cells)] for a in range(3)]
            ends.append([tables.project(field) for field in far + products_of(far)])
            ends[-1].append([far_size_ref[end, :, lanes] for end in range(2)])
        filtered = filtered_block(tables, 0, v + products + [size], ends)
        smooth_v = filtered[:3]
        factor = [2.0 * (4.0 * filtered[9][z] - size[z]) for z in range(cells)]
        model = []
        for k, (a, b) in enumerate(INDEX_PAIRS):
            model.append([])
            for z in range(cells):
                coarse = smooth_v[a][z] * smooth_v[b][z]
                leonard = filtered[3 + k][z] - coarse
                term = products[k][z] - coarse + factor[z] * strain_ref[k, z, :, lanes]
                model[k].append(term)
                leonard_ref[k, z, :, lanes] = leonard
                model_ref[k, z, :, lanes] = term
                scaled = PAIR_WEIGHTS[k] * term
                cross.append(scaled * leonard)
                square.append(scaled * term)
                blame.append(term * cot_ref[k, z, :, lanes])
            cross, square, blame = [sum_up(cross)], [sum_up(square)], [sum_up(blame)]
            for end, value in enumerate(tables.project(model[k])):
                message_ref[2 * k + end, :, lanes] = value
        for a in range(3):
            dual = [2.0 * x for x in plain_dual(model, smooth_v, a, cells)]
            for z in range(cells):
                smooth_ref[a, z, :, lanes] = smooth_v[a][z]
                dual_ref[a, z, :, lanes] = dual[z]
            for end, value in enumerate(tables.project(dual)):
                message_ref[12 + 2 * a + end, :, lanes] = value
    lane = lax.broadcasted_iota(jnp.int32, bins_ref.shape, 1)
    mine = bins_ref[...] == lane
    place = lax.broadcasted_iota(jnp.int32, (8, LANES), 0)
    table = jnp.zeros((8, LANES), jnp.float32)
    for index, sums in enumerate((cross, square, blame)):
        per_row = jnp.sum(sums[0], axis=1, keepdims=True)
        per_bin = jnp.sum(jnp.where(mine, per_row, 0.0), axis=0, keepdims=True)
        table = jnp.where(place == index, per_bin, table)
    for index in range(sums_ref.shape[0]):
        sums_ref[index] = table


def local_kernel(tables, *refs):
    peers = tables.devices - 1
    cells = tables.cells
    v_ref, cot_ref, smooth_ref, leonard_ref, model_ref, dual_ref = refs[:6]
    far_v_refs = refs[6 : 6 + peers]
    far_cot_refs = refs[6 + peers : 6 + 2 * peers]
    parts_ref = refs[-1]
    for lanes in halves(v_ref.shape[-1]):

        def load(ref, count):
            return [[ref[f, z, :, lanes] for z in range(cells)] for f in range(count)]

        fields, ends = [], []
        for ref in (v_ref, *far_v_refs):
            v = load(ref, 3)
            fields.append(v + products_of(v))
            ends.append([tables.project(field) for field in fields[-1]])
        v = fields[0][:3]
        cot, model, leonard, smooth_v = load(cot_ref, 6), load(model_ref, 6), load(leonard_ref, 6), load(smooth_ref, 3)
        smooth_cot = [tables.inside(field) for field in cot]
        duals = [weighted_dual(cot, smooth_v, a, cells) for a in range(3)]
        others = [plain_dual(leonard, smooth_v, a, cells) for a in range(3)]
        smooth_duals = [tables.inside(field) for field in duals]
        smooth_others = [tables.inside(field) for field in others]
        for place in range(1, tables.devices):
            far_cot = load(far_cot_refs[place - 1], 6)
            filtered = filtered_block(tables, place, fields[place], ends)
            far_smooth = filtered[:3]
            far_leonard = [
                [filtered[3 + k][z] - far_smooth[a][z] * far_smooth[b][z] for z in range(cells)]
                for k, (a, b) in enumerate(INDEX_PAIRS)
            ]
            for k in range(6):
                far = tables.outside(place, tables.project(far_cot[k]))
                smooth_cot[k] = add_lists(smooth_cot[k], far)
            for a in range(3):
                far = tables.outside(place, tables.project(weighted_dual(far_cot, far_smooth, a, cells)))
                smooth_duals[a] = add_lists(smooth_duals[a], far)
                far = tables.outside(place, tables.project(plain_dual(far_leonard, far_smooth, a, cells)))
                smooth_others[a] = add_lists(smooth_others[a], far)
        inner = [add_lists(tables.inside(model[k]), leonard[k]) for k in range(6)]
        for a in range(3):
            first = weighted_dual(smooth_cot, v, a, cells)
            second = weighted_dual(cot, v, a, cells)
            dual = tables.inside([dual_ref[a, z, :, lanes] for z in range(cells)])
            third = plain_dual(inner, v, a, cells)
            fourth = plain_dual(model, v, a, cells)
            for z in range(cells):
                parts_ref[a, z, :, lanes] = first[z] - smooth_duals[a][z]
                parts_ref[3 + a, z, :, lanes] = smooth_duals[a][z] - second[z]
                parts_ref[6 + a, z, :, lanes] = 2.0 * (third[z] - smooth_others[a][z]) - dual[z]
                parts_ref[9 + a, z, :, lanes] = 2.0 * dual[z] - 4.0 * fourth[z]


def finish_kernel(tables, *refs):
    peers = tables.devices - 1
    cells = tables.cells
    v_ref, leonard_ref, model_ref, parts_ref, bins_ref = refs[:5]
    sums_ref = refs[5]
    far_message_refs = refs[6 : 6 + peers]
    residual_hbm, grad_hbm, residual_ref, grad_ref, left = refs[6 + peers :]
    total = jnp.sum(sums_ref[...], axis=0)
    inverse = 1.0 / (total[1:2] + EPSILON)
    rows = v_ref.shape[2]
    lane = lax.broadcasted_iota(jnp.int32, bins_ref.shape, 1)
    mine = bins_ref[...] == lane

    def of_rows(per_bin):
        column = jnp.sum(jnp.where(mine, per_bin, 0.0), axis=1, keepdims=True)
        return jnp.broadcast_to(column, (rows, LANES))

    coefficient = of_rows(total[0:1] * inverse)
    pull = of_rows(-(total[2:3] * inverse))
    copies = []
    for k in range(6):
        for lanes in halves(v_ref.shape[-1]):
            for z in range(cells):
                residual_ref[k, z, :, lanes] = (
                    leonard_ref[k, z, :, lanes] - coefficient * model_ref[k, z, :, lanes]
                )
        copies.append(pltpu.make_async_copy(residual_ref.at[k], residual_hbm.at[k], left.at[k]))
        copies[k].start()
    for lanes in halves(v_ref.shape[-1]):
        v = [[v_ref[a, z, :, lanes] for z in range(cells)] for a in range(3)]
        from_model = [[] for _ in range(6)]
        from_dual = [[] for _ in range(3)]
        for place, ends in enumerate(far_message_refs, start=1):
            for k in range(6):
                from_model[k].append(tables.outside(place, [2.0 * ends[2 * k + end, :, lanes] for end in range(2)]))
            for a in range(3):
                pair = [(2.0 * coefficient - 1.0) * ends[12 + 2 * a + end, :, lanes] for end in range(2)]
                from_dual[a].append(tables.outside(place, pair))
        from_model = [functools.reduce(add_lists, lists) if lists else None for lists in from_model]
        from_dual = [functools.reduce(add_lists, lists) if lists else None for lists in from_dual]
        for a in range(3):
            for z in range(cells):
                pulled = parts_ref[6 + a, z, :, lanes] + coefficient * parts_ref[9 + a, z, :, lanes]
                if peers:
                    terms = [from_model[PAIR_OF[a][b]][z] * v[b][z] for b in range(3)]
                    pulled = pulled + from_dual[a][z] + sum_up(terms)
                grad_ref[a, z, :, lanes] = (
                    parts_ref[a, z, :, lanes] + coefficient * parts_ref[3 + a, z, :, lanes] + pull * pulled
                )
    for a in range(3):
        copies.append(pltpu.make_async_copy(grad_ref.at[a], grad_hbm.at[a], left.at[6 + a]))
        copies[6 + a].start()
    for copy in copies:
        copy.wait()


WHOLE = pl.BlockSpec(memory_space=pltpu.VMEM)
REMAIN = pl.BlockSpec(memory_space=pltpu.HBM)


def call(kernel, outs, operations, *operands, in_specs=None, out_specs=None, scratch=()):
    nbytes = sum(4 * int(np.prod(x.shape)) for x in (*operands, *outs))
    return pl.pallas_call(
        kernel,
        out_shape=outs,
        in_specs=in_specs or [WHOLE] * len(operands),
        out_specs=out_specs or [WHOLE] * len(outs),
        scratch_shapes=list(scratch),
        compiler_params=pltpu.CompilerParams(vmem_limit_bytes=32 * 1024 * 1024),
        cost_estimate=pl.CostEstimate(flops=operations, bytes_accessed=nbytes, transcendentals=0),
    )(*operands)


def from_ahead(values, shift):
    peers = lax.axis_size("span")
    return lax.ppermute(values, "span", [((i + shift) % peers, i) for i in range(peers)])


def on_device(velocity, strain, row_bins, cotangent):
    span, stream = lax.axis_size("span"), lax.axis_size("stream")
    cells, rows, width = velocity.shape[1:]
    tables = Tables(cells, span)
    slab = (rows, width)

    def shaped(*leading):
        return pltpu.VMEM(leading + slab, jnp.float32)

    bins = jnp.broadcast_to(row_bins[:, None], (rows, LANES))
    far_v = [from_ahead(velocity, shift) for shift in range(1, span)]
    work = cells * rows * width
    near_strain, size, size_ends = call(
        functools.partial(prepare_kernel, tables),
        [shaped(6, cells), shaped(cells), shaped(2)],
        40 * work,
        pltpu.with_memory_space_constraint(strain, pltpu.HBM),
        in_specs=[REMAIN],
        scratch=[pltpu.SemaphoreType.DMA((6,))],
    )
    size_ends, sent_cot = lax.optimization_barrier((size_ends, cotangent))
    far_size = [from_ahead(size_ends, shift) for shift in range(1, span)]
    far_cot = [from_ahead(sent_cot, shift) for shift in range(1, span)]
    (near_cot,) = call(
        fetch_kernel,
        [shaped(6, cells)],
        work,
        pltpu.with_memory_space_constraint(cotangent, pltpu.HBM),
        in_specs=[REMAIN],
        scratch=[pltpu.SemaphoreType.DMA((6,))],
    )
    smooth, leonard, model, dual, message, sums = call(
        functools.partial(forward_kernel, tables),
        [
            shaped(3, cells),
            shaped(6, cells),
            shaped(6, cells),
            shaped(3, cells),
            shaped(18),
            pltpu.VMEM((span * stream, 8, LANES), jnp.float32),
        ],
        300 * work,
        velocity,
        near_strain,
        near_cot,
        size,
        bins,
        *far_v,
        *far_size,
    )
    far_message = [from_ahead(message, shift) for shift in range(1, span)]
    all_sums = lax.all_to_all(sums, ("span", "stream"), 0, 0, tiled=True)
    (parts,) = call(
        functools.partial(local_kernel, tables),
        [shaped(12, cells)],
        500 * work,
        velocity,
        near_cot,
        smooth,
        leonard,
        model,
        dual,
        *far_v,
        *far_cot,
    )
    outs = [jax.ShapeDtypeStruct((n, cells) + slab, jnp.float32) for n in (6, 3)]
    return tuple(
        call(
            functools.partial(finish_kernel, tables),
            outs,
            200 * work,
            velocity,
            leonard,
            model,
            parts,
            bins,
            all_sums,
            *far_message,
            out_specs=[REMAIN] * 2,
            scratch=[pltpu.VMEM(x.shape, x.dtype) for x in outs] + [pltpu.SemaphoreType.DMA((9,))],
        )
    )


def solution(mesh):
    fields = P(None, "span", "stream", None)
    return jax.shard_map(
        on_device,
        mesh=mesh,
        in_specs=(fields, fields, P("stream"), fields),
        out_specs=(fields, fields),
        check_vma=False,
    )
```

```python
import functools

import jax
import jax.numpy as jnp
import numpy as np
from jax import lax
from jax.experimental import pallas as pl
from jax.experimental.pallas import tpu as pltpu
from jax.sharding import PartitionSpec as P

NBINS = 64
FILTER_ALPHA = 0.45
CENTER_WEIGHT = 0.95
SIDE_WEIGHT = 0.475
STRAIN_FLOOR = 0.25
EPSILON = 1e-06
INDEX_PAIRS = ((0, 0), (0, 1), (0, 2), (1, 1), (1, 2), (2, 2))
PAIR_WEIGHTS = (1.0, 2.0, 2.0, 1.0, 2.0, 1.0)
PAIR_OF = ((0, 1, 2), (1, 3, 4), (2, 4, 5))
LANES = 128


def filter_row(extent):
    eye = np.eye(extent)
    ring = np.roll(eye, 1, axis=1) + np.roll(eye, -1, axis=1)
    system = eye + FILTER_ALPHA * ring
    side = CENTER_WEIGHT * eye + SIDE_WEIGHT * ring
    return np.linalg.solve(system, side)[0]


def end_weights(cells):
    weights = np.zeros((2, cells))
    weights[0, 0] = 1.0
    weights[1, cells - 1] = 1.0
    inner = cells - 2
    if inner > 0:
        system = np.eye(inner) + FILTER_ALPHA * (np.eye(inner, k=1) + np.eye(inner, k=-1))
        right = np.zeros((inner, 2))
        right[0, 0] = -FILTER_ALPHA
        right[inner - 1, 1] = -FILTER_ALPHA
        weights[:, 1:-1] = np.linalg.solve(system, right).T
    return weights


class Tables:
    def __init__(self, cells, devices):
        row = filter_row(cells * devices)
        extent = cells * devices
        self.cells = cells
        self.devices = devices
        self.own = [[float(row[(z - w) % extent]) for w in range(cells)] for z in range(cells)]
        self.ends = [[float(x) for x in line] for line in end_weights(cells)]
        self.couple = [
            [[float(row[(z - shift * cells - w) % extent]) for w in (0, cells - 1)] for z in range(cells)]
            for shift in range(devices)
        ]

    def project(self, values):
        return [weighted(line, values) for line in self.ends]

    def inside(self, values):
        return [weighted(line, values) for line in self.own]

    def outside(self, shift, ends):
        return [weighted(line, ends) for line in self.couple[shift]]


def weighted(weights, values):
    total = None
    for weight, value in zip(weights, values):
        if weight == 0.0:
            continue
        term = value if weight == 1.0 else value * weight
        total = term if total is None else total + term
    return total


def add_lists(left, right):
    return [x + y for x, y in zip(left, right)]


def halves(width):
    return [pl.ds(start, LANES) for start in range(0, width, LANES)]


def sum_up(terms):
    total = terms[0]
    for term in terms[1:]:
        total = total + term
    return total


def fetch(source, target, arrived):
    copies = [pltpu.make_async_copy(source.at[k], target.at[k], arrived.at[k]) for k in range(source.shape[0])]
    for copy in copies:
        copy.start()
    return copies


def prepare_kernel(tables, strain_hbm, strain_ref, size_ref, size_ends_ref, arrived):
    cells = tables.cells
    for copy in fetch(strain_hbm, strain_ref, arrived):
        copy.wait()
    for lanes in halves(strain_ref.shape[-1]):
        size = []
        for z in range(cells):
            values = [strain_ref[k, z, :, lanes] for k in range(6)]
            total = sum_up([weight * (value * value) for weight, value in zip(PAIR_WEIGHTS, values)])
            size.append(jnp.sqrt(jnp.maximum(2.0 * total, STRAIN_FLOOR)))
            size_ref[z, :, lanes] = size[z]
        for end, value in enumerate(tables.project(size)):
            size_ends_ref[end, :, lanes] = value


def fetch_kernel(cot_hbm, size_ends_ref, cot_ref, arrived):
    for copy in fetch(cot_hbm, cot_ref, arrived):
        copy.wait()


def products_of(v):
    return [[x * y for x, y in zip(v[a], v[b])] for a, b in INDEX_PAIRS]


def filtered_block(tables, place, fields, ends):
    filtered = [tables.inside(field) for field in fields]
    for other in range(tables.devices):
        if other != place:
            shift = (other - place) % tables.devices
            filtered = [add_lists(near, tables.outside(shift, far)) for near, far in zip(filtered, ends[other])]
    return filtered


def plain_dual(tensor, vector, a, cells):
    return [sum_up([tensor[PAIR_OF[a][b]][z] * vector[b][z] for b in range(3)]) for z in range(cells)]


def weighted_dual(tensor, vector, a, cells):
    plain = plain_dual(tensor, vector, a, cells)
    return [plain[z] + tensor[PAIR_OF[a][a]][z] * vector[a][z] for z in range(cells)]


def forward_kernel(tables, *refs):
    peers = tables.devices - 1
    cells = tables.cells
    v_ref, strain_ref, cot_ref, size_ref, bins_ref = refs[:5]
    far_v_refs = refs[5 : 5 + peers]
    far_size_refs = refs[5 + peers : 5 + 2 * peers]
    smooth_ref, leonard_ref, model_ref, sums_ref = refs[5 + 2 * peers :]
    cross, square, blame = [], [], []
    for lanes in halves(v_ref.shape[-1]):
        v = [[v_ref[a, z, :, lanes] for z in range(cells)] for a in range(3)]
        size = [size_ref[z, :, lanes] for z in range(cells)]
        products = products_of(v)
        ends = [None]
        for far_v_ref, far_size_ref in zip(far_v_refs, far_size_refs):
            far = [[far_v_ref[a, z, :, lanes] for z in range(cells)] for a in range(3)]
            ends.append([tables.project(field) for field in far + products_of(far)])
            ends[-1].append([far_size_ref[end, :, lanes] for end in range(2)])
        filtered = filtered_block(tables, 0, v + products + [size], ends)
        smooth_v = filtered[:3]
        factor = [2.0 * (4.0 * filtered[9][z] - size[z]) for z in range(cells)]
        for k, (a, b) in enumerate(INDEX_PAIRS):
            for z in range(cells):
                coarse = smooth_v[a][z] * smooth_v[b][z]
                leonard = filtered[3 + k][z] - coarse
                term = products[k][z] - coarse + factor[z] * strain_ref[k, z, :, lanes]
                leonard_ref[k, z, :, lanes] = leonard
                model_ref[k, z, :, lanes] = term
                scaled = PAIR_WEIGHTS[k] * term
                cross.append(scaled * leonard)
                square.append(scaled * term)
                blame.append(term * cot_ref[k, z, :, lanes])
            cross, square, blame = [sum_up(cross)], [sum_up(square)], [sum_up(blame)]
        for a in range(3):
            for z in range(cells):
                smooth_ref[a, z, :, lanes] = smooth_v[a][z]
    lane = lax.broadcasted_iota(jnp.int32, bins_ref.shape, 1)
    mine = bins_ref[...] == lane
    place = lax.broadcasted_iota(jnp.int32, (8, LANES), 0)
    table = jnp.zeros((8, LANES), jnp.float32)
    for index, sums in enumerate((cross, square, blame)):
        per_row = jnp.sum(sums[0], axis=1, keepdims=True)
        per_bin = jnp.sum(jnp.where(mine, per_row, 0.0), axis=0, keepdims=True)
        table = jnp.where(place == index, per_bin, table)
    sums_ref[...] = table


def message_kernel(tables, smooth_ref, model_ref, sums_ref, other_sums_ref, dual_ref, message_ref, pair_ref):
    cells = tables.cells
    pair_sums = sums_ref[...] + other_sums_ref[...]
    pair_ref[...] = pair_sums
    message_ref[18, 0:8, 0:LANES] = pair_sums
    for lanes in halves(model_ref.shape[-1]):
        model = [[model_ref[k, z, :, lanes] for z in range(cells)] for k in range(6)]
        smooth_v = [[smooth_ref[a, z, :, lanes] for z in range(cells)] for a in range(3)]
        for k in range(6):
            for end, value in enumerate(tables.project(model[k])):
                message_ref[2 * k + end, :, lanes] = value
        for a in range(3):
            dual = [2.0 * x for x in plain_dual(model, smooth_v, a, cells)]
            for z in range(cells):
                dual_ref[a, z, :, lanes] = dual[z]
            for end, value in enumerate(tables.project(dual)):
                message_ref[12 + 2 * a + end, :, lanes] = value


def local_kernel(tables, *refs):
    peers = tables.devices - 1
    cells = tables.cells
    v_ref, cot_ref, smooth_ref, leonard_ref, model_ref, dual_ref = refs[:6]
    far_v_refs = refs[6 : 6 + peers]
    far_cot_refs = refs[6 + peers : 6 + 2 * peers]
    parts_ref = refs[-1]
    for lanes in halves(v_ref.shape[-1]):

        def load(ref, count):
            return [[ref[f, z, :, lanes] for z in range(cells)] for f in range(count)]

        fields, ends = [], []
        for ref in (v_ref, *far_v_refs):
            v = load(ref, 3)
            fields.append(v + products_of(v))
            ends.append([tables.project(field) for field in fields[-1]])
        v = fields[0][:3]
        cot, model, leonard, smooth_v = load(cot_ref, 6), load(model_ref, 6), load(leonard_ref, 6), load(smooth_ref, 3)
        smooth_cot = [tables.inside(field) for field in cot]
        duals = [weighted_dual(cot, smooth_v, a, cells) for a in range(3)]
        others = [plain_dual(leonard, smooth_v, a, cells) for a in range(3)]
        smooth_duals = [tables.inside(field) for field in duals]
        smooth_others = [tables.inside(field) for field in others]
        for place in range(1, tables.devices):
            far_cot = load(far_cot_refs[place - 1], 6)
            filtered = filtered_block(tables, place, fields[place], ends)
            far_smooth = filtered[:3]
            far_leonard = [
                [filtered[3 + k][z] - far_smooth[a][z] * far_smooth[b][z] for z in range(cells)]
                for k, (a, b) in enumerate(INDEX_PAIRS)
            ]
            for k in range(6):
                far = tables.outside(place, tables.project(far_cot[k]))
                smooth_cot[k] = add_lists(smooth_cot[k], far)
            for a in range(3):
                far = tables.outside(place, tables.project(weighted_dual(far_cot, far_smooth, a, cells)))
                smooth_duals[a] = add_lists(smooth_duals[a], far)
                far = tables.outside(place, tables.project(plain_dual(far_leonard, far_smooth, a, cells)))
                smooth_others[a] = add_lists(smooth_others[a], far)
        inner = [add_lists(tables.inside(model[k]), leonard[k]) for k in range(6)]
        for a in range(3):
            first = weighted_dual(smooth_cot, v, a, cells)
            second = weighted_dual(cot, v, a, cells)
            dual = tables.inside([dual_ref[a, z, :, lanes] for z in range(cells)])
            third = plain_dual(inner, v, a, cells)
            fourth = plain_dual(model, v, a, cells)
            for z in range(cells):
                parts_ref[a, z, :, lanes] = first[z] - smooth_duals[a][z]
                parts_ref[3 + a, z, :, lanes] = smooth_duals[a][z] - second[z]
                parts_ref[6 + a, z, :, lanes] = 2.0 * (third[z] - smooth_others[a][z]) - dual[z]
                parts_ref[9 + a, z, :, lanes] = 2.0 * dual[z] - 4.0 * fourth[z]


def finish_kernel(tables, count, turning, *refs):
    peers = tables.devices - 1
    cells = tables.cells
    v_ref, leonard_ref, model_ref, parts_ref, bins_ref = refs[:5]
    pair_ref = refs[5]
    near_refs = refs[6 : 6 + count]
    far_message_refs = refs[6 + count : 6 + count + peers]
    residual_hbm, grad_hbm, residual_ref, grad_ref, left = refs[6 + count + peers :]
    total = sum_up([pair_ref[...]] + [ref[18, 0:8, 0:LANES] for ref in far_message_refs])
    near = sum_up([ref[...] for ref in near_refs])
    if turning:
        place = lax.axis_index("stream")
        inner = jnp.logical_and(place > 0, place < lax.axis_size("stream") - 1)
        near = jnp.where(inner, near, 0.0)
    total = total + near
    inverse = 1.0 / (total[1:2] + EPSILON)
    rows = v_ref.shape[2]
    lane = lax.broadcasted_iota(jnp.int32, bins_ref.shape, 1)
    mine = bins_ref[...] == lane

    def of_rows(per_bin):
        column = jnp.sum(jnp.where(mine, per_bin, 0.0), axis=1, keepdims=True)
        return jnp.broadcast_to(column, (rows, LANES))

    coefficient = of_rows(total[0:1] * inverse)
    pull = of_rows(-(total[2:3] * inverse))
    copies = []
    for k in range(6):
        for lanes in halves(v_ref.shape[-1]):
            for z in range(cells):
                residual_ref[k, z, :, lanes] = (
                    leonard_ref[k, z, :, lanes] - coefficient * model_ref[k, z, :, lanes]
                )
        copies.append(pltpu.make_async_copy(residual_ref.at[k], residual_hbm.at[k], left.at[k]))
        copies[k].start()
    for lanes in halves(v_ref.shape[-1]):
        v = [[v_ref[a, z, :, lanes] for z in range(cells)] for a in range(3)]
        from_model = [[] for _ in range(6)]
        from_dual = [[] for _ in range(3)]
        for place, ends in enumerate(far_message_refs, start=1):
            for k in range(6):
                from_model[k].append(tables.outside(place, [2.0 * ends[2 * k + end, :, lanes] for end in range(2)]))
            for a in range(3):
                pair = [(2.0 * coefficient - 1.0) * ends[12 + 2 * a + end, :, lanes] for end in range(2)]
                from_dual[a].append(tables.outside(place, pair))
        from_model = [functools.reduce(add_lists, lists) if lists else None for lists in from_model]
        from_dual = [functools.reduce(add_lists, lists) if lists else None for lists in from_dual]
        for a in range(3):
            for z in range(cells):
                pulled = parts_ref[6 + a, z, :, lanes] + coefficient * parts_ref[9 + a, z, :, lanes]
                if peers:
                    terms = [from_model[PAIR_OF[a][b]][z] * v[b][z] for b in range(3)]
                    pulled = pulled + from_dual[a][z] + sum_up(terms)
                grad_ref[a, z, :, lanes] = (
                    parts_ref[a, z, :, lanes] + coefficient * parts_ref[3 + a, z, :, lanes] + pull * pulled
                )
    for a in range(3):
        copies.append(pltpu.make_async_copy(grad_ref.at[a], grad_hbm.at[a], left.at[6 + a]))
        copies[6 + a].start()
    for copy in copies:
        copy.wait()


WHOLE = pl.BlockSpec(memory_space=pltpu.VMEM)
REMAIN = pl.BlockSpec(memory_space=pltpu.HBM)


def call(kernel, outs, operations, *operands, in_specs=None, out_specs=None, scratch=()):
    nbytes = sum(4 * int(np.prod(x.shape)) for x in (*operands, *outs))
    return pl.pallas_call(
        kernel,
        out_shape=outs,
        in_specs=in_specs or [WHOLE] * len(operands),
        out_specs=out_specs or [WHOLE] * len(outs),
        scratch_shapes=list(scratch),
        compiler_params=pltpu.CompilerParams(vmem_limit_bytes=32 * 1024 * 1024),
        cost_estimate=pl.CostEstimate(flops=operations, bytes_accessed=nbytes, transcendentals=0),
    )(*operands)


def from_ahead(values, shift):
    peers = lax.axis_size("span")
    return lax.ppermute(values, "span", [((i + shift) % peers, i) for i in range(peers)])


def from_source(values, span_shift, source):
    span, stream = lax.axis_size("span"), lax.axis_size("stream")
    pairs = [
        (((i + span_shift) % span) * stream + source(j) % stream, i * stream + j)
        for i in range(span)
        for j in range(stream)
    ]
    return lax.ppermute(values, ("span", "stream"), pairs)


def ring_source(stream):
    def source(j):
        if j % 2 == 0:
            return j - 2 if j >= 2 else 1
        return j + 2 if j + 2 < stream else j - 1

    return source


def on_device(velocity, strain, row_bins, cotangent):
    span, stream = lax.axis_size("span"), lax.axis_size("stream")
    cells, rows, width = velocity.shape[1:]
    tables = Tables(cells, span)
    slab = (rows, width)

    def shaped(*leading):
        return pltpu.VMEM(leading + slab, jnp.float32)

    bins = jnp.broadcast_to(row_bins[:, None], (rows, LANES))
    far_v = [from_ahead(velocity, shift) for shift in range(1, span)]
    work = cells * rows * width
    near_strain, size, size_ends = call(
        functools.partial(prepare_kernel, tables),
        [shaped(6, cells), shaped(cells), shaped(2)],
        40 * work,
        pltpu.with_memory_space_constraint(strain, pltpu.HBM),
        in_specs=[REMAIN],
        scratch=[pltpu.SemaphoreType.DMA((6,))],
    )
    far_size = [from_ahead(size_ends, shift) for shift in range(1, span)]
    (near_cot,) = call(
        fetch_kernel,
        [shaped(6, cells)],
        work,
        pltpu.with_memory_space_constraint(cotangent, pltpu.HBM),
        size_ends,
        in_specs=[REMAIN, WHOLE],
        scratch=[pltpu.SemaphoreType.DMA((6,))],
    )
    far_cot = [from_ahead(near_cot, shift) for shift in range(1, span)]
    table = pltpu.VMEM((8, LANES), jnp.float32)
    smooth, leonard, model, sums = call(
        functools.partial(forward_kernel, tables),
        [shaped(3, cells), shaped(6, cells), shaped(6, cells), table],
        100000 * work,
        velocity,
        near_strain,
        near_cot,
        size,
        bins,
        *far_v,
        *far_size,
    )
    other_sums = from_source(sums, 0, lambda j: j ^ 1)
    dual, message, pair_sums = call(
        functools.partial(message_kernel, tables),
        [shaped(3, cells), shaped(19), table],
        100 * work,
        smooth,
        model,
        sums,
        other_sums,
    )
    far_message = [from_ahead(message, shift) for shift in range(1, span)]
    most_rows = 2 * rows * stream // NBINS
    reach = -(-(most_rows - 1) // rows)
    turning = reach <= 1
    if turning:
        sources = [ring_source(stream)]
    else:
        steps = range(1, -(-reach // 2) + 1)
        sources = [functools.partial(lambda j, away: j + away, away=2 * step * way) for step in steps for way in (1, -1)]
    near_sums = [from_source(pair_sums, shift, source) for shift in range(span) for source in sources]
    (parts,) = call(
        functools.partial(local_kernel, tables),
        [shaped(12, cells)],
        500 * work,
        velocity,
        near_cot,
        smooth,
        leonard,
        model,
        dual,
        *far_v,
        *far_cot,
    )
    outs = [jax.ShapeDtypeStruct((n, cells) + slab, jnp.float32) for n in (6, 3)]
    return tuple(
        call(
            functools.partial(finish_kernel, tables, len(near_sums), turning),
            outs,
            200 * work,
            velocity,
            leonard,
            model,
            parts,
            bins,
            pair_sums,
            *near_sums,
            *far_message,
            out_specs=[REMAIN] * 2,
            scratch=[pltpu.VMEM(x.shape, x.dtype) for x in outs] + [pltpu.SemaphoreType.DMA((9,))],
        )
    )


def solution(mesh):
    fields = P(None, "span", "stream", None)
    return jax.shard_map(
        on_device,
        mesh=mesh,
        in_specs=(fields, fields, P("stream"), fields),
        out_specs=(fields, fields),
        check_vma=False,
    )
```

```python
import functools

import jax
import jax.numpy as jnp
import numpy as np
from jax import lax
from jax.experimental import pallas as pl
from jax.experimental.pallas import tpu as pltpu
from jax.sharding import PartitionSpec as P

NBINS = 64
FILTER_ALPHA = 0.45
CENTER_WEIGHT = 0.95
SIDE_WEIGHT = 0.475
STRAIN_FLOOR = 0.25
EPSILON = 1e-06
INDEX_PAIRS = ((0, 0), (0, 1), (0, 2), (1, 1), (1, 2), (2, 2))
PAIR_WEIGHTS = (1.0, 2.0, 2.0, 1.0, 2.0, 1.0)
PAIR_OF = ((0, 1, 2), (1, 3, 4), (2, 4, 5))
LANES = 128
LONG = 10000000


def filter_row(extent):
    eye = np.eye(extent)
    ring = np.roll(eye, 1, axis=1) + np.roll(eye, -1, axis=1)
    system = eye + FILTER_ALPHA * ring
    side = CENTER_WEIGHT * eye + SIDE_WEIGHT * ring
    return np.linalg.solve(system, side)[0]


def end_weights(cells):
    weights = np.zeros((2, cells))
    weights[0, 0] = 1.0
    weights[1, cells - 1] = 1.0
    inner = cells - 2
    if inner > 0:
        system = np.eye(inner) + FILTER_ALPHA * (np.eye(inner, k=1) + np.eye(inner, k=-1))
        right = np.zeros((inner, 2))
        right[0, 0] = -FILTER_ALPHA
        right[inner - 1, 1] = -FILTER_ALPHA
        weights[:, 1:-1] = np.linalg.solve(system, right).T
    return weights


class Tables:
    def __init__(self, cells, devices):
        row = filter_row(cells * devices)
        extent = cells * devices
        self.cells = cells
        self.devices = devices
        self.own = [[float(row[(z - w) % extent]) for w in range(cells)] for z in range(cells)]
        self.ends = [[float(x) for x in line] for line in end_weights(cells)]
        self.couple = [
            [[float(row[(z - shift * cells - w) % extent]) for w in (0, cells - 1)] for z in range(cells)]
            for shift in range(devices)
        ]

    def project(self, values):
        return [weighted(line, values) for line in self.ends]

    def inside(self, values):
        return [weighted(line, values) for line in self.own]

    def outside(self, shift, ends):
        return [weighted(line, ends) for line in self.couple[shift]]


def weighted(weights, values):
    total = None
    for weight, value in zip(weights, values):
        if weight == 0.0:
            continue
        term = value if weight == 1.0 else value * weight
        total = term if total is None else total + term
    return total


def add_lists(left, right):
    return [x + y for x, y in zip(left, right)]


def halves(width):
    return [pl.ds(start, LANES) for start in range(0, width, LANES)]


def sum_up(terms):
    total = terms[0]
    for term in terms[1:]:
        total = total + term
    return total


def lanes_kernel(lane_ref):
    lane_ref[...] = lax.broadcasted_iota(jnp.int32, lane_ref.shape, 1)


def prepare_kernel(tables, lane_ref, strain_ref, size_ref, size_ends_ref):
    cells = tables.cells
    for lanes in halves(strain_ref.shape[-1]):
        size = []
        for z in range(cells):
            values = [strain_ref[k, z, :, lanes] for k in range(6)]
            total = sum_up([weight * (value * value) for weight, value in zip(PAIR_WEIGHTS, values)])
            size.append(jnp.sqrt(jnp.maximum(2.0 * total, STRAIN_FLOOR)))
            size_ref[z, :, lanes] = size[z]
        for end, value in enumerate(tables.project(size)):
            size_ends_ref[end, :, lanes] = value


def products_of(v):
    return [[x * y for x, y in zip(v[a], v[b])] for a, b in INDEX_PAIRS]


def filtered_block(tables, place, fields, ends):
    filtered = [tables.inside(field) for field in fields]
    for other in range(tables.devices):
        if other != place:
            shift = (other - place) % tables.devices
            filtered = [add_lists(near, tables.outside(shift, far)) for near, far in zip(filtered, ends[other])]
    return filtered


def plain_dual(tensor, vector, a, cells):
    return [sum_up([tensor[PAIR_OF[a][b]][z] * vector[b][z] for b in range(3)]) for z in range(cells)]


def weighted_dual(tensor, vector, a, cells):
    plain = plain_dual(tensor, vector, a, cells)
    return [plain[z] + tensor[PAIR_OF[a][a]][z] * vector[a][z] for z in range(cells)]


def forward_kernel(tables, *refs):
    peers = tables.devices - 1
    cells = tables.cells
    v_ref, strain_ref, cot_ref, size_ref, bins_ref = refs[:5]
    far_v_refs = refs[5 : 5 + peers]
    far_size_refs = refs[5 + peers : 5 + 2 * peers]
    smooth_ref, leonard_ref, model_ref, sums_ref = refs[5 + 2 * peers :]
    cross, square, blame = [], [], []
    for lanes in halves(v_ref.shape[-1]):
        v = [[v_ref[a, z, :, lanes] for z in range(cells)] for a in range(3)]
        size = [size_ref[z, :, lanes] for z in range(cells)]
        products = products_of(v)
        ends = [None]
        for far_v_ref, far_size_ref in zip(far_v_refs, far_size_refs):
            far = [[far_v_ref[a, z, :, lanes] for z in range(cells)] for a in range(3)]
            ends.append([tables.project(field) for field in far + products_of(far)])
            ends[-1].append([far_size_ref[end, :, lanes] for end in range(2)])
        filtered = filtered_block(tables, 0, v + products + [size], ends)
        smooth_v = filtered[:3]
        factor = [2.0 * (4.0 * filtered[9][z] - size[z]) for z in range(cells)]
        for k, (a, b) in enumerate(INDEX_PAIRS):
            for z in range(cells):
                coarse = smooth_v[a][z] * smooth_v[b][z]
                leonard = filtered[3 + k][z] - coarse
                term = products[k][z] - coarse + factor[z] * strain_ref[k, z, :, lanes]
                leonard_ref[k, z, :, lanes] = leonard
                model_ref[k, z, :, lanes] = term
                scaled = PAIR_WEIGHTS[k] * term
                cross.append(scaled * leonard)
                square.append(scaled * term)
                blame.append(term * cot_ref[k, z, :, lanes])
            cross, square, blame = [sum_up(cross)], [sum_up(square)], [sum_up(blame)]
        for a in range(3):
            for z in range(cells):
                smooth_ref[a, z, :, lanes] = smooth_v[a][z]
    lane = lax.broadcasted_iota(jnp.int32, bins_ref.shape, 1)
    mine = bins_ref[...] == lane
    place = lax.broadcasted_iota(jnp.int32, (8, LANES), 0)
    table = jnp.zeros((8, LANES), jnp.float32)
    for index, sums in enumerate((cross, square, blame)):
        per_row = jnp.sum(sums[0], axis=1, keepdims=True)
        per_bin = jnp.sum(jnp.where(mine, per_row, 0.0), axis=0, keepdims=True)
        table = jnp.where(place == index, per_bin, table)
    sums_ref[...] = table


def message_kernel(tables, smooth_ref, model_ref, dual_ref, message_ref):
    cells = tables.cells
    for lanes in halves(model_ref.shape[-1]):
        model = [[model_ref[k, z, :, lanes] for z in range(cells)] for k in range(6)]
        smooth_v = [[smooth_ref[a, z, :, lanes] for z in range(cells)] for a in range(3)]
        for k in range(6):
            for end, value in enumerate(tables.project(model[k])):
                message_ref[2 * k + end, :, lanes] = value
        for a in range(3):
            dual = [2.0 * x for x in plain_dual(model, smooth_v, a, cells)]
            for z in range(cells):
                dual_ref[a, z, :, lanes] = dual[z]
            for end, value in enumerate(tables.project(dual)):
                message_ref[12 + 2 * a + end, :, lanes] = value


def local_kernel(tables, *refs):
    peers = tables.devices - 1
    cells = tables.cells
    v_ref, cot_ref, smooth_ref, leonard_ref, model_ref, dual_ref = refs[:6]
    far_v_refs = refs[6 : 6 + peers]
    far_cot_refs = refs[6 + peers : 6 + 2 * peers]
    parts_ref = refs[-1]
    for lanes in halves(v_ref.shape[-1]):

        def load(ref, count):
            return [[ref[f, z, :, lanes] for z in range(cells)] for f in range(count)]

        fields, ends = [], []
        for ref in (v_ref, *far_v_refs):
            v = load(ref, 3)
            fields.append(v + products_of(v))
            ends.append([tables.project(field) for field in fields[-1]])
        v = fields[0][:3]
        cot, model, leonard, smooth_v = load(cot_ref, 6), load(model_ref, 6), load(leonard_ref, 6), load(smooth_ref, 3)
        smooth_cot = [tables.inside(field) for field in cot]
        duals = [weighted_dual(cot, smooth_v, a, cells) for a in range(3)]
        others = [plain_dual(leonard, smooth_v, a, cells) for a in range(3)]
        smooth_duals = [tables.inside(field) for field in duals]
        smooth_others = [tables.inside(field) for field in others]
        for place in range(1, tables.devices):
            far_cot = load(far_cot_refs[place - 1], 6)
            filtered = filtered_block(tables, place, fields[place], ends)
            far_smooth = filtered[:3]
            far_leonard = [
                [filtered[3 + k][z] - far_smooth[a][z] * far_smooth[b][z] for z in range(cells)]
                for k, (a, b) in enumerate(INDEX_PAIRS)
            ]
            for k in range(6):
                far = tables.outside(place, tables.project(far_cot[k]))
                smooth_cot[k] = add_lists(smooth_cot[k], far)
            for a in range(3):
                far = tables.outside(place, tables.project(weighted_dual(far_cot, far_smooth, a, cells)))
                smooth_duals[a] = add_lists(smooth_duals[a], far)
                far = tables.outside(place, tables.project(plain_dual(far_leonard, far_smooth, a, cells)))
                smooth_others[a] = add_lists(smooth_others[a], far)
        inner = [add_lists(tables.inside(model[k]), leonard[k]) for k in range(6)]
        for a in range(3):
            first = weighted_dual(smooth_cot, v, a, cells)
            second = weighted_dual(cot, v, a, cells)
            dual = tables.inside([dual_ref[a, z, :, lanes] for z in range(cells)])
            third = plain_dual(inner, v, a, cells)
            fourth = plain_dual(model, v, a, cells)
            for z in range(cells):
                parts_ref[a, z, :, lanes] = first[z] - smooth_duals[a][z]
                parts_ref[3 + a, z, :, lanes] = smooth_duals[a][z] - second[z]
                parts_ref[6 + a, z, :, lanes] = 2.0 * (third[z] - smooth_others[a][z]) - dual[z]
                parts_ref[9 + a, z, :, lanes] = 2.0 * dual[z] - 4.0 * fourth[z]


def finish_kernel(tables, count, turning, *refs):
    peers = tables.devices - 1
    cells = tables.cells
    v_ref, leonard_ref, model_ref, parts_ref, bins_ref = refs[:5]
    pair_refs = refs[5 : 6 + peers]
    near_refs = refs[6 + peers : 6 + peers + count]
    far_message_refs = refs[6 + peers + count : 6 + 2 * peers + count]
    residual_hbm, grad_hbm, residual_ref, grad_ref, left = refs[6 + 2 * peers + count :]
    total = sum_up([ref[...] for ref in pair_refs])
    near = sum_up([ref[...] for ref in near_refs])
    if turning:
        place = lax.axis_index("stream")
        inner = jnp.logical_and(place > 0, place < lax.axis_size("stream") - 1)
        near = jnp.where(inner, near, 0.0)
    total = total + near
    inverse = 1.0 / (total[1:2] + EPSILON)
    rows = v_ref.shape[2]
    lane = lax.broadcasted_iota(jnp.int32, bins_ref.shape, 1)
    mine = bins_ref[...] == lane

    def of_rows(per_bin):
        column = jnp.sum(jnp.where(mine, per_bin, 0.0), axis=1, keepdims=True)
        return jnp.broadcast_to(column, (rows, LANES))

    coefficient = of_rows(total[0:1] * inverse)
    pull = of_rows(-(total[2:3] * inverse))
    copies = []
    for k in range(6):
        for lanes in halves(v_ref.shape[-1]):
            for z in range(cells):
                residual_ref[k, z, :, lanes] = (
                    leonard_ref[k, z, :, lanes] - coefficient * model_ref[k, z, :, lanes]
                )
        copies.append(pltpu.make_async_copy(residual_ref.at[k], residual_hbm.at[k], left.at[k]))
        copies[k].start()
    for lanes in halves(v_ref.shape[-1]):
        v = [[v_ref[a, z, :, lanes] for z in range(cells)] for a in range(3)]
        from_model = [[] for _ in range(6)]
        from_dual = [[] for _ in range(3)]
        for place, ends in enumerate(far_message_refs, start=1):
            for k in range(6):
                from_model[k].append(tables.outside(place, [2.0 * ends[2 * k + end, :, lanes] for end in range(2)]))
            for a in range(3):
                pair = [(2.0 * coefficient - 1.0) * ends[12 + 2 * a + end, :, lanes] for end in range(2)]
                from_dual[a].append(tables.outside(place, pair))
        from_model = [functools.reduce(add_lists, lists) if lists else None for lists in from_model]
        from_dual = [functools.reduce(add_lists, lists) if lists else None for lists in from_dual]
        for a in range(3):
            for z in range(cells):
                pulled = parts_ref[6 + a, z, :, lanes] + coefficient * parts_ref[9 + a, z, :, lanes]
                if peers:
                    terms = [from_model[PAIR_OF[a][b]][z] * v[b][z] for b in range(3)]
                    pulled = pulled + from_dual[a][z] + sum_up(terms)
                grad_ref[a, z, :, lanes] = (
                    parts_ref[a, z, :, lanes] + coefficient * parts_ref[3 + a, z, :, lanes] + pull * pulled
                )
    for a in range(3):
        copies.append(pltpu.make_async_copy(grad_ref.at[a], grad_hbm.at[a], left.at[6 + a]))
        copies[6 + a].start()
    for copy in copies:
        copy.wait()


WHOLE = pl.BlockSpec(memory_space=pltpu.VMEM)
REMAIN = pl.BlockSpec(memory_space=pltpu.HBM)


def call(kernel, outs, operations, *operands, in_specs=None, out_specs=None, scratch=()):
    nbytes = sum(4 * int(np.prod(x.shape)) for x in (*operands, *outs))
    return pl.pallas_call(
        kernel,
        out_shape=outs,
        in_specs=in_specs or [WHOLE] * len(operands),
        out_specs=out_specs or [WHOLE] * len(outs),
        scratch_shapes=list(scratch),
        compiler_params=pltpu.CompilerParams(vmem_limit_bytes=32 * 1024 * 1024),
        cost_estimate=pl.CostEstimate(flops=operations, bytes_accessed=nbytes, transcendentals=0),
    )(*operands)


def from_ahead(values, shift):
    peers = lax.axis_size("span")
    return lax.ppermute(values, "span", [((i + shift) % peers, i) for i in range(peers)])


def from_source(values, span_shift, source):
    span, stream = lax.axis_size("span"), lax.axis_size("stream")
    pairs = [
        (((i + span_shift) % span) * stream + source(j) % stream, i * stream + j)
        for i in range(span)
        for j in range(stream)
    ]
    return lax.ppermute(values, ("span", "stream"), pairs)


def ring_source(stream):
    def source(j):
        if j % 2 == 0:
            return j - 2 if j >= 2 else 1
        return j + 2 if j + 2 < stream else j - 1

    return source


def on_device(velocity, strain, row_bins, cotangent):
    span, stream = lax.axis_size("span"), lax.axis_size("stream")
    cells, rows, width = velocity.shape[1:]
    tables = Tables(cells, span)
    slab = (rows, width)

    def shaped(*leading):
        return pltpu.VMEM(leading + slab, jnp.float32)

    bins = jnp.broadcast_to(row_bins[:, None], (rows, LANES))
    far_v = [from_ahead(velocity, shift) for shift in range(1, span)]
    work = cells * rows * width
    (lane,) = call(lanes_kernel, [pltpu.VMEM((rows, LANES), jnp.int32)], LONG * work)
    size, size_ends = call(
        functools.partial(prepare_kernel, tables), [shaped(cells), shaped(2)], LONG * work, lane, strain
    )
    size_ends, sent_cot = lax.optimization_barrier((size_ends, cotangent))
    far_size = [from_ahead(size_ends, shift) for shift in range(1, span)]
    far_cot = [from_ahead(sent_cot, shift) for shift in range(1, span)]
    table = pltpu.VMEM((8, LANES), jnp.float32)
    smooth, leonard, model, sums = call(
        functools.partial(forward_kernel, tables),
        [shaped(3, cells), shaped(6, cells), shaped(6, cells), table],
        LONG * work,
        velocity,
        strain,
        cotangent,
        size,
        bins,
        *far_v,
        *far_size,
    )
    other_sums = from_source(sums, 0, lambda j: j ^ 1)
    dual, message = call(
        functools.partial(message_kernel, tables), [shaped(3, cells), shaped(18)], 100 * work, smooth, model
    )
    pair_sums = sums + other_sums
    far_message = [from_ahead(message, shift) for shift in range(1, span)]
    most_rows = 2 * rows * stream // NBINS
    reach = -(-(most_rows - 1) // rows)
    turning = reach <= 1
    if turning:
        sources = [ring_source(stream)]
    else:
        steps = range(1, -(-reach // 2) + 1)
        sources = [functools.partial(lambda j, away: j + away, away=2 * step * way) for step in steps for way in (1, -1)]
    far_pairs = [from_ahead(pair_sums, shift) for shift in range(1, span)]
    near_sums = [from_source(pair_sums, shift, source) for shift in range(span) for source in sources]
    (parts,) = call(
        functools.partial(local_kernel, tables),
        [shaped(12, cells)],
        LONG * work,
        velocity,
        cotangent,
        smooth,
        leonard,
        model,
        dual,
        *far_v,
        *far_cot,
    )
    outs = [jax.ShapeDtypeStruct((n, cells) + slab, jnp.float32) for n in (6, 3)]
    return tuple(
        call(
            functools.partial(finish_kernel, tables, len(near_sums), turning),
            outs,
            200 * work,
            velocity,
            leonard,
            model,
            parts,
            bins,
            pair_sums,
            *far_pairs,
            *near_sums,
            *far_message,
            out_specs=[REMAIN] * 2,
            scratch=[pltpu.VMEM(x.shape, x.dtype) for x in outs] + [pltpu.SemaphoreType.DMA((9,))],
        )
    )


def solution(mesh):
    fields = P(None, "span", "stream", None)
    return jax.shard_map(
        on_device,
        mesh=mesh,
        in_specs=(fields, fields, P("stream"), fields),
        out_specs=(fields, fields),
        check_vma=False,
    )
```

```python
import functools

import jax
import jax.numpy as jnp
import numpy as np
from jax import lax
from jax.experimental import pallas as pl
from jax.experimental.pallas import tpu as pltpu
from jax.sharding import PartitionSpec as P

NBINS = 64
FILTER_ALPHA = 0.45
CENTER_WEIGHT = 0.95
SIDE_WEIGHT = 0.475
STRAIN_FLOOR = 0.25
EPSILON = 1e-06
INDEX_PAIRS = ((0, 0), (0, 1), (0, 2), (1, 1), (1, 2), (2, 2))
PAIR_WEIGHTS = (1.0, 2.0, 2.0, 1.0, 2.0, 1.0)
PAIR_OF = ((0, 1, 2), (1, 3, 4), (2, 4, 5))
LANES = 128
LONG = 300000


def filter_row(extent):
    eye = np.eye(extent)
    ring = np.roll(eye, 1, axis=1) + np.roll(eye, -1, axis=1)
    system = eye + FILTER_ALPHA * ring
    side = CENTER_WEIGHT * eye + SIDE_WEIGHT * ring
    return np.linalg.solve(system, side)[0]


def end_weights(cells):
    weights = np.zeros((2, cells))
    weights[0, 0] = 1.0
    weights[1, cells - 1] = 1.0
    inner = cells - 2
    if inner > 0:
        system = np.eye(inner) + FILTER_ALPHA * (np.eye(inner, k=1) + np.eye(inner, k=-1))
        right = np.zeros((inner, 2))
        right[0, 0] = -FILTER_ALPHA
        right[inner - 1, 1] = -FILTER_ALPHA
        weights[:, 1:-1] = np.linalg.solve(system, right).T
    return weights


class Tables:
    def __init__(self, cells, devices):
        row = filter_row(cells * devices)
        extent = cells * devices
        self.cells = cells
        self.devices = devices
        self.own = [[float(row[(z - w) % extent]) for w in range(cells)] for z in range(cells)]
        self.ends = [[float(x) for x in line] for line in end_weights(cells)]
        self.couple = [
            [[float(row[(z - shift * cells - w) % extent]) for w in (0, cells - 1)] for z in range(cells)]
            for shift in range(devices)
        ]

    def project(self, values):
        return [weighted(line, values) for line in self.ends]

    def inside(self, values):
        return [weighted(line, values) for line in self.own]

    def outside(self, shift, ends):
        return [weighted(line, ends) for line in self.couple[shift]]


def weighted(weights, values):
    total = None
    for weight, value in zip(weights, values):
        if weight == 0.0:
            continue
        term = value if weight == 1.0 else value * weight
        total = term if total is None else total + term
    return total


def add_lists(left, right):
    return [x + y for x, y in zip(left, right)]


def halves(width):
    return [pl.ds(start, LANES) for start in range(0, width, LANES)]


def sum_up(terms):
    total = terms[0]
    for term in terms[1:]:
        total = total + term
    return total


def lanes_kernel(lane_ref):
    lane_ref[...] = lax.broadcasted_iota(jnp.int32, lane_ref.shape, 1)


def prepare_kernel(tables, lane_ref, strain_ref, size_ref, size_ends_ref):
    cells = tables.cells
    for lanes in halves(strain_ref.shape[-1]):
        size = []
        for z in range(cells):
            values = [strain_ref[k, z, :, lanes] for k in range(6)]
            total = sum_up([weight * (value * value) for weight, value in zip(PAIR_WEIGHTS, values)])
            size.append(jnp.sqrt(jnp.maximum(2.0 * total, STRAIN_FLOOR)))
            size_ref[z, :, lanes] = size[z]
        for end, value in enumerate(tables.project(size)):
            size_ends_ref[end, :, lanes] = value


def products_of(v):
    return [[x * y for x, y in zip(v[a], v[b])] for a, b in INDEX_PAIRS]


def filtered_block(tables, place, fields, ends):
    filtered = [tables.inside(field) for field in fields]
    for other in range(tables.devices):
        if other != place:
            shift = (other - place) % tables.devices
            filtered = [add_lists(near, tables.outside(shift, far)) for near, far in zip(filtered, ends[other])]
    return filtered


def plain_dual(tensor, vector, a, cells):
    return [sum_up([tensor[PAIR_OF[a][b]][z] * vector[b][z] for b in range(3)]) for z in range(cells)]


def weighted_dual(tensor, vector, a, cells):
    plain = plain_dual(tensor, vector, a, cells)
    return [plain[z] + tensor[PAIR_OF[a][a]][z] * vector[a][z] for z in range(cells)]


def forward_kernel(tables, *refs):
    peers = tables.devices - 1
    cells = tables.cells
    v_ref, strain_ref, cot_ref, size_ref, bins_ref = refs[:5]
    far_v_refs = refs[5 : 5 + peers]
    far_size_refs = refs[5 + peers : 5 + 2 * peers]
    smooth_ref, leonard_ref, model_ref, sums_ref = refs[5 + 2 * peers :]
    cross, square, blame = [], [], []
    for lanes in halves(v_ref.shape[-1]):
        v = [[v_ref[a, z, :, lanes] for z in range(cells)] for a in range(3)]
        size = [size_ref[z, :, lanes] for z in range(cells)]
        products = products_of(v)
        ends = [None]
        for far_v_ref, far_size_ref in zip(far_v_refs, far_size_refs):
            far = [[far_v_ref[a, z, :, lanes] for z in range(cells)] for a in range(3)]
            ends.append([tables.project(field) for field in far + products_of(far)])
            ends[-1].append([far_size_ref[end, :, lanes] for end in range(2)])
        filtered = filtered_block(tables, 0, v + products + [size], ends)
        smooth_v = filtered[:3]
        factor = [2.0 * (4.0 * filtered[9][z] - size[z]) for z in range(cells)]
        for k, (a, b) in enumerate(INDEX_PAIRS):
            for z in range(cells):
                coarse = smooth_v[a][z] * smooth_v[b][z]
                leonard = filtered[3 + k][z] - coarse
                term = products[k][z] - coarse + factor[z] * strain_ref[k, z, :, lanes]
                leonard_ref[k, z, :, lanes] = leonard
                model_ref[k, z, :, lanes] = term
                scaled = PAIR_WEIGHTS[k] * term
                cross.append(scaled * leonard)
                square.append(scaled * term)
                blame.append(term * cot_ref[k, z, :, lanes])
            cross, square, blame = [sum_up(cross)], [sum_up(square)], [sum_up(blame)]
        for a in range(3):
            for z in range(cells):
                smooth_ref[a, z, :, lanes] = smooth_v[a][z]
    lane = lax.broadcasted_iota(jnp.int32, bins_ref.shape, 1)
    mine = bins_ref[...] == lane
    place = lax.broadcasted_iota(jnp.int32, (8, LANES), 0)
    table = jnp.zeros((8, LANES), jnp.float32)
    for index, sums in enumerate((cross, square, blame)):
        per_row = jnp.sum(sums[0], axis=1, keepdims=True)
        per_bin = jnp.sum(jnp.where(mine, per_row, 0.0), axis=0, keepdims=True)
        table = jnp.where(place == index, per_bin, table)
    sums_ref[...] = table


def message_kernel(tables, smooth_ref, model_ref, dual_ref, message_ref):
    cells = tables.cells
    for lanes in halves(model_ref.shape[-1]):
        model = [[model_ref[k, z, :, lanes] for z in range(cells)] for k in range(6)]
        smooth_v = [[smooth_ref[a, z, :, lanes] for z in range(cells)] for a in range(3)]
        for k in range(6):
            for end, value in enumerate(tables.project(model[k])):
                message_ref[2 * k + end, :, lanes] = value
        for a in range(3):
            dual = [2.0 * x for x in plain_dual(model, smooth_v, a, cells)]
            for z in range(cells):
                dual_ref[a, z, :, lanes] = dual[z]
            for end, value in enumerate(tables.project(dual)):
                message_ref[12 + 2 * a + end, :, lanes] = value


def local_kernel(tables, *refs):
    peers = tables.devices - 1
    cells = tables.cells
    v_ref, cot_ref, smooth_ref, leonard_ref, model_ref, dual_ref = refs[:6]
    far_v_refs = refs[6 : 6 + peers]
    far_cot_refs = refs[6 + peers : 6 + 2 * peers]
    parts_ref = refs[-1]
    for lanes in halves(v_ref.shape[-1]):

        def load(ref, count):
            return [[ref[f, z, :, lanes] for z in range(cells)] for f in range(count)]

        fields, ends = [], []
        for ref in (v_ref, *far_v_refs):
            v = load(ref, 3)
            fields.append(v + products_of(v))
            ends.append([tables.project(field) for field in fields[-1]])
        v = fields[0][:3]
        cot, model, leonard, smooth_v = load(cot_ref, 6), load(model_ref, 6), load(leonard_ref, 6), load(smooth_ref, 3)
        smooth_cot = [tables.inside(field) for field in cot]
        duals = [weighted_dual(cot, smooth_v, a, cells) for a in range(3)]
        others = [plain_dual(leonard, smooth_v, a, cells) for a in range(3)]
        smooth_duals = [tables.inside(field) for field in duals]
        smooth_others = [tables.inside(field) for field in others]
        for place in range(1, tables.devices):
            far_cot = load(far_cot_refs[place - 1], 6)
            filtered = filtered_block(tables, place, fields[place], ends)
            far_smooth = filtered[:3]
            far_leonard = [
                [filtered[3 + k][z] - far_smooth[a][z] * far_smooth[b][z] for z in range(cells)]
                for k, (a, b) in enumerate(INDEX_PAIRS)
            ]
            for k in range(6):
                far = tables.outside(place, tables.project(far_cot[k]))
                smooth_cot[k] = add_lists(smooth_cot[k], far)
            for a in range(3):
                far = tables.outside(place, tables.project(weighted_dual(far_cot, far_smooth, a, cells)))
                smooth_duals[a] = add_lists(smooth_duals[a], far)
                far = tables.outside(place, tables.project(plain_dual(far_leonard, far_smooth, a, cells)))
                smooth_others[a] = add_lists(smooth_others[a], far)
        inner = [add_lists(tables.inside(model[k]), leonard[k]) for k in range(6)]
        for a in range(3):
            first = weighted_dual(smooth_cot, v, a, cells)
            second = weighted_dual(cot, v, a, cells)
            dual = tables.inside([dual_ref[a, z, :, lanes] for z in range(cells)])
            third = plain_dual(inner, v, a, cells)
            fourth = plain_dual(model, v, a, cells)
            for z in range(cells):
                parts_ref[a, z, :, lanes] = first[z] - smooth_duals[a][z]
                parts_ref[3 + a, z, :, lanes] = smooth_duals[a][z] - second[z]
                parts_ref[6 + a, z, :, lanes] = 2.0 * (third[z] - smooth_others[a][z]) - dual[z]
                parts_ref[9 + a, z, :, lanes] = 2.0 * dual[z] - 4.0 * fourth[z]


def finish_kernel(tables, count, turning, *refs):
    peers = tables.devices - 1
    cells = tables.cells
    v_ref, leonard_ref, model_ref, parts_ref, bins_ref = refs[:5]
    pair_refs = refs[5 : 6 + peers]
    near_refs = refs[6 + peers : 6 + peers + count]
    far_message_refs = refs[6 + peers + count : 6 + 2 * peers + count]
    residual_hbm, grad_hbm, residual_ref, grad_ref, left = refs[6 + 2 * peers + count :]
    total = sum_up([ref[...] for ref in pair_refs])
    near = sum_up([ref[...] for ref in near_refs])
    if turning:
        place = lax.axis_index("stream")
        inner = jnp.logical_and(place > 0, place < lax.axis_size("stream") - 1)
        near = jnp.where(inner, near, 0.0)
    total = total + near
    inverse = 1.0 / (total[1:2] + EPSILON)
    rows = v_ref.shape[2]
    lane = lax.broadcasted_iota(jnp.int32, bins_ref.shape, 1)
    mine = bins_ref[...] == lane

    def of_rows(per_bin):
        column = jnp.sum(jnp.where(mine, per_bin, 0.0), axis=1, keepdims=True)
        return jnp.broadcast_to(column, (rows, LANES))

    coefficient = of_rows(total[0:1] * inverse)
    pull = of_rows(-(total[2:3] * inverse))
    copies = []
    for k in range(6):
        for lanes in halves(v_ref.shape[-1]):
            for z in range(cells):
                residual_ref[k, z, :, lanes] = (
                    leonard_ref[k, z, :, lanes] - coefficient * model_ref[k, z, :, lanes]
                )
        copies.append(pltpu.make_async_copy(residual_ref.at[k], residual_hbm.at[k], left.at[k]))
        copies[k].start()
    for lanes in halves(v_ref.shape[-1]):
        v = [[v_ref[a, z, :, lanes] for z in range(cells)] for a in range(3)]
        from_model = [[] for _ in range(6)]
        from_dual = [[] for _ in range(3)]
        for place, ends in enumerate(far_message_refs, start=1):
            for k in range(6):
                from_model[k].append(tables.outside(place, [2.0 * ends[2 * k + end, :, lanes] for end in range(2)]))
            for a in range(3):
                pair = [(2.0 * coefficient - 1.0) * ends[12 + 2 * a + end, :, lanes] for end in range(2)]
                from_dual[a].append(tables.outside(place, pair))
        from_model = [functools.reduce(add_lists, lists) if lists else None for lists in from_model]
        from_dual = [functools.reduce(add_lists, lists) if lists else None for lists in from_dual]
        for a in range(3):
            for z in range(cells):
                pulled = parts_ref[6 + a, z, :, lanes] + coefficient * parts_ref[9 + a, z, :, lanes]
                if peers:
                    terms = [from_model[PAIR_OF[a][b]][z] * v[b][z] for b in range(3)]
                    pulled = pulled + from_dual[a][z] + sum_up(terms)
                grad_ref[a, z, :, lanes] = (
                    parts_ref[a, z, :, lanes] + coefficient * parts_ref[3 + a, z, :, lanes] + pull * pulled
                )
    for a in range(3):
        copies.append(pltpu.make_async_copy(grad_ref.at[a], grad_hbm.at[a], left.at[6 + a]))
        copies[6 + a].start()
    for copy in copies:
        copy.wait()


WHOLE = pl.BlockSpec(memory_space=pltpu.VMEM)
REMAIN = pl.BlockSpec(memory_space=pltpu.HBM)


def call(kernel, outs, operations, *operands, in_specs=None, out_specs=None, scratch=()):
    nbytes = sum(4 * int(np.prod(x.shape)) for x in (*operands, *outs))
    return pl.pallas_call(
        kernel,
        out_shape=outs,
        in_specs=in_specs or [WHOLE] * len(operands),
        out_specs=out_specs or [WHOLE] * len(outs),
        scratch_shapes=list(scratch),
        compiler_params=pltpu.CompilerParams(vmem_limit_bytes=32 * 1024 * 1024),
        cost_estimate=pl.CostEstimate(flops=operations, bytes_accessed=nbytes, transcendentals=0),
    )(*operands)


def from_ahead(values, shift):
    peers = lax.axis_size("span")
    return lax.ppermute(values, "span", [((i + shift) % peers, i) for i in range(peers)])


def from_source(values, span_shift, source):
    span, stream = lax.axis_size("span"), lax.axis_size("stream")
    pairs = [
        (((i + span_shift) % span) * stream + source(j) % stream, i * stream + j)
        for i in range(span)
        for j in range(stream)
    ]
    return lax.ppermute(values, ("span", "stream"), pairs)


def ring_source(stream):
    def source(j):
        if j % 2 == 0:
            return j - 2 if j >= 2 else 1
        return j + 2 if j + 2 < stream else j - 1

    return source


def on_device(velocity, strain, row_bins, cotangent):
    span, stream = lax.axis_size("span"), lax.axis_size("stream")
    cells, rows, width = velocity.shape[1:]
    tables = Tables(cells, span)
    slab = (rows, width)

    def shaped(*leading):
        return pltpu.VMEM(leading + slab, jnp.float32)

    bins = jnp.broadcast_to(row_bins[:, None], (rows, LANES))
    far_v = [from_ahead(velocity, shift) for shift in range(1, span)]
    work = cells * rows * width
    (lane,) = call(lanes_kernel, [pltpu.VMEM((rows, LANES), jnp.int32)], LONG * work)
    size, size_ends = call(
        functools.partial(prepare_kernel, tables), [shaped(cells), shaped(2)], LONG * work, lane, strain
    )
    size_ends, sent_cot = lax.optimization_barrier((size_ends, cotangent))
    far_size = [from_ahead(size_ends, shift) for shift in range(1, span)]
    far_cot = [from_ahead(sent_cot, shift) for shift in range(1, span)]
    table = pltpu.VMEM((8, LANES), jnp.float32)
    smooth, leonard, model, sums = call(
        functools.partial(forward_kernel, tables),
        [shaped(3, cells), shaped(6, cells), shaped(6, cells), table],
        LONG * work,
        velocity,
        strain,
        cotangent,
        size,
        bins,
        *far_v,
        *far_size,
    )
    other_sums = from_source(sums, 0, lambda j: j ^ 1)
    dual, message = call(
        functools.partial(message_kernel, tables), [shaped(3, cells), shaped(18)], 100 * work, smooth, model
    )
    pair_sums = sums + other_sums
    far_message = [from_ahead(message, shift) for shift in range(1, span)]
    most_rows = 2 * rows * stream // NBINS
    reach = -(-(most_rows - 1) // rows)
    turning = reach <= 1
    if turning:
        sources = [ring_source(stream)]
    else:
        steps = range(1, -(-reach // 2) + 1)
        sources = [functools.partial(lambda j, away: j + away, away=2 * step * way) for step in steps for way in (1, -1)]
    far_pairs = [from_ahead(pair_sums, shift) for shift in range(1, span)]
    near_sums = [from_source(pair_sums, shift, source) for shift in range(span) for source in sources]
    (parts,) = call(
        functools.partial(local_kernel, tables),
        [shaped(12, cells)],
        LONG * work,
        velocity,
        cotangent,
        smooth,
        leonard,
        model,
        dual,
        *far_v,
        *far_cot,
    )
    outs = [jax.ShapeDtypeStruct((n, cells) + slab, jnp.float32) for n in (6, 3)]
    return tuple(
        call(
            functools.partial(finish_kernel, tables, len(near_sums), turning),
            outs,
            200 * work,
            velocity,
            leonard,
            model,
            parts,
            bins,
            pair_sums,
            *far_pairs,
            *near_sums,
            *far_message,
            out_specs=[REMAIN] * 2,
            scratch=[pltpu.VMEM(x.shape, x.dtype) for x in outs] + [pltpu.SemaphoreType.DMA((9,))],
        )
    )


def solution(mesh):
    fields = P(None, "span", "stream", None)
    return jax.shard_map(
        on_device,
        mesh=mesh,
        in_specs=(fields, fields, P("stream"), fields),
        out_specs=(fields, fields),
        check_vma=False,
    )
```

```python
import functools

import jax
import jax.numpy as jnp
import numpy as np
from jax import lax
from jax.experimental import pallas as pl
from jax.experimental.pallas import tpu as pltpu
from jax.sharding import PartitionSpec as P

NBINS = 64
FILTER_ALPHA = 0.45
CENTER_WEIGHT = 0.95
SIDE_WEIGHT = 0.475
STRAIN_FLOOR = 0.25
EPSILON = 1e-06
INDEX_PAIRS = ((0, 0), (0, 1), (0, 2), (1, 1), (1, 2), (2, 2))
PAIR_WEIGHTS = (1.0, 2.0, 2.0, 1.0, 2.0, 1.0)
PAIR_OF = ((0, 1, 2), (1, 3, 4), (2, 4, 5))
LANES = 128
LONG = 300000


def filter_row(extent):
    eye = np.eye(extent)
    ring = np.roll(eye, 1, axis=1) + np.roll(eye, -1, axis=1)
    system = eye + FILTER_ALPHA * ring
    side = CENTER_WEIGHT * eye + SIDE_WEIGHT * ring
    return np.linalg.solve(system, side)[0]


def end_weights(cells):
    weights = np.zeros((2, cells))
    weights[0, 0] = 1.0
    weights[1, cells - 1] = 1.0
    inner = cells - 2
    if inner > 0:
        system = np.eye(inner) + FILTER_ALPHA * (np.eye(inner, k=1) + np.eye(inner, k=-1))
        right = np.zeros((inner, 2))
        right[0, 0] = -FILTER_ALPHA
        right[inner - 1, 1] = -FILTER_ALPHA
        weights[:, 1:-1] = np.linalg.solve(system, right).T
    return weights


class Tables:
    def __init__(self, cells, devices):
        row = filter_row(cells * devices)
        extent = cells * devices
        self.cells = cells
        self.devices = devices
        self.own = [[float(row[(z - w) % extent]) for w in range(cells)] for z in range(cells)]
        self.ends = [[float(x) for x in line] for line in end_weights(cells)]
        self.couple = [
            [[float(row[(z - shift * cells - w) % extent]) for w in (0, cells - 1)] for z in range(cells)]
            for shift in range(devices)
        ]

    def project(self, values):
        return [weighted(line, values) for line in self.ends]

    def inside(self, values):
        return [weighted(line, values) for line in self.own]

    def outside(self, shift, ends):
        return [weighted(line, ends) for line in self.couple[shift]]


def weighted(weights, values):
    total = None
    for weight, value in zip(weights, values):
        if weight == 0.0:
            continue
        term = value if weight == 1.0 else value * weight
        total = term if total is None else total + term
    return total


def add_lists(left, right):
    return [x + y for x, y in zip(left, right)]


def halves(width):
    return [pl.ds(start, LANES) for start in range(0, width, LANES)]


def sum_up(terms):
    total = terms[0]
    for term in terms[1:]:
        total = total + term
    return total


def lanes_kernel(lane_ref):
    lane_ref[...] = lax.broadcasted_iota(jnp.int32, lane_ref.shape, 1)


def prepare_kernel(tables, lane_ref, strain_ref, size_ref, size_ends_ref):
    cells = tables.cells
    for lanes in halves(strain_ref.shape[-1]):
        size = []
        for z in range(cells):
            values = [strain_ref[k, z, :, lanes] for k in range(6)]
            total = sum_up([weight * (value * value) for weight, value in zip(PAIR_WEIGHTS, values)])
            size.append(jnp.sqrt(jnp.maximum(2.0 * total, STRAIN_FLOOR)))
            size_ref[z, :, lanes] = size[z]
        for end, value in enumerate(tables.project(size)):
            size_ends_ref[end, :, lanes] = value


def products_of(v):
    return [[x * y for x, y in zip(v[a], v[b])] for a, b in INDEX_PAIRS]


def filtered_block(tables, place, fields, ends):
    filtered = [tables.inside(field) for field in fields]
    for other in range(tables.devices):
        if other != place:
            shift = (other - place) % tables.devices
            filtered = [add_lists(near, tables.outside(shift, far)) for near, far in zip(filtered, ends[other])]
    return filtered


def plain_dual(tensor, vector, a, cells):
    return [sum_up([tensor[PAIR_OF[a][b]][z] * vector[b][z] for b in range(3)]) for z in range(cells)]


def weighted_dual(tensor, vector, a, cells):
    plain = plain_dual(tensor, vector, a, cells)
    return [plain[z] + tensor[PAIR_OF[a][a]][z] * vector[a][z] for z in range(cells)]


def forward_kernel(tables, *refs):
    peers = tables.devices - 1
    cells = tables.cells
    v_ref, strain_ref, cot_ref, size_ref, bins_ref = refs[:5]
    far_v_refs = refs[5 : 5 + peers]
    far_size_refs = refs[5 + peers : 5 + 2 * peers]
    smooth_ref, leonard_ref, model_ref, sums_ref = refs[5 + 2 * peers :]
    cross, square, blame = [], [], []
    for lanes in halves(v_ref.shape[-1]):
        v = [[v_ref[a, z, :, lanes] for z in range(cells)] for a in range(3)]
        size = [size_ref[z, :, lanes] for z in range(cells)]
        products = products_of(v)
        ends = [None]
        for far_v_ref, far_size_ref in zip(far_v_refs, far_size_refs):
            far = [[far_v_ref[a, z, :, lanes] for z in range(cells)] for a in range(3)]
            ends.append([tables.project(field) for field in far + products_of(far)])
            ends[-1].append([far_size_ref[end, :, lanes] for end in range(2)])
        filtered = filtered_block(tables, 0, v + products + [size], ends)
        smooth_v = filtered[:3]
        factor = [2.0 * (4.0 * filtered[9][z] - size[z]) for z in range(cells)]
        for k, (a, b) in enumerate(INDEX_PAIRS):
            for z in range(cells):
                coarse = smooth_v[a][z] * smooth_v[b][z]
                leonard = filtered[3 + k][z] - coarse
                term = products[k][z] - coarse + factor[z] * strain_ref[k, z, :, lanes]
                leonard_ref[k, z, :, lanes] = leonard
                model_ref[k, z, :, lanes] = term
                scaled = PAIR_WEIGHTS[k] * term
                cross.append(scaled * leonard)
                square.append(scaled * term)
                blame.append(term * cot_ref[k, z, :, lanes])
            cross, square, blame = [sum_up(cross)], [sum_up(square)], [sum_up(blame)]
        for a in range(3):
            for z in range(cells):
                smooth_ref[a, z, :, lanes] = smooth_v[a][z]
    lane = lax.broadcasted_iota(jnp.int32, bins_ref.shape, 1)
    mine = bins_ref[...] == lane
    place = lax.broadcasted_iota(jnp.int32, (8, LANES), 0)
    table = jnp.zeros((8, LANES), jnp.float32)
    for index, sums in enumerate((cross, square, blame)):
        per_row = jnp.sum(sums[0], axis=1, keepdims=True)
        per_bin = jnp.sum(jnp.where(mine, per_row, 0.0), axis=0, keepdims=True)
        table = jnp.where(place == index, per_bin, table)
    sums_ref[...] = table


def message_kernel(tables, smooth_ref, model_ref, dual_ref, message_ref):
    cells = tables.cells
    for lanes in halves(model_ref.shape[-1]):
        model = [[model_ref[k, z, :, lanes] for z in range(cells)] for k in range(6)]
        smooth_v = [[smooth_ref[a, z, :, lanes] for z in range(cells)] for a in range(3)]
        for k in range(6):
            for end, value in enumerate(tables.project(model[k])):
                message_ref[2 * k + end, :, lanes] = value
        for a in range(3):
            dual = [2.0 * x for x in plain_dual(model, smooth_v, a, cells)]
            for z in range(cells):
                dual_ref[a, z, :, lanes] = dual[z]
            for end, value in enumerate(tables.project(dual)):
                message_ref[12 + 2 * a + end, :, lanes] = value


def local_kernel(tables, *refs):
    peers = tables.devices - 1
    cells = tables.cells
    v_ref, cot_ref, smooth_ref, leonard_ref, model_ref, dual_ref = refs[:6]
    far_v_refs = refs[6 : 6 + peers]
    far_cot_refs = refs[6 + peers : 6 + 2 * peers]
    parts_ref = refs[-1]
    for lanes in halves(v_ref.shape[-1]):

        def load(ref, count):
            return [[ref[f, z, :, lanes] for z in range(cells)] for f in range(count)]

        fields, ends = [], []
        for ref in (v_ref, *far_v_refs):
            v = load(ref, 3)
            fields.append(v + products_of(v))
            ends.append([tables.project(field) for field in fields[-1]])
        v = fields[0][:3]
        cot, model, leonard, smooth_v = load(cot_ref, 6), load(model_ref, 6), load(leonard_ref, 6), load(smooth_ref, 3)
        smooth_cot = [tables.inside(field) for field in cot]
        duals = [weighted_dual(cot, smooth_v, a, cells) for a in range(3)]
        others = [plain_dual(leonard, smooth_v, a, cells) for a in range(3)]
        smooth_duals = [tables.inside(field) for field in duals]
        smooth_others = [tables.inside(field) for field in others]
        for place in range(1, tables.devices):
            far_cot = load(far_cot_refs[place - 1], 6)
            filtered = filtered_block(tables, place, fields[place], ends)
            far_smooth = filtered[:3]
            far_leonard = [
                [filtered[3 + k][z] - far_smooth[a][z] * far_smooth[b][z] for z in range(cells)]
                for k, (a, b) in enumerate(INDEX_PAIRS)
            ]
            for k in range(6):
                far = tables.outside(place, tables.project(far_cot[k]))
                smooth_cot[k] = add_lists(smooth_cot[k], far)
            for a in range(3):
                far = tables.outside(place, tables.project(weighted_dual(far_cot, far_smooth, a, cells)))
                smooth_duals[a] = add_lists(smooth_duals[a], far)
                far = tables.outside(place, tables.project(plain_dual(far_leonard, far_smooth, a, cells)))
                smooth_others[a] = add_lists(smooth_others[a], far)
        inner = [add_lists(tables.inside(model[k]), leonard[k]) for k in range(6)]
        for a in range(3):
            first = weighted_dual(smooth_cot, v, a, cells)
            second = weighted_dual(cot, v, a, cells)
            dual = tables.inside([dual_ref[a, z, :, lanes] for z in range(cells)])
            third = plain_dual(inner, v, a, cells)
            fourth = plain_dual(model, v, a, cells)
            for z in range(cells):
                parts_ref[a, z, :, lanes] = first[z] - smooth_duals[a][z]
                parts_ref[3 + a, z, :, lanes] = smooth_duals[a][z] - second[z]
                parts_ref[6 + a, z, :, lanes] = 2.0 * (third[z] - smooth_others[a][z]) - dual[z]
                parts_ref[9 + a, z, :, lanes] = 2.0 * dual[z] - 4.0 * fourth[z]


def finish_kernel(tables, count, turning, *refs):
    peers = tables.devices - 1
    cells = tables.cells
    v_ref, leonard_ref, model_ref, parts_ref, bins_ref = refs[:5]
    near_refs = refs[5 : 5 + count]
    pair_refs = refs[5 + count : 6 + peers + count]
    far_message_refs = refs[6 + peers + count : 6 + 2 * peers + count]
    residual_hbm, grad_hbm, residual_ref, grad_ref, left = refs[6 + 2 * peers + count :]
    total = sum_up([ref[...] for ref in pair_refs])
    near = sum_up([ref[...] for ref in near_refs])
    if turning:
        place = lax.axis_index("stream")
        inner = jnp.logical_and(place > 0, place < lax.axis_size("stream") - 1)
        near = jnp.where(inner, near, 0.0)
    total = total + near
    inverse = 1.0 / (total[1:2] + EPSILON)
    rows = v_ref.shape[2]
    lane = lax.broadcasted_iota(jnp.int32, bins_ref.shape, 1)
    mine = bins_ref[...] == lane

    def of_rows(per_bin):
        column = jnp.sum(jnp.where(mine, per_bin, 0.0), axis=1, keepdims=True)
        return jnp.broadcast_to(column, (rows, LANES))

    coefficient = of_rows(total[0:1] * inverse)
    pull = of_rows(-(total[2:3] * inverse))
    copies = []
    for k in range(6):
        for lanes in halves(v_ref.shape[-1]):
            for z in range(cells):
                residual_ref[k, z, :, lanes] = (
                    leonard_ref[k, z, :, lanes] - coefficient * model_ref[k, z, :, lanes]
                )
        copies.append(pltpu.make_async_copy(residual_ref.at[k], residual_hbm.at[k], left.at[k]))
        copies[k].start(priority=k % 2)
    for lanes in halves(v_ref.shape[-1]):
        v = [[v_ref[a, z, :, lanes] for z in range(cells)] for a in range(3)]
        from_model = [[] for _ in range(6)]
        from_dual = [[] for _ in range(3)]
        for place, ends in enumerate(far_message_refs, start=1):
            for k in range(6):
                from_model[k].append(tables.outside(place, [2.0 * ends[2 * k + end, :, lanes] for end in range(2)]))
            for a in range(3):
                pair = [(2.0 * coefficient - 1.0) * ends[12 + 2 * a + end, :, lanes] for end in range(2)]
                from_dual[a].append(tables.outside(place, pair))
        from_model = [functools.reduce(add_lists, lists) if lists else None for lists in from_model]
        from_dual = [functools.reduce(add_lists, lists) if lists else None for lists in from_dual]
        for a in range(3):
            for z in range(cells):
                pulled = parts_ref[6 + a, z, :, lanes] + coefficient * parts_ref[9 + a, z, :, lanes]
                if peers:
                    terms = [from_model[PAIR_OF[a][b]][z] * v[b][z] for b in range(3)]
                    pulled = pulled + from_dual[a][z] + sum_up(terms)
                grad_ref[a, z, :, lanes] = (
                    parts_ref[a, z, :, lanes] + coefficient * parts_ref[3 + a, z, :, lanes] + pull * pulled
                )
    for a in range(3):
        copies.append(pltpu.make_async_copy(grad_ref.at[a], grad_hbm.at[a], left.at[6 + a]))
        copies[6 + a].start(priority=a % 2)
    for copy in copies:
        copy.wait()


WHOLE = pl.BlockSpec(memory_space=pltpu.VMEM)
REMAIN = pl.BlockSpec(memory_space=pltpu.HBM)


def call(kernel, outs, operations, *operands, in_specs=None, out_specs=None, scratch=()):
    nbytes = sum(4 * int(np.prod(x.shape)) for x in (*operands, *outs))
    return pl.pallas_call(
        kernel,
        out_shape=outs,
        in_specs=in_specs or [WHOLE] * len(operands),
        out_specs=out_specs or [WHOLE] * len(outs),
        scratch_shapes=list(scratch),
        compiler_params=pltpu.CompilerParams(vmem_limit_bytes=32 * 1024 * 1024),
        cost_estimate=pl.CostEstimate(flops=operations, bytes_accessed=nbytes, transcendentals=0),
    )(*operands)


def from_ahead(values, shift):
    peers = lax.axis_size("span")
    return lax.ppermute(values, "span", [((i + shift) % peers, i) for i in range(peers)])


def from_source(values, span_shift, source):
    span, stream = lax.axis_size("span"), lax.axis_size("stream")
    pairs = [
        (((i + span_shift) % span) * stream + source(j) % stream, i * stream + j)
        for i in range(span)
        for j in range(stream)
    ]
    return lax.ppermute(values, ("span", "stream"), pairs)


def ring_source(stream):
    def source(j):
        if j % 2 == 0:
            return j - 2 if j >= 2 else 1
        return j + 2 if j + 2 < stream else j - 1

    return source


def on_device(velocity, strain, row_bins, cotangent):
    span, stream = lax.axis_size("span"), lax.axis_size("stream")
    cells, rows, width = velocity.shape[1:]
    tables = Tables(cells, span)
    slab = (rows, width)

    def shaped(*leading):
        return pltpu.VMEM(leading + slab, jnp.float32)

    bins = jnp.broadcast_to(row_bins[:, None], (rows, LANES))
    far_v = [from_ahead(velocity, shift) for shift in range(1, span)]
    work = cells * rows * width
    (lane,) = call(lanes_kernel, [pltpu.VMEM((rows, LANES), jnp.int32)], LONG * work)
    size, size_ends = call(
        functools.partial(prepare_kernel, tables), [shaped(cells), shaped(2)], LONG * work, lane, strain
    )
    size_ends, sent_cot = lax.optimization_barrier((size_ends, cotangent))
    far_size = [from_ahead(size_ends, shift) for shift in range(1, span)]
    far_cot = [from_ahead(sent_cot, shift) for shift in range(1, span)]
    table = pltpu.VMEM((8, LANES), jnp.float32)
    smooth, leonard, model, sums = call(
        functools.partial(forward_kernel, tables),
        [shaped(3, cells), shaped(6, cells), shaped(6, cells), table],
        LONG * work,
        velocity,
        strain,
        cotangent,
        size,
        bins,
        *far_v,
        *far_size,
    )
    other_sums = from_source(sums, 0, lambda j: j ^ 1)
    dual, message = call(
        functools.partial(message_kernel, tables), [shaped(3, cells), shaped(18)], 100 * work, smooth, model
    )
    pair_sums = sums + other_sums
    far_message = [from_ahead(message, shift) for shift in range(1, span)]
    most_rows = 2 * rows * stream // NBINS
    reach = -(-(most_rows - 1) // rows)
    turning = reach <= 1
    if turning:
        sources = [ring_source(stream)]
    else:
        steps = range(1, -(-reach // 2) + 1)
        sources = [functools.partial(lambda j, away: j + away, away=2 * step * way) for step in steps for way in (1, -1)]
    near_sums = [from_source(pair_sums, shift, source) for shift in reversed(range(span)) for source in sources]
    far_pairs = [from_ahead(pair_sums, shift) for shift in range(1, span)]
    (parts,) = call(
        functools.partial(local_kernel, tables),
        [shaped(12, cells)],
        LONG * work,
        velocity,
        cotangent,
        smooth,
        leonard,
        model,
        dual,
        *far_v,
        *far_cot,
    )
    outs = [jax.ShapeDtypeStruct((n, cells) + slab, jnp.float32) for n in (6, 3)]
    return tuple(
        call(
            functools.partial(finish_kernel, tables, len(near_sums), turning),
            outs,
            200 * work,
            velocity,
            leonard,
            model,
            parts,
            bins,
            *near_sums,
            pair_sums,
            *far_pairs,
            *far_message,
            out_specs=[REMAIN] * 2,
            scratch=[pltpu.VMEM(x.shape, x.dtype) for x in outs] + [pltpu.SemaphoreType.DMA((9,))],
        )
    )


def solution(mesh):
    fields = P(None, "span", "stream", None)
    return jax.shard_map(
        on_device,
        mesh=mesh,
        in_specs=(fields, fields, P("stream"), fields),
        out_specs=(fields, fields),
        check_vma=False,
    )
```

```python
import functools

import jax
import jax.numpy as jnp
import numpy as np
from jax import lax
from jax.experimental import pallas as pl
from jax.experimental.pallas import tpu as pltpu
from jax.sharding import PartitionSpec as P

NBINS = 64
FILTER_ALPHA = 0.45
CENTER_WEIGHT = 0.95
SIDE_WEIGHT = 0.475
STRAIN_FLOOR = 0.25
EPSILON = 1e-06
INDEX_PAIRS = ((0, 0), (0, 1), (0, 2), (1, 1), (1, 2), (2, 2))
PAIR_WEIGHTS = (1.0, 2.0, 2.0, 1.0, 2.0, 1.0)
PAIR_OF = ((0, 1, 2), (1, 3, 4), (2, 4, 5))
LANES = 128
LONG = 300000


def filter_row(extent):
    eye = np.eye(extent)
    ring = np.roll(eye, 1, axis=1) + np.roll(eye, -1, axis=1)
    system = eye + FILTER_ALPHA * ring
    side = CENTER_WEIGHT * eye + SIDE_WEIGHT * ring
    return np.linalg.solve(system, side)[0]


def end_weights(cells):
    weights = np.zeros((2, cells))
    weights[0, 0] = 1.0
    weights[1, cells - 1] = 1.0
    inner = cells - 2
    if inner > 0:
        system = np.eye(inner) + FILTER_ALPHA * (np.eye(inner, k=1) + np.eye(inner, k=-1))
        right = np.zeros((inner, 2))
        right[0, 0] = -FILTER_ALPHA
        right[inner - 1, 1] = -FILTER_ALPHA
        weights[:, 1:-1] = np.linalg.solve(system, right).T
    return weights


class Tables:
    def __init__(self, cells, devices):
        row = filter_row(cells * devices)
        extent = cells * devices
        self.cells = cells
        self.devices = devices
        self.own = [[float(row[(z - w) % extent]) for w in range(cells)] for z in range(cells)]
        self.ends = [[float(x) for x in line] for line in end_weights(cells)]
        self.couple = [
            [[float(row[(z - shift * cells - w) % extent]) for w in (0, cells - 1)] for z in range(cells)]
            for shift in range(devices)
        ]

    def project(self, values):
        return [weighted(line, values) for line in self.ends]

    def inside(self, values):
        return [weighted(line, values) for line in self.own]

    def outside(self, shift, ends):
        return [weighted(line, ends) for line in self.couple[shift]]


def weighted(weights, values):
    total = None
    for weight, value in zip(weights, values):
        if weight == 0.0:
            continue
        term = value if weight == 1.0 else value * weight
        total = term if total is None else total + term
    return total


def add_lists(left, right):
    return [x + y for x, y in zip(left, right)]


def halves(width):
    return [pl.ds(start, LANES) for start in range(0, width, LANES)]


def sum_up(terms):
    total = terms[0]
    for term in terms[1:]:
        total = total + term
    return total


def lanes_kernel(lane_ref):
    lane_ref[...] = lax.broadcasted_iota(jnp.int32, lane_ref.shape, 1)


def prepare_kernel(tables, lane_ref, strain_ref, size_ref, size_ends_ref):
    cells = tables.cells
    for lanes in halves(strain_ref.shape[-1]):
        size = []
        for z in range(cells):
            values = [strain_ref[k, z, :, lanes] for k in range(6)]
            total = sum_up([weight * (value * value) for weight, value in zip(PAIR_WEIGHTS, values)])
            size.append(jnp.sqrt(jnp.maximum(2.0 * total, STRAIN_FLOOR)))
            size_ref[z, :, lanes] = size[z]
        for end, value in enumerate(tables.project(size)):
            size_ends_ref[end, :, lanes] = value


def products_of(v):
    return [[x * y for x, y in zip(v[a], v[b])] for a, b in INDEX_PAIRS]


def filtered_block(tables, place, fields, ends):
    filtered = [tables.inside(field) for field in fields]
    for other in range(tables.devices):
        if other != place:
            shift = (other - place) % tables.devices
            filtered = [add_lists(near, tables.outside(shift, far)) for near, far in zip(filtered, ends[other])]
    return filtered


def plain_dual(tensor, vector, a, cells):
    return [sum_up([tensor[PAIR_OF[a][b]][z] * vector[b][z] for b in range(3)]) for z in range(cells)]


def weighted_dual(tensor, vector, a, cells):
    plain = plain_dual(tensor, vector, a, cells)
    return [plain[z] + tensor[PAIR_OF[a][a]][z] * vector[a][z] for z in range(cells)]


def forward_kernel(tables, *refs):
    peers = tables.devices - 1
    cells = tables.cells
    v_ref, strain_ref, cot_ref, size_ref, bins_ref = refs[:5]
    far_v_refs = refs[5 : 5 + peers]
    far_size_refs = refs[5 + peers : 5 + 2 * peers]
    smooth_ref, leonard_ref, model_ref, sums_ref = refs[5 + 2 * peers :]
    cross, square, blame = [], [], []
    for lanes in halves(v_ref.shape[-1]):
        v = [[v_ref[a, z, :, lanes] for z in range(cells)] for a in range(3)]
        size = [size_ref[z, :, lanes] for z in range(cells)]
        products = products_of(v)
        ends = [None]
        for far_v_ref, far_size_ref in zip(far_v_refs, far_size_refs):
            far = [[far_v_ref[a, z, :, lanes] for z in range(cells)] for a in range(3)]
            ends.append([tables.project(field) for field in far + products_of(far)])
            ends[-1].append([far_size_ref[end, :, lanes] for end in range(2)])
        filtered = filtered_block(tables, 0, v + products + [size], ends)
        smooth_v = filtered[:3]
        factor = [2.0 * (4.0 * filtered[9][z] - size[z]) for z in range(cells)]
        for k, (a, b) in enumerate(INDEX_PAIRS):
            for z in range(cells):
                coarse = smooth_v[a][z] * smooth_v[b][z]
                leonard = filtered[3 + k][z] - coarse
                term = products[k][z] - coarse + factor[z] * strain_ref[k, z, :, lanes]
                leonard_ref[k, z, :, lanes] = leonard
                model_ref[k, z, :, lanes] = term
                scaled = PAIR_WEIGHTS[k] * term
                cross.append(scaled * leonard)
                square.append(scaled * term)
                blame.append(term * cot_ref[k, z, :, lanes])
            cross, square, blame = [sum_up(cross)], [sum_up(square)], [sum_up(blame)]
        for a in range(3):
            for z in range(cells):
                smooth_ref[a, z, :, lanes] = smooth_v[a][z]
    lane = lax.broadcasted_iota(jnp.int32, bins_ref.shape, 1)
    mine = bins_ref[...] == lane
    place = lax.broadcasted_iota(jnp.int32, (8, LANES), 0)
    table = jnp.zeros((8, LANES), jnp.float32)
    for index, sums in enumerate((cross, square, blame)):
        per_row = jnp.sum(sums[0], axis=1, keepdims=True)
        per_bin = jnp.sum(jnp.where(mine, per_row, 0.0), axis=0, keepdims=True)
        table = jnp.where(place == index, per_bin, table)
    sums_ref[...] = table


def message_kernel(tables, smooth_ref, model_ref, sums_ref, other_sums_ref, dual_ref, message_ref, pair_ref):
    cells = tables.cells
    pair_sums = sums_ref[...] + other_sums_ref[...]
    pair_ref[...] = pair_sums
    message_ref[18, 0:8, 0:LANES] = pair_sums
    for lanes in halves(model_ref.shape[-1]):
        model = [[model_ref[k, z, :, lanes] for z in range(cells)] for k in range(6)]
        smooth_v = [[smooth_ref[a, z, :, lanes] for z in range(cells)] for a in range(3)]
        for k in range(6):
            for end, value in enumerate(tables.project(model[k])):
                message_ref[2 * k + end, :, lanes] = value
        for a in range(3):
            dual = [2.0 * x for x in plain_dual(model, smooth_v, a, cells)]
            for z in range(cells):
                dual_ref[a, z, :, lanes] = dual[z]
            for end, value in enumerate(tables.project(dual)):
                message_ref[12 + 2 * a + end, :, lanes] = value


def local_kernel(tables, *refs):
    peers = tables.devices - 1
    cells = tables.cells
    v_ref, cot_ref, smooth_ref, leonard_ref, model_ref, dual_ref = refs[:6]
    far_v_refs = refs[6 : 6 + peers]
    far_cot_refs = refs[6 + peers : 6 + 2 * peers]
    parts_ref = refs[-1]
    for lanes in halves(v_ref.shape[-1]):

        def load(ref, count):
            return [[ref[f, z, :, lanes] for z in range(cells)] for f in range(count)]

        fields, ends = [], []
        for ref in (v_ref, *far_v_refs):
            v = load(ref, 3)
            fields.append(v + products_of(v))
            ends.append([tables.project(field) for field in fields[-1]])
        v = fields[0][:3]
        cot, model, leonard, smooth_v = load(cot_ref, 6), load(model_ref, 6), load(leonard_ref, 6), load(smooth_ref, 3)
        smooth_cot = [tables.inside(field) for field in cot]
        duals = [weighted_dual(cot, smooth_v, a, cells) for a in range(3)]
        others = [plain_dual(leonard, smooth_v, a, cells) for a in range(3)]
        smooth_duals = [tables.inside(field) for field in duals]
        smooth_others = [tables.inside(field) for field in others]
        for place in range(1, tables.devices):
            far_cot = load(far_cot_refs[place - 1], 6)
            filtered = filtered_block(tables, place, fields[place], ends)
            far_smooth = filtered[:3]
            far_leonard = [
                [filtered[3 + k][z] - far_smooth[a][z] * far_smooth[b][z] for z in range(cells)]
                for k, (a, b) in enumerate(INDEX_PAIRS)
            ]
            for k in range(6):
                far = tables.outside(place, tables.project(far_cot[k]))
                smooth_cot[k] = add_lists(smooth_cot[k], far)
            for a in range(3):
                far = tables.outside(place, tables.project(weighted_dual(far_cot, far_smooth, a, cells)))
                smooth_duals[a] = add_lists(smooth_duals[a], far)
                far = tables.outside(place, tables.project(plain_dual(far_leonard, far_smooth, a, cells)))
                smooth_others[a] = add_lists(smooth_others[a], far)
        inner = [add_lists(tables.inside(model[k]), leonard[k]) for k in range(6)]
        for a in range(3):
            first = weighted_dual(smooth_cot, v, a, cells)
            second = weighted_dual(cot, v, a, cells)
            dual = tables.inside([dual_ref[a, z, :, lanes] for z in range(cells)])
            third = plain_dual(inner, v, a, cells)
            fourth = plain_dual(model, v, a, cells)
            for z in range(cells):
                parts_ref[a, z, :, lanes] = first[z] - smooth_duals[a][z]
                parts_ref[3 + a, z, :, lanes] = smooth_duals[a][z] - second[z]
                parts_ref[6 + a, z, :, lanes] = 2.0 * (third[z] - smooth_others[a][z]) - dual[z]
                parts_ref[9 + a, z, :, lanes] = 2.0 * dual[z] - 4.0 * fourth[z]


def finish_kernel(tables, count, turning, *refs):
    peers = tables.devices - 1
    cells = tables.cells
    v_ref, leonard_ref, model_ref, parts_ref, bins_ref = refs[:5]
    near_refs = refs[5 : 5 + count]
    pair_ref = refs[5 + count]
    far_message_refs = refs[6 + count : 6 + count + peers]
    residual_hbm, grad_hbm, residual_ref, grad_ref, left = refs[6 + count + peers :]
    total = sum_up([pair_ref[...]] + [ref[18, 0:8, 0:LANES] for ref in far_message_refs])
    near = sum_up([ref[...] for ref in near_refs])
    if turning:
        place = lax.axis_index("stream")
        inner = jnp.logical_and(place > 0, place < lax.axis_size("stream") - 1)
        near = jnp.where(inner, near, 0.0)
    total = total + near
    inverse = 1.0 / (total[1:2] + EPSILON)
    rows = v_ref.shape[2]
    lane = lax.broadcasted_iota(jnp.int32, bins_ref.shape, 1)
    mine = bins_ref[...] == lane

    def of_rows(per_bin):
        column = jnp.sum(jnp.where(mine, per_bin, 0.0), axis=1, keepdims=True)
        return jnp.broadcast_to(column, (rows, LANES))

    coefficient = of_rows(total[0:1] * inverse)
    pull = of_rows(-(total[2:3] * inverse))
    copies = []
    for k in range(6):
        for lanes in halves(v_ref.shape[-1]):
            for z in range(cells):
                residual_ref[k, z, :, lanes] = (
                    leonard_ref[k, z, :, lanes] - coefficient * model_ref[k, z, :, lanes]
                )
        if k % 3 == 2:
            some = pl.ds(k - 2, 3)
            copies.append(pltpu.make_async_copy(residual_ref.at[some], residual_hbm.at[some], left.at[k // 3]))
            copies[-1].start()
    for lanes in halves(v_ref.shape[-1]):
        v = [[v_ref[a, z, :, lanes] for z in range(cells)] for a in range(3)]
        from_model = [[] for _ in range(6)]
        from_dual = [[] for _ in range(3)]
        for place, ends in enumerate(far_message_refs, start=1):
            for k in range(6):
                from_model[k].append(tables.outside(place, [2.0 * ends[2 * k + end, :, lanes] for end in range(2)]))
            for a in range(3):
                pair = [(2.0 * coefficient - 1.0) * ends[12 + 2 * a + end, :, lanes] for end in range(2)]
                from_dual[a].append(tables.outside(place, pair))
        from_model = [functools.reduce(add_lists, lists) if lists else None for lists in from_model]
        from_dual = [functools.reduce(add_lists, lists) if lists else None for lists in from_dual]
        for a in range(3):
            for z in range(cells):
                pulled = parts_ref[6 + a, z, :, lanes] + coefficient * parts_ref[9 + a, z, :, lanes]
                if peers:
                    terms = [from_model[PAIR_OF[a][b]][z] * v[b][z] for b in range(3)]
                    pulled = pulled + from_dual[a][z] + sum_up(terms)
                grad_ref[a, z, :, lanes] = (
                    parts_ref[a, z, :, lanes] + coefficient * parts_ref[3 + a, z, :, lanes] + pull * pulled
                )
    copies.append(pltpu.make_async_copy(grad_ref, grad_hbm, left.at[2]))
    copies[-1].start()
    for copy in copies:
        copy.wait()


WHOLE = pl.BlockSpec(memory_space=pltpu.VMEM)
REMAIN = pl.BlockSpec(memory_space=pltpu.HBM)


def call(kernel, outs, operations, *operands, in_specs=None, out_specs=None, scratch=()):
    nbytes = sum(4 * int(np.prod(x.shape)) for x in (*operands, *outs))
    return pl.pallas_call(
        kernel,
        out_shape=outs,
        in_specs=in_specs or [WHOLE] * len(operands),
        out_specs=out_specs or [WHOLE] * len(outs),
        scratch_shapes=list(scratch),
        compiler_params=pltpu.CompilerParams(vmem_limit_bytes=32 * 1024 * 1024),
        cost_estimate=pl.CostEstimate(flops=operations, bytes_accessed=nbytes, transcendentals=0),
    )(*operands)


def from_ahead(values, shift):
    peers = lax.axis_size("span")
    return lax.ppermute(values, "span", [((i + shift) % peers, i) for i in range(peers)])


def from_source(values, span_shift, source):
    span, stream = lax.axis_size("span"), lax.axis_size("stream")
    pairs = [
        (((i + span_shift) % span) * stream + source(j) % stream, i * stream + j)
        for i in range(span)
        for j in range(stream)
    ]
    return lax.ppermute(values, ("span", "stream"), pairs)


def ring_source(stream):
    def source(j):
        if j % 2 == 0:
            return j - 2 if j >= 2 else 1
        return j + 2 if j + 2 < stream else j - 1

    return source


def on_device(velocity, strain, row_bins, cotangent):
    span, stream = lax.axis_size("span"), lax.axis_size("stream")
    cells, rows, width = velocity.shape[1:]
    tables = Tables(cells, span)
    slab = (rows, width)

    def shaped(*leading):
        return pltpu.VMEM(leading + slab, jnp.float32)

    bins = jnp.broadcast_to(row_bins[:, None], (rows, LANES))
    far_v = [from_ahead(velocity, shift) for shift in range(1, span)]
    work = cells * rows * width
    (lane,) = call(lanes_kernel, [pltpu.VMEM((rows, LANES), jnp.int32)], LONG * work)
    size, size_ends = call(
        functools.partial(prepare_kernel, tables), [shaped(cells), shaped(2)], LONG * work, lane, strain
    )
    size_ends, sent_cot = lax.optimization_barrier((size_ends, cotangent))
    far_size = [from_ahead(size_ends, shift) for shift in range(1, span)]
    far_cot = [from_ahead(sent_cot, shift) for shift in range(1, span)]
    table = pltpu.VMEM((8, LANES), jnp.float32)
    smooth, leonard, model, sums = call(
        functools.partial(forward_kernel, tables),
        [shaped(3, cells), shaped(6, cells), shaped(6, cells), table],
        LONG * work,
        velocity,
        strain,
        cotangent,
        size,
        bins,
        *far_v,
        *far_size,
    )
    other_sums = from_source(sums, 0, lambda j: j ^ 1)
    dual, message, pair_sums = call(
        functools.partial(message_kernel, tables),
        [shaped(3, cells), shaped(19), table],
        100 * work,
        smooth,
        model,
        sums,
        other_sums,
    )
    far_message = [from_ahead(message, shift) for shift in range(1, span)]
    most_rows = 2 * rows * stream // NBINS
    reach = -(-(most_rows - 1) // rows)
    turning = reach <= 1
    if turning:
        sources = [ring_source(stream)]
    else:
        steps = range(1, -(-reach // 2) + 1)
        sources = [functools.partial(lambda j, away: j + away, away=2 * step * way) for step in steps for way in (1, -1)]
    near_sums = [from_source(pair_sums, shift, source) for shift in range(span) for source in sources]
    (parts,) = call(
        functools.partial(local_kernel, tables),
        [shaped(12, cells)],
        500 * work,
        velocity,
        cotangent,
        smooth,
        leonard,
        model,
        dual,
        *far_v,
        *far_cot,
    )
    outs = [jax.ShapeDtypeStruct((n, cells) + slab, jnp.float32) for n in (6, 3)]
    return tuple(
        call(
            functools.partial(finish_kernel, tables, len(near_sums), turning),
            outs,
            200 * work,
            velocity,
            leonard,
            model,
            parts,
            bins,
            *near_sums,
            pair_sums,
            *far_message,
            out_specs=[REMAIN] * 2,
            scratch=[pltpu.VMEM(x.shape, x.dtype) for x in outs] + [pltpu.SemaphoreType.DMA((3,))],
        )
    )


def solution(mesh):
    fields = P(None, "span", "stream", None)
    return jax.shard_map(
        on_device,
        mesh=mesh,
        in_specs=(fields, fields, P("stream"), fields),
        out_specs=(fields, fields),
        check_vma=False,
    )
```

```python
import functools

import jax
import jax.numpy as jnp
import numpy as np
from jax import lax
from jax.experimental import pallas as pl
from jax.experimental.pallas import tpu as pltpu
from jax.sharding import PartitionSpec as P

NBINS = 64
FILTER_ALPHA = 0.45
CENTER_WEIGHT = 0.95
SIDE_WEIGHT = 0.475
STRAIN_FLOOR = 0.25
EPSILON = 1e-06
INDEX_PAIRS = ((0, 0), (0, 1), (0, 2), (1, 1), (1, 2), (2, 2))
PAIR_WEIGHTS = (1.0, 2.0, 2.0, 1.0, 2.0, 1.0)
PAIR_OF = ((0, 1, 2), (1, 3, 4), (2, 4, 5))
LANES = 128
LONG = 300000


def filter_row(extent):
    eye = np.eye(extent)
    ring = np.roll(eye, 1, axis=1) + np.roll(eye, -1, axis=1)
    system = eye + FILTER_ALPHA * ring
    side = CENTER_WEIGHT * eye + SIDE_WEIGHT * ring
    return np.linalg.solve(system, side)[0]


def end_weights(cells):
    weights = np.zeros((2, cells))
    weights[0, 0] = 1.0
    weights[1, cells - 1] = 1.0
    inner = cells - 2
    if inner > 0:
        system = np.eye(inner) + FILTER_ALPHA * (np.eye(inner, k=1) + np.eye(inner, k=-1))
        right = np.zeros((inner, 2))
        right[0, 0] = -FILTER_ALPHA
        right[inner - 1, 1] = -FILTER_ALPHA
        weights[:, 1:-1] = np.linalg.solve(system, right).T
    return weights


class Tables:
    def __init__(self, cells, devices):
        row = filter_row(cells * devices)
        extent = cells * devices
        self.cells = cells
        self.devices = devices
        self.own = [[float(row[(z - w) % extent]) for w in range(cells)] for z in range(cells)]
        self.ends = [[float(x) for x in line] for line in end_weights(cells)]
        self.couple = [
            [[float(row[(z - shift * cells - w) % extent]) for w in (0, cells - 1)] for z in range(cells)]
            for shift in range(devices)
        ]

    def project(self, values):
        return [weighted(line, values) for line in self.ends]

    def inside(self, values):
        return [weighted(line, values) for line in self.own]

    def outside(self, shift, ends):
        return [weighted(line, ends) for line in self.couple[shift]]


def weighted(weights, values):
    total = None
    for weight, value in zip(weights, values):
        if weight == 0.0:
            continue
        term = value if weight == 1.0 else value * weight
        total = term if total is None else total + term
    return total


def add_lists(left, right):
    return [x + y for x, y in zip(left, right)]


def halves(width):
    return [pl.ds(start, LANES) for start in range(0, width, LANES)]


def sum_up(terms):
    total = terms[0]
    for term in terms[1:]:
        total = total + term
    return total


def lanes_kernel(lane_ref):
    lane_ref[...] = lax.broadcasted_iota(jnp.int32, lane_ref.shape, 1)


def prepare_kernel(tables, lane_ref, strain_ref, size_ref, size_ends_ref):
    cells = tables.cells
    for lanes in halves(strain_ref.shape[-1]):
        size = []
        for z in range(cells):
            values = [strain_ref[k, z, :, lanes] for k in range(6)]
            total = sum_up([weight * (value * value) for weight, value in zip(PAIR_WEIGHTS, values)])
            size.append(jnp.sqrt(jnp.maximum(2.0 * total, STRAIN_FLOOR)))
            size_ref[z, :, lanes] = size[z]
        for end, value in enumerate(tables.project(size)):
            size_ends_ref[end, :, lanes] = value


def fetch_kernel(cot_hbm, size_ends_ref, cot_ref, arrived):
    copy = pltpu.make_async_copy(cot_hbm, cot_ref, arrived)
    copy.start()
    copy.wait()


def products_of(v):
    return [[x * y for x, y in zip(v[a], v[b])] for a, b in INDEX_PAIRS]


def filtered_block(tables, place, fields, ends):
    filtered = [tables.inside(field) for field in fields]
    for other in range(tables.devices):
        if other != place:
            shift = (other - place) % tables.devices
            filtered = [add_lists(near, tables.outside(shift, far)) for near, far in zip(filtered, ends[other])]
    return filtered


def plain_dual(tensor, vector, a, cells):
    return [sum_up([tensor[PAIR_OF[a][b]][z] * vector[b][z] for b in range(3)]) for z in range(cells)]


def weighted_dual(tensor, vector, a, cells):
    plain = plain_dual(tensor, vector, a, cells)
    return [plain[z] + tensor[PAIR_OF[a][a]][z] * vector[a][z] for z in range(cells)]


def forward_kernel(tables, *refs):
    peers = tables.devices - 1
    cells = tables.cells
    v_ref, strain_ref, cot_ref, size_ref, bins_ref = refs[:5]
    far_v_refs = refs[5 : 5 + peers]
    far_size_refs = refs[5 + peers : 5 + 2 * peers]
    smooth_ref, leonard_ref, model_ref, sums_ref = refs[5 + 2 * peers :]
    cross, square, blame = [], [], []
    for lanes in halves(v_ref.shape[-1]):
        v = [[v_ref[a, z, :, lanes] for z in range(cells)] for a in range(3)]
        size = [size_ref[z, :, lanes] for z in range(cells)]
        products = products_of(v)
        ends = [None]
        for far_v_ref, far_size_ref in zip(far_v_refs, far_size_refs):
            far = [[far_v_ref[a, z, :, lanes] for z in range(cells)] for a in range(3)]
            ends.append([tables.project(field) for field in far + products_of(far)])
            ends[-1].append([far_size_ref[end, :, lanes] for end in range(2)])
        filtered = filtered_block(tables, 0, v + products + [size], ends)
        smooth_v = filtered[:3]
        factor = [2.0 * (4.0 * filtered[9][z] - size[z]) for z in range(cells)]
        for k, (a, b) in enumerate(INDEX_PAIRS):
            for z in range(cells):
                coarse = smooth_v[a][z] * smooth_v[b][z]
                leonard = filtered[3 + k][z] - coarse
                term = products[k][z] - coarse + factor[z] * strain_ref[k, z, :, lanes]
                leonard_ref[k, z, :, lanes] = leonard
                model_ref[k, z, :, lanes] = term
                scaled = PAIR_WEIGHTS[k] * term
                cross.append(scaled * leonard)
                square.append(scaled * term)
                blame.append(term * cot_ref[k, z, :, lanes])
            cross, square, blame = [sum_up(cross)], [sum_up(square)], [sum_up(blame)]
        for a in range(3):
            for z in range(cells):
                smooth_ref[a, z, :, lanes] = smooth_v[a][z]
    lane = lax.broadcasted_iota(jnp.int32, bins_ref.shape, 1)
    mine = bins_ref[...] == lane
    place = lax.broadcasted_iota(jnp.int32, (8, LANES), 0)
    table = jnp.zeros((8, LANES), jnp.float32)
    for index, sums in enumerate((cross, square, blame)):
        per_row = jnp.sum(sums[0], axis=1, keepdims=True)
        per_bin = jnp.sum(jnp.where(mine, per_row, 0.0), axis=0, keepdims=True)
        table = jnp.where(place == index, per_bin, table)
    sums_ref[...] = table


def message_kernel(tables, smooth_ref, model_ref, sums_ref, other_sums_ref, dual_ref, message_ref, pair_ref):
    cells = tables.cells
    pair_sums = sums_ref[...] + other_sums_ref[...]
    pair_ref[...] = pair_sums
    message_ref[18, 0:8, 0:LANES] = pair_sums
    for lanes in halves(model_ref.shape[-1]):
        model = [[model_ref[k, z, :, lanes] for z in range(cells)] for k in range(6)]
        smooth_v = [[smooth_ref[a, z, :, lanes] for z in range(cells)] for a in range(3)]
        for k in range(6):
            for end, value in enumerate(tables.project(model[k])):
                message_ref[2 * k + end, :, lanes] = value
        for a in range(3):
            dual = [2.0 * x for x in plain_dual(model, smooth_v, a, cells)]
            for z in range(cells):
                dual_ref[a, z, :, lanes] = dual[z]
            for end, value in enumerate(tables.project(dual)):
                message_ref[12 + 2 * a + end, :, lanes] = value


def local_kernel(tables, *refs):
    peers = tables.devices - 1
    cells = tables.cells
    v_ref, cot_ref, smooth_ref, leonard_ref, model_ref, dual_ref = refs[:6]
    far_v_refs = refs[6 : 6 + peers]
    far_cot_refs = refs[6 + peers : 6 + 2 * peers]
    parts_ref = refs[-1]
    for lanes in halves(v_ref.shape[-1]):

        def load(ref, count):
            return [[ref[f, z, :, lanes] for z in range(cells)] for f in range(count)]

        fields, ends = [], []
        for ref in (v_ref, *far_v_refs):
            v = load(ref, 3)
            fields.append(v + products_of(v))
            ends.append([tables.project(field) for field in fields[-1]])
        v = fields[0][:3]
        cot, model, leonard, smooth_v = load(cot_ref, 6), load(model_ref, 6), load(leonard_ref, 6), load(smooth_ref, 3)
        smooth_cot = [tables.inside(field) for field in cot]
        duals = [weighted_dual(cot, smooth_v, a, cells) for a in range(3)]
        others = [plain_dual(leonard, smooth_v, a, cells) for a in range(3)]
        smooth_duals = [tables.inside(field) for field in duals]
        smooth_others = [tables.inside(field) for field in others]
        for place in range(1, tables.devices):
            far_cot = load(far_cot_refs[place - 1], 6)
            filtered = filtered_block(tables, place, fields[place], ends)
            far_smooth = filtered[:3]
            far_leonard = [
                [filtered[3 + k][z] - far_smooth[a][z] * far_smooth[b][z] for z in range(cells)]
                for k, (a, b) in enumerate(INDEX_PAIRS)
            ]
            for k in range(6):
                far = tables.outside(place, tables.project(far_cot[k]))
                smooth_cot[k] = add_lists(smooth_cot[k], far)
            for a in range(3):
                far = tables.outside(place, tables.project(weighted_dual(far_cot, far_smooth, a, cells)))
                smooth_duals[a] = add_lists(smooth_duals[a], far)
                far = tables.outside(place, tables.project(plain_dual(far_leonard, far_smooth, a, cells)))
                smooth_others[a] = add_lists(smooth_others[a], far)
        inner = [add_lists(tables.inside(model[k]), leonard[k]) for k in range(6)]
        for a in range(3):
            first = weighted_dual(smooth_cot, v, a, cells)
            second = weighted_dual(cot, v, a, cells)
            dual = tables.inside([dual_ref[a, z, :, lanes] for z in range(cells)])
            third = plain_dual(inner, v, a, cells)
            fourth = plain_dual(model, v, a, cells)
            for z in range(cells):
                parts_ref[a, z, :, lanes] = first[z] - smooth_duals[a][z]
                parts_ref[3 + a, z, :, lanes] = smooth_duals[a][z] - second[z]
                parts_ref[6 + a, z, :, lanes] = 2.0 * (third[z] - smooth_others[a][z]) - dual[z]
                parts_ref[9 + a, z, :, lanes] = 2.0 * dual[z] - 4.0 * fourth[z]


def finish_kernel(tables, count, turning, *refs):
    peers = tables.devices - 1
    cells = tables.cells
    v_ref, leonard_ref, model_ref, parts_ref, bins_ref = refs[:5]
    near_refs = refs[5 : 5 + count]
    pair_ref = refs[5 + count]
    far_message_refs = refs[6 + count : 6 + count + peers]
    residual_hbm, grad_hbm, residual_ref, grad_ref, left = refs[6 + count + peers :]
    total = sum_up([pair_ref[...]] + [ref[18, 0:8, 0:LANES] for ref in far_message_refs])
    near = sum_up([ref[...] for ref in near_refs])
    if turning:
        place = lax.axis_index("stream")
        inner = jnp.logical_and(place > 0, place < lax.axis_size("stream") - 1)
        near = jnp.where(inner, near, 0.0)
    total = total + near
    inverse = 1.0 / (total[1:2] + EPSILON)
    rows = v_ref.shape[2]
    lane = lax.broadcasted_iota(jnp.int32, bins_ref.shape, 1)
    mine = bins_ref[...] == lane

    def of_rows(per_bin):
        column = jnp.sum(jnp.where(mine, per_bin, 0.0), axis=1, keepdims=True)
        return jnp.broadcast_to(column, (rows, LANES))

    coefficient = of_rows(total[0:1] * inverse)
    pull = of_rows(-(total[2:3] * inverse))
    copies = []
    for k in range(6):
        for lanes in halves(v_ref.shape[-1]):
            for z in range(cells):
                residual_ref[k, z, :, lanes] = (
                    leonard_ref[k, z, :, lanes] - coefficient * model_ref[k, z, :, lanes]
                )
        if k % 3 == 2:
            some = pl.ds(k - 2, 3)
            copies.append(pltpu.make_async_copy(residual_ref.at[some], residual_hbm.at[some], left.at[k // 3]))
            copies[-1].start()
    for lanes in halves(v_ref.shape[-1]):
        v = [[v_ref[a, z, :, lanes] for z in range(cells)] for a in range(3)]
        from_model = [[] for _ in range(6)]
        from_dual = [[] for _ in range(3)]
        for place, ends in enumerate(far_message_refs, start=1):
            for k in range(6):
                from_model[k].append(tables.outside(place, [2.0 * ends[2 * k + end, :, lanes] for end in range(2)]))
            for a in range(3):
                pair = [(2.0 * coefficient - 1.0) * ends[12 + 2 * a + end, :, lanes] for end in range(2)]
                from_dual[a].append(tables.outside(place, pair))
        from_model = [functools.reduce(add_lists, lists) if lists else None for lists in from_model]
        from_dual = [functools.reduce(add_lists, lists) if lists else None for lists in from_dual]
        for a in range(3):
            for z in range(cells):
                pulled = parts_ref[6 + a, z, :, lanes] + coefficient * parts_ref[9 + a, z, :, lanes]
                if peers:
                    terms = [from_model[PAIR_OF[a][b]][z] * v[b][z] for b in range(3)]
                    pulled = pulled + from_dual[a][z] + sum_up(terms)
                grad_ref[a, z, :, lanes] = (
                    parts_ref[a, z, :, lanes] + coefficient * parts_ref[3 + a, z, :, lanes] + pull * pulled
                )
    copies.append(pltpu.make_async_copy(grad_ref, grad_hbm, left.at[2]))
    copies[-1].start()
    for copy in copies:
        copy.wait()


WHOLE = pl.BlockSpec(memory_space=pltpu.VMEM)
REMAIN = pl.BlockSpec(memory_space=pltpu.HBM)


def call(kernel, outs, operations, *operands, in_specs=None, out_specs=None, scratch=()):
    nbytes = sum(4 * int(np.prod(x.shape)) for x in (*operands, *outs))
    return pl.pallas_call(
        kernel,
        out_shape=outs,
        in_specs=in_specs or [WHOLE] * len(operands),
        out_specs=out_specs or [WHOLE] * len(outs),
        scratch_shapes=list(scratch),
        compiler_params=pltpu.CompilerParams(vmem_limit_bytes=32 * 1024 * 1024),
        cost_estimate=pl.CostEstimate(flops=operations, bytes_accessed=nbytes, transcendentals=0),
    )(*operands)


def from_ahead(values, shift):
    peers = lax.axis_size("span")
    return lax.ppermute(values, "span", [((i + shift) % peers, i) for i in range(peers)])


def from_source(values, span_shift, source):
    span, stream = lax.axis_size("span"), lax.axis_size("stream")
    pairs = [
        (((i + span_shift) % span) * stream + source(j) % stream, i * stream + j)
        for i in range(span)
        for j in range(stream)
    ]
    return lax.ppermute(values, ("span", "stream"), pairs)


def ring_source(stream):
    def source(j):
        if j % 2 == 0:
            return j - 2 if j >= 2 else 1
        return j + 2 if j + 2 < stream else j - 1

    return source


def on_device(velocity, strain, row_bins, cotangent):
    span, stream = lax.axis_size("span"), lax.axis_size("stream")
    cells, rows, width = velocity.shape[1:]
    tables = Tables(cells, span)
    slab = (rows, width)

    def shaped(*leading):
        return pltpu.VMEM(leading + slab, jnp.float32)

    bins = jnp.broadcast_to(row_bins[:, None], (rows, LANES))
    far_v = [from_ahead(velocity, shift) for shift in range(1, span)]
    work = cells * rows * width
    (lane,) = call(lanes_kernel, [pltpu.VMEM((rows, LANES), jnp.int32)], LONG * work)
    size, size_ends = call(
        functools.partial(prepare_kernel, tables), [shaped(cells), shaped(2)], LONG * work, lane, strain
    )
    far_size = [from_ahead(size_ends, shift) for shift in range(1, span)]
    (near_cot,) = call(
        fetch_kernel,
        [shaped(6, cells)],
        work,
        pltpu.with_memory_space_constraint(cotangent, pltpu.HBM),
        size_ends,
        in_specs=[REMAIN, WHOLE],
        scratch=[pltpu.SemaphoreType.DMA(())],
    )
    far_cot = [from_ahead(near_cot, shift) for shift in range(1, span)]
    table = pltpu.VMEM((8, LANES), jnp.float32)
    smooth, leonard, model, sums = call(
        functools.partial(forward_kernel, tables),
        [shaped(3, cells), shaped(6, cells), shaped(6, cells), table],
        LONG * work,
        velocity,
        strain,
        near_cot,
        size,
        bins,
        *far_v,
        *far_size,
    )
    other_sums = from_source(sums, 0, lambda j: j ^ 1)
    dual, message, pair_sums = call(
        functools.partial(message_kernel, tables),
        [shaped(3, cells), shaped(19), table],
        100 * work,
        smooth,
        model,
        sums,
        other_sums,
    )
    far_message = [from_ahead(message, shift) for shift in range(1, span)]
    most_rows = 2 * rows * stream // NBINS
    reach = -(-(most_rows - 1) // rows)
    turning = reach <= 1
    if turning:
        sources = [ring_source(stream)]
    else:
        steps = range(1, -(-reach // 2) + 1)
        sources = [functools.partial(lambda j, away: j + away, away=2 * step * way) for step in steps for way in (1, -1)]
    near_sums = [from_source(pair_sums, shift, source) for shift in range(span) for source in sources]
    (parts,) = call(
        functools.partial(local_kernel, tables),
        [shaped(12, cells)],
        500 * work,
        velocity,
        near_cot,
        smooth,
        leonard,
        model,
        dual,
        *far_v,
        *far_cot,
    )
    outs = [jax.ShapeDtypeStruct((n, cells) + slab, jnp.float32) for n in (6, 3)]
    return tuple(
        call(
            functools.partial(finish_kernel, tables, len(near_sums), turning),
            outs,
            200 * work,
            velocity,
            leonard,
            model,
            parts,
            bins,
            *near_sums,
            pair_sums,
            *far_message,
            out_specs=[REMAIN] * 2,
            scratch=[pltpu.VMEM(x.shape, x.dtype) for x in outs] + [pltpu.SemaphoreType.DMA((3,))],
        )
    )


def solution(mesh):
    fields = P(None, "span", "stream", None)
    return jax.shard_map(
        on_device,
        mesh=mesh,
        in_specs=(fields, fields, P("stream"), fields),
        out_specs=(fields, fields),
        check_vma=False,
    )
```

```python
import functools

import jax
import jax.numpy as jnp
import numpy as np
from jax import lax
from jax.experimental import pallas as pl
from jax.experimental.pallas import tpu as pltpu
from jax.sharding import PartitionSpec as P

NBINS = 64
FILTER_ALPHA = 0.45
CENTER_WEIGHT = 0.95
SIDE_WEIGHT = 0.475
STRAIN_FLOOR = 0.25
EPSILON = 1e-06
INDEX_PAIRS = ((0, 0), (0, 1), (0, 2), (1, 1), (1, 2), (2, 2))
PAIR_WEIGHTS = (1.0, 2.0, 2.0, 1.0, 2.0, 1.0)
PAIR_OF = ((0, 1, 2), (1, 3, 4), (2, 4, 5))
LANES = 128
LONG = 300000


def filter_row(extent):
    eye = np.eye(extent)
    ring = np.roll(eye, 1, axis=1) + np.roll(eye, -1, axis=1)
    system = eye + FILTER_ALPHA * ring
    side = CENTER_WEIGHT * eye + SIDE_WEIGHT * ring
    return np.linalg.solve(system, side)[0]


def end_weights(cells):
    weights = np.zeros((2, cells))
    weights[0, 0] = 1.0
    weights[1, cells - 1] = 1.0
    inner = cells - 2
    if inner > 0:
        system = np.eye(inner) + FILTER_ALPHA * (np.eye(inner, k=1) + np.eye(inner, k=-1))
        right = np.zeros((inner, 2))
        right[0, 0] = -FILTER_ALPHA
        right[inner - 1, 1] = -FILTER_ALPHA
        weights[:, 1:-1] = np.linalg.solve(system, right).T
    return weights


class Tables:
    def __init__(self, cells, devices):
        row = filter_row(cells * devices)
        extent = cells * devices
        self.cells = cells
        self.devices = devices
        self.own = [[float(row[(z - w) % extent]) for w in range(cells)] for z in range(cells)]
        self.ends = [[float(x) for x in line] for line in end_weights(cells)]
        self.couple = [
            [[float(row[(z - shift * cells - w) % extent]) for w in (0, cells - 1)] for z in range(cells)]
            for shift in range(devices)
        ]

    def project(self, values):
        return [weighted(line, values) for line in self.ends]

    def inside(self, values):
        return [weighted(line, values) for line in self.own]

    def outside(self, shift, ends):
        return [weighted(line, ends) for line in self.couple[shift]]


def weighted(weights, values):
    total = None
    for weight, value in zip(weights, values):
        if weight == 0.0:
            continue
        term = value if weight == 1.0 else value * weight
        total = term if total is None else total + term
    return total


def add_lists(left, right):
    return [x + y for x, y in zip(left, right)]


def halves(width):
    return [pl.ds(start, LANES) for start in range(0, width, LANES)]


def sum_up(terms):
    total = terms[0]
    for term in terms[1:]:
        total = total + term
    return total


def lanes_kernel(lane_ref):
    lane_ref[...] = lax.broadcasted_iota(jnp.int32, lane_ref.shape, 1)


def prepare_kernel(tables, lane_ref, strain_ref, size_ref, size_ends_ref):
    cells = tables.cells
    for lanes in halves(strain_ref.shape[-1]):
        size = []
        for z in range(cells):
            values = [strain_ref[k, z, :, lanes] for k in range(6)]
            total = sum_up([weight * (value * value) for weight, value in zip(PAIR_WEIGHTS, values)])
            size.append(jnp.sqrt(jnp.maximum(2.0 * total, STRAIN_FLOOR)))
            size_ref[z, :, lanes] = size[z]
        for end, value in enumerate(tables.project(size)):
            size_ends_ref[end, :, lanes] = value


def fetch_kernel(cot_hbm, size_ends_ref, cot_ref, arrived):
    copy = pltpu.make_async_copy(cot_hbm, cot_ref, arrived)
    copy.start()
    copy.wait()


def products_of(v):
    return [[x * y for x, y in zip(v[a], v[b])] for a, b in INDEX_PAIRS]


def filtered_block(tables, place, fields, ends):
    filtered = [tables.inside(field) for field in fields]
    for other in range(tables.devices):
        if other != place:
            shift = (other - place) % tables.devices
            filtered = [add_lists(near, tables.outside(shift, far)) for near, far in zip(filtered, ends[other])]
    return filtered


def plain_dual(tensor, vector, a, cells):
    return [sum_up([tensor[PAIR_OF[a][b]][z] * vector[b][z] for b in range(3)]) for z in range(cells)]


def weighted_dual(tensor, vector, a, cells):
    plain = plain_dual(tensor, vector, a, cells)
    return [plain[z] + tensor[PAIR_OF[a][a]][z] * vector[a][z] for z in range(cells)]


def forward_kernel(tables, *refs):
    peers = tables.devices - 1
    cells = tables.cells
    v_ref, strain_ref, cot_ref, size_ref, bins_ref = refs[:5]
    far_v_refs = refs[5 : 5 + peers]
    far_size_refs = refs[5 + peers : 5 + 2 * peers]
    smooth_ref, leonard_ref, model_ref, sums_ref = refs[5 + 2 * peers :]
    cross, square, blame = [], [], []
    for lanes in halves(v_ref.shape[-1]):
        v = [[v_ref[a, z, :, lanes] for z in range(cells)] for a in range(3)]
        size = [size_ref[z, :, lanes] for z in range(cells)]
        products = products_of(v)
        ends = [None]
        for far_v_ref, far_size_ref in zip(far_v_refs, far_size_refs):
            far = [[far_v_ref[a, z, :, lanes] for z in range(cells)] for a in range(3)]
            ends.append([tables.project(field) for field in far + products_of(far)])
            ends[-1].append([far_size_ref[end, :, lanes] for end in range(2)])
        filtered = filtered_block(tables, 0, v + products + [size], ends)
        smooth_v = filtered[:3]
        factor = [2.0 * (4.0 * filtered[9][z] - size[z]) for z in range(cells)]
        for k, (a, b) in enumerate(INDEX_PAIRS):
            for z in range(cells):
                coarse = smooth_v[a][z] * smooth_v[b][z]
                leonard = filtered[3 + k][z] - coarse
                term = products[k][z] - coarse + factor[z] * strain_ref[k, z, :, lanes]
                leonard_ref[k, z, :, lanes] = leonard
                model_ref[k, z, :, lanes] = term
                scaled = PAIR_WEIGHTS[k] * term
                cross.append(scaled * leonard)
                square.append(scaled * term)
                blame.append(term * cot_ref[k, z, :, lanes])
            cross, square, blame = [sum_up(cross)], [sum_up(square)], [sum_up(blame)]
        for a in range(3):
            for z in range(cells):
                smooth_ref[a, z, :, lanes] = smooth_v[a][z]
    lane = lax.broadcasted_iota(jnp.int32, bins_ref.shape, 1)
    mine = bins_ref[...] == lane
    place = lax.broadcasted_iota(jnp.int32, (8, LANES), 0)
    table = jnp.zeros((8, LANES), jnp.float32)
    for index, sums in enumerate((cross, square, blame)):
        per_row = jnp.sum(sums[0], axis=1, keepdims=True)
        per_bin = jnp.sum(jnp.where(mine, per_row, 0.0), axis=0, keepdims=True)
        table = jnp.where(place == index, per_bin, table)
    sums_ref[...] = table


def message_kernel(tables, smooth_ref, model_ref, dual_ref, message_ref):
    cells = tables.cells
    for lanes in halves(model_ref.shape[-1]):
        model = [[model_ref[k, z, :, lanes] for z in range(cells)] for k in range(6)]
        smooth_v = [[smooth_ref[a, z, :, lanes] for z in range(cells)] for a in range(3)]
        for k in range(6):
            for end, value in enumerate(tables.project(model[k])):
                message_ref[2 * k + end, :, lanes] = value
        for a in range(3):
            dual = [2.0 * x for x in plain_dual(model, smooth_v, a, cells)]
            for z in range(cells):
                dual_ref[a, z, :, lanes] = dual[z]
            for end, value in enumerate(tables.project(dual)):
                message_ref[12 + 2 * a + end, :, lanes] = value


def local_kernel(tables, *refs):
    peers = tables.devices - 1
    cells = tables.cells
    v_ref, cot_ref, smooth_ref, leonard_ref, model_ref, dual_ref = refs[:6]
    far_v_refs = refs[6 : 6 + peers]
    far_cot_refs = refs[6 + peers : 6 + 2 * peers]
    parts_ref = refs[-1]
    for lanes in halves(v_ref.shape[-1]):

        def load(ref, count):
            return [[ref[f, z, :, lanes] for z in range(cells)] for f in range(count)]

        fields, ends = [], []
        for ref in (v_ref, *far_v_refs):
            v = load(ref, 3)
            fields.append(v + products_of(v))
            ends.append([tables.project(field) for field in fields[-1]])
        v = fields[0][:3]
        cot, model, leonard, smooth_v = load(cot_ref, 6), load(model_ref, 6), load(leonard_ref, 6), load(smooth_ref, 3)
        smooth_cot = [tables.inside(field) for field in cot]
        duals = [weighted_dual(cot, smooth_v, a, cells) for a in range(3)]
        others = [plain_dual(leonard, smooth_v, a, cells) for a in range(3)]
        smooth_duals = [tables.inside(field) for field in duals]
        smooth_others = [tables.inside(field) for field in others]
        for place in range(1, tables.devices):
            far_cot = load(far_cot_refs[place - 1], 6)
            filtered = filtered_block(tables, place, fields[place], ends)
            far_smooth = filtered[:3]
            far_leonard = [
                [filtered[3 + k][z] - far_smooth[a][z] * far_smooth[b][z] for z in range(cells)]
                for k, (a, b) in enumerate(INDEX_PAIRS)
            ]
            for k in range(6):
                far = tables.outside(place, tables.project(far_cot[k]))
                smooth_cot[k] = add_lists(smooth_cot[k], far)
            for a in range(3):
                far = tables.outside(place, tables.project(weighted_dual(far_cot, far_smooth, a, cells)))
                smooth_duals[a] = add_lists(smooth_duals[a], far)
                far = tables.outside(place, tables.project(plain_dual(far_leonard, far_smooth, a, cells)))
                smooth_others[a] = add_lists(smooth_others[a], far)
        inner = [add_lists(tables.inside(model[k]), leonard[k]) for k in range(6)]
        for a in range(3):
            first = weighted_dual(smooth_cot, v, a, cells)
            second = weighted_dual(cot, v, a, cells)
            dual = tables.inside([dual_ref[a, z, :, lanes] for z in range(cells)])
            third = plain_dual(inner, v, a, cells)
            fourth = plain_dual(model, v, a, cells)
            for z in range(cells):
                parts_ref[a, z, :, lanes] = first[z] - smooth_duals[a][z]
                parts_ref[3 + a, z, :, lanes] = smooth_duals[a][z] - second[z]
                parts_ref[6 + a, z, :, lanes] = 2.0 * (third[z] - smooth_others[a][z]) - dual[z]
                parts_ref[9 + a, z, :, lanes] = 2.0 * dual[z] - 4.0 * fourth[z]


def finish_kernel(tables, count, turning, *refs):
    peers = tables.devices - 1
    cells = tables.cells
    v_ref, leonard_ref, model_ref, parts_ref, bins_ref = refs[:5]
    near_refs = refs[5 : 5 + count]
    pair_ref = refs[5 + count]
    far_message_refs = refs[6 + count : 6 + count + peers]
    residual_hbm, grad_hbm, residual_ref, grad_ref, left = refs[6 + count + peers :]
    total = pair_ref[...]
    near = sum_up([ref[...] for ref in near_refs])
    if turning:
        place = 2 * lax.axis_index("pair") + lax.axis_index("core")
        inner = jnp.logical_and(place > 0, place < 2 * lax.axis_size("pair") - 1)
        near = jnp.where(inner, near, 0.0)
    total = total + near
    inverse = 1.0 / (total[1:2] + EPSILON)
    rows = v_ref.shape[2]
    lane = lax.broadcasted_iota(jnp.int32, bins_ref.shape, 1)
    mine = bins_ref[...] == lane

    def of_rows(per_bin):
        column = jnp.sum(jnp.where(mine, per_bin, 0.0), axis=1, keepdims=True)
        return jnp.broadcast_to(column, (rows, LANES))

    coefficient = of_rows(total[0:1] * inverse)
    pull = of_rows(-(total[2:3] * inverse))
    copies = []
    for k in range(6):
        for lanes in halves(v_ref.shape[-1]):
            for z in range(cells):
                residual_ref[k, z, :, lanes] = (
                    leonard_ref[k, z, :, lanes] - coefficient * model_ref[k, z, :, lanes]
                )
        if k % 3 == 2:
            some = pl.ds(k - 2, 3)
            copies.append(pltpu.make_async_copy(residual_ref.at[some], residual_hbm.at[some], left.at[k // 3]))
            copies[-1].start()
    for lanes in halves(v_ref.shape[-1]):
        v = [[v_ref[a, z, :, lanes] for z in range(cells)] for a in range(3)]
        from_model = [[] for _ in range(6)]
        from_dual = [[] for _ in range(3)]
        for place, ends in enumerate(far_message_refs, start=1):
            for k in range(6):
                from_model[k].append(tables.outside(place, [2.0 * ends[2 * k + end, :, lanes] for end in range(2)]))
            for a in range(3):
                pair = [(2.0 * coefficient - 1.0) * ends[12 + 2 * a + end, :, lanes] for end in range(2)]
                from_dual[a].append(tables.outside(place, pair))
        from_model = [functools.reduce(add_lists, lists) if lists else None for lists in from_model]
        from_dual = [functools.reduce(add_lists, lists) if lists else None for lists in from_dual]
        for a in range(3):
            for z in range(cells):
                pulled = parts_ref[6 + a, z, :, lanes] + coefficient * parts_ref[9 + a, z, :, lanes]
                if peers:
                    terms = [from_model[PAIR_OF[a][b]][z] * v[b][z] for b in range(3)]
                    pulled = pulled + from_dual[a][z] + sum_up(terms)
                grad_ref[a, z, :, lanes] = (
                    parts_ref[a, z, :, lanes] + coefficient * parts_ref[3 + a, z, :, lanes] + pull * pulled
                )
    copies.append(pltpu.make_async_copy(grad_ref, grad_hbm, left.at[2]))
    copies[-1].start()
    for copy in copies:
        copy.wait()


WHOLE = pl.BlockSpec(memory_space=pltpu.VMEM)
REMAIN = pl.BlockSpec(memory_space=pltpu.HBM)


def call(kernel, outs, operations, *operands, in_specs=None, out_specs=None, scratch=()):
    nbytes = sum(4 * int(np.prod(x.shape)) for x in (*operands, *outs))
    return pl.pallas_call(
        kernel,
        out_shape=outs,
        in_specs=in_specs or [WHOLE] * len(operands),
        out_specs=out_specs or [WHOLE] * len(outs),
        scratch_shapes=list(scratch),
        compiler_params=pltpu.CompilerParams(vmem_limit_bytes=32 * 1024 * 1024),
        cost_estimate=pl.CostEstimate(flops=operations, bytes_accessed=nbytes, transcendentals=0),
    )(*operands)


def from_ahead(values, shift):
    peers = lax.axis_size("span")
    return lax.ppermute(values, "span", [((i + shift) % peers, i) for i in range(peers)])


def from_source(values, source):
    stream = 2 * lax.axis_size("pair")
    return lax.ppermute(values, ("pair", "core"), [(source(j) % stream, j) for j in range(stream)])


def ring_source(stream):
    def source(j):
        if j % 2 == 0:
            return j - 2 if j >= 2 else 1
        return j + 2 if j + 2 < stream else j - 1

    return source


def on_device(velocity, strain, row_bins, cotangent):
    span, stream = lax.axis_size("span"), 2 * lax.axis_size("pair")
    cells, rows, width = velocity.shape[1:]
    tables = Tables(cells, span)
    slab = (rows, width)

    def shaped(*leading):
        return pltpu.VMEM(leading + slab, jnp.float32)

    bins = jnp.broadcast_to(row_bins[:, None], (rows, LANES))
    far_v = [from_ahead(velocity, shift) for shift in range(1, span)]
    work = cells * rows * width
    (lane,) = call(lanes_kernel, [pltpu.VMEM((rows, LANES), jnp.int32)], LONG * work)
    size, size_ends = call(
        functools.partial(prepare_kernel, tables), [shaped(cells), shaped(2)], LONG * work, lane, strain
    )
    far_size = [from_ahead(size_ends, shift) for shift in range(1, span)]
    (near_cot,) = call(
        fetch_kernel,
        [shaped(6, cells)],
        work,
        pltpu.with_memory_space_constraint(cotangent, pltpu.HBM),
        size_ends,
        in_specs=[REMAIN, WHOLE],
        scratch=[pltpu.SemaphoreType.DMA(())],
    )
    far_cot = [from_ahead(near_cot, shift) for shift in range(1, span)]
    table = pltpu.VMEM((8, LANES), jnp.float32)
    smooth, leonard, model, sums = call(
        functools.partial(forward_kernel, tables),
        [shaped(3, cells), shaped(6, cells), shaped(6, cells), table],
        LONG * work,
        velocity,
        strain,
        near_cot,
        size,
        bins,
        *far_v,
        *far_size,
    )
    dual, message = call(
        functools.partial(message_kernel, tables), [shaped(3, cells), shaped(18)], 100 * work, smooth, model
    )
    pair_sums = lax.psum(sums, ("span", "core"))
    far_message = [from_ahead(message, shift) for shift in range(1, span)]
    most_rows = 2 * rows * stream // NBINS
    reach = -(-(most_rows - 1) // rows)
    turning = reach <= 1
    if turning:
        sources = [ring_source(stream)]
    else:
        steps = range(1, -(-reach // 2) + 1)
        sources = [functools.partial(lambda j, away: j + away, away=2 * step * way) for step in steps for way in (1, -1)]
    near_sums = [from_source(pair_sums, source) for source in sources]
    (parts,) = call(
        functools.partial(local_kernel, tables),
        [shaped(12, cells)],
        500 * work,
        velocity,
        near_cot,
        smooth,
        leonard,
        model,
        dual,
        *far_v,
        *far_cot,
    )
    outs = [jax.ShapeDtypeStruct((n, cells) + slab, jnp.float32) for n in (6, 3)]
    return tuple(
        call(
            functools.partial(finish_kernel, tables, len(near_sums), turning),
            outs,
            200 * work,
            velocity,
            leonard,
            model,
            parts,
            bins,
            *near_sums,
            pair_sums,
            *far_message,
            out_specs=[REMAIN] * 2,
            scratch=[pltpu.VMEM(x.shape, x.dtype) for x in outs] + [pltpu.SemaphoreType.DMA((3,))],
        )
    )


def solution(mesh):
    span, stream = mesh.devices.shape
    cut = jax.sharding.Mesh(mesh.devices.reshape(span, stream // 2, 2), ("span", "pair", "core"))
    fields = P(None, "span", ("pair", "core"), None)
    return jax.shard_map(
        on_device,
        mesh=cut,
        in_specs=(fields, fields, P(("pair", "core")), fields),
        out_specs=(fields, fields),
        check_vma=False,
    )
```

```python
import functools

import jax
import jax.numpy as jnp
import numpy as np
from jax import lax
from jax.experimental import pallas as pl
from jax.experimental.pallas import tpu as pltpu
from jax.sharding import PartitionSpec as P

NBINS = 64
FILTER_ALPHA = 0.45
CENTER_WEIGHT = 0.95
SIDE_WEIGHT = 0.475
STRAIN_FLOOR = 0.25
EPSILON = 1e-06
INDEX_PAIRS = ((0, 0), (0, 1), (0, 2), (1, 1), (1, 2), (2, 2))
PAIR_WEIGHTS = (1.0, 2.0, 2.0, 1.0, 2.0, 1.0)
PAIR_OF = ((0, 1, 2), (1, 3, 4), (2, 4, 5))
LANES = 128
LONG = 300000


def filter_row(extent):
    eye = np.eye(extent)
    ring = np.roll(eye, 1, axis=1) + np.roll(eye, -1, axis=1)
    system = eye + FILTER_ALPHA * ring
    side = CENTER_WEIGHT * eye + SIDE_WEIGHT * ring
    return np.linalg.solve(system, side)[0]


def end_weights(cells):
    weights = np.zeros((2, cells))
    weights[0, 0] = 1.0
    weights[1, cells - 1] = 1.0
    inner = cells - 2
    if inner > 0:
        system = np.eye(inner) + FILTER_ALPHA * (np.eye(inner, k=1) + np.eye(inner, k=-1))
        right = np.zeros((inner, 2))
        right[0, 0] = -FILTER_ALPHA
        right[inner - 1, 1] = -FILTER_ALPHA
        weights[:, 1:-1] = np.linalg.solve(system, right).T
    return weights


class Tables:
    def __init__(self, cells, devices):
        row = filter_row(cells * devices)
        extent = cells * devices
        self.cells = cells
        self.devices = devices
        self.own = [[float(row[(z - w) % extent]) for w in range(cells)] for z in range(cells)]
        self.ends = [[float(x) for x in line] for line in end_weights(cells)]
        self.couple = [
            [[float(row[(z - shift * cells - w) % extent]) for w in (0, cells - 1)] for z in range(cells)]
            for shift in range(devices)
        ]

    def project(self, values):
        return [weighted(line, values) for line in self.ends]

    def inside(self, values):
        return [weighted(line, values) for line in self.own]

    def outside(self, shift, ends):
        return [weighted(line, ends) for line in self.couple[shift]]


def weighted(weights, values):
    total = None
    for weight, value in zip(weights, values):
        if weight == 0.0:
            continue
        term = value if weight == 1.0 else value * weight
        total = term if total is None else total + term
    return total


def add_lists(left, right):
    return [x + y for x, y in zip(left, right)]


def halves(width):
    return [pl.ds(start, LANES) for start in range(0, width, LANES)]


def sum_up(terms):
    total = terms[0]
    for term in terms[1:]:
        total = total + term
    return total


def lanes_kernel(lane_ref):
    lane_ref[...] = lax.broadcasted_iota(jnp.int32, lane_ref.shape, 1)


def prepare_kernel(tables, lane_ref, strain_ref, size_ref, size_ends_ref):
    cells = tables.cells
    for lanes in halves(strain_ref.shape[-1]):
        size = []
        for z in range(cells):
            values = [strain_ref[k, z, :, lanes] for k in range(6)]
            total = sum_up([weight * (value * value) for weight, value in zip(PAIR_WEIGHTS, values)])
            size.append(jnp.sqrt(jnp.maximum(2.0 * total, STRAIN_FLOOR)))
            size_ref[z, :, lanes] = size[z]
        for end, value in enumerate(tables.project(size)):
            size_ends_ref[end, :, lanes] = value


def fetch_kernel(cot_hbm, size_ends_ref, bins_ref, cot_ref, arrived):
    copy = pltpu.make_async_copy(cot_hbm, cot_ref, arrived)
    copy.start()
    copy.wait()


def products_of(v):
    return [[x * y for x, y in zip(v[a], v[b])] for a, b in INDEX_PAIRS]


def filtered_block(tables, place, fields, ends):
    filtered = [tables.inside(field) for field in fields]
    for other in range(tables.devices):
        if other != place:
            shift = (other - place) % tables.devices
            filtered = [add_lists(near, tables.outside(shift, far)) for near, far in zip(filtered, ends[other])]
    return filtered


def plain_dual(tensor, vector, a, cells):
    return [sum_up([tensor[PAIR_OF[a][b]][z] * vector[b][z] for b in range(3)]) for z in range(cells)]


def weighted_dual(tensor, vector, a, cells):
    plain = plain_dual(tensor, vector, a, cells)
    return [plain[z] + tensor[PAIR_OF[a][a]][z] * vector[a][z] for z in range(cells)]


def forward_kernel(tables, *refs):
    peers = tables.devices - 1
    cells = tables.cells
    v_ref, strain_ref, cot_ref, size_ref, bins_ref = refs[:5]
    far_v_refs = refs[5 : 5 + peers]
    far_size_refs = refs[5 + peers : 5 + 2 * peers]
    smooth_ref, leonard_ref, model_ref, sums_ref = refs[5 + 2 * peers :]
    cross, square, blame = [], [], []
    for lanes in halves(v_ref.shape[-1]):
        v = [[v_ref[a, z, :, lanes] for z in range(cells)] for a in range(3)]
        size = [size_ref[z, :, lanes] for z in range(cells)]
        products = products_of(v)
        ends = [None]
        for far_v_ref, far_size_ref in zip(far_v_refs, far_size_refs):
            far = [[far_v_ref[a, z, :, lanes] for z in range(cells)] for a in range(3)]
            ends.append([tables.project(field) for field in far + products_of(far)])
            ends[-1].append([far_size_ref[end, :, lanes] for end in range(2)])
        filtered = filtered_block(tables, 0, v + products + [size], ends)
        smooth_v = filtered[:3]
        factor = [2.0 * (4.0 * filtered[9][z] - size[z]) for z in range(cells)]
        for k, (a, b) in enumerate(INDEX_PAIRS):
            for z in range(cells):
                coarse = smooth_v[a][z] * smooth_v[b][z]
                leonard = filtered[3 + k][z] - coarse
                term = products[k][z] - coarse + factor[z] * strain_ref[k, z, :, lanes]
                leonard_ref[k, z, :, lanes] = leonard
                model_ref[k, z, :, lanes] = term
                scaled = PAIR_WEIGHTS[k] * term
                cross.append(scaled * leonard)
                square.append(scaled * term)
                blame.append(term * cot_ref[k, z, :, lanes])
            cross, square, blame = [sum_up(cross)], [sum_up(square)], [sum_up(blame)]
        for a in range(3):
            for z in range(cells):
                smooth_ref[a, z, :, lanes] = smooth_v[a][z]
    lane = lax.broadcasted_iota(jnp.int32, bins_ref.shape, 1)
    mine = bins_ref[...] == lane
    place = lax.broadcasted_iota(jnp.int32, (8, LANES), 0)
    table = jnp.zeros((8, LANES), jnp.float32)
    for index, sums in enumerate((cross, square, blame)):
        per_row = jnp.sum(sums[0], axis=1, keepdims=True)
        per_bin = jnp.sum(jnp.where(mine, per_row, 0.0), axis=0, keepdims=True)
        table = jnp.where(place == index, per_bin, table)
    sums_ref[...] = table


def message_kernel(tables, smooth_ref, model_ref, sums_ref, other_sums_ref, dual_ref, message_ref, pair_ref):
    cells = tables.cells
    pair_sums = sums_ref[...] + other_sums_ref[...]
    pair_ref[...] = pair_sums
    message_ref[18, 0:8, 0:LANES] = pair_sums
    for lanes in halves(model_ref.shape[-1]):
        model = [[model_ref[k, z, :, lanes] for z in range(cells)] for k in range(6)]
        smooth_v = [[smooth_ref[a, z, :, lanes] for z in range(cells)] for a in range(3)]
        for k in range(6):
            for end, value in enumerate(tables.project(model[k])):
                message_ref[2 * k + end, :, lanes] = value
        for a in range(3):
            dual = [2.0 * x for x in plain_dual(model, smooth_v, a, cells)]
            for z in range(cells):
                dual_ref[a, z, :, lanes] = dual[z]
            for end, value in enumerate(tables.project(dual)):
                message_ref[12 + 2 * a + end, :, lanes] = value


def local_kernel(tables, *refs):
    peers = tables.devices - 1
    cells = tables.cells
    v_ref, cot_ref, smooth_ref, leonard_ref, model_ref, dual_ref = refs[:6]
    far_v_refs = refs[6 : 6 + peers]
    far_cot_refs = refs[6 + peers : 6 + 2 * peers]
    parts_ref = refs[-1]
    for lanes in halves(v_ref.shape[-1]):

        def load(ref, count):
            return [[ref[f, z, :, lanes] for z in range(cells)] for f in range(count)]

        fields, ends = [], []
        for ref in (v_ref, *far_v_refs):
            v = load(ref, 3)
            fields.append(v + products_of(v))
            ends.append([tables.project(field) for field in fields[-1]])
        v = fields[0][:3]
        cot, model, leonard, smooth_v = load(cot_ref, 6), load(model_ref, 6), load(leonard_ref, 6), load(smooth_ref, 3)
        smooth_cot = [tables.inside(field) for field in cot]
        duals = [weighted_dual(cot, smooth_v, a, cells) for a in range(3)]
        others = [plain_dual(leonard, smooth_v, a, cells) for a in range(3)]
        smooth_duals = [tables.inside(field) for field in duals]
        smooth_others = [tables.inside(field) for field in others]
        for place in range(1, tables.devices):
            far_cot = load(far_cot_refs[place - 1], 6)
            filtered = filtered_block(tables, place, fields[place], ends)
            far_smooth = filtered[:3]
            far_leonard = [
                [filtered[3 + k][z] - far_smooth[a][z] * far_smooth[b][z] for z in range(cells)]
                for k, (a, b) in enumerate(INDEX_PAIRS)
            ]
            for k in range(6):
                far = tables.outside(place, tables.project(far_cot[k]))
                smooth_cot[k] = add_lists(smooth_cot[k], far)
            for a in range(3):
                far = tables.outside(place, tables.project(weighted_dual(far_cot, far_smooth, a, cells)))
                smooth_duals[a] = add_lists(smooth_duals[a], far)
                far = tables.outside(place, tables.project(plain_dual(far_leonard, far_smooth, a, cells)))
                smooth_others[a] = add_lists(smooth_others[a], far)
        inner = [add_lists(tables.inside(model[k]), leonard[k]) for k in range(6)]
        for a in range(3):
            first = weighted_dual(smooth_cot, v, a, cells)
            second = weighted_dual(cot, v, a, cells)
            dual = tables.inside([dual_ref[a, z, :, lanes] for z in range(cells)])
            third = plain_dual(inner, v, a, cells)
            fourth = plain_dual(model, v, a, cells)
            for z in range(cells):
                parts_ref[a, z, :, lanes] = first[z] - smooth_duals[a][z]
                parts_ref[3 + a, z, :, lanes] = smooth_duals[a][z] - second[z]
                parts_ref[6 + a, z, :, lanes] = 2.0 * (third[z] - smooth_others[a][z]) - dual[z]
                parts_ref[9 + a, z, :, lanes] = 2.0 * dual[z] - 4.0 * fourth[z]


def far_kernel(tables, v_ref, parts_ref, *refs):
    message_refs, whole_ref = refs[:-1], refs[-1]
    cells = tables.cells
    for lanes in halves(v_ref.shape[-1]):
        v = [[v_ref[a, z, :, lanes] for z in range(cells)] for a in range(3)]
        pulled = [[parts_ref[6 + a, z, :, lanes] for z in range(cells)] for a in range(3)]
        crossed = [[parts_ref[9 + a, z, :, lanes] for z in range(cells)] for a in range(3)]
        for place, ends in enumerate(message_refs, start=1):
            from_model = [
                tables.outside(place, [2.0 * ends[2 * k + end, :, lanes] for end in range(2)]) for k in range(6)
            ]
            for a in range(3):
                dual = tables.outside(place, [ends[12 + 2 * a + end, :, lanes] for end in range(2)])
                through = plain_dual(from_model, v, a, cells)
                for z in range(cells):
                    pulled[a][z] = pulled[a][z] + (through[z] - dual[z])
                    crossed[a][z] = crossed[a][z] + 2.0 * dual[z]
        for a in range(3):
            for z in range(cells):
                whole_ref[a, z, :, lanes] = pulled[a][z]
                whole_ref[3 + a, z, :, lanes] = crossed[a][z]


def finish_kernel(tables, count, turning, *refs):
    cells = tables.cells
    leonard_ref, model_ref, parts_ref, whole_ref, bins_ref, pair_ref = refs[:6]
    near_refs = refs[6 : 6 + count]
    table_refs = refs[6 + count : 5 + count + tables.devices]
    residual_hbm, grad_hbm, residual_ref, grad_ref, left = refs[5 + count + tables.devices :]
    total = sum_up([pair_ref[...]] + [ref[18, 0:8, 0:LANES] for ref in table_refs])
    near = sum_up([ref[...] for ref in near_refs])
    if turning:
        place = lax.axis_index("stream")
        inner = jnp.logical_and(place > 0, place < lax.axis_size("stream") - 1)
        near = jnp.where(inner, near, 0.0)
    total = total + near
    inverse = 1.0 / (total[1:2] + EPSILON)
    rows = leonard_ref.shape[2]
    lane = lax.broadcasted_iota(jnp.int32, bins_ref.shape, 1)
    mine = bins_ref[...] == lane

    def of_rows(per_bin):
        column = jnp.sum(jnp.where(mine, per_bin, 0.0), axis=1, keepdims=True)
        return jnp.broadcast_to(column, (rows, LANES))

    coefficient = of_rows(total[0:1] * inverse)
    pull = of_rows(-(total[2:3] * inverse))
    copies = []
    for k in range(6):
        for lanes in halves(leonard_ref.shape[-1]):
            for z in range(cells):
                residual_ref[k, z, :, lanes] = leonard_ref[k, z, :, lanes] - coefficient * model_ref[k, z, :, lanes]
        if k % 3 == 2:
            some = pl.ds(k - 2, 3)
            copies.append(pltpu.make_async_copy(residual_ref.at[some], residual_hbm.at[some], left.at[k // 3]))
            copies[-1].start()
    for a in range(3):
        for lanes in halves(leonard_ref.shape[-1]):
            for z in range(cells):
                grad_ref[a, z, :, lanes] = (
                    parts_ref[a, z, :, lanes]
                    + coefficient * parts_ref[3 + a, z, :, lanes]
                    + pull * (whole_ref[a, z, :, lanes] + coefficient * whole_ref[3 + a, z, :, lanes])
                )
    copies.append(pltpu.make_async_copy(grad_ref, grad_hbm, left.at[2]))
    copies[-1].start()
    for copy in copies:
        copy.wait()


WHOLE = pl.BlockSpec(memory_space=pltpu.VMEM)
REMAIN = pl.BlockSpec(memory_space=pltpu.HBM)


def call(kernel, outs, operations, *operands, in_specs=None, out_specs=None, scratch=()):
    nbytes = sum(4 * int(np.prod(x.shape)) for x in (*operands, *outs))
    return pl.pallas_call(
        kernel,
        out_shape=outs,
        in_specs=in_specs or [WHOLE] * len(operands),
        out_specs=out_specs or [WHOLE] * len(outs),
        scratch_shapes=list(scratch),
        compiler_params=pltpu.CompilerParams(vmem_limit_bytes=32 * 1024 * 1024),
        cost_estimate=pl.CostEstimate(flops=operations, bytes_accessed=nbytes, transcendentals=0),
    )(*operands)


def from_ahead(values, shift):
    peers = lax.axis_size("span")
    return lax.ppermute(values, "span", [((i + shift) % peers, i) for i in range(peers)])


def from_source(values, span_shift, source):
    span, stream = lax.axis_size("span"), lax.axis_size("stream")
    pairs = [
        (((i + span_shift) % span) * stream + source(j) % stream, i * stream + j)
        for i in range(span)
        for j in range(stream)
    ]
    return lax.ppermute(values, ("span", "stream"), pairs)


def ring_source(stream):
    def source(j):
        if j % 2 == 0:
            return j - 2 if j >= 2 else 1
        return j + 2 if j + 2 < stream else j - 1

    return source


def on_device(velocity, strain, row_bins, cotangent):
    span, stream = lax.axis_size("span"), lax.axis_size("stream")
    cells, rows, width = velocity.shape[1:]
    tables = Tables(cells, span)
    slab = (rows, width)

    def shaped(*leading):
        return pltpu.VMEM(leading + slab, jnp.float32)

    bins = jnp.broadcast_to(row_bins[:, None], (rows, LANES))
    far_v = [from_ahead(velocity, shift) for shift in range(1, span)]
    work = cells * rows * width
    (lane,) = call(lanes_kernel, [pltpu.VMEM((rows, LANES), jnp.int32)], LONG * work)
    size, size_ends = call(
        functools.partial(prepare_kernel, tables), [shaped(cells), shaped(2)], LONG * work, lane, strain
    )
    far_size = [from_ahead(size_ends, shift) for shift in range(1, span)]
    (near_cot,) = call(
        fetch_kernel,
        [shaped(6, cells)],
        work,
        pltpu.with_memory_space_constraint(cotangent, pltpu.HBM),
        size_ends,
        bins,
        in_specs=[REMAIN, WHOLE, WHOLE],
        scratch=[pltpu.SemaphoreType.DMA(())],
    )
    far_cot = [from_ahead(near_cot, shift) for shift in range(1, span)]
    table = pltpu.VMEM((8, LANES), jnp.float32)
    smooth, leonard, model, sums = call(
        functools.partial(forward_kernel, tables),
        [shaped(3, cells), shaped(6, cells), shaped(6, cells), table],
        LONG * work,
        velocity,
        strain,
        near_cot,
        size,
        bins,
        *far_v,
        *far_size,
    )
    other_sums = from_source(sums, 0, lambda j: j ^ 1)
    dual, message, pair_sums = call(
        functools.partial(message_kernel, tables),
        [shaped(3, cells), shaped(19), table],
        100 * work,
        smooth,
        model,
        sums,
        other_sums,
    )
    far_message = [from_ahead(message, shift) for shift in range(1, span)]
    most_rows = 2 * rows * stream // NBINS
    reach = -(-(most_rows - 1) // rows)
    turning = reach <= 1
    if turning:
        sources = [ring_source(stream)]
    else:
        steps = range(1, -(-reach // 2) + 1)
        sources = [functools.partial(lambda j, away: j + away, away=2 * step * way) for step in steps for way in (1, -1)]
    near_sums = [from_source(pair_sums, shift, source) for shift in range(span) for source in sources]
    (parts,) = call(
        functools.partial(local_kernel, tables),
        [shaped(12, cells)],
        500 * work,
        velocity,
        near_cot,
        smooth,
        leonard,
        model,
        dual,
        *far_v,
        *far_cot,
    )
    (whole,) = call(
        functools.partial(far_kernel, tables), [shaped(6, cells)], 100 * work, velocity, parts, *far_message
    )
    outs = [jax.ShapeDtypeStruct((n, cells) + slab, jnp.float32) for n in (6, 3)]
    return tuple(
        call(
            functools.partial(finish_kernel, tables, len(near_sums), turning),
            outs,
            200 * work,
            leonard,
            model,
            parts,
            whole,
            bins,
            pair_sums,
            *near_sums,
            *far_message,
            out_specs=[REMAIN] * 2,
            scratch=[pltpu.VMEM(x.shape, x.dtype) for x in outs] + [pltpu.SemaphoreType.DMA((3,))],
        )
    )


def solution(mesh):
    fields = P(None, "span", "stream", None)
    return jax.shard_map(
        on_device,
        mesh=mesh,
        in_specs=(fields, fields, P("stream"), fields),
        out_specs=(fields, fields),
        check_vma=False,
    )
```

```python
import functools

import jax
import jax.numpy as jnp
import numpy as np
from jax import lax
from jax.experimental import pallas as pl
from jax.experimental.pallas import tpu as pltpu
from jax.sharding import PartitionSpec as P

NBINS = 64
FILTER_ALPHA = 0.45
CENTER_WEIGHT = 0.95
SIDE_WEIGHT = 0.475
STRAIN_FLOOR = 0.25
EPSILON = 1e-06
INDEX_PAIRS = ((0, 0), (0, 1), (0, 2), (1, 1), (1, 2), (2, 2))
PAIR_WEIGHTS = (1.0, 2.0, 2.0, 1.0, 2.0, 1.0)
PAIR_OF = ((0, 1, 2), (1, 3, 4), (2, 4, 5))
LANES = 128
LONG = 300000


def filter_row(extent):
    eye = np.eye(extent)
    ring = np.roll(eye, 1, axis=1) + np.roll(eye, -1, axis=1)
    system = eye + FILTER_ALPHA * ring
    side = CENTER_WEIGHT * eye + SIDE_WEIGHT * ring
    return np.linalg.solve(system, side)[0]


def end_weights(cells):
    weights = np.zeros((2, cells))
    weights[0, 0] = 1.0
    weights[1, cells - 1] = 1.0
    inner = cells - 2
    if inner > 0:
        system = np.eye(inner) + FILTER_ALPHA * (np.eye(inner, k=1) + np.eye(inner, k=-1))
        right = np.zeros((inner, 2))
        right[0, 0] = -FILTER_ALPHA
        right[inner - 1, 1] = -FILTER_ALPHA
        weights[:, 1:-1] = np.linalg.solve(system, right).T
    return weights


class Tables:
    def __init__(self, cells, devices):
        row = filter_row(cells * devices)
        extent = cells * devices
        self.cells = cells
        self.devices = devices
        self.own = [[float(row[(z - w) % extent]) for w in range(cells)] for z in range(cells)]
        self.ends = [[float(x) for x in line] for line in end_weights(cells)]
        self.couple = [
            [[float(row[(z - shift * cells - w) % extent]) for w in (0, cells - 1)] for z in range(cells)]
            for shift in range(devices)
        ]

    def project(self, values):
        return [weighted(line, values) for line in self.ends]

    def inside(self, values):
        return [weighted(line, values) for line in self.own]

    def outside(self, shift, ends):
        return [weighted(line, ends) for line in self.couple[shift]]


def weighted(weights, values):
    total = None
    for weight, value in zip(weights, values):
        if weight == 0.0:
            continue
        term = value if weight == 1.0 else value * weight
        total = term if total is None else total + term
    return total


def add_lists(left, right):
    return [x + y for x, y in zip(left, right)]


def halves(width):
    return [pl.ds(start, LANES) for start in range(0, width, LANES)]


def sum_up(terms):
    total = terms[0]
    for term in terms[1:]:
        total = total + term
    return total


def lanes_kernel(lane_ref):
    lane_ref[...] = lax.broadcasted_iota(jnp.int32, lane_ref.shape, 1)


def prepare_kernel(tables, lane_ref, strain_ref, size_ref, size_ends_ref):
    cells = tables.cells
    for lanes in halves(strain_ref.shape[-1]):
        size = []
        for z in range(cells):
            values = [strain_ref[k, z, :, lanes] for k in range(6)]
            total = sum_up([weight * (value * value) for weight, value in zip(PAIR_WEIGHTS, values)])
            size.append(jnp.sqrt(jnp.maximum(2.0 * total, STRAIN_FLOOR)))
            size_ref[z, :, lanes] = size[z]
        for end, value in enumerate(tables.project(size)):
            size_ends_ref[end, :, lanes] = value


def fetch_kernel(v_hbm, size_ends_ref, bins_ref, v_ref, arrived):
    copy = pltpu.make_async_copy(v_hbm, v_ref, arrived)
    copy.start()
    copy.wait()


def products_of(v):
    return [[x * y for x, y in zip(v[a], v[b])] for a, b in INDEX_PAIRS]


def filtered_block(tables, place, fields, ends):
    filtered = [tables.inside(field) for field in fields]
    for other in range(tables.devices):
        if other != place:
            shift = (other - place) % tables.devices
            filtered = [add_lists(near, tables.outside(shift, far)) for near, far in zip(filtered, ends[other])]
    return filtered


def plain_dual(tensor, vector, a, cells):
    return [sum_up([tensor[PAIR_OF[a][b]][z] * vector[b][z] for b in range(3)]) for z in range(cells)]


def weighted_dual(tensor, vector, a, cells):
    plain = plain_dual(tensor, vector, a, cells)
    return [plain[z] + tensor[PAIR_OF[a][a]][z] * vector[a][z] for z in range(cells)]


def forward_kernel(tables, *refs):
    peers = tables.devices - 1
    cells = tables.cells
    v_ref, strain_ref, cot_ref, size_ref, bins_ref = refs[:5]
    far_v_refs = refs[5 : 5 + peers]
    far_size_refs = refs[5 + peers : 5 + 2 * peers]
    smooth_ref, leonard_ref, model_ref, sums_ref = refs[5 + 2 * peers :]
    cross, square, blame = [], [], []
    for lanes in halves(v_ref.shape[-1]):
        v = [[v_ref[a, z, :, lanes] for z in range(cells)] for a in range(3)]
        size = [size_ref[z, :, lanes] for z in range(cells)]
        products = products_of(v)
        ends = [None]
        for far_v_ref, far_size_ref in zip(far_v_refs, far_size_refs):
            far = [[far_v_ref[a, z, :, lanes] for z in range(cells)] for a in range(3)]
            ends.append([tables.project(field) for field in far + products_of(far)])
            ends[-1].append([far_size_ref[end, :, lanes] for end in range(2)])
        filtered = filtered_block(tables, 0, v + products + [size], ends)
        smooth_v = filtered[:3]
        factor = [2.0 * (4.0 * filtered[9][z] - size[z]) for z in range(cells)]
        for k, (a, b) in enumerate(INDEX_PAIRS):
            for z in range(cells):
                coarse = smooth_v[a][z] * smooth_v[b][z]
                leonard = filtered[3 + k][z] - coarse
                term = products[k][z] - coarse + factor[z] * strain_ref[k, z, :, lanes]
                leonard_ref[k, z, :, lanes] = leonard
                model_ref[k, z, :, lanes] = term
                scaled = PAIR_WEIGHTS[k] * term
                cross.append(scaled * leonard)
                square.append(scaled * term)
                blame.append(term * cot_ref[k, z, :, lanes])
            cross, square, blame = [sum_up(cross)], [sum_up(square)], [sum_up(blame)]
        for a in range(3):
            for z in range(cells):
                smooth_ref[a, z, :, lanes] = smooth_v[a][z]
    lane = lax.broadcasted_iota(jnp.int32, bins_ref.shape, 1)
    mine = bins_ref[...] == lane
    place = lax.broadcasted_iota(jnp.int32, (8, LANES), 0)
    table = jnp.zeros((8, LANES), jnp.float32)
    for index, sums in enumerate((cross, square, blame)):
        per_row = jnp.sum(sums[0], axis=1, keepdims=True)
        per_bin = jnp.sum(jnp.where(mine, per_row, 0.0), axis=0, keepdims=True)
        table = jnp.where(place == index, per_bin, table)
    sums_ref[...] = table


def message_kernel(tables, smooth_ref, model_ref, sums_ref, other_sums_ref, dual_ref, message_ref, pair_ref):
    cells = tables.cells
    pair_sums = sums_ref[...] + other_sums_ref[...]
    pair_ref[...] = pair_sums
    message_ref[18, 0:8, 0:LANES] = pair_sums
    for lanes in halves(model_ref.shape[-1]):
        model = [[model_ref[k, z, :, lanes] for z in range(cells)] for k in range(6)]
        smooth_v = [[smooth_ref[a, z, :, lanes] for z in range(cells)] for a in range(3)]
        for k in range(6):
            for end, value in enumerate(tables.project(model[k])):
                message_ref[2 * k + end, :, lanes] = value
        for a in range(3):
            dual = [2.0 * x for x in plain_dual(model, smooth_v, a, cells)]
            for z in range(cells):
                dual_ref[a, z, :, lanes] = dual[z]
            for end, value in enumerate(tables.project(dual)):
                message_ref[12 + 2 * a + end, :, lanes] = value


def local_kernel(tables, *refs):
    peers = tables.devices - 1
    cells = tables.cells
    v_ref, cot_ref, smooth_ref, leonard_ref, model_ref, dual_ref = refs[:6]
    far_v_refs = refs[6 : 6 + peers]
    far_cot_refs = refs[6 + peers : 6 + 2 * peers]
    parts_ref = refs[-1]
    for lanes in halves(v_ref.shape[-1]):

        def load(ref, count):
            return [[ref[f, z, :, lanes] for z in range(cells)] for f in range(count)]

        fields, ends = [], []
        for ref in (v_ref, *far_v_refs):
            v = load(ref, 3)
            fields.append(v + products_of(v))
            ends.append([tables.project(field) for field in fields[-1]])
        v = fields[0][:3]
        cot, model, leonard, smooth_v = load(cot_ref, 6), load(model_ref, 6), load(leonard_ref, 6), load(smooth_ref, 3)
        smooth_cot = [tables.inside(field) for field in cot]
        duals = [weighted_dual(cot, smooth_v, a, cells) for a in range(3)]
        others = [plain_dual(leonard, smooth_v, a, cells) for a in range(3)]
        smooth_duals = [tables.inside(field) for field in duals]
        smooth_others = [tables.inside(field) for field in others]
        for place in range(1, tables.devices):
            far_cot = load(far_cot_refs[place - 1], 6)
            filtered = filtered_block(tables, place, fields[place], ends)
            far_smooth = filtered[:3]
            far_leonard = [
                [filtered[3 + k][z] - far_smooth[a][z] * far_smooth[b][z] for z in range(cells)]
                for k, (a, b) in enumerate(INDEX_PAIRS)
            ]
            for k in range(6):
                far = tables.outside(place, tables.project(far_cot[k]))
                smooth_cot[k] = add_lists(smooth_cot[k], far)
            for a in range(3):
                far = tables.outside(place, tables.project(weighted_dual(far_cot, far_smooth, a, cells)))
                smooth_duals[a] = add_lists(smooth_duals[a], far)
                far = tables.outside(place, tables.project(plain_dual(far_leonard, far_smooth, a, cells)))
                smooth_others[a] = add_lists(smooth_others[a], far)
        inner = [add_lists(tables.inside(model[k]), leonard[k]) for k in range(6)]
        for a in range(3):
            first = weighted_dual(smooth_cot, v, a, cells)
            second = weighted_dual(cot, v, a, cells)
            dual = tables.inside([dual_ref[a, z, :, lanes] for z in range(cells)])
            third = plain_dual(inner, v, a, cells)
            fourth = plain_dual(model, v, a, cells)
            for z in range(cells):
                parts_ref[a, z, :, lanes] = first[z] - smooth_duals[a][z]
                parts_ref[3 + a, z, :, lanes] = smooth_duals[a][z] - second[z]
                parts_ref[6 + a, z, :, lanes] = 2.0 * (third[z] - smooth_others[a][z]) - dual[z]
                parts_ref[9 + a, z, :, lanes] = 2.0 * dual[z] - 4.0 * fourth[z]


def finish_kernel(tables, count, turning, *refs):
    peers = tables.devices - 1
    cells = tables.cells
    v_ref, leonard_ref, model_ref, parts_ref, bins_ref = refs[:5]
    near_refs = refs[5 : 5 + count]
    pair_ref = refs[5 + count]
    far_message_refs = refs[6 + count : 6 + count + peers]
    residual_hbm, grad_hbm, residual_ref, grad_ref, left = refs[6 + count + peers :]
    total = sum_up([pair_ref[...]] + [ref[18, 0:8, 0:LANES] for ref in far_message_refs])
    near = sum_up([ref[...] for ref in near_refs])
    if turning:
        place = lax.axis_index("stream")
        inner = jnp.logical_and(place > 0, place < lax.axis_size("stream") - 1)
        near = jnp.where(inner, near, 0.0)
    total = total + near
    inverse = 1.0 / (total[1:2] + EPSILON)
    rows = v_ref.shape[2]
    lane = lax.broadcasted_iota(jnp.int32, bins_ref.shape, 1)
    mine = bins_ref[...] == lane

    def of_rows(per_bin):
        column = jnp.sum(jnp.where(mine, per_bin, 0.0), axis=1, keepdims=True)
        return jnp.broadcast_to(column, (rows, LANES))

    coefficient = of_rows(total[0:1] * inverse)
    pull = of_rows(-(total[2:3] * inverse))
    copies = []
    for k in range(6):
        for lanes in halves(v_ref.shape[-1]):
            for z in range(cells):
                residual_ref[k, z, :, lanes] = (
                    leonard_ref[k, z, :, lanes] - coefficient * model_ref[k, z, :, lanes]
                )
        if k % 3 == 2:
            some = pl.ds(k - 2, 3)
            copies.append(pltpu.make_async_copy(residual_ref.at[some], residual_hbm.at[some], left.at[k // 3]))
            copies[-1].start()
    for lanes in halves(v_ref.shape[-1]):
        v = [[v_ref[a, z, :, lanes] for z in range(cells)] for a in range(3)]
        from_model = [[] for _ in range(6)]
        from_dual = [[] for _ in range(3)]
        for place, ends in enumerate(far_message_refs, start=1):
            for k in range(6):
                from_model[k].append(tables.outside(place, [2.0 * ends[2 * k + end, :, lanes] for end in range(2)]))
            for a in range(3):
                pair = [(2.0 * coefficient - 1.0) * ends[12 + 2 * a + end, :, lanes] for end in range(2)]
                from_dual[a].append(tables.outside(place, pair))
        from_model = [functools.reduce(add_lists, lists) if lists else None for lists in from_model]
        from_dual = [functools.reduce(add_lists, lists) if lists else None for lists in from_dual]
        for a in range(3):
            for z in range(cells):
                pulled = parts_ref[6 + a, z, :, lanes] + coefficient * parts_ref[9 + a, z, :, lanes]
                if peers:
                    terms = [from_model[PAIR_OF[a][b]][z] * v[b][z] for b in range(3)]
                    pulled = pulled + from_dual[a][z] + sum_up(terms)
                grad_ref[a, z, :, lanes] = (
                    parts_ref[a, z, :, lanes] + coefficient * parts_ref[3 + a, z, :, lanes] + pull * pulled
                )
    copies.append(pltpu.make_async_copy(grad_ref, grad_hbm, left.at[2]))
    copies[-1].start()
    for copy in copies:
        copy.wait()


WHOLE = pl.BlockSpec(memory_space=pltpu.VMEM)
REMAIN = pl.BlockSpec(memory_space=pltpu.HBM)


def call(kernel, outs, operations, *operands, in_specs=None, out_specs=None, scratch=()):
    nbytes = sum(4 * int(np.prod(x.shape)) for x in (*operands, *outs))
    return pl.pallas_call(
        kernel,
        out_shape=outs,
        in_specs=in_specs or [WHOLE] * len(operands),
        out_specs=out_specs or [WHOLE] * len(outs),
        scratch_shapes=list(scratch),
        compiler_params=pltpu.CompilerParams(vmem_limit_bytes=32 * 1024 * 1024),
        cost_estimate=pl.CostEstimate(flops=operations, bytes_accessed=nbytes, transcendentals=0),
    )(*operands)


def from_ahead(values, shift):
    peers = lax.axis_size("span")
    return lax.ppermute(values, "span", [((i + shift) % peers, i) for i in range(peers)])


def from_source(values, span_shift, source):
    span, stream = lax.axis_size("span"), lax.axis_size("stream")
    pairs = [
        (((i + span_shift) % span) * stream + source(j) % stream, i * stream + j)
        for i in range(span)
        for j in range(stream)
    ]
    return lax.ppermute(values, ("span", "stream"), pairs)


def ring_source(stream):
    def source(j):
        if j % 2 == 0:
            return j - 2 if j >= 2 else 1
        return j + 2 if j + 2 < stream else j - 1

    return source


def on_device(velocity, strain, row_bins, cotangent):
    span, stream = lax.axis_size("span"), lax.axis_size("stream")
    cells, rows, width = velocity.shape[1:]
    tables = Tables(cells, span)
    slab = (rows, width)

    def shaped(*leading):
        return pltpu.VMEM(leading + slab, jnp.float32)

    bins = jnp.broadcast_to(row_bins[:, None], (rows, LANES))
    far_v = [from_ahead(velocity, shift) for shift in range(1, span)]
    work = cells * rows * width
    (lane,) = call(lanes_kernel, [pltpu.VMEM((rows, LANES), jnp.int32)], LONG * work)
    size, size_ends = call(
        functools.partial(prepare_kernel, tables), [shaped(cells), shaped(2)], LONG * work, lane, strain
    )
    far_size = [from_ahead(size_ends, shift) for shift in range(1, span)]
    (near_v,) = call(
        fetch_kernel,
        [shaped(3, cells)],
        work,
        pltpu.with_memory_space_constraint(velocity, pltpu.HBM),
        size_ends,
        bins,
        in_specs=[REMAIN, WHOLE, WHOLE],
        scratch=[pltpu.SemaphoreType.DMA(())],
    )
    near_v, near_cot = lax.optimization_barrier((near_v, cotangent))
    far_cot = [from_ahead(near_cot, shift) for shift in range(1, span)]
    table = pltpu.VMEM((8, LANES), jnp.float32)
    smooth, leonard, model, sums = call(
        functools.partial(forward_kernel, tables),
        [shaped(3, cells), shaped(6, cells), shaped(6, cells), table],
        LONG * work,
        near_v,
        strain,
        near_cot,
        size,
        bins,
        *far_v,
        *far_size,
    )
    other_sums = from_source(sums, 0, lambda j: j ^ 1)
    dual, message, pair_sums = call(
        functools.partial(message_kernel, tables),
        [shaped(3, cells), shaped(19), table],
        100 * work,
        smooth,
        model,
        sums,
        other_sums,
    )
    far_message = [from_ahead(message, shift) for shift in range(1, span)]
    most_rows = 2 * rows * stream // NBINS
    reach = -(-(most_rows - 1) // rows)
    turning = reach <= 1
    if turning:
        sources = [ring_source(stream)]
    else:
        steps = range(1, -(-reach // 2) + 1)
        sources = [functools.partial(lambda j, away: j + away, away=2 * step * way) for step in steps for way in (1, -1)]
    near_sums = [from_source(pair_sums, shift, source) for shift in range(span) for source in sources]
    (parts,) = call(
        functools.partial(local_kernel, tables),
        [shaped(12, cells)],
        500 * work,
        near_v,
        near_cot,
        smooth,
        leonard,
        model,
        dual,
        *far_v,
        *far_cot,
    )
    outs = [jax.ShapeDtypeStruct((n, cells) + slab, jnp.float32) for n in (6, 3)]
    return tuple(
        call(
            functools.partial(finish_kernel, tables, len(near_sums), turning),
            outs,
            200 * work,
            near_v,
            leonard,
            model,
            parts,
            bins,
            *near_sums,
            pair_sums,
            *far_message,
            out_specs=[REMAIN] * 2,
            scratch=[pltpu.VMEM(x.shape, x.dtype) for x in outs] + [pltpu.SemaphoreType.DMA((3,))],
        )
    )


def solution(mesh):
    fields = P(None, "span", "stream", None)
    return jax.shard_map(
        on_device,
        mesh=mesh,
        in_specs=(fields, fields, P("stream"), fields),
        out_specs=(fields, fields),
        check_vma=False,
    )
```

```python
import functools

import jax
import jax.numpy as jnp
import numpy as np
from jax import lax
from jax.experimental import pallas as pl
from jax.experimental.pallas import tpu as pltpu
from jax.sharding import PartitionSpec as P

NBINS = 64
FILTER_ALPHA = 0.45
CENTER_WEIGHT = 0.95
SIDE_WEIGHT = 0.475
STRAIN_FLOOR = 0.25
EPSILON = 1e-06
INDEX_PAIRS = ((0, 0), (0, 1), (0, 2), (1, 1), (1, 2), (2, 2))
PAIR_WEIGHTS = (1.0, 2.0, 2.0, 1.0, 2.0, 1.0)
PAIR_OF = ((0, 1, 2), (1, 3, 4), (2, 4, 5))
LANES = 128
LONG = 300000


def filter_row(extent):
    eye = np.eye(extent)
    ring = np.roll(eye, 1, axis=1) + np.roll(eye, -1, axis=1)
    system = eye + FILTER_ALPHA * ring
    side = CENTER_WEIGHT * eye + SIDE_WEIGHT * ring
    return np.linalg.solve(system, side)[0]


def end_weights(cells):
    weights = np.zeros((2, cells))
    weights[0, 0] = 1.0
    weights[1, cells - 1] = 1.0
    inner = cells - 2
    if inner > 0:
        system = np.eye(inner) + FILTER_ALPHA * (np.eye(inner, k=1) + np.eye(inner, k=-1))
        right = np.zeros((inner, 2))
        right[0, 0] = -FILTER_ALPHA
        right[inner - 1, 1] = -FILTER_ALPHA
        weights[:, 1:-1] = np.linalg.solve(system, right).T
    return weights


class Tables:
    def __init__(self, cells, devices):
        row = filter_row(cells * devices)
        extent = cells * devices
        self.cells = cells
        self.devices = devices
        self.own = [[float(row[(z - w) % extent]) for w in range(cells)] for z in range(cells)]
        self.ends = [[float(x) for x in line] for line in end_weights(cells)]
        self.couple = [
            [[float(row[(z - shift * cells - w) % extent]) for w in (0, cells - 1)] for z in range(cells)]
            for shift in range(devices)
        ]

    def project(self, values):
        return [weighted(line, values) for line in self.ends]

    def inside(self, values):
        return [weighted(line, values) for line in self.own]

    def outside(self, shift, ends):
        return [weighted(line, ends) for line in self.couple[shift]]


def weighted(weights, values):
    total = None
    for weight, value in zip(weights, values):
        if weight == 0.0:
            continue
        term = value if weight == 1.0 else value * weight
        total = term if total is None else total + term
    return total


def add_lists(left, right):
    return [x + y for x, y in zip(left, right)]


def halves(width):
    return [pl.ds(start, LANES) for start in range(0, width, LANES)]


def sum_up(terms):
    total = terms[0]
    for term in terms[1:]:
        total = total + term
    return total


def lanes_kernel(lane_ref):
    lane_ref[...] = lax.broadcasted_iota(jnp.int32, lane_ref.shape, 1)


def prepare_kernel(tables, lane_ref, strain_ref, size_ref, size_ends_ref):
    cells = tables.cells
    for lanes in halves(strain_ref.shape[-1]):
        size = []
        for z in range(cells):
            values = [strain_ref[k, z, :, lanes] for k in range(6)]
            total = sum_up([weight * (value * value) for weight, value in zip(PAIR_WEIGHTS, values)])
            size.append(jnp.sqrt(jnp.maximum(2.0 * total, STRAIN_FLOOR)))
            size_ref[z, :, lanes] = size[z]
        for end, value in enumerate(tables.project(size)):
            size_ends_ref[end, :, lanes] = value


def fetch_kernel(cot_hbm, size_ends_ref, cot_ref, arrived):
    copy = pltpu.make_async_copy(cot_hbm, cot_ref, arrived)
    copy.start()
    copy.wait()


def products_of(v):
    return [[x * y for x, y in zip(v[a], v[b])] for a, b in INDEX_PAIRS]


def filtered_block(tables, place, fields, ends):
    filtered = [tables.inside(field) for field in fields]
    for other in range(tables.devices):
        if other != place:
            shift = (other - place) % tables.devices
            filtered = [add_lists(near, tables.outside(shift, far)) for near, far in zip(filtered, ends[other])]
    return filtered


def plain_dual(tensor, vector, a, cells):
    return [sum_up([tensor[PAIR_OF[a][b]][z] * vector[b][z] for b in range(3)]) for z in range(cells)]


def weighted_dual(tensor, vector, a, cells):
    plain = plain_dual(tensor, vector, a, cells)
    return [plain[z] + tensor[PAIR_OF[a][a]][z] * vector[a][z] for z in range(cells)]


def forward_kernel(tables, *refs):
    peers = tables.devices - 1
    cells = tables.cells
    v_ref, strain_ref, cot_ref, size_ref, bins_ref = refs[:5]
    far_v_refs = refs[5 : 5 + peers]
    far_size_refs = refs[5 + peers : 5 + 2 * peers]
    smooth_ref, leonard_ref, model_ref, sums_ref = refs[5 + 2 * peers :]
    cross, square, blame = [], [], []
    for lanes in halves(v_ref.shape[-1]):
        v = [[v_ref[a, z, :, lanes] for z in range(cells)] for a in range(3)]
        size = [size_ref[z, :, lanes] for z in range(cells)]
        products = products_of(v)
        ends = [None]
        for far_v_ref, far_size_ref in zip(far_v_refs, far_size_refs):
            far = [[far_v_ref[a, z, :, lanes] for z in range(cells)] for a in range(3)]
            ends.append([tables.project(field) for field in far + products_of(far)])
            ends[-1].append([far_size_ref[end, :, lanes] for end in range(2)])
        filtered = filtered_block(tables, 0, v + products + [size], ends)
        smooth_v = filtered[:3]
        factor = [2.0 * (4.0 * filtered[9][z] - size[z]) for z in range(cells)]
        for k, (a, b) in enumerate(INDEX_PAIRS):
            for z in range(cells):
                coarse = smooth_v[a][z] * smooth_v[b][z]
                leonard = filtered[3 + k][z] - coarse
                term = products[k][z] - coarse + factor[z] * strain_ref[k, z, :, lanes]
                leonard_ref[k, z, :, lanes] = leonard
                model_ref[k, z, :, lanes] = term
                scaled = PAIR_WEIGHTS[k] * term
                cross.append(scaled * leonard)
                square.append(scaled * term)
                blame.append(term * cot_ref[k, z, :, lanes])
            cross, square, blame = [sum_up(cross)], [sum_up(square)], [sum_up(blame)]
        for a in range(3):
            for z in range(cells):
                smooth_ref[a, z, :, lanes] = smooth_v[a][z]
    lane = lax.broadcasted_iota(jnp.int32, bins_ref.shape, 1)
    mine = bins_ref[...] == lane
    place = lax.broadcasted_iota(jnp.int32, (8, LANES), 0)
    table = jnp.zeros((8, LANES), jnp.float32)
    for index, sums in enumerate((cross, square, blame)):
        per_row = jnp.sum(sums[0], axis=1, keepdims=True)
        per_bin = jnp.sum(jnp.where(mine, per_row, 0.0), axis=0, keepdims=True)
        table = jnp.where(place == index, per_bin, table)
    sums_ref[...] = table


def message_kernel(tables, smooth_ref, model_ref, dual_ref, message_ref):
    cells = tables.cells
    for lanes in halves(model_ref.shape[-1]):
        model = [[model_ref[k, z, :, lanes] for z in range(cells)] for k in range(6)]
        smooth_v = [[smooth_ref[a, z, :, lanes] for z in range(cells)] for a in range(3)]
        for k in range(6):
            for end, value in enumerate(tables.project(model[k])):
                message_ref[2 * k + end, :, lanes] = value
        for a in range(3):
            dual = [2.0 * x for x in plain_dual(model, smooth_v, a, cells)]
            for z in range(cells):
                dual_ref[a, z, :, lanes] = dual[z]
            for end, value in enumerate(tables.project(dual)):
                message_ref[12 + 2 * a + end, :, lanes] = value


def local_kernel(tables, *refs):
    peers = tables.devices - 1
    cells = tables.cells
    v_ref, cot_ref, smooth_ref, leonard_ref, model_ref, dual_ref = refs[:6]
    far_v_refs = refs[6 : 6 + peers]
    far_cot_refs = refs[6 + peers : 6 + 2 * peers]
    parts_ref = refs[-1]
    for lanes in halves(v_ref.shape[-1]):

        def load(ref, count):
            return [[ref[f, z, :, lanes] for z in range(cells)] for f in range(count)]

        fields, ends = [], []
        for ref in (v_ref, *far_v_refs):
            v = load(ref, 3)
            fields.append(v + products_of(v))
            ends.append([tables.project(field) for field in fields[-1]])
        v = fields[0][:3]
        cot, model, leonard, smooth_v = load(cot_ref, 6), load(model_ref, 6), load(leonard_ref, 6), load(smooth_ref, 3)
        smooth_cot = [tables.inside(field) for field in cot]
        duals = [weighted_dual(cot, smooth_v, a, cells) for a in range(3)]
        others = [plain_dual(leonard, smooth_v, a, cells) for a in range(3)]
        smooth_duals = [tables.inside(field) for field in duals]
        smooth_others = [tables.inside(field) for field in others]
        for place in range(1, tables.devices):
            far_cot = load(far_cot_refs[place - 1], 6)
            filtered = filtered_block(tables, place, fields[place], ends)
            far_smooth = filtered[:3]
            far_leonard = [
                [filtered[3 + k][z] - far_smooth[a][z] * far_smooth[b][z] for z in range(cells)]
                for k, (a, b) in enumerate(INDEX_PAIRS)
            ]
            for k in range(6):
                far = tables.outside(place, tables.project(far_cot[k]))
                smooth_cot[k] = add_lists(smooth_cot[k], far)
            for a in range(3):
                far = tables.outside(place, tables.project(weighted_dual(far_cot, far_smooth, a, cells)))
                smooth_duals[a] = add_lists(smooth_duals[a], far)
                far = tables.outside(place, tables.project(plain_dual(far_leonard, far_smooth, a, cells)))
                smooth_others[a] = add_lists(smooth_others[a], far)
        inner = [add_lists(tables.inside(model[k]), leonard[k]) for k in range(6)]
        for a in range(3):
            first = weighted_dual(smooth_cot, v, a, cells)
            second = weighted_dual(cot, v, a, cells)
            dual = tables.inside([dual_ref[a, z, :, lanes] for z in range(cells)])
            third = plain_dual(inner, v, a, cells)
            fourth = plain_dual(model, v, a, cells)
            for z in range(cells):
                parts_ref[a, z, :, lanes] = first[z] - smooth_duals[a][z]
                parts_ref[3 + a, z, :, lanes] = smooth_duals[a][z] - second[z]
                parts_ref[6 + a, z, :, lanes] = 2.0 * (third[z] - smooth_others[a][z]) - dual[z]
                parts_ref[9 + a, z, :, lanes] = 2.0 * dual[z] - 4.0 * fourth[z]


def finish_kernel(tables, count, turning, *refs):
    peers = tables.devices - 1
    cells = tables.cells
    v_ref, leonard_ref, model_ref, parts_ref, bins_ref = refs[:5]
    split = count - count // tables.devices
    near_refs = refs[5 : 5 + split] + refs[6 + split + peers : 6 + count + peers]
    pair_refs = refs[5 + split : 6 + split + peers]
    far_message_refs = refs[6 + count + peers : 6 + count + 2 * peers]
    residual_hbm, grad_hbm, residual_ref, grad_ref, left = refs[6 + count + 2 * peers :]
    total = sum_up([ref[...] for ref in pair_refs])
    near = sum_up([ref[...] for ref in near_refs])
    if turning:
        place = lax.axis_index("stream")
        inner = jnp.logical_and(place > 0, place < lax.axis_size("stream") - 1)
        near = jnp.where(inner, near, 0.0)
    total = total + near
    inverse = 1.0 / (total[1:2] + EPSILON)
    rows = v_ref.shape[2]
    lane = lax.broadcasted_iota(jnp.int32, bins_ref.shape, 1)
    mine = bins_ref[...] == lane

    def of_rows(per_bin):
        column = jnp.sum(jnp.where(mine, per_bin, 0.0), axis=1, keepdims=True)
        return jnp.broadcast_to(column, (rows, LANES))

    coefficient = of_rows(total[0:1] * inverse)
    pull = of_rows(-(total[2:3] * inverse))
    copies = []
    for k in range(6):
        for lanes in halves(v_ref.shape[-1]):
            for z in range(cells):
                residual_ref[k, z, :, lanes] = (
                    leonard_ref[k, z, :, lanes] - coefficient * model_ref[k, z, :, lanes]
                )
        if k % 3 == 2:
            some = pl.ds(k - 2, 3)
            copies.append(pltpu.make_async_copy(residual_ref.at[some], residual_hbm.at[some], left.at[k // 3]))
            copies[-1].start()
    for lanes in halves(v_ref.shape[-1]):
        v = [[v_ref[a, z, :, lanes] for z in range(cells)] for a in range(3)]
        from_model = [[] for _ in range(6)]
        from_dual = [[] for _ in range(3)]
        for place, ends in enumerate(far_message_refs, start=1):
            for k in range(6):
                from_model[k].append(tables.outside(place, [2.0 * ends[2 * k + end, :, lanes] for end in range(2)]))
            for a in range(3):
                pair = [(2.0 * coefficient - 1.0) * ends[12 + 2 * a + end, :, lanes] for end in range(2)]
                from_dual[a].append(tables.outside(place, pair))
        from_model = [functools.reduce(add_lists, lists) if lists else None for lists in from_model]
        from_dual = [functools.reduce(add_lists, lists) if lists else None for lists in from_dual]
        for a in range(3):
            for z in range(cells):
                pulled = parts_ref[6 + a, z, :, lanes] + coefficient * parts_ref[9 + a, z, :, lanes]
                if peers:
                    terms = [from_model[PAIR_OF[a][b]][z] * v[b][z] for b in range(3)]
                    pulled = pulled + from_dual[a][z] + sum_up(terms)
                grad_ref[a, z, :, lanes] = (
                    parts_ref[a, z, :, lanes] + coefficient * parts_ref[3 + a, z, :, lanes] + pull * pulled
                )
    copies.append(pltpu.make_async_copy(grad_ref, grad_hbm, left.at[2]))
    copies[-1].start()
    for copy in copies:
        copy.wait()


WHOLE = pl.BlockSpec(memory_space=pltpu.VMEM)
REMAIN = pl.BlockSpec(memory_space=pltpu.HBM)


def call(kernel, outs, operations, *operands, in_specs=None, out_specs=None, scratch=()):
    nbytes = sum(4 * int(np.prod(x.shape)) for x in (*operands, *outs))
    return pl.pallas_call(
        kernel,
        out_shape=outs,
        in_specs=in_specs or [WHOLE] * len(operands),
        out_specs=out_specs or [WHOLE] * len(outs),
        scratch_shapes=list(scratch),
        compiler_params=pltpu.CompilerParams(vmem_limit_bytes=32 * 1024 * 1024),
        cost_estimate=pl.CostEstimate(flops=operations, bytes_accessed=nbytes, transcendentals=0),
    )(*operands)


def from_ahead(values, shift):
    peers = lax.axis_size("span")
    return lax.ppermute(values, "span", [((i + shift) % peers, i) for i in range(peers)])


def from_source(values, span_shift, source):
    span, stream = lax.axis_size("span"), lax.axis_size("stream")
    pairs = [
        (((i + span_shift) % span) * stream + source(j) % stream, i * stream + j)
        for i in range(span)
        for j in range(stream)
    ]
    return lax.ppermute(values, ("span", "stream"), pairs)


def ring_source(stream):
    def source(j):
        if j % 2 == 0:
            return j - 2 if j >= 2 else 1
        return j + 2 if j + 2 < stream else j - 1

    return source


def on_device(velocity, strain, row_bins, cotangent):
    span, stream = lax.axis_size("span"), lax.axis_size("stream")
    cells, rows, width = velocity.shape[1:]
    tables = Tables(cells, span)
    slab = (rows, width)

    def shaped(*leading):
        return pltpu.VMEM(leading + slab, jnp.float32)

    bins = jnp.broadcast_to(row_bins[:, None], (rows, LANES))
    far_v = [from_ahead(velocity, shift) for shift in range(1, span)]
    work = cells * rows * width
    (lane,) = call(lanes_kernel, [pltpu.VMEM((rows, LANES), jnp.int32)], LONG * work)
    size, size_ends = call(
        functools.partial(prepare_kernel, tables), [shaped(cells), shaped(2)], LONG * work, lane, strain
    )
    far_size = [from_ahead(size_ends, shift) for shift in range(1, span)]
    (near_cot,) = call(
        fetch_kernel,
        [shaped(6, cells)],
        work,
        pltpu.with_memory_space_constraint(cotangent, pltpu.HBM),
        size_ends,
        in_specs=[REMAIN, WHOLE],
        scratch=[pltpu.SemaphoreType.DMA(())],
    )
    far_cot = [from_ahead(near_cot, shift) for shift in range(1, span)]
    table = pltpu.VMEM((8, LANES), jnp.float32)
    smooth, leonard, model, sums = call(
        functools.partial(forward_kernel, tables),
        [shaped(3, cells), shaped(6, cells), shaped(6, cells), table],
        LONG * work,
        velocity,
        strain,
        near_cot,
        size,
        bins,
        *far_v,
        *far_size,
    )
    other_sums = from_source(sums, 0, lambda j: j ^ 1)
    dual, message = call(
        functools.partial(message_kernel, tables), [shaped(3, cells), shaped(18)], 100 * work, smooth, model
    )
    pair_sums = sums + other_sums
    far_message = [from_ahead(message, shift) for shift in range(1, span)]
    most_rows = 2 * rows * stream // NBINS
    reach = -(-(most_rows - 1) // rows)
    turning = reach <= 1
    if turning:
        sources = [ring_source(stream)]
    else:
        steps = range(1, -(-reach // 2) + 1)
        sources = [functools.partial(lambda j, away: j + away, away=2 * step * way) for step in steps for way in (1, -1)]
    across_sums = [from_source(pair_sums, shift, source) for shift in range(1, span) for source in sources]
    far_pairs = [from_ahead(pair_sums, shift) for shift in range(1, span)]
    near_sums = [from_source(pair_sums, 0, source) for source in sources]
    (parts,) = call(
        functools.partial(local_kernel, tables),
        [shaped(12, cells)],
        LONG * work,
        velocity,
        near_cot,
        smooth,
        leonard,
        model,
        dual,
        *far_v,
        *far_cot,
    )
    outs = [jax.ShapeDtypeStruct((n, cells) + slab, jnp.float32) for n in (6, 3)]
    return tuple(
        call(
            functools.partial(finish_kernel, tables, len(across_sums) + len(near_sums), turning),
            outs,
            200 * work,
            velocity,
            leonard,
            model,
            parts,
            bins,
            *across_sums,
            *far_pairs,
            pair_sums,
            *near_sums,
            *far_message,
            out_specs=[REMAIN] * 2,
            scratch=[pltpu.VMEM(x.shape, x.dtype) for x in outs] + [pltpu.SemaphoreType.DMA((3,))],
        )
    )


def solution(mesh):
    fields = P(None, "span", "stream", None)
    return jax.shard_map(
        on_device,
        mesh=mesh,
        in_specs=(fields, fields, P("stream"), fields),
        out_specs=(fields, fields),
        check_vma=False,
    )
```

```python
import functools

import jax
import jax.numpy as jnp
import numpy as np
from jax import lax
from jax.experimental import pallas as pl
from jax.experimental.pallas import tpu as pltpu
from jax.sharding import PartitionSpec as P

NBINS = 64
FILTER_ALPHA = 0.45
CENTER_WEIGHT = 0.95
SIDE_WEIGHT = 0.475
STRAIN_FLOOR = 0.25
EPSILON = 1e-06
INDEX_PAIRS = ((0, 0), (0, 1), (0, 2), (1, 1), (1, 2), (2, 2))
PAIR_WEIGHTS = (1.0, 2.0, 2.0, 1.0, 2.0, 1.0)
PAIR_OF = ((0, 1, 2), (1, 3, 4), (2, 4, 5))
LANES = 128
LONG = 300000


def filter_row(extent):
    eye = np.eye(extent)
    ring = np.roll(eye, 1, axis=1) + np.roll(eye, -1, axis=1)
    system = eye + FILTER_ALPHA * ring
    side = CENTER_WEIGHT * eye + SIDE_WEIGHT * ring
    return np.linalg.solve(system, side)[0]


def end_weights(cells):
    weights = np.zeros((2, cells))
    weights[0, 0] = 1.0
    weights[1, cells - 1] = 1.0
    inner = cells - 2
    if inner > 0:
        system = np.eye(inner) + FILTER_ALPHA * (np.eye(inner, k=1) + np.eye(inner, k=-1))
        right = np.zeros((inner, 2))
        right[0, 0] = -FILTER_ALPHA
        right[inner - 1, 1] = -FILTER_ALPHA
        weights[:, 1:-1] = np.linalg.solve(system, right).T
    return weights


class Tables:
    def __init__(self, cells, devices):
        row = filter_row(cells * devices)
        extent = cells * devices
        self.cells = cells
        self.devices = devices
        self.own = [[float(row[(z - w) % extent]) for w in range(cells)] for z in range(cells)]
        self.ends = [[float(x) for x in line] for line in end_weights(cells)]
        self.couple = [
            [[float(row[(z - shift * cells - w) % extent]) for w in (0, cells - 1)] for z in range(cells)]
            for shift in range(devices)
        ]

    def project(self, values):
        return [weighted(line, values) for line in self.ends]

    def inside(self, values):
        return [weighted(line, values) for line in self.own]

    def outside(self, shift, ends):
        return [weighted(line, ends) for line in self.couple[shift]]


def weighted(weights, values):
    total = None
    for weight, value in zip(weights, values):
        if weight == 0.0:
            continue
        term = value if weight == 1.0 else value * weight
        total = term if total is None else total + term
    return total


def add_lists(left, right):
    return [x + y for x, y in zip(left, right)]


def halves(width):
    return [pl.ds(start, LANES) for start in range(0, width, LANES)]


def sum_up(terms):
    total = terms[0]
    for term in terms[1:]:
        total = total + term
    return total


def lanes_kernel(lane_ref):
    lane_ref[...] = lax.broadcasted_iota(jnp.int32, lane_ref.shape, 1)


def prepare_kernel(tables, lane_ref, strain_ref, size_ref, size_ends_ref):
    cells = tables.cells
    for lanes in halves(strain_ref.shape[-1]):
        size = []
        for z in range(cells):
            values = [strain_ref[k, z, :, lanes] for k in range(6)]
            total = sum_up([weight * (value * value) for weight, value in zip(PAIR_WEIGHTS, values)])
            size.append(jnp.sqrt(jnp.maximum(2.0 * total, STRAIN_FLOOR)))
            size_ref[z, :, lanes] = size[z]
        for end, value in enumerate(tables.project(size)):
            size_ends_ref[end, :, lanes] = value


def fetch_kernel(cot_hbm, size_ends_ref, cot_ref, arrived):
    copy = pltpu.make_async_copy(cot_hbm, cot_ref, arrived)
    copy.start()
    copy.wait()


def products_of(v):
    return [[x * y for x, y in zip(v[a], v[b])] for a, b in INDEX_PAIRS]


def filtered_block(tables, place, fields, ends):
    filtered = [tables.inside(field) for field in fields]
    for other in range(tables.devices):
        if other != place:
            shift = (other - place) % tables.devices
            filtered = [add_lists(near, tables.outside(shift, far)) for near, far in zip(filtered, ends[other])]
    return filtered


def plain_dual(tensor, vector, a, cells):
    return [sum_up([tensor[PAIR_OF[a][b]][z] * vector[b][z] for b in range(3)]) for z in range(cells)]


def weighted_dual(tensor, vector, a, cells):
    plain = plain_dual(tensor, vector, a, cells)
    return [plain[z] + tensor[PAIR_OF[a][a]][z] * vector[a][z] for z in range(cells)]


def velocity_kernel(tables, v_ref, bins_ref, *refs):
    far_v_refs = refs[:-4]
    smooth_ref, leonard_ref, rest_ref, mask_ref = refs[-4:]
    cells = tables.cells
    for lanes in halves(v_ref.shape[-1]):
        v = [[v_ref[a, z, :, lanes] for z in range(cells)] for a in range(3)]
        products = products_of(v)
        ends = [None]
        for far_v_ref in far_v_refs:
            far = [[far_v_ref[a, z, :, lanes] for z in range(cells)] for a in range(3)]
            ends.append([tables.project(field) for field in far + products_of(far)])
        filtered = filtered_block(tables, 0, v + products, ends)
        for a in range(3):
            for z in range(cells):
                smooth_ref[a, z, :, lanes] = filtered[a][z]
        for k, (a, b) in enumerate(INDEX_PAIRS):
            for z in range(cells):
                coarse = filtered[a][z] * filtered[b][z]
                leonard_ref[k, z, :, lanes] = filtered[3 + k][z] - coarse
                rest_ref[k, z, :, lanes] = products[k][z] - coarse
    lane = lax.broadcasted_iota(jnp.int32, bins_ref.shape, 1)
    mask_ref[...] = jnp.where(bins_ref[...] == lane, 1.0, 0.0)


def model_kernel(tables, strain_ref, cot_ref, size_ref, leonard_ref, rest_ref, mask_ref, *refs):
    far_size_refs = refs[:-2]
    model_ref, sums_ref = refs[-2:]
    cells = tables.cells
    cross, square, blame = [], [], []
    for lanes in halves(strain_ref.shape[-1]):
        size = [size_ref[z, :, lanes] for z in range(cells)]
        ends = [None] + [[[far[end, :, lanes] for end in range(2)]] for far in far_size_refs]
        smooth_size = filtered_block(tables, 0, [size], ends)[0]
        factor = [2.0 * (4.0 * smooth_size[z] - size[z]) for z in range(cells)]
        for k in range(6):
            for z in range(cells):
                leonard = leonard_ref[k, z, :, lanes]
                term = rest_ref[k, z, :, lanes] + factor[z] * strain_ref[k, z, :, lanes]
                model_ref[k, z, :, lanes] = term
                scaled = PAIR_WEIGHTS[k] * term
                cross.append(scaled * leonard)
                square.append(scaled * term)
                blame.append(term * cot_ref[k, z, :, lanes])
            cross, square, blame = [sum_up(cross)], [sum_up(square)], [sum_up(blame)]
    mine = mask_ref[...] > 0.5
    place = lax.broadcasted_iota(jnp.int32, (8, LANES), 0)
    table = jnp.zeros((8, LANES), jnp.float32)
    for index, sums in enumerate((cross, square, blame)):
        per_row = jnp.sum(sums[0], axis=1, keepdims=True)
        per_bin = jnp.sum(jnp.where(mine, per_row, 0.0), axis=0, keepdims=True)
        table = jnp.where(place == index, per_bin, table)
    sums_ref[...] = table


def message_kernel(tables, smooth_ref, model_ref, sums_ref, other_sums_ref, dual_ref, message_ref, pair_ref):
    cells = tables.cells
    pair_sums = sums_ref[...] + other_sums_ref[...]
    pair_ref[...] = pair_sums
    message_ref[18, 0:8, 0:LANES] = pair_sums
    for lanes in halves(model_ref.shape[-1]):
        model = [[model_ref[k, z, :, lanes] for z in range(cells)] for k in range(6)]
        smooth_v = [[smooth_ref[a, z, :, lanes] for z in range(cells)] for a in range(3)]
        for k in range(6):
            for end, value in enumerate(tables.project(model[k])):
                message_ref[2 * k + end, :, lanes] = value
        for a in range(3):
            dual = [2.0 * x for x in plain_dual(model, smooth_v, a, cells)]
            for z in range(cells):
                dual_ref[a, z, :, lanes] = dual[z]
            for end, value in enumerate(tables.project(dual)):
                message_ref[12 + 2 * a + end, :, lanes] = value


def local_kernel(tables, *refs):
    peers = tables.devices - 1
    cells = tables.cells
    v_ref, cot_ref, smooth_ref, leonard_ref, model_ref, dual_ref = refs[:6]
    far_v_refs = refs[6 : 6 + peers]
    far_cot_refs = refs[6 + peers : 6 + 2 * peers]
    parts_ref = refs[-1]
    for lanes in halves(v_ref.shape[-1]):

        def load(ref, count):
            return [[ref[f, z, :, lanes] for z in range(cells)] for f in range(count)]

        fields, ends = [], []
        for ref in (v_ref, *far_v_refs):
            v = load(ref, 3)
            fields.append(v + products_of(v))
            ends.append([tables.project(field) for field in fields[-1]])
        v = fields[0][:3]
        cot, model, leonard, smooth_v = load(cot_ref, 6), load(model_ref, 6), load(leonard_ref, 6), load(smooth_ref, 3)
        smooth_cot = [tables.inside(field) for field in cot]
        duals = [weighted_dual(cot, smooth_v, a, cells) for a in range(3)]
        others = [plain_dual(leonard, smooth_v, a, cells) for a in range(3)]
        smooth_duals = [tables.inside(field) for field in duals]
        smooth_others = [tables.inside(field) for field in others]
        for place in range(1, tables.devices):
            far_cot = load(far_cot_refs[place - 1], 6)
            filtered = filtered_block(tables, place, fields[place], ends)
            far_smooth = filtered[:3]
            far_leonard = [
                [filtered[3 + k][z] - far_smooth[a][z] * far_smooth[b][z] for z in range(cells)]
                for k, (a, b) in enumerate(INDEX_PAIRS)
            ]
            for k in range(6):
                far = tables.outside(place, tables.project(far_cot[k]))
                smooth_cot[k] = add_lists(smooth_cot[k], far)
            for a in range(3):
                far = tables.outside(place, tables.project(weighted_dual(far_cot, far_smooth, a, cells)))
                smooth_duals[a] = add_lists(smooth_duals[a], far)
                far = tables.outside(place, tables.project(plain_dual(far_leonard, far_smooth, a, cells)))
                smooth_others[a] = add_lists(smooth_others[a], far)
        inner = [add_lists(tables.inside(model[k]), leonard[k]) for k in range(6)]
        for a in range(3):
            first = weighted_dual(smooth_cot, v, a, cells)
            second = weighted_dual(cot, v, a, cells)
            dual = tables.inside([dual_ref[a, z, :, lanes] for z in range(cells)])
            third = plain_dual(inner, v, a, cells)
            fourth = plain_dual(model, v, a, cells)
            for z in range(cells):
                parts_ref[a, z, :, lanes] = first[z] - smooth_duals[a][z]
                parts_ref[3 + a, z, :, lanes] = smooth_duals[a][z] - second[z]
                parts_ref[6 + a, z, :, lanes] = 2.0 * (third[z] - smooth_others[a][z]) - dual[z]
                parts_ref[9 + a, z, :, lanes] = 2.0 * dual[z] - 4.0 * fourth[z]


def finish_kernel(tables, count, turning, *refs):
    peers = tables.devices - 1
    cells = tables.cells
    v_ref, leonard_ref, model_ref, parts_ref, mask_ref = refs[:5]
    near_refs = refs[5 : 5 + count]
    pair_ref = refs[5 + count]
    far_message_refs = refs[6 + count : 6 + count + peers]
    residual_hbm, grad_hbm, residual_ref, grad_ref, left = refs[6 + count + peers :]
    total = sum_up([pair_ref[...]] + [ref[18, 0:8, 0:LANES] for ref in far_message_refs])
    near = sum_up([ref[...] for ref in near_refs])
    if turning:
        place = lax.axis_index("stream")
        inner = jnp.logical_and(place > 0, place < lax.axis_size("stream") - 1)
        near = jnp.where(inner, near, 0.0)
    total = total + near
    inverse = 1.0 / (total[1:2] + EPSILON)
    rows = v_ref.shape[2]
    mine = mask_ref[...] > 0.5

    def of_rows(per_bin):
        column = jnp.sum(jnp.where(mine, per_bin, 0.0), axis=1, keepdims=True)
        return jnp.broadcast_to(column, (rows, LANES))

    coefficient = of_rows(total[0:1] * inverse)
    pull = of_rows(-(total[2:3] * inverse))
    copies = []
    for k in range(6):
        for lanes in halves(v_ref.shape[-1]):
            for z in range(cells):
                residual_ref[k, z, :, lanes] = (
                    leonard_ref[k, z, :, lanes] - coefficient * model_ref[k, z, :, lanes]
                )
        if k % 3 == 2:
            some = pl.ds(k - 2, 3)
            copies.append(pltpu.make_async_copy(residual_ref.at[some], residual_hbm.at[some], left.at[k // 3]))
            copies[-1].start()
    for lanes in halves(v_ref.shape[-1]):
        v = [[v_ref[a, z, :, lanes] for z in range(cells)] for a in range(3)]
        from_model = [[] for _ in range(6)]
        from_dual = [[] for _ in range(3)]
        for place, ends in enumerate(far_message_refs, start=1):
            for k in range(6):
                from_model[k].append(tables.outside(place, [2.0 * ends[2 * k + end, :, lanes] for end in range(2)]))
            for a in range(3):
                pair = [(2.0 * coefficient - 1.0) * ends[12 + 2 * a + end, :, lanes] for end in range(2)]
                from_dual[a].append(tables.outside(place, pair))
        from_model = [functools.reduce(add_lists, lists) if lists else None for lists in from_model]
        from_dual = [functools.reduce(add_lists, lists) if lists else None for lists in from_dual]
        for a in range(3):
            for z in range(cells):
                pulled = parts_ref[6 + a, z, :, lanes] + coefficient * parts_ref[9 + a, z, :, lanes]
                if peers:
                    terms = [from_model[PAIR_OF[a][b]][z] * v[b][z] for b in range(3)]
                    pulled = pulled + from_dual[a][z] + sum_up(terms)
                grad_ref[a, z, :, lanes] = (
                    parts_ref[a, z, :, lanes] + coefficient * parts_ref[3 + a, z, :, lanes] + pull * pulled
                )
    copies.append(pltpu.make_async_copy(grad_ref, grad_hbm, left.at[2]))
    copies[-1].start()
    for copy in copies:
        copy.wait()


WHOLE = pl.BlockSpec(memory_space=pltpu.VMEM)
REMAIN = pl.BlockSpec(memory_space=pltpu.HBM)


def call(kernel, outs, operations, *operands, in_specs=None, out_specs=None, scratch=()):
    nbytes = sum(4 * int(np.prod(x.shape)) for x in (*operands, *outs))
    return pl.pallas_call(
        kernel,
        out_shape=outs,
        in_specs=in_specs or [WHOLE] * len(operands),
        out_specs=out_specs or [WHOLE] * len(outs),
        scratch_shapes=list(scratch),
        compiler_params=pltpu.CompilerParams(vmem_limit_bytes=32 * 1024 * 1024),
        cost_estimate=pl.CostEstimate(flops=operations, bytes_accessed=nbytes, transcendentals=0),
    )(*operands)


def from_ahead(values, shift):
    peers = lax.axis_size("span")
    return lax.ppermute(values, "span", [((i + shift) % peers, i) for i in range(peers)])


def from_source(values, span_shift, source):
    span, stream = lax.axis_size("span"), lax.axis_size("stream")
    pairs = [
        (((i + span_shift) % span) * stream + source(j) % stream, i * stream + j)
        for i in range(span)
        for j in range(stream)
    ]
    return lax.ppermute(values, ("span", "stream"), pairs)


def ring_source(stream):
    def source(j):
        if j % 2 == 0:
            return j - 2 if j >= 2 else 1
        return j + 2 if j + 2 < stream else j - 1

    return source


def on_device(velocity, strain, row_bins, cotangent):
    span, stream = lax.axis_size("span"), lax.axis_size("stream")
    cells, rows, width = velocity.shape[1:]
    tables = Tables(cells, span)
    slab = (rows, width)

    def shaped(*leading):
        return pltpu.VMEM(leading + slab, jnp.float32)

    bins = jnp.broadcast_to(row_bins[:, None], (rows, LANES))
    far_v = [from_ahead(velocity, shift) for shift in range(1, span)]
    work = cells * rows * width
    (lane,) = call(lanes_kernel, [pltpu.VMEM((rows, LANES), jnp.int32)], LONG * work)
    size, size_ends = call(
        functools.partial(prepare_kernel, tables), [shaped(cells), shaped(2)], LONG * work, lane, strain
    )
    far_size = [from_ahead(size_ends, shift) for shift in range(1, span)]
    (near_cot,) = call(
        fetch_kernel,
        [shaped(6, cells)],
        work,
        pltpu.with_memory_space_constraint(cotangent, pltpu.HBM),
        size_ends,
        in_specs=[REMAIN, WHOLE],
        scratch=[pltpu.SemaphoreType.DMA(())],
    )
    far_cot = [from_ahead(near_cot, shift) for shift in range(1, span)]
    table = pltpu.VMEM((8, LANES), jnp.float32)
    smooth, leonard, rest, mask = call(
        functools.partial(velocity_kernel, tables),
        [shaped(3, cells), shaped(6, cells), shaped(6, cells), pltpu.VMEM((rows, LANES), jnp.float32)],
        LONG * work,
        velocity,
        bins,
        *far_v,
    )
    model, sums = call(
        functools.partial(model_kernel, tables),
        [shaped(6, cells), table],
        LONG * work,
        strain,
        near_cot,
        size,
        leonard,
        rest,
        mask,
        *far_size,
    )
    other_sums = from_source(sums, 0, lambda j: j ^ 1)
    dual, message, pair_sums = call(
        functools.partial(message_kernel, tables),
        [shaped(3, cells), shaped(19), table],
        100 * work,
        smooth,
        model,
        sums,
        other_sums,
    )
    far_message = [from_ahead(message, shift) for shift in range(1, span)]
    most_rows = 2 * rows * stream // NBINS
    reach = -(-(most_rows - 1) // rows)
    turning = reach <= 1
    if turning:
        sources = [ring_source(stream)]
    else:
        steps = range(1, -(-reach // 2) + 1)
        sources = [functools.partial(lambda j, away: j + away, away=2 * step * way) for step in steps for way in (1, -1)]
    near_sums = [from_source(pair_sums, shift, source) for shift in range(span) for source in sources]
    (parts,) = call(
        functools.partial(local_kernel, tables),
        [shaped(12, cells)],
        500 * work,
        velocity,
        near_cot,
        smooth,
        leonard,
        model,
        dual,
        *far_v,
        *far_cot,
    )
    outs = [jax.ShapeDtypeStruct((n, cells) + slab, jnp.float32) for n in (6, 3)]
    return tuple(
        call(
            functools.partial(finish_kernel, tables, len(near_sums), turning),
            outs,
            200 * work,
            velocity,
            leonard,
            model,
            parts,
            mask,
            *near_sums,
            pair_sums,
            *far_message,
            out_specs=[REMAIN] * 2,
            scratch=[pltpu.VMEM(x.shape, x.dtype) for x in outs] + [pltpu.SemaphoreType.DMA((3,))],
        )
    )


def solution(mesh):
    fields = P(None, "span", "stream", None)
    return jax.shard_map(
        on_device,
        mesh=mesh,
        in_specs=(fields, fields, P("stream"), fields),
        out_specs=(fields, fields),
        check_vma=False,
    )
```

```python
import functools

import jax
import jax.numpy as jnp
import numpy as np
from jax import lax
from jax.experimental import pallas as pl
from jax.experimental.pallas import tpu as pltpu
from jax.sharding import PartitionSpec as P

NBINS = 64
FILTER_ALPHA = 0.45
CENTER_WEIGHT = 0.95
SIDE_WEIGHT = 0.475
STRAIN_FLOOR = 0.25
EPSILON = 1e-06
INDEX_PAIRS = ((0, 0), (0, 1), (0, 2), (1, 1), (1, 2), (2, 2))
PAIR_WEIGHTS = (1.0, 2.0, 2.0, 1.0, 2.0, 1.0)
PAIR_OF = ((0, 1, 2), (1, 3, 4), (2, 4, 5))
LANES = 128
LONG = 300000


def filter_row(extent):
    eye = np.eye(extent)
    ring = np.roll(eye, 1, axis=1) + np.roll(eye, -1, axis=1)
    system = eye + FILTER_ALPHA * ring
    side = CENTER_WEIGHT * eye + SIDE_WEIGHT * ring
    return np.linalg.solve(system, side)[0]


def end_weights(cells):
    weights = np.zeros((2, cells))
    weights[0, 0] = 1.0
    weights[1, cells - 1] = 1.0
    inner = cells - 2
    if inner > 0:
        system = np.eye(inner) + FILTER_ALPHA * (np.eye(inner, k=1) + np.eye(inner, k=-1))
        right = np.zeros((inner, 2))
        right[0, 0] = -FILTER_ALPHA
        right[inner - 1, 1] = -FILTER_ALPHA
        weights[:, 1:-1] = np.linalg.solve(system, right).T
    return weights


class Tables:
    def __init__(self, cells, devices):
        row = filter_row(cells * devices)
        extent = cells * devices
        self.cells = cells
        self.devices = devices
        self.own = [[float(row[(z - w) % extent]) for w in range(cells)] for z in range(cells)]
        self.ends = [[float(x) for x in line] for line in end_weights(cells)]
        self.couple = [
            [[float(row[(z - shift * cells - w) % extent]) for w in (0, cells - 1)] for z in range(cells)]
            for shift in range(devices)
        ]

    def project(self, values):
        return [weighted(line, values) for line in self.ends]

    def inside(self, values):
        return [weighted(line, values) for line in self.own]

    def outside(self, shift, ends):
        return [weighted(line, ends) for line in self.couple[shift]]


def weighted(weights, values):
    total = None
    for weight, value in zip(weights, values):
        if weight == 0.0:
            continue
        term = value if weight == 1.0 else value * weight
        total = term if total is None else total + term
    return total


def add_lists(left, right):
    return [x + y for x, y in zip(left, right)]


def halves(width):
    return [pl.ds(start, LANES) for start in range(0, width, LANES)]


def sum_up(terms):
    total = terms[0]
    for term in terms[1:]:
        total = total + term
    return total


def lanes_kernel(lane_ref):
    lane_ref[...] = lax.broadcasted_iota(jnp.int32, lane_ref.shape, 1)


def prepare_kernel(tables, lane_ref, strain_ref, size_ref, size_ends_ref):
    cells = tables.cells
    for lanes in halves(strain_ref.shape[-1]):
        size = []
        for z in range(cells):
            values = [strain_ref[k, z, :, lanes] for k in range(6)]
            total = sum_up([weight * (value * value) for weight, value in zip(PAIR_WEIGHTS, values)])
            size.append(jnp.sqrt(jnp.maximum(2.0 * total, STRAIN_FLOOR)))
            size_ref[z, :, lanes] = size[z]
        for end, value in enumerate(tables.project(size)):
            size_ends_ref[end, :, lanes] = value


def fetch_kernel(cot_hbm, size_ends_ref, cot_ref, arrived):
    copy = pltpu.make_async_copy(cot_hbm, cot_ref, arrived)
    copy.start()
    copy.wait()


def products_of(v):
    return [[x * y for x, y in zip(v[a], v[b])] for a, b in INDEX_PAIRS]


def filtered_block(tables, place, fields, ends):
    filtered = [tables.inside(field) for field in fields]
    for other in range(tables.devices):
        if other != place:
            shift = (other - place) % tables.devices
            filtered = [add_lists(near, tables.outside(shift, far)) for near, far in zip(filtered, ends[other])]
    return filtered


def plain_dual(tensor, vector, a, cells):
    return [sum_up([tensor[PAIR_OF[a][b]][z] * vector[b][z] for b in range(3)]) for z in range(cells)]


def weighted_dual(tensor, vector, a, cells):
    plain = plain_dual(tensor, vector, a, cells)
    return [plain[z] + tensor[PAIR_OF[a][a]][z] * vector[a][z] for z in range(cells)]


def velocity_kernel(tables, v_ref, bins_ref, *refs):
    far_v_refs = refs[:-4]
    smooth_ref, leonard_ref, rest_ref, mask_ref = refs[-4:]
    cells = tables.cells
    for lanes in halves(v_ref.shape[-1]):
        v = [[v_ref[a, z, :, lanes] for z in range(cells)] for a in range(3)]
        products = products_of(v)
        ends = [None]
        for far_v_ref in far_v_refs:
            far = [[far_v_ref[a, z, :, lanes] for z in range(cells)] for a in range(3)]
            ends.append([tables.project(field) for field in far + products_of(far)])
        filtered = filtered_block(tables, 0, v + products, ends)
        for a in range(3):
            for z in range(cells):
                smooth_ref[a, z, :, lanes] = filtered[a][z]
        for k, (a, b) in enumerate(INDEX_PAIRS):
            for z in range(cells):
                coarse = filtered[a][z] * filtered[b][z]
                leonard_ref[k, z, :, lanes] = filtered[3 + k][z] - coarse
                rest_ref[k, z, :, lanes] = products[k][z] - coarse
    lane = lax.broadcasted_iota(jnp.int32, bins_ref.shape, 1)
    mask_ref[...] = jnp.where(bins_ref[...] == lane, 1.0, 0.0)


def model_kernel(tables, strain_ref, cot_ref, size_ref, leonard_ref, rest_ref, mask_ref, *refs):
    far_size_refs = refs[:-2]
    model_ref, sums_ref = refs[-2:]
    cells = tables.cells
    cross, square, blame = [], [], []
    for lanes in halves(strain_ref.shape[-1]):
        size = [size_ref[z, :, lanes] for z in range(cells)]
        ends = [None] + [[[far[end, :, lanes] for end in range(2)]] for far in far_size_refs]
        smooth_size = filtered_block(tables, 0, [size], ends)[0]
        factor = [2.0 * (4.0 * smooth_size[z] - size[z]) for z in range(cells)]
        for k in range(6):
            for z in range(cells):
                leonard = leonard_ref[k, z, :, lanes]
                term = rest_ref[k, z, :, lanes] + factor[z] * strain_ref[k, z, :, lanes]
                model_ref[k, z, :, lanes] = term
                scaled = PAIR_WEIGHTS[k] * term
                cross.append(scaled * leonard)
                square.append(scaled * term)
                blame.append(term * cot_ref[k, z, :, lanes])
            cross, square, blame = [sum_up(cross)], [sum_up(square)], [sum_up(blame)]
    mine = mask_ref[...] > 0.5
    place = lax.broadcasted_iota(jnp.int32, (8, LANES), 0)
    table = jnp.zeros((8, LANES), jnp.float32)
    for index, sums in enumerate((cross, square, blame)):
        per_row = jnp.sum(sums[0], axis=1, keepdims=True)
        per_bin = jnp.sum(jnp.where(mine, per_row, 0.0), axis=0, keepdims=True)
        table = jnp.where(place == index, per_bin, table)
    sums_ref[...] = table


def on_second_core():
    return lax.rem(lax.axis_index("stream"), 2) == 1


def velocity_fields(tables, refs, lanes):
    fields, ends = [], []
    for ref in refs:
        v = [[ref[a, z, :, lanes] for z in range(tables.cells)] for a in range(3)]
        fields.append(v + products_of(v))
        ends.append([tables.project(field) for field in fields[-1]])
    return fields, ends


def own_parts(tables, v_ref, cot_ref, smooth_ref, leonard_ref, model_ref, dual_ref, far_v_refs, parts_ref):
    cells = tables.cells
    for lanes in halves(v_ref.shape[-1]):

        def load(ref, count):
            return [[ref[f, z, :, lanes] for z in range(cells)] for f in range(count)]

        fields, ends = velocity_fields(tables, (v_ref, *far_v_refs), lanes)
        v = fields[0][:3]
        cot, model, leonard, smooth_v = load(cot_ref, 6), load(model_ref, 6), load(leonard_ref, 6), load(smooth_ref, 3)
        smooth_cot = [tables.inside(field) for field in cot]
        smooth_duals = [tables.inside(weighted_dual(cot, smooth_v, a, cells)) for a in range(3)]
        smooth_others = [tables.inside(plain_dual(leonard, smooth_v, a, cells)) for a in range(3)]
        for place in range(1, tables.devices):
            filtered = filtered_block(tables, place, fields[place], ends)
            far_leonard = [
                [filtered[3 + k][z] - filtered[a][z] * filtered[b][z] for z in range(cells)]
                for k, (a, b) in enumerate(INDEX_PAIRS)
            ]
            for a in range(3):
                far = tables.outside(place, tables.project(plain_dual(far_leonard, filtered, a, cells)))
                smooth_others[a] = add_lists(smooth_others[a], far)
        inner = [add_lists(tables.inside(model[k]), leonard[k]) for k in range(6)]
        for a in range(3):
            first = weighted_dual(smooth_cot, v, a, cells)
            second = weighted_dual(cot, v, a, cells)
            dual = tables.inside([dual_ref[a, z, :, lanes] for z in range(cells)])
            third = plain_dual(inner, v, a, cells)
            fourth = plain_dual(model, v, a, cells)
            for z in range(cells):
                parts_ref[a, z, :, lanes] = first[z] - smooth_duals[a][z]
                parts_ref[3 + a, z, :, lanes] = smooth_duals[a][z] - second[z]
                parts_ref[6 + a, z, :, lanes] = 2.0 * (third[z] - smooth_others[a][z]) - dual[z]
                parts_ref[9 + a, z, :, lanes] = 2.0 * dual[z] - 4.0 * fourth[z]


def message_kernel(tables, v_ref, cot_ref, smooth_ref, leonard_ref, model_ref, sums_ref, other_sums_ref, *refs):
    far_v_refs = refs[:-4]
    dual_ref, message_ref, pair_ref, early_ref = refs[-4:]
    cells = tables.cells
    pair_sums = sums_ref[...] + other_sums_ref[...]
    pair_ref[...] = pair_sums
    message_ref[18, 0:8, 0:LANES] = pair_sums
    for lanes in halves(model_ref.shape[-1]):
        model = [[model_ref[k, z, :, lanes] for z in range(cells)] for k in range(6)]
        smooth_v = [[smooth_ref[a, z, :, lanes] for z in range(cells)] for a in range(3)]
        for k in range(6):
            for end, value in enumerate(tables.project(model[k])):
                message_ref[2 * k + end, :, lanes] = value
        for a in range(3):
            dual = [2.0 * x for x in plain_dual(model, smooth_v, a, cells)]
            for z in range(cells):
                dual_ref[a, z, :, lanes] = dual[z]
            for end, value in enumerate(tables.project(dual)):
                message_ref[12 + 2 * a + end, :, lanes] = value

    @pl.when(on_second_core())
    def _():
        own_parts(tables, v_ref, cot_ref, smooth_ref, leonard_ref, model_ref, dual_ref, far_v_refs, early_ref)


def local_kernel(tables, early_ref, v_ref, cot_ref, smooth_ref, leonard_ref, model_ref, dual_ref, *refs):
    peers = tables.devices - 1
    cells = tables.cells
    far_v_refs, far_cot_refs, parts_ref = refs[:peers], refs[peers : 2 * peers], refs[-1]

    @pl.when(on_second_core())
    def _():
        parts_ref[...] = early_ref[...]

    @pl.when(jnp.logical_not(on_second_core()))
    def _():
        own_parts(tables, v_ref, cot_ref, smooth_ref, leonard_ref, model_ref, dual_ref, far_v_refs, parts_ref)

    for lanes in halves(v_ref.shape[-1]):
        fields, ends = velocity_fields(tables, (v_ref, *far_v_refs), lanes)
        v = fields[0][:3]
        smooth_cot, smooth_duals = [[] for _ in range(6)], [[] for _ in range(3)]
        for place in range(1, tables.devices):
            far_cot_ref = far_cot_refs[place - 1]
            far_cot = [[far_cot_ref[k, z, :, lanes] for z in range(cells)] for k in range(6)]
            far_smooth = filtered_block(tables, place, fields[place][:3], [x[:3] for x in ends])
            for k in range(6):
                smooth_cot[k].append(tables.outside(place, tables.project(far_cot[k])))
            for a in range(3):
                dual = weighted_dual(far_cot, far_smooth, a, cells)
                smooth_duals[a].append(tables.outside(place, tables.project(dual)))
        if not peers:
            continue
        smooth_cot = [functools.reduce(add_lists, lists) for lists in smooth_cot]
        smooth_duals = [functools.reduce(add_lists, lists) for lists in smooth_duals]
        for a in range(3):
            first = weighted_dual(smooth_cot, v, a, cells)
            for z in range(cells):
                parts_ref[a, z, :, lanes] = parts_ref[a, z, :, lanes] + (first[z] - smooth_duals[a][z])
                parts_ref[3 + a, z, :, lanes] = parts_ref[3 + a, z, :, lanes] + smooth_duals[a][z]


def finish_kernel(tables, count, turning, *refs):
    peers = tables.devices - 1
    cells = tables.cells
    v_ref, leonard_ref, model_ref, parts_ref, mask_ref = refs[:5]
    near_refs = refs[5 : 5 + count]
    pair_ref = refs[5 + count]
    far_message_refs = refs[6 + count : 6 + count + peers]
    residual_hbm, grad_hbm, residual_ref, grad_ref, left = refs[6 + count + peers :]
    total = sum_up([pair_ref[...]] + [ref[18, 0:8, 0:LANES] for ref in far_message_refs])
    near = sum_up([ref[...] for ref in near_refs])
    if turning:
        place = lax.axis_index("stream")
        inner = jnp.logical_and(place > 0, place < lax.axis_size("stream") - 1)
        near = jnp.where(inner, near, 0.0)
    total = total + near
    inverse = 1.0 / (total[1:2] + EPSILON)
    rows = v_ref.shape[2]
    mine = mask_ref[...] > 0.5

    def of_rows(per_bin):
        column = jnp.sum(jnp.where(mine, per_bin, 0.0), axis=1, keepdims=True)
        return jnp.broadcast_to(column, (rows, LANES))

    coefficient = of_rows(total[0:1] * inverse)
    pull = of_rows(-(total[2:3] * inverse))
    copies = []
    for k in range(6):
        for lanes in halves(v_ref.shape[-1]):
            for z in range(cells):
                residual_ref[k, z, :, lanes] = (
                    leonard_ref[k, z, :, lanes] - coefficient * model_ref[k, z, :, lanes]
                )
        if k % 3 == 2:
            some = pl.ds(k - 2, 3)
            copies.append(pltpu.make_async_copy(residual_ref.at[some], residual_hbm.at[some], left.at[k // 3]))
            copies[-1].start()
    for lanes in halves(v_ref.shape[-1]):
        v = [[v_ref[a, z, :, lanes] for z in range(cells)] for a in range(3)]
        from_model = [[] for _ in range(6)]
        from_dual = [[] for _ in range(3)]
        for place, ends in enumerate(far_message_refs, start=1):
            for k in range(6):
                from_model[k].append(tables.outside(place, [2.0 * ends[2 * k + end, :, lanes] for end in range(2)]))
            for a in range(3):
                pair = [(2.0 * coefficient - 1.0) * ends[12 + 2 * a + end, :, lanes] for end in range(2)]
                from_dual[a].append(tables.outside(place, pair))
        from_model = [functools.reduce(add_lists, lists) if lists else None for lists in from_model]
        from_dual = [functools.reduce(add_lists, lists) if lists else None for lists in from_dual]
        for a in range(3):
            for z in range(cells):
                pulled = parts_ref[6 + a, z, :, lanes] + coefficient * parts_ref[9 + a, z, :, lanes]
                if peers:
                    terms = [from_model[PAIR_OF[a][b]][z] * v[b][z] for b in range(3)]
                    pulled = pulled + from_dual[a][z] + sum_up(terms)
                grad_ref[a, z, :, lanes] = (
                    parts_ref[a, z, :, lanes] + coefficient * parts_ref[3 + a, z, :, lanes] + pull * pulled
                )
    copies.append(pltpu.make_async_copy(grad_ref, grad_hbm, left.at[2]))
    copies[-1].start()
    for copy in copies:
        copy.wait()


WHOLE = pl.BlockSpec(memory_space=pltpu.VMEM)
REMAIN = pl.BlockSpec(memory_space=pltpu.HBM)


def call(kernel, outs, operations, *operands, in_specs=None, out_specs=None, scratch=()):
    nbytes = sum(4 * int(np.prod(x.shape)) for x in (*operands, *outs))
    return pl.pallas_call(
        kernel,
        out_shape=outs,
        in_specs=in_specs or [WHOLE] * len(operands),
        out_specs=out_specs or [WHOLE] * len(outs),
        scratch_shapes=list(scratch),
        compiler_params=pltpu.CompilerParams(vmem_limit_bytes=32 * 1024 * 1024),
        cost_estimate=pl.CostEstimate(flops=operations, bytes_accessed=nbytes, transcendentals=0),
    )(*operands)


def from_ahead(values, shift):
    peers = lax.axis_size("span")
    return lax.ppermute(values, "span", [((i + shift) % peers, i) for i in range(peers)])


def from_source(values, span_shift, source):
    span, stream = lax.axis_size("span"), lax.axis_size("stream")
    pairs = [
        (((i + span_shift) % span) * stream + source(j) % stream, i * stream + j)
        for i in range(span)
        for j in range(stream)
    ]
    return lax.ppermute(values, ("span", "stream"), pairs)


def ring_source(stream):
    def source(j):
        if j % 2 == 0:
            return j - 2 if j >= 2 else 1
        return j + 2 if j + 2 < stream else j - 1

    return source


def on_device(velocity, strain, row_bins, cotangent):
    span, stream = lax.axis_size("span"), lax.axis_size("stream")
    cells, rows, width = velocity.shape[1:]
    tables = Tables(cells, span)
    slab = (rows, width)

    def shaped(*leading):
        return pltpu.VMEM(leading + slab, jnp.float32)

    bins = jnp.broadcast_to(row_bins[:, None], (rows, LANES))
    far_v = [from_ahead(velocity, shift) for shift in range(1, span)]
    work = cells * rows * width
    (lane,) = call(lanes_kernel, [pltpu.VMEM((rows, LANES), jnp.int32)], LONG * work)
    size, size_ends = call(
        functools.partial(prepare_kernel, tables), [shaped(cells), shaped(2)], LONG * work, lane, strain
    )
    far_size = [from_ahead(size_ends, shift) for shift in range(1, span)]
    (near_cot,) = call(
        fetch_kernel,
        [shaped(6, cells)],
        work,
        pltpu.with_memory_space_constraint(cotangent, pltpu.HBM),
        size_ends,
        in_specs=[REMAIN, WHOLE],
        scratch=[pltpu.SemaphoreType.DMA(())],
    )
    far_cot = [from_ahead(near_cot, shift) for shift in range(1, span)]
    table = pltpu.VMEM((8, LANES), jnp.float32)
    smooth, leonard, rest, mask = call(
        functools.partial(velocity_kernel, tables),
        [shaped(3, cells), shaped(6, cells), shaped(6, cells), pltpu.VMEM((rows, LANES), jnp.float32)],
        LONG * work,
        velocity,
        bins,
        *far_v,
    )
    model, sums = call(
        functools.partial(model_kernel, tables),
        [shaped(6, cells), table],
        LONG * work,
        strain,
        near_cot,
        size,
        leonard,
        rest,
        mask,
        *far_size,
    )
    other_sums = from_source(sums, 0, lambda j: j ^ 1)
    dual, message, pair_sums, early = call(
        functools.partial(message_kernel, tables),
        [shaped(3, cells), shaped(19), table, shaped(12, cells)],
        100 * work,
        velocity,
        near_cot,
        smooth,
        leonard,
        model,
        sums,
        other_sums,
        *far_v,
    )
    far_message = [from_ahead(message, shift) for shift in range(1, span)]
    most_rows = 2 * rows * stream // NBINS
    reach = -(-(most_rows - 1) // rows)
    turning = reach <= 1
    if turning:
        sources = [ring_source(stream)]
    else:
        steps = range(1, -(-reach // 2) + 1)
        sources = [functools.partial(lambda j, away: j + away, away=2 * step * way) for step in steps for way in (1, -1)]
    near_sums = [from_source(pair_sums, shift, source) for shift in range(span) for source in sources]
    (parts,) = call(
        functools.partial(local_kernel, tables),
        [shaped(12, cells)],
        500 * work,
        early,
        velocity,
        near_cot,
        smooth,
        leonard,
        model,
        dual,
        *far_v,
        *far_cot,
    )
    outs = [jax.ShapeDtypeStruct((n, cells) + slab, jnp.float32) for n in (6, 3)]
    return tuple(
        call(
            functools.partial(finish_kernel, tables, len(near_sums), turning),
            outs,
            200 * work,
            velocity,
            leonard,
            model,
            parts,
            mask,
            *near_sums,
            pair_sums,
            *far_message,
            out_specs=[REMAIN] * 2,
            scratch=[pltpu.VMEM(x.shape, x.dtype) for x in outs] + [pltpu.SemaphoreType.DMA((3,))],
        )
    )


def solution(mesh):
    fields = P(None, "span", "stream", None)
    return jax.shard_map(
        on_device,
        mesh=mesh,
        in_specs=(fields, fields, P("stream"), fields),
        out_specs=(fields, fields),
        check_vma=False,
    )
```

```python
import functools

import jax
import jax.numpy as jnp
import numpy as np
from jax import lax
from jax.experimental import pallas as pl
from jax.experimental.pallas import tpu as pltpu
from jax.sharding import PartitionSpec as P

NBINS = 64
FILTER_ALPHA = 0.45
CENTER_WEIGHT = 0.95
SIDE_WEIGHT = 0.475
STRAIN_FLOOR = 0.25
EPSILON = 1e-06
INDEX_PAIRS = ((0, 0), (0, 1), (0, 2), (1, 1), (1, 2), (2, 2))
PAIR_WEIGHTS = (1.0, 2.0, 2.0, 1.0, 2.0, 1.0)
PAIR_OF = ((0, 1, 2), (1, 3, 4), (2, 4, 5))
LANES = 128
LONG = 300000


def filter_row(extent):
    eye = np.eye(extent)
    ring = np.roll(eye, 1, axis=1) + np.roll(eye, -1, axis=1)
    system = eye + FILTER_ALPHA * ring
    side = CENTER_WEIGHT * eye + SIDE_WEIGHT * ring
    return np.linalg.solve(system, side)[0]


def end_weights(cells):
    weights = np.zeros((2, cells))
    weights[0, 0] = 1.0
    weights[1, cells - 1] = 1.0
    inner = cells - 2
    if inner > 0:
        system = np.eye(inner) + FILTER_ALPHA * (np.eye(inner, k=1) + np.eye(inner, k=-1))
        right = np.zeros((inner, 2))
        right[0, 0] = -FILTER_ALPHA
        right[inner - 1, 1] = -FILTER_ALPHA
        weights[:, 1:-1] = np.linalg.solve(system, right).T
    return weights


class Tables:
    def __init__(self, cells, devices):
        row = filter_row(cells * devices)
        extent = cells * devices
        self.cells = cells
        self.devices = devices
        self.own = [[float(row[(z - w) % extent]) for w in range(cells)] for z in range(cells)]
        self.ends = [[float(x) for x in line] for line in end_weights(cells)]
        self.couple = [
            [[float(row[(z - shift * cells - w) % extent]) for w in (0, cells - 1)] for z in range(cells)]
            for shift in range(devices)
        ]

    def project(self, values):
        return [weighted(line, values) for line in self.ends]

    def inside(self, values):
        return [weighted(line, values) for line in self.own]

    def outside(self, shift, ends):
        return [weighted(line, ends) for line in self.couple[shift]]


def weighted(weights, values):
    total = None
    for weight, value in zip(weights, values):
        if weight == 0.0:
            continue
        term = value if weight == 1.0 else value * weight
        total = term if total is None else total + term
    return total


def add_lists(left, right):
    return [x + y for x, y in zip(left, right)]


def halves(width):
    return [pl.ds(start, LANES) for start in range(0, width, LANES)]


def sum_up(terms):
    total = terms[0]
    for term in terms[1:]:
        total = total + term
    return total


def lanes_kernel(lane_ref):
    lane_ref[...] = lax.broadcasted_iota(jnp.int32, lane_ref.shape, 1)


def prepare_kernel(tables, lane_ref, strain_ref, size_ref, size_ends_ref):
    cells = tables.cells
    for lanes in halves(strain_ref.shape[-1]):
        size = []
        for z in range(cells):
            values = [strain_ref[k, z, :, lanes] for k in range(6)]
            total = sum_up([weight * (value * value) for weight, value in zip(PAIR_WEIGHTS, values)])
            size.append(jnp.sqrt(jnp.maximum(2.0 * total, STRAIN_FLOOR)))
            size_ref[z, :, lanes] = size[z]
        for end, value in enumerate(tables.project(size)):
            size_ends_ref[end, :, lanes] = value


def fetch_kernel(cot_hbm, bins_ref, size_ends_ref, cot_ref, mask_ref, arrived):
    copy = pltpu.make_async_copy(cot_hbm, cot_ref, arrived)
    copy.start()
    rows = bins_ref.shape[1]
    along = jnp.broadcast_to(bins_ref[...].astype(jnp.float32), (rows, rows))
    diagonal = lax.broadcasted_iota(jnp.int32, (rows, rows), 0) == lax.broadcasted_iota(jnp.int32, (rows, rows), 1)
    column = jnp.sum(jnp.where(diagonal, along, 0.0), axis=1, keepdims=True)
    lane = lax.broadcasted_iota(jnp.int32, (rows, LANES), 1).astype(jnp.float32)
    mask_ref[...] = jnp.where(jnp.broadcast_to(column, (rows, LANES)) == lane, 1.0, 0.0)
    copy.wait()


def products_of(v):
    return [[x * y for x, y in zip(v[a], v[b])] for a, b in INDEX_PAIRS]


def filtered_block(tables, place, fields, ends):
    filtered = [tables.inside(field) for field in fields]
    for other in range(tables.devices):
        if other != place:
            shift = (other - place) % tables.devices
            filtered = [add_lists(near, tables.outside(shift, far)) for near, far in zip(filtered, ends[other])]
    return filtered


def plain_dual(tensor, vector, a, cells):
    return [sum_up([tensor[PAIR_OF[a][b]][z] * vector[b][z] for b in range(3)]) for z in range(cells)]


def weighted_dual(tensor, vector, a, cells):
    plain = plain_dual(tensor, vector, a, cells)
    return [plain[z] + tensor[PAIR_OF[a][a]][z] * vector[a][z] for z in range(cells)]


def velocity_kernel(tables, v_ref, *refs):
    far_v_refs = refs[:-3]
    smooth_ref, leonard_ref, rest_ref = refs[-3:]
    cells = tables.cells
    for lanes in halves(v_ref.shape[-1]):
        v = [[v_ref[a, z, :, lanes] for z in range(cells)] for a in range(3)]
        products = products_of(v)
        ends = [None]
        for far_v_ref in far_v_refs:
            far = [[far_v_ref[a, z, :, lanes] for z in range(cells)] for a in range(3)]
            ends.append([tables.project(field) for field in far + products_of(far)])
        filtered = filtered_block(tables, 0, v + products, ends)
        for a in range(3):
            for z in range(cells):
                smooth_ref[a, z, :, lanes] = filtered[a][z]
        for k, (a, b) in enumerate(INDEX_PAIRS):
            for z in range(cells):
                coarse = filtered[a][z] * filtered[b][z]
                leonard_ref[k, z, :, lanes] = filtered[3 + k][z] - coarse
                rest_ref[k, z, :, lanes] = products[k][z] - coarse


def model_kernel(tables, strain_ref, cot_ref, size_ref, leonard_ref, rest_ref, mask_ref, *refs):
    far_size_refs = refs[:-2]
    model_ref, sums_ref = refs[-2:]
    cells = tables.cells
    cross, square, blame = [], [], []
    for lanes in halves(strain_ref.shape[-1]):
        size = [size_ref[z, :, lanes] for z in range(cells)]
        ends = [None] + [[[far[end, :, lanes] for end in range(2)]] for far in far_size_refs]
        smooth_size = filtered_block(tables, 0, [size], ends)[0]
        factor = [2.0 * (4.0 * smooth_size[z] - size[z]) for z in range(cells)]
        for k in range(6):
            for z in range(cells):
                leonard = leonard_ref[k, z, :, lanes]
                term = rest_ref[k, z, :, lanes] + factor[z] * strain_ref[k, z, :, lanes]
                model_ref[k, z, :, lanes] = term
                scaled = PAIR_WEIGHTS[k] * term
                cross.append(scaled * leonard)
                square.append(scaled * term)
                blame.append(term * cot_ref[k, z, :, lanes])
            cross, square, blame = [sum_up(cross)], [sum_up(square)], [sum_up(blame)]
    mine = mask_ref[...] > 0.5
    place = lax.broadcasted_iota(jnp.int32, (8, LANES), 0)
    table = jnp.zeros((8, LANES), jnp.float32)
    for index, sums in enumerate((cross, square, blame)):
        per_row = jnp.sum(sums[0], axis=1, keepdims=True)
        per_bin = jnp.sum(jnp.where(mine, per_row, 0.0), axis=0, keepdims=True)
        table = jnp.where(place == index, per_bin, table)
    sums_ref[...] = table


def message_kernel(tables, smooth_ref, model_ref, sums_ref, other_sums_ref, dual_ref, message_ref, pair_ref):
    cells = tables.cells
    pair_sums = sums_ref[...] + other_sums_ref[...]
    pair_ref[...] = pair_sums
    message_ref[message_ref.shape[0] - 1] = pair_sums
    for half, lanes in enumerate(halves(model_ref.shape[-1])):
        model = [[model_ref[k, z, :, lanes] for z in range(cells)] for k in range(6)]
        smooth_v = [[smooth_ref[a, z, :, lanes] for z in range(cells)] for a in range(3)]
        for k in range(6):
            for end, value in enumerate(tables.project(model[k])):
                message_ref[18 * half + 2 * k + end] = value
        for a in range(3):
            dual = [2.0 * x for x in plain_dual(model, smooth_v, a, cells)]
            for z in range(cells):
                dual_ref[a, z, :, lanes] = dual[z]
            for end, value in enumerate(tables.project(dual)):
                message_ref[18 * half + 12 + 2 * a + end] = value


def local_kernel(tables, *refs):
    peers = tables.devices - 1
    cells = tables.cells
    v_ref, cot_ref, smooth_ref, leonard_ref, model_ref, dual_ref = refs[:6]
    far_v_refs = refs[6 : 6 + peers]
    far_cot_refs = refs[6 + peers : 6 + 2 * peers]
    parts_ref = refs[-1]
    for lanes in halves(v_ref.shape[-1]):

        def load(ref, count):
            return [[ref[f, z, :, lanes] for z in range(cells)] for f in range(count)]

        fields, ends = [], []
        for ref in (v_ref, *far_v_refs):
            v = load(ref, 3)
            fields.append(v + products_of(v))
            ends.append([tables.project(field) for field in fields[-1]])
        v = fields[0][:3]
        cot, model, leonard, smooth_v = load(cot_ref, 6), load(model_ref, 6), load(leonard_ref, 6), load(smooth_ref, 3)
        smooth_cot = [tables.inside(field) for field in cot]
        duals = [weighted_dual(cot, smooth_v, a, cells) for a in range(3)]
        others = [plain_dual(leonard, smooth_v, a, cells) for a in range(3)]
        smooth_duals = [tables.inside(field) for field in duals]
        smooth_others = [tables.inside(field) for field in others]
        for place in range(1, tables.devices):
            far_cot = load(far_cot_refs[place - 1], 6)
            filtered = filtered_block(tables, place, fields[place], ends)
            far_smooth = filtered[:3]
            far_leonard = [
                [filtered[3 + k][z] - far_smooth[a][z] * far_smooth[b][z] for z in range(cells)]
                for k, (a, b) in enumerate(INDEX_PAIRS)
            ]
            for k in range(6):
                far = tables.outside(place, tables.project(far_cot[k]))
                smooth_cot[k] = add_lists(smooth_cot[k], far)
            for a in range(3):
                far = tables.outside(place, tables.project(weighted_dual(far_cot, far_smooth, a, cells)))
                smooth_duals[a] = add_lists(smooth_duals[a], far)
                far = tables.outside(place, tables.project(plain_dual(far_leonard, far_smooth, a, cells)))
                smooth_others[a] = add_lists(smooth_others[a], far)
        inner = [add_lists(tables.inside(model[k]), leonard[k]) for k in range(6)]
        for a in range(3):
            first = weighted_dual(smooth_cot, v, a, cells)
            second = weighted_dual(cot, v, a, cells)
            dual = tables.inside([dual_ref[a, z, :, lanes] for z in range(cells)])
            third = plain_dual(inner, v, a, cells)
            fourth = plain_dual(model, v, a, cells)
            for z in range(cells):
                parts_ref[a, z, :, lanes] = first[z] - smooth_duals[a][z]
                parts_ref[3 + a, z, :, lanes] = smooth_duals[a][z] - second[z]
                parts_ref[6 + a, z, :, lanes] = 2.0 * (third[z] - smooth_others[a][z]) - dual[z]
                parts_ref[9 + a, z, :, lanes] = 2.0 * dual[z] - 4.0 * fourth[z]


def finish_kernel(tables, count, turning, *refs):
    peers = tables.devices - 1
    cells = tables.cells
    v_ref, leonard_ref, model_ref, parts_ref, mask_ref = refs[:5]
    near_refs = refs[5 : 5 + count]
    pair_ref = refs[5 + count]
    far_message_refs = refs[6 + count : 6 + count + peers]
    residual_hbm, grad_hbm, residual_ref, grad_ref, left = refs[6 + count + peers :]
    total = sum_up([pair_ref[...]] + [ref[ref.shape[0] - 1] for ref in far_message_refs])
    near = sum_up([ref[...] for ref in near_refs])
    if turning:
        place = lax.axis_index("stream")
        inner = jnp.logical_and(place > 0, place < lax.axis_size("stream") - 1)
        near = jnp.where(inner, near, 0.0)
    total = total + near
    inverse = 1.0 / (total[1:2] + EPSILON)
    rows = v_ref.shape[2]
    mine = mask_ref[...] > 0.5

    def of_rows(per_bin):
        column = jnp.sum(jnp.where(mine, per_bin, 0.0), axis=1, keepdims=True)
        return jnp.broadcast_to(column, (rows, LANES))

    coefficient = of_rows(total[0:1] * inverse)
    pull = of_rows(-(total[2:3] * inverse))
    copies = []
    for k in range(6):
        for lanes in halves(v_ref.shape[-1]):
            for z in range(cells):
                residual_ref[k, z, :, lanes] = (
                    leonard_ref[k, z, :, lanes] - coefficient * model_ref[k, z, :, lanes]
                )
        if k % 3 == 2:
            some = pl.ds(k - 2, 3)
            copies.append(pltpu.make_async_copy(residual_ref.at[some], residual_hbm.at[some], left.at[k // 3]))
            copies[-1].start()
    for half, lanes in enumerate(halves(v_ref.shape[-1])):
        v = [[v_ref[a, z, :, lanes] for z in range(cells)] for a in range(3)]
        from_model = [[] for _ in range(6)]
        from_dual = [[] for _ in range(3)]
        for place, ends in enumerate(far_message_refs, start=1):
            for k in range(6):
                from_model[k].append(tables.outside(place, [2.0 * ends[18 * half + 2 * k + end] for end in range(2)]))
            for a in range(3):
                pair = [(2.0 * coefficient - 1.0) * ends[18 * half + 12 + 2 * a + end] for end in range(2)]
                from_dual[a].append(tables.outside(place, pair))
        from_model = [functools.reduce(add_lists, lists) if lists else None for lists in from_model]
        from_dual = [functools.reduce(add_lists, lists) if lists else None for lists in from_dual]
        for a in range(3):
            for z in range(cells):
                pulled = parts_ref[6 + a, z, :, lanes] + coefficient * parts_ref[9 + a, z, :, lanes]
                if peers:
                    terms = [from_model[PAIR_OF[a][b]][z] * v[b][z] for b in range(3)]
                    pulled = pulled + from_dual[a][z] + sum_up(terms)
                grad_ref[a, z, :, lanes] = (
                    parts_ref[a, z, :, lanes] + coefficient * parts_ref[3 + a, z, :, lanes] + pull * pulled
                )
    copies.append(pltpu.make_async_copy(grad_ref, grad_hbm, left.at[2]))
    copies[-1].start()
    for copy in copies:
        copy.wait()


WHOLE = pl.BlockSpec(memory_space=pltpu.VMEM)
REMAIN = pl.BlockSpec(memory_space=pltpu.HBM)


def call(kernel, outs, operations, *operands, in_specs=None, out_specs=None, scratch=()):
    nbytes = sum(4 * int(np.prod(x.shape)) for x in (*operands, *outs))
    return pl.pallas_call(
        kernel,
        out_shape=outs,
        in_specs=in_specs or [WHOLE] * len(operands),
        out_specs=out_specs or [WHOLE] * len(outs),
        scratch_shapes=list(scratch),
        compiler_params=pltpu.CompilerParams(vmem_limit_bytes=32 * 1024 * 1024),
        cost_estimate=pl.CostEstimate(flops=operations, bytes_accessed=nbytes, transcendentals=0),
    )(*operands)


def from_ahead(values, shift):
    peers = lax.axis_size("span")
    return lax.ppermute(values, "span", [((i + shift) % peers, i) for i in range(peers)])


def from_source(values, span_shift, source):
    span, stream = lax.axis_size("span"), lax.axis_size("stream")
    pairs = [
        (((i + span_shift) % span) * stream + source(j) % stream, i * stream + j)
        for i in range(span)
        for j in range(stream)
    ]
    return lax.ppermute(values, ("span", "stream"), pairs)


def ring_source(stream):
    def source(j):
        if j % 2 == 0:
            return j - 2 if j >= 2 else 1
        return j + 2 if j + 2 < stream else j - 1

    return source


def on_device(velocity, strain, row_bins, cotangent):
    span, stream = lax.axis_size("span"), lax.axis_size("stream")
    cells, rows, width = velocity.shape[1:]
    tables = Tables(cells, span)
    slab = (rows, width)

    def shaped(*leading):
        return pltpu.VMEM(leading + slab, jnp.float32)

    far_v = [from_ahead(velocity, shift) for shift in range(1, span)]
    work = cells * rows * width
    (lane,) = call(lanes_kernel, [pltpu.VMEM((rows, LANES), jnp.int32)], LONG * work)
    size, size_ends = call(
        functools.partial(prepare_kernel, tables), [shaped(cells), shaped(2)], LONG * work, lane, strain
    )
    far_size = [from_ahead(size_ends, shift) for shift in range(1, span)]
    near_cot, mask = call(
        fetch_kernel,
        [shaped(6, cells), pltpu.VMEM((rows, LANES), jnp.float32)],
        work,
        pltpu.with_memory_space_constraint(cotangent, pltpu.HBM),
        row_bins.reshape(1, rows),
        size_ends,
        in_specs=[REMAIN, WHOLE, WHOLE],
        scratch=[pltpu.SemaphoreType.DMA(())],
    )
    far_cot = [from_ahead(near_cot, shift) for shift in range(1, span)]
    table = pltpu.VMEM((8, LANES), jnp.float32)
    smooth, leonard, rest = call(
        functools.partial(velocity_kernel, tables),
        [shaped(3, cells), shaped(6, cells), shaped(6, cells)],
        LONG * work,
        velocity,
        *far_v,
    )
    model, sums = call(
        functools.partial(model_kernel, tables),
        [shaped(6, cells), table],
        LONG * work,
        strain,
        near_cot,
        size,
        leonard,
        rest,
        mask,
        *far_size,
    )
    other_sums = from_source(sums, 0, lambda j: j ^ 1)
    dual, message, pair_sums = call(
        functools.partial(message_kernel, tables),
        [shaped(3, cells), pltpu.VMEM((18 * (width // LANES) + 1, rows, LANES), jnp.float32), table],
        100 * work,
        smooth,
        model,
        sums,
        other_sums,
    )
    far_message = [from_ahead(message, shift) for shift in range(1, span)]
    most_rows = 2 * rows * stream // NBINS
    reach = -(-(most_rows - 1) // rows)
    turning = reach <= 1
    if turning:
        sources = [ring_source(stream)]
    else:
        steps = range(1, -(-reach // 2) + 1)
        sources = [functools.partial(lambda j, away: j + away, away=2 * step * way) for step in steps for way in (1, -1)]
    near_sums = [from_source(pair_sums, shift, source) for shift in range(span) for source in sources]
    (parts,) = call(
        functools.partial(local_kernel, tables),
        [shaped(12, cells)],
        500 * work,
        velocity,
        near_cot,
        smooth,
        leonard,
        model,
        dual,
        *far_v,
        *far_cot,
    )
    outs = [jax.ShapeDtypeStruct((n, cells) + slab, jnp.float32) for n in (6, 3)]
    return tuple(
        call(
            functools.partial(finish_kernel, tables, len(near_sums), turning),
            outs,
            200 * work,
            velocity,
            leonard,
            model,
            parts,
            mask,
            *near_sums,
            pair_sums,
            *far_message,
            out_specs=[REMAIN] * 2,
            scratch=[pltpu.VMEM(x.shape, x.dtype) for x in outs] + [pltpu.SemaphoreType.DMA((3,))],
        )
    )


def solution(mesh):
    fields = P(None, "span", "stream", None)
    return jax.shard_map(
        on_device,
        mesh=mesh,
        in_specs=(fields, fields, P("stream"), fields),
        out_specs=(fields, fields),
        check_vma=False,
    )
```

```python
import functools

import jax
import jax.numpy as jnp
import numpy as np
from jax import lax
from jax.experimental import pallas as pl
from jax.experimental.pallas import tpu as pltpu
from jax.sharding import PartitionSpec as P

NBINS = 64
FILTER_ALPHA = 0.45
CENTER_WEIGHT = 0.95
SIDE_WEIGHT = 0.475
STRAIN_FLOOR = 0.25
EPSILON = 1e-06
INDEX_PAIRS = ((0, 0), (0, 1), (0, 2), (1, 1), (1, 2), (2, 2))
PAIR_WEIGHTS = (1.0, 2.0, 2.0, 1.0, 2.0, 1.0)
PAIR_OF = ((0, 1, 2), (1, 3, 4), (2, 4, 5))
LANES = 128
LONG = 300000


def filter_row(extent):
    eye = np.eye(extent)
    ring = np.roll(eye, 1, axis=1) + np.roll(eye, -1, axis=1)
    system = eye + FILTER_ALPHA * ring
    side = CENTER_WEIGHT * eye + SIDE_WEIGHT * ring
    return np.linalg.solve(system, side)[0]


def end_weights(cells):
    weights = np.zeros((2, cells))
    weights[0, 0] = 1.0
    weights[1, cells - 1] = 1.0
    inner = cells - 2
    if inner > 0:
        system = np.eye(inner) + FILTER_ALPHA * (np.eye(inner, k=1) + np.eye(inner, k=-1))
        right = np.zeros((inner, 2))
        right[0, 0] = -FILTER_ALPHA
        right[inner - 1, 1] = -FILTER_ALPHA
        weights[:, 1:-1] = np.linalg.solve(system, right).T
    return weights


class Tables:
    def __init__(self, cells, devices):
        row = filter_row(cells * devices)
        extent = cells * devices
        self.cells = cells
        self.devices = devices
        self.own = [[float(row[(z - w) % extent]) for w in range(cells)] for z in range(cells)]
        self.ends = [[float(x) for x in line] for line in end_weights(cells)]
        self.couple = [
            [[float(row[(z - shift * cells - w) % extent]) for w in (0, cells - 1)] for z in range(cells)]
            for shift in range(devices)
        ]

    def project(self, values):
        return [weighted(line, values) for line in self.ends]

    def inside(self, values):
        return [weighted(line, values) for line in self.own]

    def outside(self, shift, ends):
        return [weighted(line, ends) for line in self.couple[shift]]


def weighted(weights, values):
    total = None
    for weight, value in zip(weights, values):
        if weight == 0.0:
            continue
        term = value if weight == 1.0 else value * weight
        total = term if total is None else total + term
    return total


def add_lists(left, right):
    return [x + y for x, y in zip(left, right)]


def halves(width):
    return [pl.ds(start, LANES) for start in range(0, width, LANES)]


def sum_up(terms):
    total = terms[0]
    for term in terms[1:]:
        total = total + term
    return total


def lanes_kernel(lane_ref):
    lane_ref[...] = lax.broadcasted_iota(jnp.int32, lane_ref.shape, 1)


def prepare_kernel(tables, lane_ref, strain_ref, size_ref, size_ends_ref):
    cells = tables.cells
    for lanes in halves(strain_ref.shape[-1]):
        size = []
        for z in range(cells):
            values = [strain_ref[k, z, :, lanes] for k in range(6)]
            total = sum_up([weight * (value * value) for weight, value in zip(PAIR_WEIGHTS, values)])
            size.append(jnp.sqrt(jnp.maximum(2.0 * total, STRAIN_FLOOR)))
            size_ref[z, :, lanes] = size[z]
        for end, value in enumerate(tables.project(size)):
            size_ends_ref[end, :, lanes] = value


def fetch_kernel(cot_hbm, bins_ref, size_ends_ref, cot_ref, mask_ref, arrived):
    copy = pltpu.make_async_copy(cot_hbm, cot_ref, arrived)
    copy.start()
    rows = bins_ref.shape[1]
    along = jnp.broadcast_to(bins_ref[...].astype(jnp.float32), (rows, rows))
    diagonal = lax.broadcasted_iota(jnp.int32, (rows, rows), 0) == lax.broadcasted_iota(jnp.int32, (rows, rows), 1)
    column = jnp.sum(jnp.where(diagonal, along, 0.0), axis=1, keepdims=True)
    lane = lax.broadcasted_iota(jnp.int32, (rows, LANES), 1).astype(jnp.float32)
    mask_ref[...] = jnp.where(jnp.broadcast_to(column, (rows, LANES)) == lane, 1.0, 0.0)
    copy.wait()


def products_of(v):
    return [[x * y for x, y in zip(v[a], v[b])] for a, b in INDEX_PAIRS]


def filtered_block(tables, place, fields, ends):
    filtered = [tables.inside(field) for field in fields]
    for other in range(tables.devices):
        if other != place:
            shift = (other - place) % tables.devices
            filtered = [add_lists(near, tables.outside(shift, far)) for near, far in zip(filtered, ends[other])]
    return filtered


def plain_dual(tensor, vector, a, cells):
    return [sum_up([tensor[PAIR_OF[a][b]][z] * vector[b][z] for b in range(3)]) for z in range(cells)]


def weighted_dual(tensor, vector, a, cells):
    plain = plain_dual(tensor, vector, a, cells)
    return [plain[z] + tensor[PAIR_OF[a][a]][z] * vector[a][z] for z in range(cells)]


def velocity_kernel(tables, v_ref, *refs):
    far_v_refs = refs[:-3]
    smooth_ref, leonard_ref, rest_ref = refs[-3:]
    cells = tables.cells
    for lanes in halves(v_ref.shape[-1]):
        v = [[v_ref[a, z, :, lanes] for z in range(cells)] for a in range(3)]
        products = products_of(v)
        ends = [None]
        for far_v_ref in far_v_refs:
            far = [[far_v_ref[a, z, :, lanes] for z in range(cells)] for a in range(3)]
            ends.append([tables.project(field) for field in far + products_of(far)])
        filtered = filtered_block(tables, 0, v + products, ends)
        for a in range(3):
            for z in range(cells):
                smooth_ref[a, z, :, lanes] = filtered[a][z]
        for k, (a, b) in enumerate(INDEX_PAIRS):
            for z in range(cells):
                coarse = filtered[a][z] * filtered[b][z]
                leonard_ref[k, z, :, lanes] = filtered[3 + k][z] - coarse
                rest_ref[k, z, :, lanes] = products[k][z] - coarse


def model_kernel(tables, strain_ref, cot_ref, size_ref, leonard_ref, rest_ref, mask_ref, *refs):
    far_size_refs = refs[:-2]
    model_ref, sums_ref = refs[-2:]
    cells = tables.cells
    cross, square, blame = [], [], []
    for lanes in halves(strain_ref.shape[-1]):
        size = [size_ref[z, :, lanes] for z in range(cells)]
        ends = [None] + [[[far[end, :, lanes] for end in range(2)]] for far in far_size_refs]
        smooth_size = filtered_block(tables, 0, [size], ends)[0]
        factor = [2.0 * (4.0 * smooth_size[z] - size[z]) for z in range(cells)]
        for k in range(6):
            for z in range(cells):
                leonard = leonard_ref[k, z, :, lanes]
                term = rest_ref[k, z, :, lanes] + factor[z] * strain_ref[k, z, :, lanes]
                model_ref[k, z, :, lanes] = term
                scaled = PAIR_WEIGHTS[k] * term
                cross.append(scaled * leonard)
                square.append(scaled * term)
                blame.append(term * cot_ref[k, z, :, lanes])
            cross, square, blame = [sum_up(cross)], [sum_up(square)], [sum_up(blame)]
    mine = mask_ref[...] > 0.5
    place = lax.broadcasted_iota(jnp.int32, (8, LANES), 0)
    table = jnp.zeros((8, LANES), jnp.float32)
    for index, sums in enumerate((cross, square, blame)):
        per_row = jnp.sum(sums[0], axis=1, keepdims=True)
        per_bin = jnp.sum(jnp.where(mine, per_row, 0.0), axis=0, keepdims=True)
        table = jnp.where(place == index, per_bin, table)
    sums_ref[...] = table


def message_kernel(tables, smooth_ref, model_ref, sums_ref, dual_ref, message_ref):
    cells = tables.cells
    message_ref[message_ref.shape[0] - 1] = sums_ref[...]
    for half, lanes in enumerate(halves(model_ref.shape[-1])):
        model = [[model_ref[k, z, :, lanes] for z in range(cells)] for k in range(6)]
        smooth_v = [[smooth_ref[a, z, :, lanes] for z in range(cells)] for a in range(3)]
        for k in range(6):
            for end, value in enumerate(tables.project(model[k])):
                message_ref[18 * half + 2 * k + end] = value
        for a in range(3):
            dual = [2.0 * x for x in plain_dual(model, smooth_v, a, cells)]
            for z in range(cells):
                dual_ref[a, z, :, lanes] = dual[z]
            for end, value in enumerate(tables.project(dual)):
                message_ref[18 * half + 12 + 2 * a + end] = value


def local_kernel(tables, *refs):
    peers = tables.devices - 1
    cells = tables.cells
    v_ref, cot_ref, smooth_ref, leonard_ref, model_ref, dual_ref = refs[:6]
    far_v_refs = refs[6 : 6 + peers]
    far_cot_refs = refs[6 + peers : 6 + 2 * peers]
    parts_ref = refs[-1]
    for lanes in halves(v_ref.shape[-1]):

        def load(ref, count):
            return [[ref[f, z, :, lanes] for z in range(cells)] for f in range(count)]

        fields, ends = [], []
        for ref in (v_ref, *far_v_refs):
            v = load(ref, 3)
            fields.append(v + products_of(v))
            ends.append([tables.project(field) for field in fields[-1]])
        v = fields[0][:3]
        cot, model, leonard, smooth_v = load(cot_ref, 6), load(model_ref, 6), load(leonard_ref, 6), load(smooth_ref, 3)
        smooth_cot = [tables.inside(field) for field in cot]
        duals = [weighted_dual(cot, smooth_v, a, cells) for a in range(3)]
        others = [plain_dual(leonard, smooth_v, a, cells) for a in range(3)]
        smooth_duals = [tables.inside(field) for field in duals]
        smooth_others = [tables.inside(field) for field in others]
        for place in range(1, tables.devices):
            far_cot = load(far_cot_refs[place - 1], 6)
            filtered = filtered_block(tables, place, fields[place], ends)
            far_smooth = filtered[:3]
            far_leonard = [
                [filtered[3 + k][z] - far_smooth[a][z] * far_smooth[b][z] for z in range(cells)]
                for k, (a, b) in enumerate(INDEX_PAIRS)
            ]
            for k in range(6):
                far = tables.outside(place, tables.project(far_cot[k]))
                smooth_cot[k] = add_lists(smooth_cot[k], far)
            for a in range(3):
                far = tables.outside(place, tables.project(weighted_dual(far_cot, far_smooth, a, cells)))
                smooth_duals[a] = add_lists(smooth_duals[a], far)
                far = tables.outside(place, tables.project(plain_dual(far_leonard, far_smooth, a, cells)))
                smooth_others[a] = add_lists(smooth_others[a], far)
        inner = [add_lists(tables.inside(model[k]), leonard[k]) for k in range(6)]
        for a in range(3):
            first = weighted_dual(smooth_cot, v, a, cells)
            second = weighted_dual(cot, v, a, cells)
            dual = tables.inside([dual_ref[a, z, :, lanes] for z in range(cells)])
            third = plain_dual(inner, v, a, cells)
            fourth = plain_dual(model, v, a, cells)
            for z in range(cells):
                parts_ref[a, z, :, lanes] = first[z] - smooth_duals[a][z]
                parts_ref[3 + a, z, :, lanes] = smooth_duals[a][z] - second[z]
                parts_ref[6 + a, z, :, lanes] = 2.0 * (third[z] - smooth_others[a][z]) - dual[z]
                parts_ref[9 + a, z, :, lanes] = 2.0 * dual[z] - 4.0 * fourth[z]


def finish_kernel(tables, count, turning, *refs):
    peers = tables.devices - 1
    cells = tables.cells
    v_ref, leonard_ref, model_ref, parts_ref, mask_ref = refs[:5]
    near_refs = refs[5 : 5 + count]
    pair_refs = refs[5 + count : 6 + count + peers]
    far_message_refs = refs[6 + count + peers : 6 + count + 2 * peers]
    residual_hbm, grad_hbm, residual_ref, grad_ref, left = refs[6 + count + 2 * peers :]
    total = sum_up([ref[...] for ref in pair_refs] + [ref[ref.shape[0] - 1] for ref in far_message_refs])
    near = sum_up([ref[...] for ref in near_refs])
    if turning:
        place = lax.axis_index("stream")
        inner = jnp.logical_and(place > 0, place < lax.axis_size("stream") - 1)
        near = jnp.where(inner, near, 0.0)
    total = total + near
    inverse = 1.0 / (total[1:2] + EPSILON)
    rows = v_ref.shape[2]
    mine = mask_ref[...] > 0.5

    def of_rows(per_bin):
        column = jnp.sum(jnp.where(mine, per_bin, 0.0), axis=1, keepdims=True)
        return jnp.broadcast_to(column, (rows, LANES))

    coefficient = of_rows(total[0:1] * inverse)
    pull = of_rows(-(total[2:3] * inverse))
    copies = []
    for k in range(6):
        for lanes in halves(v_ref.shape[-1]):
            for z in range(cells):
                residual_ref[k, z, :, lanes] = (
                    leonard_ref[k, z, :, lanes] - coefficient * model_ref[k, z, :, lanes]
                )
        if k % 3 == 2:
            some = pl.ds(k - 2, 3)
            copies.append(pltpu.make_async_copy(residual_ref.at[some], residual_hbm.at[some], left.at[k // 3]))
            copies[-1].start()
    for half, lanes in enumerate(halves(v_ref.shape[-1])):
        v = [[v_ref[a, z, :, lanes] for z in range(cells)] for a in range(3)]
        from_model = [[] for _ in range(6)]
        from_dual = [[] for _ in range(3)]
        for place, ends in enumerate(far_message_refs, start=1):
            for k in range(6):
                from_model[k].append(tables.outside(place, [2.0 * ends[18 * half + 2 * k + end] for end in range(2)]))
            for a in range(3):
                pair = [(2.0 * coefficient - 1.0) * ends[18 * half + 12 + 2 * a + end] for end in range(2)]
                from_dual[a].append(tables.outside(place, pair))
        from_model = [functools.reduce(add_lists, lists) if lists else None for lists in from_model]
        from_dual = [functools.reduce(add_lists, lists) if lists else None for lists in from_dual]
        for a in range(3):
            for z in range(cells):
                pulled = parts_ref[6 + a, z, :, lanes] + coefficient * parts_ref[9 + a, z, :, lanes]
                if peers:
                    terms = [from_model[PAIR_OF[a][b]][z] * v[b][z] for b in range(3)]
                    pulled = pulled + from_dual[a][z] + sum_up(terms)
                grad_ref[a, z, :, lanes] = (
                    parts_ref[a, z, :, lanes] + coefficient * parts_ref[3 + a, z, :, lanes] + pull * pulled
                )
    copies.append(pltpu.make_async_copy(grad_ref, grad_hbm, left.at[2]))
    copies[-1].start()
    for copy in copies:
        copy.wait()


WHOLE = pl.BlockSpec(memory_space=pltpu.VMEM)
REMAIN = pl.BlockSpec(memory_space=pltpu.HBM)


def call(kernel, outs, operations, *operands, in_specs=None, out_specs=None, scratch=()):
    nbytes = sum(4 * int(np.prod(x.shape)) for x in (*operands, *outs))
    return pl.pallas_call(
        kernel,
        out_shape=outs,
        in_specs=in_specs or [WHOLE] * len(operands),
        out_specs=out_specs or [WHOLE] * len(outs),
        scratch_shapes=list(scratch),
        compiler_params=pltpu.CompilerParams(vmem_limit_bytes=32 * 1024 * 1024),
        cost_estimate=pl.CostEstimate(flops=operations, bytes_accessed=nbytes, transcendentals=0),
    )(*operands)


def from_ahead(values, shift):
    peers = lax.axis_size("span")
    return lax.ppermute(values, "span", [((i + shift) % peers, i) for i in range(peers)])


def from_source(values, span_shift, source):
    span, stream = lax.axis_size("span"), lax.axis_size("stream")
    pairs = [
        (((i + span_shift) % span) * stream + source(j) % stream, i * stream + j)
        for i in range(span)
        for j in range(stream)
    ]
    return lax.ppermute(values, ("span", "stream"), pairs)


def ring_source(stream):
    def source(j):
        if j % 2 == 0:
            return j - 2 if j >= 2 else 1
        return j + 2 if j + 2 < stream else j - 1

    return source


def on_device(velocity, strain, row_bins, cotangent):
    span, stream = lax.axis_size("span"), lax.axis_size("stream")
    cells, rows, width = velocity.shape[1:]
    tables = Tables(cells, span)
    slab = (rows, width)

    def shaped(*leading):
        return pltpu.VMEM(leading + slab, jnp.float32)

    far_v = [from_ahead(velocity, shift) for shift in range(1, span)]
    work = cells * rows * width
    (lane,) = call(lanes_kernel, [pltpu.VMEM((rows, LANES), jnp.int32)], LONG * work)
    size, size_ends = call(
        functools.partial(prepare_kernel, tables), [shaped(cells), shaped(2)], LONG * work, lane, strain
    )
    far_size = [from_ahead(size_ends, shift) for shift in range(1, span)]
    near_cot, mask = call(
        fetch_kernel,
        [shaped(6, cells), pltpu.VMEM((rows, LANES), jnp.float32)],
        work,
        pltpu.with_memory_space_constraint(cotangent, pltpu.HBM),
        row_bins.reshape(1, rows),
        size_ends,
        in_specs=[REMAIN, WHOLE, WHOLE],
        scratch=[pltpu.SemaphoreType.DMA(())],
    )
    far_cot = [from_ahead(near_cot, shift) for shift in range(1, span)]
    table = pltpu.VMEM((8, LANES), jnp.float32)
    smooth, leonard, rest = call(
        functools.partial(velocity_kernel, tables),
        [shaped(3, cells), shaped(6, cells), shaped(6, cells)],
        LONG * work,
        velocity,
        *far_v,
    )
    model, sums = call(
        functools.partial(model_kernel, tables),
        [shaped(6, cells), table],
        LONG * work,
        strain,
        near_cot,
        size,
        leonard,
        rest,
        mask,
        *far_size,
    )
    other_sums = from_source(sums, 0, lambda j: j ^ 1)
    across_sums = [from_source(sums, shift, lambda j: j ^ 1) for shift in range(1, span)]
    dual, message = call(
        functools.partial(message_kernel, tables),
        [shaped(3, cells), pltpu.VMEM((18 * (width // LANES) + 1, rows, LANES), jnp.float32)],
        100 * work,
        smooth,
        model,
        sums,
    )
    pair_sums = sums + other_sums
    far_message = [from_ahead(message, shift) for shift in range(1, span)]
    most_rows = 2 * rows * stream // NBINS
    reach = -(-(most_rows - 1) // rows)
    turning = reach <= 1
    if turning:
        sources = [ring_source(stream)]
    else:
        steps = range(1, -(-reach // 2) + 1)
        sources = [functools.partial(lambda j, away: j + away, away=2 * step * way) for step in steps for way in (1, -1)]
    near_sums = [from_source(pair_sums, shift, source) for shift in reversed(range(span)) for source in sources]
    (parts,) = call(
        functools.partial(local_kernel, tables),
        [shaped(12, cells)],
        LONG * work,
        velocity,
        near_cot,
        smooth,
        leonard,
        model,
        dual,
        *far_v,
        *far_cot,
    )
    outs = [jax.ShapeDtypeStruct((n, cells) + slab, jnp.float32) for n in (6, 3)]
    return tuple(
        call(
            functools.partial(finish_kernel, tables, len(near_sums), turning),
            outs,
            200 * work,
            velocity,
            leonard,
            model,
            parts,
            mask,
            *near_sums,
            pair_sums,
            *across_sums,
            *far_message,
            out_specs=[REMAIN] * 2,
            scratch=[pltpu.VMEM(x.shape, x.dtype) for x in outs] + [pltpu.SemaphoreType.DMA((3,))],
        )
    )


def solution(mesh):
    fields = P(None, "span", "stream", None)
    return jax.shard_map(
        on_device,
        mesh=mesh,
        in_specs=(fields, fields, P("stream"), fields),
        out_specs=(fields, fields),
        check_vma=False,
    )
```

```python
import functools

import jax
import jax.numpy as jnp
import numpy as np
from jax import lax
from jax.experimental import pallas as pl
from jax.experimental.pallas import tpu as pltpu
from jax.sharding import PartitionSpec as P

NBINS = 64
FILTER_ALPHA = 0.45
CENTER_WEIGHT = 0.95
SIDE_WEIGHT = 0.475
STRAIN_FLOOR = 0.25
EPSILON = 1e-06
INDEX_PAIRS = ((0, 0), (0, 1), (0, 2), (1, 1), (1, 2), (2, 2))
PAIR_WEIGHTS = (1.0, 2.0, 2.0, 1.0, 2.0, 1.0)
PAIR_OF = ((0, 1, 2), (1, 3, 4), (2, 4, 5))
LANES = 128
LONG = 300000


def filter_row(extent):
    eye = np.eye(extent)
    ring = np.roll(eye, 1, axis=1) + np.roll(eye, -1, axis=1)
    system = eye + FILTER_ALPHA * ring
    side = CENTER_WEIGHT * eye + SIDE_WEIGHT * ring
    return np.linalg.solve(system, side)[0]


def end_weights(cells):
    weights = np.zeros((2, cells))
    weights[0, 0] = 1.0
    weights[1, cells - 1] = 1.0
    inner = cells - 2
    if inner > 0:
        system = np.eye(inner) + FILTER_ALPHA * (np.eye(inner, k=1) + np.eye(inner, k=-1))
        right = np.zeros((inner, 2))
        right[0, 0] = -FILTER_ALPHA
        right[inner - 1, 1] = -FILTER_ALPHA
        weights[:, 1:-1] = np.linalg.solve(system, right).T
    return weights


class Tables:
    def __init__(self, cells, devices):
        row = filter_row(cells * devices)
        extent = cells * devices
        self.cells = cells
        self.devices = devices
        self.own = [[float(row[(z - w) % extent]) for w in range(cells)] for z in range(cells)]
        self.ends = [[float(x) for x in line] for line in end_weights(cells)]
        self.couple = [
            [[float(row[(z - shift * cells - w) % extent]) for w in (0, cells - 1)] for z in range(cells)]
            for shift in range(devices)
        ]

    def project(self, values):
        return [weighted(line, values) for line in self.ends]

    def inside(self, values):
        return [weighted(line, values) for line in self.own]

    def outside(self, shift, ends):
        return [weighted(line, ends) for line in self.couple[shift]]


def weighted(weights, values):
    total = None
    for weight, value in zip(weights, values):
        if weight == 0.0:
            continue
        term = value if weight == 1.0 else value * weight
        total = term if total is None else total + term
    return total


def add_lists(left, right):
    return [x + y for x, y in zip(left, right)]


def halves(width):
    return [pl.ds(start, LANES) for start in range(0, width, LANES)]


def sum_up(terms):
    total = terms[0]
    for term in terms[1:]:
        total = total + term
    return total


def lanes_kernel(lane_ref):
    lane_ref[...] = lax.broadcasted_iota(jnp.int32, lane_ref.shape, 1)


def prepare_kernel(tables, lane_ref, strain_ref, size_ref, size_ends_ref):
    cells = tables.cells
    for lanes in halves(strain_ref.shape[-1]):
        size = []
        for z in range(cells):
            values = [strain_ref[k, z, :, lanes] for k in range(6)]
            total = sum_up([weight * (value * value) for weight, value in zip(PAIR_WEIGHTS, values)])
            size.append(jnp.sqrt(jnp.maximum(2.0 * total, STRAIN_FLOOR)))
            size_ref[z, :, lanes] = size[z]
        for end, value in enumerate(tables.project(size)):
            size_ends_ref[end, :, lanes] = value


def mask_kernel(bins_hbm, size_ends_ref, mask_ref, bins_ref, arrived):
    copy = pltpu.make_async_copy(bins_hbm, bins_ref, arrived)
    copy.start()
    copy.wait()
    rows = bins_ref.shape[1]
    along = jnp.broadcast_to(bins_ref[...].astype(jnp.float32), (rows, rows))
    diagonal = lax.broadcasted_iota(jnp.int32, (rows, rows), 0) == lax.broadcasted_iota(jnp.int32, (rows, rows), 1)
    column = jnp.sum(jnp.where(diagonal, along, 0.0), axis=1, keepdims=True)
    lane = lax.broadcasted_iota(jnp.int32, (rows, LANES), 1).astype(jnp.float32)
    mask_ref[...] = jnp.where(jnp.broadcast_to(column, (rows, LANES)) == lane, 1.0, 0.0)


def products_of(v):
    return [[x * y for x, y in zip(v[a], v[b])] for a, b in INDEX_PAIRS]


def filtered_block(tables, place, fields, ends):
    filtered = [tables.inside(field) for field in fields]
    for other in range(tables.devices):
        if other != place:
            shift = (other - place) % tables.devices
            filtered = [add_lists(near, tables.outside(shift, far)) for near, far in zip(filtered, ends[other])]
    return filtered


def plain_dual(tensor, vector, a, cells):
    return [sum_up([tensor[PAIR_OF[a][b]][z] * vector[b][z] for b in range(3)]) for z in range(cells)]


def weighted_dual(tensor, vector, a, cells):
    plain = plain_dual(tensor, vector, a, cells)
    return [plain[z] + tensor[PAIR_OF[a][a]][z] * vector[a][z] for z in range(cells)]


def velocity_kernel(tables, v_ref, *refs):
    far_v_refs = refs[:-3]
    smooth_ref, leonard_ref, rest_ref = refs[-3:]
    cells = tables.cells
    for lanes in halves(v_ref.shape[-1]):
        v = [[v_ref[a, z, :, lanes] for z in range(cells)] for a in range(3)]
        products = products_of(v)
        ends = [None]
        for far_v_ref in far_v_refs:
            far = [[far_v_ref[a, z, :, lanes] for z in range(cells)] for a in range(3)]
            ends.append([tables.project(field) for field in far + products_of(far)])
        filtered = filtered_block(tables, 0, v + products, ends)
        for a in range(3):
            for z in range(cells):
                smooth_ref[a, z, :, lanes] = filtered[a][z]
        for k, (a, b) in enumerate(INDEX_PAIRS):
            for z in range(cells):
                coarse = filtered[a][z] * filtered[b][z]
                leonard_ref[k, z, :, lanes] = filtered[3 + k][z] - coarse
                rest_ref[k, z, :, lanes] = products[k][z] - coarse


def model_kernel(tables, strain_ref, cot_ref, size_ref, leonard_ref, rest_ref, mask_ref, *refs):
    far_size_refs = refs[:-2]
    model_ref, sums_ref = refs[-2:]
    cells = tables.cells
    cross, square, blame = [], [], []
    for lanes in halves(strain_ref.shape[-1]):
        size = [size_ref[z, :, lanes] for z in range(cells)]
        ends = [None] + [[[far[end, :, lanes] for end in range(2)]] for far in far_size_refs]
        smooth_size = filtered_block(tables, 0, [size], ends)[0]
        factor = [2.0 * (4.0 * smooth_size[z] - size[z]) for z in range(cells)]
        for k in range(6):
            for z in range(cells):
                leonard = leonard_ref[k, z, :, lanes]
                term = rest_ref[k, z, :, lanes] + factor[z] * strain_ref[k, z, :, lanes]
                model_ref[k, z, :, lanes] = term
                scaled = PAIR_WEIGHTS[k] * term
                cross.append(scaled * leonard)
                square.append(scaled * term)
                blame.append(term * cot_ref[k, z, :, lanes])
            cross, square, blame = [sum_up(cross)], [sum_up(square)], [sum_up(blame)]
    mine = mask_ref[...] > 0.5
    place = lax.broadcasted_iota(jnp.int32, (8, LANES), 0)
    table = jnp.zeros((8, LANES), jnp.float32)
    for index, sums in enumerate((cross, square, blame)):
        per_row = jnp.sum(sums[0], axis=1, keepdims=True)
        per_bin = jnp.sum(jnp.where(mine, per_row, 0.0), axis=0, keepdims=True)
        table = jnp.where(place == index, per_bin, table)
    sums_ref[...] = table


def message_kernel(tables, smooth_ref, model_ref, sums_ref, other_sums_ref, dual_ref, message_ref, pair_ref):
    cells = tables.cells
    pair_sums = sums_ref[...] + other_sums_ref[...]
    pair_ref[...] = pair_sums
    message_ref[message_ref.shape[0] - 1] = pair_sums
    for half, lanes in enumerate(halves(model_ref.shape[-1])):
        model = [[model_ref[k, z, :, lanes] for z in range(cells)] for k in range(6)]
        smooth_v = [[smooth_ref[a, z, :, lanes] for z in range(cells)] for a in range(3)]
        for k in range(6):
            for end, value in enumerate(tables.project(model[k])):
                message_ref[18 * half + 2 * k + end] = value
        for a in range(3):
            dual = [2.0 * x for x in plain_dual(model, smooth_v, a, cells)]
            for z in range(cells):
                dual_ref[a, z, :, lanes] = dual[z]
            for end, value in enumerate(tables.project(dual)):
                message_ref[18 * half + 12 + 2 * a + end] = value


def local_kernel(tables, *refs):
    peers = tables.devices - 1
    cells = tables.cells
    v_ref, cot_ref, smooth_ref, leonard_ref, model_ref, dual_ref = refs[:6]
    far_v_refs = refs[6 : 6 + peers]
    far_cot_refs = refs[6 + peers : 6 + 2 * peers]
    parts_ref = refs[-1]
    for lanes in halves(v_ref.shape[-1]):

        def load(ref, count):
            return [[ref[f, z, :, lanes] for z in range(cells)] for f in range(count)]

        fields, ends = [], []
        for ref in (v_ref, *far_v_refs):
            v = load(ref, 3)
            fields.append(v + products_of(v))
            ends.append([tables.project(field) for field in fields[-1]])
        v = fields[0][:3]
        cot, model, leonard, smooth_v = load(cot_ref, 6), load(model_ref, 6), load(leonard_ref, 6), load(smooth_ref, 3)
        smooth_cot = [tables.inside(field) for field in cot]
        duals = [weighted_dual(cot, smooth_v, a, cells) for a in range(3)]
        others = [plain_dual(leonard, smooth_v, a, cells) for a in range(3)]
        smooth_duals = [tables.inside(field) for field in duals]
        smooth_others = [tables.inside(field) for field in others]
        for place in range(1, tables.devices):
            far_cot = load(far_cot_refs[place - 1], 6)
            filtered = filtered_block(tables, place, fields[place], ends)
            far_smooth = filtered[:3]
            far_leonard = [
                [filtered[3 + k][z] - far_smooth[a][z] * far_smooth[b][z] for z in range(cells)]
                for k, (a, b) in enumerate(INDEX_PAIRS)
            ]
            for k in range(6):
                far = tables.outside(place, tables.project(far_cot[k]))
                smooth_cot[k] = add_lists(smooth_cot[k], far)
            for a in range(3):
                far = tables.outside(place, tables.project(weighted_dual(far_cot, far_smooth, a, cells)))
                smooth_duals[a] = add_lists(smooth_duals[a], far)
                far = tables.outside(place, tables.project(plain_dual(far_leonard, far_smooth, a, cells)))
                smooth_others[a] = add_lists(smooth_others[a], far)
        inner = [add_lists(tables.inside(model[k]), leonard[k]) for k in range(6)]
        for a in range(3):
            first = weighted_dual(smooth_cot, v, a, cells)
            second = weighted_dual(cot, v, a, cells)
            dual = tables.inside([dual_ref[a, z, :, lanes] for z in range(cells)])
            third = plain_dual(inner, v, a, cells)
            fourth = plain_dual(model, v, a, cells)
            for z in range(cells):
                parts_ref[a, z, :, lanes] = first[z] - smooth_duals[a][z]
                parts_ref[3 + a, z, :, lanes] = smooth_duals[a][z] - second[z]
                parts_ref[6 + a, z, :, lanes] = 2.0 * (third[z] - smooth_others[a][z]) - dual[z]
                parts_ref[9 + a, z, :, lanes] = 2.0 * dual[z] - 4.0 * fourth[z]


def finish_kernel(tables, count, turning, *refs):
    peers = tables.devices - 1
    cells = tables.cells
    v_ref, leonard_ref, model_ref, parts_ref, mask_ref = refs[:5]
    near_refs = refs[5 : 5 + count]
    pair_ref = refs[5 + count]
    far_message_refs = refs[6 + count : 6 + count + peers]
    residual_hbm, grad_hbm, residual_ref, grad_ref, left = refs[6 + count + peers :]
    total = sum_up([pair_ref[...]] + [ref[ref.shape[0] - 1] for ref in far_message_refs])
    near = sum_up([ref[...] for ref in near_refs])
    if turning:
        place = lax.axis_index("stream")
        inner = jnp.logical_and(place > 0, place < lax.axis_size("stream") - 1)
        near = jnp.where(inner, near, 0.0)
    total = total + near
    inverse = 1.0 / (total[1:2] + EPSILON)
    rows = v_ref.shape[2]
    mine = mask_ref[...] > 0.5

    def of_rows(per_bin):
        column = jnp.sum(jnp.where(mine, per_bin, 0.0), axis=1, keepdims=True)
        return jnp.broadcast_to(column, (rows, LANES))

    coefficient = of_rows(total[0:1] * inverse)
    pull = of_rows(-(total[2:3] * inverse))
    copies = []
    for k in range(6):
        for lanes in halves(v_ref.shape[-1]):
            for z in range(cells):
                residual_ref[k, z, :, lanes] = (
                    leonard_ref[k, z, :, lanes] - coefficient * model_ref[k, z, :, lanes]
                )
        if k % 3 == 2:
            some = pl.ds(k - 2, 3)
            copies.append(pltpu.make_async_copy(residual_ref.at[some], residual_hbm.at[some], left.at[k // 3]))
            copies[-1].start()
    for half, lanes in enumerate(halves(v_ref.shape[-1])):
        v = [[v_ref[a, z, :, lanes] for z in range(cells)] for a in range(3)]
        from_model = [[] for _ in range(6)]
        from_dual = [[] for _ in range(3)]
        for place, ends in enumerate(far_message_refs, start=1):
            for k in range(6):
                from_model[k].append(tables.outside(place, [2.0 * ends[18 * half + 2 * k + end] for end in range(2)]))
            for a in range(3):
                pair = [(2.0 * coefficient - 1.0) * ends[18 * half + 12 + 2 * a + end] for end in range(2)]
                from_dual[a].append(tables.outside(place, pair))
        from_model = [functools.reduce(add_lists, lists) if lists else None for lists in from_model]
        from_dual = [functools.reduce(add_lists, lists) if lists else None for lists in from_dual]
        for a in range(3):
            for z in range(cells):
                pulled = parts_ref[6 + a, z, :, lanes] + coefficient * parts_ref[9 + a, z, :, lanes]
                if peers:
                    terms = [from_model[PAIR_OF[a][b]][z] * v[b][z] for b in range(3)]
                    pulled = pulled + from_dual[a][z] + sum_up(terms)
                grad_ref[a, z, :, lanes] = (
                    parts_ref[a, z, :, lanes] + coefficient * parts_ref[3 + a, z, :, lanes] + pull * pulled
                )
    copies.append(pltpu.make_async_copy(grad_ref, grad_hbm, left.at[2]))
    copies[-1].start()
    for copy in copies:
        copy.wait()


WHOLE = pl.BlockSpec(memory_space=pltpu.VMEM)
REMAIN = pl.BlockSpec(memory_space=pltpu.HBM)


def call(kernel, outs, operations, *operands, in_specs=None, out_specs=None, scratch=()):
    nbytes = sum(4 * int(np.prod(x.shape)) for x in (*operands, *outs))
    return pl.pallas_call(
        kernel,
        out_shape=outs,
        in_specs=in_specs or [WHOLE] * len(operands),
        out_specs=out_specs or [WHOLE] * len(outs),
        scratch_shapes=list(scratch),
        compiler_params=pltpu.CompilerParams(vmem_limit_bytes=32 * 1024 * 1024),
        cost_estimate=pl.CostEstimate(flops=operations, bytes_accessed=nbytes, transcendentals=0),
    )(*operands)


def from_ahead(values, shift):
    peers = lax.axis_size("span")
    return lax.ppermute(values, "span", [((i + shift) % peers, i) for i in range(peers)])


def from_source(values, span_shift, source):
    span, stream = lax.axis_size("span"), lax.axis_size("stream")
    pairs = [
        (((i + span_shift) % span) * stream + source(j) % stream, i * stream + j)
        for i in range(span)
        for j in range(stream)
    ]
    return lax.ppermute(values, ("span", "stream"), pairs)


def ring_source(stream):
    def source(j):
        if j % 2 == 0:
            return j - 2 if j >= 2 else 1
        return j + 2 if j + 2 < stream else j - 1

    return source


def on_device(velocity, strain, row_bins, cotangent):
    span, stream = lax.axis_size("span"), lax.axis_size("stream")
    cells, rows, width = velocity.shape[1:]
    tables = Tables(cells, span)
    slab = (rows, width)

    def shaped(*leading):
        return pltpu.VMEM(leading + slab, jnp.float32)

    far_v = [from_ahead(velocity, shift) for shift in range(1, span)]
    work = cells * rows * width
    (lane,) = call(lanes_kernel, [pltpu.VMEM((rows, LANES), jnp.int32)], LONG * work)
    size, size_ends = call(
        functools.partial(prepare_kernel, tables), [shaped(cells), shaped(2)], LONG * work, lane, strain
    )
    far_size = [from_ahead(size_ends, shift) for shift in range(1, span)]
    (mask,) = call(
        mask_kernel,
        [pltpu.VMEM((rows, LANES), jnp.float32)],
        work,
        pltpu.with_memory_space_constraint(row_bins.reshape(1, rows), pltpu.HBM),
        size_ends,
        in_specs=[REMAIN, WHOLE],
        scratch=[pltpu.VMEM((1, rows), jnp.int32), pltpu.SemaphoreType.DMA(())],
    )
    mask, near_cot = lax.optimization_barrier((mask, cotangent))
    far_cot = [from_ahead(near_cot, shift) for shift in range(1, span)]
    table = pltpu.VMEM((8, LANES), jnp.float32)
    smooth, leonard, rest = call(
        functools.partial(velocity_kernel, tables),
        [shaped(3, cells), shaped(6, cells), shaped(6, cells)],
        LONG * work,
        velocity,
        *far_v,
    )
    model, sums = call(
        functools.partial(model_kernel, tables),
        [shaped(6, cells), table],
        LONG * work,
        strain,
        near_cot,
        size,
        leonard,
        rest,
        mask,
        *far_size,
    )
    other_sums = from_source(sums, 0, lambda j: j ^ 1)
    dual, message, pair_sums = call(
        functools.partial(message_kernel, tables),
        [shaped(3, cells), pltpu.VMEM((18 * (width // LANES) + 1, rows, LANES), jnp.float32), table],
        100 * work,
        smooth,
        model,
        sums,
        other_sums,
    )
    far_message = [from_ahead(message, shift) for shift in range(1, span)]
    most_rows = 2 * rows * stream // NBINS
    reach = -(-(most_rows - 1) // rows)
    turning = reach <= 1
    if turning:
        sources = [ring_source(stream)]
    else:
        steps = range(1, -(-reach // 2) + 1)
        sources = [functools.partial(lambda j, away: j + away, away=2 * step * way) for step in steps for way in (1, -1)]
    near_sums = [from_source(pair_sums, shift, source) for shift in range(span) for source in sources]
    (parts,) = call(
        functools.partial(local_kernel, tables),
        [shaped(12, cells)],
        500 * work,
        velocity,
        near_cot,
        smooth,
        leonard,
        model,
        dual,
        *far_v,
        *far_cot,
    )
    outs = [jax.ShapeDtypeStruct((n, cells) + slab, jnp.float32) for n in (6, 3)]
    return tuple(
        call(
            functools.partial(finish_kernel, tables, len(near_sums), turning),
            outs,
            200 * work,
            velocity,
            leonard,
            model,
            parts,
            mask,
            *near_sums,
            pair_sums,
            *far_message,
            out_specs=[REMAIN] * 2,
            scratch=[pltpu.VMEM(x.shape, x.dtype) for x in outs] + [pltpu.SemaphoreType.DMA((3,))],
        )
    )


def solution(mesh):
    fields = P(None, "span", "stream", None)
    return jax.shard_map(
        on_device,
        mesh=mesh,
        in_specs=(fields, fields, P("stream"), fields),
        out_specs=(fields, fields),
        check_vma=False,
    )
```

```python
import functools

import jax
import jax.numpy as jnp
import numpy as np
from jax import lax
from jax.experimental import pallas as pl
from jax.experimental.pallas import tpu as pltpu
from jax.sharding import PartitionSpec as P

NBINS = 64
FILTER_ALPHA = 0.45
CENTER_WEIGHT = 0.95
SIDE_WEIGHT = 0.475
STRAIN_FLOOR = 0.25
EPSILON = 1e-06
INDEX_PAIRS = ((0, 0), (0, 1), (0, 2), (1, 1), (1, 2), (2, 2))
PAIR_WEIGHTS = (1.0, 2.0, 2.0, 1.0, 2.0, 1.0)
PAIR_OF = ((0, 1, 2), (1, 3, 4), (2, 4, 5))
LANES = 128
LONG = 300000


def filter_row(extent):
    eye = np.eye(extent)
    ring = np.roll(eye, 1, axis=1) + np.roll(eye, -1, axis=1)
    system = eye + FILTER_ALPHA * ring
    side = CENTER_WEIGHT * eye + SIDE_WEIGHT * ring
    return np.linalg.solve(system, side)[0]


def end_weights(cells):
    weights = np.zeros((2, cells))
    weights[0, 0] = 1.0
    weights[1, cells - 1] = 1.0
    inner = cells - 2
    if inner > 0:
        system = np.eye(inner) + FILTER_ALPHA * (np.eye(inner, k=1) + np.eye(inner, k=-1))
        right = np.zeros((inner, 2))
        right[0, 0] = -FILTER_ALPHA
        right[inner - 1, 1] = -FILTER_ALPHA
        weights[:, 1:-1] = np.linalg.solve(system, right).T
    return weights


class Tables:
    def __init__(self, cells, devices):
        row = filter_row(cells * devices)
        extent = cells * devices
        self.cells = cells
        self.devices = devices
        self.own = [[float(row[(z - w) % extent]) for w in range(cells)] for z in range(cells)]
        self.ends = [[float(x) for x in line] for line in end_weights(cells)]
        self.couple = [
            [[float(row[(z - shift * cells - w) % extent]) for w in (0, cells - 1)] for z in range(cells)]
            for shift in range(devices)
        ]

    def project(self, values):
        return [weighted(line, values) for line in self.ends]

    def inside(self, values):
        return [weighted(line, values) for line in self.own]

    def outside(self, shift, ends):
        return [weighted(line, ends) for line in self.couple[shift]]


def weighted(weights, values):
    total = None
    for weight, value in zip(weights, values):
        if weight == 0.0:
            continue
        term = value if weight == 1.0 else value * weight
        total = term if total is None else total + term
    return total


def add_lists(left, right):
    return [x + y for x, y in zip(left, right)]


def halves(width):
    return [pl.ds(start, LANES) for start in range(0, width, LANES)]


def sum_up(terms):
    total = terms[0]
    for term in terms[1:]:
        total = total + term
    return total


def lanes_kernel(lane_ref):
    lane_ref[...] = lax.broadcasted_iota(jnp.int32, lane_ref.shape, 1)


def prepare_kernel(tables, lane_ref, strain_ref, size_ref, size_ends_ref):
    cells = tables.cells
    for lanes in halves(strain_ref.shape[-1]):
        size = []
        for z in range(cells):
            values = [strain_ref[k, z, :, lanes] for k in range(6)]
            total = sum_up([weight * (value * value) for weight, value in zip(PAIR_WEIGHTS, values)])
            size.append(jnp.sqrt(jnp.maximum(2.0 * total, STRAIN_FLOOR)))
            size_ref[z, :, lanes] = size[z]
        for end, value in enumerate(tables.project(size)):
            size_ends_ref[end, :, lanes] = value


def mask_kernel(bins_hbm, size_ends_ref, mask_ref, bins_ref, arrived):
    copy = pltpu.make_async_copy(bins_hbm, bins_ref, arrived)
    copy.start()
    copy.wait()
    rows = bins_ref.shape[1]
    along = jnp.broadcast_to(bins_ref[...].astype(jnp.float32), (rows, rows))
    diagonal = lax.broadcasted_iota(jnp.int32, (rows, rows), 0) == lax.broadcasted_iota(jnp.int32, (rows, rows), 1)
    column = jnp.sum(jnp.where(diagonal, along, 0.0), axis=1, keepdims=True)
    lane = lax.broadcasted_iota(jnp.int32, (rows, LANES), 1).astype(jnp.float32)
    mask_ref[...] = jnp.where(jnp.broadcast_to(column, (rows, LANES)) == lane, 1.0, 0.0)


def products_of(v):
    return [[x * y for x, y in zip(v[a], v[b])] for a, b in INDEX_PAIRS]


def filtered_block(tables, place, fields, ends):
    filtered = [tables.inside(field) for field in fields]
    for other in range(tables.devices):
        if other != place:
            shift = (other - place) % tables.devices
            filtered = [add_lists(near, tables.outside(shift, far)) for near, far in zip(filtered, ends[other])]
    return filtered


def plain_dual(tensor, vector, a, cells):
    return [sum_up([tensor[PAIR_OF[a][b]][z] * vector[b][z] for b in range(3)]) for z in range(cells)]


def weighted_dual(tensor, vector, a, cells):
    plain = plain_dual(tensor, vector, a, cells)
    return [plain[z] + tensor[PAIR_OF[a][a]][z] * vector[a][z] for z in range(cells)]


def velocity_kernel(tables, v_ref, *refs):
    far_v_refs = refs[:-3]
    smooth_ref, leonard_ref, rest_ref = refs[-3:]
    cells = tables.cells
    for lanes in halves(v_ref.shape[-1]):
        v = [[v_ref[a, z, :, lanes] for z in range(cells)] for a in range(3)]
        products = products_of(v)
        ends = [None]
        for far_v_ref in far_v_refs:
            far = [[far_v_ref[a, z, :, lanes] for z in range(cells)] for a in range(3)]
            ends.append([tables.project(field) for field in far + products_of(far)])
        filtered = filtered_block(tables, 0, v + products, ends)
        for a in range(3):
            for z in range(cells):
                smooth_ref[a, z, :, lanes] = filtered[a][z]
        for k, (a, b) in enumerate(INDEX_PAIRS):
            for z in range(cells):
                coarse = filtered[a][z] * filtered[b][z]
                leonard_ref[k, z, :, lanes] = filtered[3 + k][z] - coarse
                rest_ref[k, z, :, lanes] = products[k][z] - coarse


def model_kernel(tables, strain_ref, cot_ref, size_ref, leonard_ref, rest_ref, mask_ref, *refs):
    far_size_refs = refs[:-2]
    model_ref, sums_ref = refs[-2:]
    cells = tables.cells
    cross, square, blame = [], [], []
    for lanes in halves(strain_ref.shape[-1]):
        size = [size_ref[z, :, lanes] for z in range(cells)]
        ends = [None] + [[[far[end, :, lanes] for end in range(2)]] for far in far_size_refs]
        smooth_size = filtered_block(tables, 0, [size], ends)[0]
        factor = [2.0 * (4.0 * smooth_size[z] - size[z]) for z in range(cells)]
        for k in range(6):
            for z in range(cells):
                leonard = leonard_ref[k, z, :, lanes]
                term = rest_ref[k, z, :, lanes] + factor[z] * strain_ref[k, z, :, lanes]
                model_ref[k, z, :, lanes] = term
                scaled = PAIR_WEIGHTS[k] * term
                cross.append(scaled * leonard)
                square.append(scaled * term)
                blame.append(term * cot_ref[k, z, :, lanes])
            cross, square, blame = [sum_up(cross)], [sum_up(square)], [sum_up(blame)]
    mine = mask_ref[...] > 0.5
    place = lax.broadcasted_iota(jnp.int32, (8, LANES), 0)
    table = jnp.zeros((8, LANES), jnp.float32)
    for index, sums in enumerate((cross, square, blame)):
        per_row = jnp.sum(sums[0], axis=1, keepdims=True)
        per_bin = jnp.sum(jnp.where(mine, per_row, 0.0), axis=0, keepdims=True)
        table = jnp.where(place == index, per_bin, table)
    sums_ref[...] = table


def message_kernel(tables, smooth_ref, model_ref, sums_ref, other_sums_ref, dual_ref, message_ref, pair_ref):
    cells = tables.cells
    pair_sums = sums_ref[...] + other_sums_ref[...]
    pair_ref[...] = pair_sums
    message_ref[message_ref.shape[0] - 1] = pair_sums
    for half, lanes in enumerate(halves(model_ref.shape[-1])):
        model = [[model_ref[k, z, :, lanes] for z in range(cells)] for k in range(6)]
        smooth_v = [[smooth_ref[a, z, :, lanes] for z in range(cells)] for a in range(3)]
        for k in range(6):
            for end, value in enumerate(tables.project(model[k])):
                message_ref[18 * half + 2 * k + end] = value
        for a in range(3):
            dual = [2.0 * x for x in plain_dual(model, smooth_v, a, cells)]
            for z in range(cells):
                dual_ref[a, z, :, lanes] = dual[z]
            for end, value in enumerate(tables.project(dual)):
                message_ref[18 * half + 12 + 2 * a + end] = value


def local_kernel(tables, *refs):
    peers = tables.devices - 1
    cells = tables.cells
    v_ref, cot_ref, smooth_ref, leonard_ref, model_ref, dual_ref = refs[:6]
    far_v_refs = refs[6 : 6 + peers]
    far_cot_refs = refs[6 + peers : 6 + 2 * peers]
    parts_ref = refs[-1]
    for lanes in halves(v_ref.shape[-1]):

        def load(ref, count):
            return [[ref[f, z, :, lanes] for z in range(cells)] for f in range(count)]

        fields, ends = [], []
        for ref in (v_ref, *far_v_refs):
            v = load(ref, 3)
            fields.append(v + products_of(v))
            ends.append([tables.project(field) for field in fields[-1]])
        v = fields[0][:3]
        cot, model, leonard, smooth_v = load(cot_ref, 6), load(model_ref, 6), load(leonard_ref, 6), load(smooth_ref, 3)
        smooth_cot = [tables.inside(field) for field in cot]
        duals = [weighted_dual(cot, smooth_v, a, cells) for a in range(3)]
        others = [plain_dual(leonard, smooth_v, a, cells) for a in range(3)]
        smooth_duals = [tables.inside(field) for field in duals]
        smooth_others = [tables.inside(field) for field in others]
        for place in range(1, tables.devices):
            far_cot = load(far_cot_refs[place - 1], 6)
            filtered = filtered_block(tables, place, fields[place], ends)
            far_smooth = filtered[:3]
            far_leonard = [
                [filtered[3 + k][z] - far_smooth[a][z] * far_smooth[b][z] for z in range(cells)]
                for k, (a, b) in enumerate(INDEX_PAIRS)
            ]
            for k in range(6):
                far = tables.outside(place, tables.project(far_cot[k]))
                smooth_cot[k] = add_lists(smooth_cot[k], far)
            for a in range(3):
                far = tables.outside(place, tables.project(weighted_dual(far_cot, far_smooth, a, cells)))
                smooth_duals[a] = add_lists(smooth_duals[a], far)
                far = tables.outside(place, tables.project(plain_dual(far_leonard, far_smooth, a, cells)))
                smooth_others[a] = add_lists(smooth_others[a], far)
        inner = [add_lists(tables.inside(model[k]), leonard[k]) for k in range(6)]
        for a in range(3):
            first = weighted_dual(smooth_cot, v, a, cells)
            second = weighted_dual(cot, v, a, cells)
            dual = tables.inside([dual_ref[a, z, :, lanes] for z in range(cells)])
            third = plain_dual(inner, v, a, cells)
            fourth = plain_dual(model, v, a, cells)
            for z in range(cells):
                parts_ref[a, z, :, lanes] = first[z] - smooth_duals[a][z]
                parts_ref[3 + a, z, :, lanes] = smooth_duals[a][z] - second[z]
                parts_ref[6 + a, z, :, lanes] = 2.0 * (third[z] - smooth_others[a][z]) - dual[z]
                parts_ref[9 + a, z, :, lanes] = 2.0 * dual[z] - 4.0 * fourth[z]


def finish_kernel(tables, count, turning, *refs):
    peers = tables.devices - 1
    cells = tables.cells
    v_ref, leonard_ref, model_ref, parts_ref, mask_ref = refs[:5]
    near_refs = refs[5 : 5 + count]
    pair_ref = refs[5 + count]
    far_message_refs = refs[6 + count : 6 + count + peers]
    residual_hbm, grad_hbm, residual_ref, grad_ref, left = refs[6 + count + peers :]
    total = sum_up([pair_ref[...]] + [ref[ref.shape[0] - 1] for ref in far_message_refs])
    near = sum_up([ref[...] for ref in near_refs])
    if turning:
        place = lax.axis_index("stream")
        inner = jnp.logical_and(place > 0, place < lax.axis_size("stream") - 1)
        near = jnp.where(inner, near, 0.0)
    total = total + near
    inverse = 1.0 / (total[1:2] + EPSILON)
    rows = v_ref.shape[2]
    mine = mask_ref[...] > 0.5

    def of_rows(per_bin):
        column = jnp.sum(jnp.where(mine, per_bin, 0.0), axis=1, keepdims=True)
        return jnp.broadcast_to(column, (rows, LANES))

    coefficient = of_rows(total[0:1] * inverse)
    pull = of_rows(-(total[2:3] * inverse))
    for half, lanes in enumerate(halves(v_ref.shape[-1])):
        v = [[v_ref[a, z, :, lanes] for z in range(cells)] for a in range(3)]
        from_model = [[] for _ in range(6)]
        from_dual = [[] for _ in range(3)]
        for place, ends in enumerate(far_message_refs, start=1):
            for k in range(6):
                from_model[k].append(tables.outside(place, [2.0 * ends[18 * half + 2 * k + end] for end in range(2)]))
            for a in range(3):
                pair = [(2.0 * coefficient - 1.0) * ends[18 * half + 12 + 2 * a + end] for end in range(2)]
                from_dual[a].append(tables.outside(place, pair))
        from_model = [functools.reduce(add_lists, lists) if lists else None for lists in from_model]
        from_dual = [functools.reduce(add_lists, lists) if lists else None for lists in from_dual]
        for a in range(3):
            for z in range(cells):
                pulled = parts_ref[6 + a, z, :, lanes] + coefficient * parts_ref[9 + a, z, :, lanes]
                if peers:
                    terms = [from_model[PAIR_OF[a][b]][z] * v[b][z] for b in range(3)]
                    pulled = pulled + from_dual[a][z] + sum_up(terms)
                grad_ref[a, z, :, lanes] = (
                    parts_ref[a, z, :, lanes] + coefficient * parts_ref[3 + a, z, :, lanes] + pull * pulled
                )
    copies = [pltpu.make_async_copy(grad_ref, grad_hbm, left.at[0])]
    copies[0].start()
    for k in range(6):
        for lanes in halves(v_ref.shape[-1]):
            for z in range(cells):
                residual_ref[k, z, :, lanes] = (
                    leonard_ref[k, z, :, lanes] - coefficient * model_ref[k, z, :, lanes]
                )
        if k % 3 == 2:
            some = pl.ds(k - 2, 3)
            copies.append(pltpu.make_async_copy(residual_ref.at[some], residual_hbm.at[some], left.at[1 + k // 3]))
            copies[-1].start()
    for copy in copies:
        copy.wait()


WHOLE = pl.BlockSpec(memory_space=pltpu.VMEM)
REMAIN = pl.BlockSpec(memory_space=pltpu.HBM)


def call(kernel, outs, operations, *operands, in_specs=None, out_specs=None, scratch=()):
    nbytes = sum(4 * int(np.prod(x.shape)) for x in (*operands, *outs))
    return pl.pallas_call(
        kernel,
        out_shape=outs,
        in_specs=in_specs or [WHOLE] * len(operands),
        out_specs=out_specs or [WHOLE] * len(outs),
        scratch_shapes=list(scratch),
        compiler_params=pltpu.CompilerParams(vmem_limit_bytes=32 * 1024 * 1024),
        cost_estimate=pl.CostEstimate(flops=operations, bytes_accessed=nbytes, transcendentals=0),
    )(*operands)


def from_ahead(values, shift):
    peers = lax.axis_size("span")
    return lax.ppermute(values, "span", [((i + shift) % peers, i) for i in range(peers)])


def from_source(values, span_shift, source):
    span, stream = lax.axis_size("span"), lax.axis_size("stream")
    pairs = [
        (((i + span_shift) % span) * stream + source(j) % stream, i * stream + j)
        for i in range(span)
        for j in range(stream)
    ]
    return lax.ppermute(values, ("span", "stream"), pairs)


def ring_source(stream):
    def source(j):
        if j % 2 == 0:
            return j - 2 if j >= 2 else 1
        return j + 2 if j + 2 < stream else j - 1

    return source


def on_device(velocity, strain, row_bins, cotangent):
    span, stream = lax.axis_size("span"), lax.axis_size("stream")
    cells, rows, width = velocity.shape[1:]
    tables = Tables(cells, span)
    slab = (rows, width)

    def shaped(*leading):
        return pltpu.VMEM(leading + slab, jnp.float32)

    far_v = [from_ahead(velocity, shift) for shift in range(1, span)]
    work = cells * rows * width
    (lane,) = call(lanes_kernel, [pltpu.VMEM((rows, LANES), jnp.int32)], LONG * work)
    size, size_ends = call(
        functools.partial(prepare_kernel, tables), [shaped(cells), shaped(2)], LONG * work, lane, strain
    )
    far_size = [from_ahead(size_ends, shift) for shift in range(1, span)]
    (mask,) = call(
        mask_kernel,
        [pltpu.VMEM((rows, LANES), jnp.float32)],
        work,
        pltpu.with_memory_space_constraint(row_bins.reshape(1, rows), pltpu.HBM),
        size_ends,
        in_specs=[REMAIN, WHOLE],
        scratch=[pltpu.VMEM((1, rows), jnp.int32), pltpu.SemaphoreType.DMA(())],
    )
    mask, near_cot = lax.optimization_barrier((mask, cotangent))
    far_cot = [from_ahead(near_cot, shift) for shift in range(1, span)]
    table = pltpu.VMEM((8, LANES), jnp.float32)
    smooth, leonard, rest = call(
        functools.partial(velocity_kernel, tables),
        [shaped(3, cells), shaped(6, cells), shaped(6, cells)],
        LONG * work,
        velocity,
        *far_v,
    )
    model, sums = call(
        functools.partial(model_kernel, tables),
        [shaped(6, cells), table],
        LONG * work,
        strain,
        near_cot,
        size,
        leonard,
        rest,
        mask,
        *far_size,
    )
    other_sums = from_source(sums, 0, lambda j: j ^ 1)
    dual, message, pair_sums = call(
        functools.partial(message_kernel, tables),
        [shaped(3, cells), pltpu.VMEM((18 * (width // LANES) + 1, rows, LANES), jnp.float32), table],
        100 * work,
        smooth,
        model,
        sums,
        other_sums,
    )
    far_message = [from_ahead(message, shift) for shift in range(1, span)]
    most_rows = 2 * rows * stream // NBINS
    reach = -(-(most_rows - 1) // rows)
    turning = reach <= 1
    if turning:
        sources = [ring_source(stream)]
    else:
        steps = range(1, -(-reach // 2) + 1)
        sources = [functools.partial(lambda j, away: j + away, away=2 * step * way) for step in steps for way in (1, -1)]
    near_sums = [from_source(pair_sums, shift, source) for shift in range(span) for source in sources]
    (parts,) = call(
        functools.partial(local_kernel, tables),
        [shaped(12, cells)],
        500 * work,
        velocity,
        near_cot,
        smooth,
        leonard,
        model,
        dual,
        *far_v,
        *far_cot,
    )
    outs = [jax.ShapeDtypeStruct((n, cells) + slab, jnp.float32) for n in (6, 3)]
    return tuple(
        call(
            functools.partial(finish_kernel, tables, len(near_sums), turning),
            outs,
            200 * work,
            velocity,
            leonard,
            model,
            parts,
            mask,
            *near_sums,
            pair_sums,
            *far_message,
            out_specs=[REMAIN] * 2,
            scratch=[pltpu.VMEM(x.shape, x.dtype) for x in outs] + [pltpu.SemaphoreType.DMA((3,))],
        )
    )


def solution(mesh):
    fields = P(None, "span", "stream", None)
    return jax.shard_map(
        on_device,
        mesh=mesh,
        in_specs=(fields, fields, P("stream"), fields),
        out_specs=(fields, fields),
        check_vma=False,
    )
```

```python
import functools

import jax
import jax.numpy as jnp
import numpy as np
from jax import lax
from jax.experimental import pallas as pl
from jax.experimental.pallas import tpu as pltpu
from jax.sharding import PartitionSpec as P

NBINS = 64
FILTER_ALPHA = 0.45
CENTER_WEIGHT = 0.95
SIDE_WEIGHT = 0.475
STRAIN_FLOOR = 0.25
EPSILON = 1e-06
INDEX_PAIRS = ((0, 0), (0, 1), (0, 2), (1, 1), (1, 2), (2, 2))
PAIR_WEIGHTS = (1.0, 2.0, 2.0, 1.0, 2.0, 1.0)
PAIR_OF = ((0, 1, 2), (1, 3, 4), (2, 4, 5))
LANES = 128
LONG = 300000


def filter_row(extent):
    eye = np.eye(extent)
    ring = np.roll(eye, 1, axis=1) + np.roll(eye, -1, axis=1)
    system = eye + FILTER_ALPHA * ring
    side = CENTER_WEIGHT * eye + SIDE_WEIGHT * ring
    return np.linalg.solve(system, side)[0]


def end_weights(cells):
    weights = np.zeros((2, cells))
    weights[0, 0] = 1.0
    weights[1, cells - 1] = 1.0
    inner = cells - 2
    if inner > 0:
        system = np.eye(inner) + FILTER_ALPHA * (np.eye(inner, k=1) + np.eye(inner, k=-1))
        right = np.zeros((inner, 2))
        right[0, 0] = -FILTER_ALPHA
        right[inner - 1, 1] = -FILTER_ALPHA
        weights[:, 1:-1] = np.linalg.solve(system, right).T
    return weights


class Tables:
    def __init__(self, cells, devices):
        row = filter_row(cells * devices)
        extent = cells * devices
        self.cells = cells
        self.devices = devices
        self.own = [[float(row[(z - w) % extent]) for w in range(cells)] for z in range(cells)]
        self.ends = [[float(x) for x in line] for line in end_weights(cells)]
        self.couple = [
            [[float(row[(z - shift * cells - w) % extent]) for w in (0, cells - 1)] for z in range(cells)]
            for shift in range(devices)
        ]

    def project(self, values):
        return [weighted(line, values) for line in self.ends]

    def inside(self, values):
        return [weighted(line, values) for line in self.own]

    def outside(self, shift, ends):
        return [weighted(line, ends) for line in self.couple[shift]]


def weighted(weights, values):
    total = None
    for weight, value in zip(weights, values):
        if weight == 0.0:
            continue
        term = value if weight == 1.0 else value * weight
        total = term if total is None else total + term
    return total


def add_lists(left, right):
    return [x + y for x, y in zip(left, right)]


def halves(width):
    return [pl.ds(start, LANES) for start in range(0, width, LANES)]


def sum_up(terms):
    total = terms[0]
    for term in terms[1:]:
        total = total + term
    return total


def lanes_kernel(lane_ref):
    lane_ref[...] = lax.broadcasted_iota(jnp.int32, lane_ref.shape, 1)


def prepare_kernel(tables, lane_ref, strain_ref, size_ref, size_ends_ref):
    cells = tables.cells
    for lanes in halves(strain_ref.shape[-1]):
        size = []
        for z in range(cells):
            values = [strain_ref[k, z, :, lanes] for k in range(6)]
            total = sum_up([weight * (value * value) for weight, value in zip(PAIR_WEIGHTS, values)])
            size.append(jnp.sqrt(jnp.maximum(2.0 * total, STRAIN_FLOOR)))
            size_ref[z, :, lanes] = size[z]
        for end, value in enumerate(tables.project(size)):
            size_ends_ref[end, :, lanes] = value


def mask_kernel(bins_hbm, size_ends_ref, mask_ref, bins_ref, arrived):
    copy = pltpu.make_async_copy(bins_hbm, bins_ref, arrived)
    copy.start()
    copy.wait()
    rows = bins_ref.shape[1]
    along = jnp.broadcast_to(bins_ref[...].astype(jnp.float32), (rows, rows))
    diagonal = lax.broadcasted_iota(jnp.int32, (rows, rows), 0) == lax.broadcasted_iota(jnp.int32, (rows, rows), 1)
    column = jnp.sum(jnp.where(diagonal, along, 0.0), axis=1, keepdims=True)
    lane = lax.broadcasted_iota(jnp.int32, (rows, LANES), 1).astype(jnp.float32)
    mask_ref[...] = jnp.where(jnp.broadcast_to(column, (rows, LANES)) == lane, 1.0, 0.0)


def products_of(v):
    return [[x * y for x, y in zip(v[a], v[b])] for a, b in INDEX_PAIRS]


def filtered_block(tables, place, fields, ends):
    filtered = [tables.inside(field) for field in fields]
    for other in range(tables.devices):
        if other != place:
            shift = (other - place) % tables.devices
            filtered = [add_lists(near, tables.outside(shift, far)) for near, far in zip(filtered, ends[other])]
    return filtered


def plain_dual(tensor, vector, a, cells):
    return [sum_up([tensor[PAIR_OF[a][b]][z] * vector[b][z] for b in range(3)]) for z in range(cells)]


def weighted_dual(tensor, vector, a, cells):
    plain = plain_dual(tensor, vector, a, cells)
    return [plain[z] + tensor[PAIR_OF[a][a]][z] * vector[a][z] for z in range(cells)]


def velocity_kernel(tables, v_ref, strain_ref, cot_ref, *refs):
    far_v_refs = refs[:-4]
    smooth_ref, leonard_ref, rest_ref, powers_ref = refs[-4:]
    cells = tables.cells
    for lanes in halves(v_ref.shape[-1]):
        v = [[v_ref[a, z, :, lanes] for z in range(cells)] for a in range(3)]
        products = products_of(v)
        ends = [None]
        for far_v_ref in far_v_refs:
            far = [[far_v_ref[a, z, :, lanes] for z in range(cells)] for a in range(3)]
            ends.append([tables.project(field) for field in far + products_of(far)])
        filtered = filtered_block(tables, 0, v + products, ends)
        for a in range(3):
            for z in range(cells):
                smooth_ref[a, z, :, lanes] = filtered[a][z]
        for z in range(cells):
            powers = [[] for _ in range(7)]
            for k, (a, b) in enumerate(INDEX_PAIRS):
                coarse = filtered[a][z] * filtered[b][z]
                leonard = filtered[3 + k][z] - coarse
                rest = products[k][z] - coarse
                leonard_ref[k, z, :, lanes] = leonard
                rest_ref[k, z, :, lanes] = rest
                strain, cot = strain_ref[k, z, :, lanes], cot_ref[k, z, :, lanes]
                scaled_rest, scaled_strain = PAIR_WEIGHTS[k] * rest, PAIR_WEIGHTS[k] * strain
                terms = (
                    scaled_rest * leonard,
                    scaled_strain * leonard,
                    scaled_rest * rest,
                    scaled_strain * rest,
                    scaled_strain * strain,
                    cot * rest,
                    cot * strain,
                )
                for power, term in zip(powers, terms):
                    power.append(term)
            for index, power in enumerate(powers):
                powers_ref[index, z, :, lanes] = sum_up(power)


def sums_kernel(tables, size_ref, powers_ref, mask_ref, *refs):
    far_size_refs = refs[:-2]
    factor_ref, sums_ref = refs[-2:]
    cells = tables.cells
    cross, square, blame = [], [], []
    for lanes in halves(size_ref.shape[-1]):
        size = [size_ref[z, :, lanes] for z in range(cells)]
        ends = [None] + [[[far[end, :, lanes] for end in range(2)]] for far in far_size_refs]
        smooth_size = filtered_block(tables, 0, [size], ends)[0]
        for z in range(cells):
            factor = 2.0 * (4.0 * smooth_size[z] - size[z])
            factor_ref[z, :, lanes] = factor
            power = [powers_ref[index, z, :, lanes] for index in range(7)]
            cross.append(power[0] + factor * power[1])
            square.append(power[2] + factor * (2.0 * power[3] + factor * power[4]))
            blame.append(power[5] + factor * power[6])
    cross, square, blame = [sum_up(cross)], [sum_up(square)], [sum_up(blame)]
    mine = mask_ref[...] > 0.5
    place = lax.broadcasted_iota(jnp.int32, (8, LANES), 0)
    table = jnp.zeros((8, LANES), jnp.float32)
    for index, sums in enumerate((cross, square, blame)):
        per_row = jnp.sum(sums[0], axis=1, keepdims=True)
        per_bin = jnp.sum(jnp.where(mine, per_row, 0.0), axis=0, keepdims=True)
        table = jnp.where(place == index, per_bin, table)
    sums_ref[...] = table


def model_kernel(tables, strain_ref, rest_ref, factor_ref, model_ref):
    for lanes in halves(strain_ref.shape[-1]):
        for z in range(tables.cells):
            factor = factor_ref[z, :, lanes]
            for k in range(6):
                model_ref[k, z, :, lanes] = rest_ref[k, z, :, lanes] + factor * strain_ref[k, z, :, lanes]


def message_kernel(tables, smooth_ref, model_ref, sums_ref, other_sums_ref, dual_ref, message_ref, pair_ref):
    cells = tables.cells
    pair_sums = sums_ref[...] + other_sums_ref[...]
    pair_ref[...] = pair_sums
    message_ref[message_ref.shape[0] - 1] = pair_sums
    for half, lanes in enumerate(halves(model_ref.shape[-1])):
        model = [[model_ref[k, z, :, lanes] for z in range(cells)] for k in range(6)]
        smooth_v = [[smooth_ref[a, z, :, lanes] for z in range(cells)] for a in range(3)]
        for k in range(6):
            for end, value in enumerate(tables.project(model[k])):
                message_ref[18 * half + 2 * k + end] = value
        for a in range(3):
            dual = [2.0 * x for x in plain_dual(model, smooth_v, a, cells)]
            for z in range(cells):
                dual_ref[a, z, :, lanes] = dual[z]
            for end, value in enumerate(tables.project(dual)):
                message_ref[18 * half + 12 + 2 * a + end] = value


def local_kernel(tables, *refs):
    peers = tables.devices - 1
    cells = tables.cells
    v_ref, cot_ref, smooth_ref, leonard_ref, model_ref, dual_ref = refs[:6]
    far_v_refs = refs[6 : 6 + peers]
    far_cot_refs = refs[6 + peers : 6 + 2 * peers]
    parts_ref = refs[-1]
    for lanes in halves(v_ref.shape[-1]):

        def load(ref, count):
            return [[ref[f, z, :, lanes] for z in range(cells)] for f in range(count)]

        fields, ends = [], []
        for ref in (v_ref, *far_v_refs):
            v = load(ref, 3)
            fields.append(v + products_of(v))
            ends.append([tables.project(field) for field in fields[-1]])
        v = fields[0][:3]
        cot, model, leonard, smooth_v = load(cot_ref, 6), load(model_ref, 6), load(leonard_ref, 6), load(smooth_ref, 3)
        smooth_cot = [tables.inside(field) for field in cot]
        duals = [weighted_dual(cot, smooth_v, a, cells) for a in range(3)]
        others = [plain_dual(leonard, smooth_v, a, cells) for a in range(3)]
        smooth_duals = [tables.inside(field) for field in duals]
        smooth_others = [tables.inside(field) for field in others]
        for place in range(1, tables.devices):
            far_cot = load(far_cot_refs[place - 1], 6)
            filtered = filtered_block(tables, place, fields[place], ends)
            far_smooth = filtered[:3]
            far_leonard = [
                [filtered[3 + k][z] - far_smooth[a][z] * far_smooth[b][z] for z in range(cells)]
                for k, (a, b) in enumerate(INDEX_PAIRS)
            ]
            for k in range(6):
                far = tables.outside(place, tables.project(far_cot[k]))
                smooth_cot[k] = add_lists(smooth_cot[k], far)
            for a in range(3):
                far = tables.outside(place, tables.project(weighted_dual(far_cot, far_smooth, a, cells)))
                smooth_duals[a] = add_lists(smooth_duals[a], far)
                far = tables.outside(place, tables.project(plain_dual(far_leonard, far_smooth, a, cells)))
                smooth_others[a] = add_lists(smooth_others[a], far)
        inner = [add_lists(tables.inside(model[k]), leonard[k]) for k in range(6)]
        for a in range(3):
            first = weighted_dual(smooth_cot, v, a, cells)
            second = weighted_dual(cot, v, a, cells)
            dual = tables.inside([dual_ref[a, z, :, lanes] for z in range(cells)])
            third = plain_dual(inner, v, a, cells)
            fourth = plain_dual(model, v, a, cells)
            for z in range(cells):
                parts_ref[a, z, :, lanes] = first[z] - smooth_duals[a][z]
                parts_ref[3 + a, z, :, lanes] = smooth_duals[a][z] - second[z]
                parts_ref[6 + a, z, :, lanes] = 2.0 * (third[z] - smooth_others[a][z]) - dual[z]
                parts_ref[9 + a, z, :, lanes] = 2.0 * dual[z] - 4.0 * fourth[z]


def finish_kernel(tables, count, turning, *refs):
    peers = tables.devices - 1
    cells = tables.cells
    v_ref, leonard_ref, model_ref, parts_ref, mask_ref = refs[:5]
    near_refs = refs[5 : 5 + count]
    pair_ref = refs[5 + count]
    far_message_refs = refs[6 + count : 6 + count + peers]
    residual_hbm, grad_hbm, residual_ref, grad_ref, left = refs[6 + count + peers :]
    total = sum_up([pair_ref[...]] + [ref[ref.shape[0] - 1] for ref in far_message_refs])
    near = sum_up([ref[...] for ref in near_refs])
    if turning:
        place = lax.axis_index("stream")
        inner = jnp.logical_and(place > 0, place < lax.axis_size("stream") - 1)
        near = jnp.where(inner, near, 0.0)
    total = total + near
    inverse = 1.0 / (total[1:2] + EPSILON)
    rows = v_ref.shape[2]
    mine = mask_ref[...] > 0.5

    def of_rows(per_bin):
        column = jnp.sum(jnp.where(mine, per_bin, 0.0), axis=1, keepdims=True)
        return jnp.broadcast_to(column, (rows, LANES))

    coefficient = of_rows(total[0:1] * inverse)
    pull = of_rows(-(total[2:3] * inverse))
    copies = []
    for k in range(6):
        for lanes in halves(v_ref.shape[-1]):
            for z in range(cells):
                residual_ref[k, z, :, lanes] = (
                    leonard_ref[k, z, :, lanes] - coefficient * model_ref[k, z, :, lanes]
                )
        if k % 3 == 2:
            some = pl.ds(k - 2, 3)
            copies.append(pltpu.make_async_copy(residual_ref.at[some], residual_hbm.at[some], left.at[k // 3]))
            copies[-1].start()
    for half, lanes in enumerate(halves(v_ref.shape[-1])):
        v = [[v_ref[a, z, :, lanes] for z in range(cells)] for a in range(3)]
        from_model = [[] for _ in range(6)]
        from_dual = [[] for _ in range(3)]
        for place, ends in enumerate(far_message_refs, start=1):
            for k in range(6):
                from_model[k].append(tables.outside(place, [2.0 * ends[18 * half + 2 * k + end] for end in range(2)]))
            for a in range(3):
                pair = [(2.0 * coefficient - 1.0) * ends[18 * half + 12 + 2 * a + end] for end in range(2)]
                from_dual[a].append(tables.outside(place, pair))
        from_model = [functools.reduce(add_lists, lists) if lists else None for lists in from_model]
        from_dual = [functools.reduce(add_lists, lists) if lists else None for lists in from_dual]
        for a in range(3):
            for z in range(cells):
                pulled = parts_ref[6 + a, z, :, lanes] + coefficient * parts_ref[9 + a, z, :, lanes]
                if peers:
                    terms = [from_model[PAIR_OF[a][b]][z] * v[b][z] for b in range(3)]
                    pulled = pulled + from_dual[a][z] + sum_up(terms)
                grad_ref[a, z, :, lanes] = (
                    parts_ref[a, z, :, lanes] + coefficient * parts_ref[3 + a, z, :, lanes] + pull * pulled
                )
    copies.append(pltpu.make_async_copy(grad_ref, grad_hbm, left.at[2]))
    copies[-1].start()
    for copy in copies:
        copy.wait()


WHOLE = pl.BlockSpec(memory_space=pltpu.VMEM)
REMAIN = pl.BlockSpec(memory_space=pltpu.HBM)


def call(kernel, outs, operations, *operands, in_specs=None, out_specs=None, scratch=()):
    nbytes = sum(4 * int(np.prod(x.shape)) for x in (*operands, *outs))
    return pl.pallas_call(
        kernel,
        out_shape=outs,
        in_specs=in_specs or [WHOLE] * len(operands),
        out_specs=out_specs or [WHOLE] * len(outs),
        scratch_shapes=list(scratch),
        compiler_params=pltpu.CompilerParams(vmem_limit_bytes=32 * 1024 * 1024),
        cost_estimate=pl.CostEstimate(flops=operations, bytes_accessed=nbytes, transcendentals=0),
    )(*operands)


def from_ahead(values, shift):
    peers = lax.axis_size("span")
    return lax.ppermute(values, "span", [((i + shift) % peers, i) for i in range(peers)])


def from_source(values, span_shift, source):
    span, stream = lax.axis_size("span"), lax.axis_size("stream")
    pairs = [
        (((i + span_shift) % span) * stream + source(j) % stream, i * stream + j)
        for i in range(span)
        for j in range(stream)
    ]
    return lax.ppermute(values, ("span", "stream"), pairs)


def ring_source(stream):
    def source(j):
        if j % 2 == 0:
            return j - 2 if j >= 2 else 1
        return j + 2 if j + 2 < stream else j - 1

    return source


def on_device(velocity, strain, row_bins, cotangent):
    span, stream = lax.axis_size("span"), lax.axis_size("stream")
    cells, rows, width = velocity.shape[1:]
    tables = Tables(cells, span)
    slab = (rows, width)

    def shaped(*leading):
        return pltpu.VMEM(leading + slab, jnp.float32)

    far_v = [from_ahead(velocity, shift) for shift in range(1, span)]
    work = cells * rows * width
    (lane,) = call(lanes_kernel, [pltpu.VMEM((rows, LANES), jnp.int32)], LONG * work)
    size, size_ends = call(
        functools.partial(prepare_kernel, tables), [shaped(cells), shaped(2)], LONG * work, lane, strain
    )
    far_size = [from_ahead(size_ends, shift) for shift in range(1, span)]
    (mask,) = call(
        mask_kernel,
        [pltpu.VMEM((rows, LANES), jnp.float32)],
        work,
        pltpu.with_memory_space_constraint(row_bins.reshape(1, rows), pltpu.HBM),
        size_ends,
        in_specs=[REMAIN, WHOLE],
        scratch=[pltpu.VMEM((1, rows), jnp.int32), pltpu.SemaphoreType.DMA(())],
    )
    mask, near_cot = lax.optimization_barrier((mask, cotangent))
    far_cot = [from_ahead(near_cot, shift) for shift in range(1, span)]
    table = pltpu.VMEM((8, LANES), jnp.float32)
    smooth, leonard, rest, powers = call(
        functools.partial(velocity_kernel, tables),
        [shaped(3, cells), shaped(6, cells), shaped(6, cells), shaped(7, cells)],
        LONG * work,
        velocity,
        strain,
        near_cot,
        *far_v,
    )
    factor, sums = call(
        functools.partial(sums_kernel, tables), [shaped(cells), table], LONG * work, size, powers, mask, *far_size
    )
    (model,) = call(
        functools.partial(model_kernel, tables), [shaped(6, cells)], LONG * work, strain, rest, factor
    )
    other_sums = from_source(sums, 0, lambda j: j ^ 1)
    dual, message, pair_sums = call(
        functools.partial(message_kernel, tables),
        [shaped(3, cells), pltpu.VMEM((18 * (width // LANES) + 1, rows, LANES), jnp.float32), table],
        100 * work,
        smooth,
        model,
        sums,
        other_sums,
    )
    far_message = [from_ahead(message, shift) for shift in range(1, span)]
    most_rows = 2 * rows * stream // NBINS
    reach = -(-(most_rows - 1) // rows)
    turning = reach <= 1
    if turning:
        sources = [ring_source(stream)]
    else:
        steps = range(1, -(-reach // 2) + 1)
        sources = [functools.partial(lambda j, away: j + away, away=2 * step * way) for step in steps for way in (1, -1)]
    near_sums = [from_source(pair_sums, shift, source) for shift in range(span) for source in sources]
    (parts,) = call(
        functools.partial(local_kernel, tables),
        [shaped(12, cells)],
        500 * work,
        velocity,
        near_cot,
        smooth,
        leonard,
        model,
        dual,
        *far_v,
        *far_cot,
    )
    outs = [jax.ShapeDtypeStruct((n, cells) + slab, jnp.float32) for n in (6, 3)]
    return tuple(
        call(
            functools.partial(finish_kernel, tables, len(near_sums), turning),
            outs,
            200 * work,
            velocity,
            leonard,
            model,
            parts,
            mask,
            *near_sums,
            pair_sums,
            *far_message,
            out_specs=[REMAIN] * 2,
            scratch=[pltpu.VMEM(x.shape, x.dtype) for x in outs] + [pltpu.SemaphoreType.DMA((3,))],
        )
    )


def solution(mesh):
    fields = P(None, "span", "stream", None)
    return jax.shard_map(
        on_device,
        mesh=mesh,
        in_specs=(fields, fields, P("stream"), fields),
        out_specs=(fields, fields),
        check_vma=False,
    )
```

```python
import functools

import jax
import jax.numpy as jnp
import numpy as np
from jax import lax
from jax.experimental import pallas as pl
from jax.experimental.pallas import tpu as pltpu
from jax.sharding import PartitionSpec as P

NBINS = 64
FILTER_ALPHA = 0.45
CENTER_WEIGHT = 0.95
SIDE_WEIGHT = 0.475
STRAIN_FLOOR = 0.25
EPSILON = 1e-06
INDEX_PAIRS = ((0, 0), (0, 1), (0, 2), (1, 1), (1, 2), (2, 2))
PAIR_WEIGHTS = (1.0, 2.0, 2.0, 1.0, 2.0, 1.0)
PAIR_OF = ((0, 1, 2), (1, 3, 4), (2, 4, 5))
LANES = 128
LONG = 300000


def filter_row(extent):
    eye = np.eye(extent)
    ring = np.roll(eye, 1, axis=1) + np.roll(eye, -1, axis=1)
    system = eye + FILTER_ALPHA * ring
    side = CENTER_WEIGHT * eye + SIDE_WEIGHT * ring
    return np.linalg.solve(system, side)[0]


def end_weights(cells):
    weights = np.zeros((2, cells))
    weights[0, 0] = 1.0
    weights[1, cells - 1] = 1.0
    inner = cells - 2
    if inner > 0:
        system = np.eye(inner) + FILTER_ALPHA * (np.eye(inner, k=1) + np.eye(inner, k=-1))
        right = np.zeros((inner, 2))
        right[0, 0] = -FILTER_ALPHA
        right[inner - 1, 1] = -FILTER_ALPHA
        weights[:, 1:-1] = np.linalg.solve(system, right).T
    return weights


class Tables:
    def __init__(self, cells, devices):
        row = filter_row(cells * devices)
        extent = cells * devices
        self.cells = cells
        self.devices = devices
        self.own = [[float(row[(z - w) % extent]) for w in range(cells)] for z in range(cells)]
        self.ends = [[float(x) for x in line] for line in end_weights(cells)]
        self.couple = [
            [[float(row[(z - shift * cells - w) % extent]) for w in (0, cells - 1)] for z in range(cells)]
            for shift in range(devices)
        ]

    def project(self, values):
        return [weighted(line, values) for line in self.ends]

    def inside(self, values):
        return [weighted(line, values) for line in self.own]

    def outside(self, shift, ends):
        return [weighted(line, ends) for line in self.couple[shift]]


def weighted(weights, values):
    total = None
    for weight, value in zip(weights, values):
        if weight == 0.0:
            continue
        term = value if weight == 1.0 else value * weight
        total = term if total is None else total + term
    return total


def add_lists(left, right):
    return [x + y for x, y in zip(left, right)]


def halves(width):
    return [pl.ds(start, LANES) for start in range(0, width, LANES)]


def sum_up(terms):
    total = terms[0]
    for term in terms[1:]:
        total = total + term
    return total


def lanes_kernel(lane_ref):
    lane_ref[...] = lax.broadcasted_iota(jnp.int32, lane_ref.shape, 1)


def prepare_kernel(tables, lane_ref, strain_ref, size_ref, size_ends_ref):
    cells = tables.cells
    for lanes in halves(strain_ref.shape[-1]):
        size = []
        for z in range(cells):
            values = [strain_ref[k, z, :, lanes] for k in range(6)]
            total = sum_up([weight * (value * value) for weight, value in zip(PAIR_WEIGHTS, values)])
            size.append(jnp.sqrt(jnp.maximum(2.0 * total, STRAIN_FLOOR)))
            size_ref[z, :, lanes] = size[z]
        for end, value in enumerate(tables.project(size)):
            size_ends_ref[end, :, lanes] = value


def mask_kernel(tables, bins_hbm, v_ref, size_ends_ref, mask_ref, own_ref, bins_ref, arrived):
    copy = pltpu.make_async_copy(bins_hbm, bins_ref, arrived)
    copy.start()
    for lanes in halves(v_ref.shape[-1]):
        v = [[v_ref[a, z, :, lanes] for z in range(tables.cells)] for a in range(3)]
        for f, field in enumerate(v + products_of(v)):
            for z, value in enumerate(tables.inside(field)):
                own_ref[f, z, :, lanes] = value
    copy.wait()
    rows = bins_ref.shape[1]
    along = jnp.broadcast_to(bins_ref[...].astype(jnp.float32), (rows, rows))
    diagonal = lax.broadcasted_iota(jnp.int32, (rows, rows), 0) == lax.broadcasted_iota(jnp.int32, (rows, rows), 1)
    column = jnp.sum(jnp.where(diagonal, along, 0.0), axis=1, keepdims=True)
    lane = lax.broadcasted_iota(jnp.int32, (rows, LANES), 1).astype(jnp.float32)
    mask_ref[...] = jnp.where(jnp.broadcast_to(column, (rows, LANES)) == lane, 1.0, 0.0)


def products_of(v):
    return [[x * y for x, y in zip(v[a], v[b])] for a, b in INDEX_PAIRS]


def filtered_block(tables, place, fields, ends):
    filtered = [tables.inside(field) for field in fields]
    for other in range(tables.devices):
        if other != place:
            shift = (other - place) % tables.devices
            filtered = [add_lists(near, tables.outside(shift, far)) for near, far in zip(filtered, ends[other])]
    return filtered


def plain_dual(tensor, vector, a, cells):
    return [sum_up([tensor[PAIR_OF[a][b]][z] * vector[b][z] for b in range(3)]) for z in range(cells)]


def weighted_dual(tensor, vector, a, cells):
    plain = plain_dual(tensor, vector, a, cells)
    return [plain[z] + tensor[PAIR_OF[a][a]][z] * vector[a][z] for z in range(cells)]


def velocity_kernel(tables, v_ref, strain_ref, cot_ref, own_ref, *refs):
    far_v_refs = refs[:-4]
    smooth_ref, leonard_ref, rest_ref, powers_ref = refs[-4:]
    cells = tables.cells
    for lanes in halves(v_ref.shape[-1]):
        v = [[v_ref[a, z, :, lanes] for z in range(cells)] for a in range(3)]
        products = products_of(v)
        ends = [None]
        for far_v_ref in far_v_refs:
            far = [[far_v_ref[a, z, :, lanes] for z in range(cells)] for a in range(3)]
            ends.append([tables.project(field) for field in far + products_of(far)])
        filtered = [[own_ref[f, z, :, lanes] for z in range(cells)] for f in range(9)]
        for place in range(1, tables.devices):
            filtered = [add_lists(near, tables.outside(place, far)) for near, far in zip(filtered, ends[place])]
        for a in range(3):
            for z in range(cells):
                smooth_ref[a, z, :, lanes] = filtered[a][z]
        for z in range(cells):
            powers = [[] for _ in range(7)]
            for k, (a, b) in enumerate(INDEX_PAIRS):
                coarse = filtered[a][z] * filtered[b][z]
                leonard = filtered[3 + k][z] - coarse
                rest = products[k][z] - coarse
                leonard_ref[k, z, :, lanes] = leonard
                rest_ref[k, z, :, lanes] = rest
                strain, cot = strain_ref[k, z, :, lanes], cot_ref[k, z, :, lanes]
                scaled_rest, scaled_strain = PAIR_WEIGHTS[k] * rest, PAIR_WEIGHTS[k] * strain
                terms = (
                    scaled_rest * leonard,
                    scaled_strain * leonard,
                    scaled_rest * rest,
                    scaled_strain * rest,
                    scaled_strain * strain,
                    cot * rest,
                    cot * strain,
                )
                for power, term in zip(powers, terms):
                    power.append(term)
            for index, power in enumerate(powers):
                powers_ref[index, z, :, lanes] = sum_up(power)


def sums_kernel(tables, size_ref, powers_ref, mask_ref, *refs):
    far_size_refs = refs[:-2]
    factor_ref, sums_ref = refs[-2:]
    cells = tables.cells
    cross, square, blame = [], [], []
    for lanes in halves(size_ref.shape[-1]):
        size = [size_ref[z, :, lanes] for z in range(cells)]
        ends = [None] + [[[far[end, :, lanes] for end in range(2)]] for far in far_size_refs]
        smooth_size = filtered_block(tables, 0, [size], ends)[0]
        for z in range(cells):
            factor = 2.0 * (4.0 * smooth_size[z] - size[z])
            factor_ref[z, :, lanes] = factor
            power = [powers_ref[index, z, :, lanes] for index in range(7)]
            cross.append(power[0] + factor * power[1])
            square.append(power[2] + factor * (2.0 * power[3] + factor * power[4]))
            blame.append(power[5] + factor * power[6])
    cross, square, blame = [sum_up(cross)], [sum_up(square)], [sum_up(blame)]
    mine = mask_ref[...] > 0.5
    place = lax.broadcasted_iota(jnp.int32, (8, LANES), 0)
    table = jnp.zeros((8, LANES), jnp.float32)
    for index, sums in enumerate((cross, square, blame)):
        per_row = jnp.sum(sums[0], axis=1, keepdims=True)
        per_bin = jnp.sum(jnp.where(mine, per_row, 0.0), axis=0, keepdims=True)
        table = jnp.where(place == index, per_bin, table)
    sums_ref[...] = table


def model_kernel(tables, strain_ref, rest_ref, factor_ref, model_ref):
    for lanes in halves(strain_ref.shape[-1]):
        for z in range(tables.cells):
            factor = factor_ref[z, :, lanes]
            for k in range(6):
                model_ref[k, z, :, lanes] = rest_ref[k, z, :, lanes] + factor * strain_ref[k, z, :, lanes]


def message_kernel(tables, smooth_ref, model_ref, sums_ref, other_sums_ref, dual_ref, message_ref, pair_ref):
    cells = tables.cells
    pair_sums = sums_ref[...] + other_sums_ref[...]
    pair_ref[...] = pair_sums
    message_ref[message_ref.shape[0] - 1] = pair_sums
    for half, lanes in enumerate(halves(model_ref.shape[-1])):
        model = [[model_ref[k, z, :, lanes] for z in range(cells)] for k in range(6)]
        smooth_v = [[smooth_ref[a, z, :, lanes] for z in range(cells)] for a in range(3)]
        for k in range(6):
            for end, value in enumerate(tables.project(model[k])):
                message_ref[18 * half + 2 * k + end] = value
        for a in range(3):
            dual = [2.0 * x for x in plain_dual(model, smooth_v, a, cells)]
            for z in range(cells):
                dual_ref[a, z, :, lanes] = dual[z]
            for end, value in enumerate(tables.project(dual)):
                message_ref[18 * half + 12 + 2 * a + end] = value


def local_kernel(tables, *refs):
    peers = tables.devices - 1
    cells = tables.cells
    v_ref, cot_ref, smooth_ref, leonard_ref, model_ref, dual_ref = refs[:6]
    far_v_refs = refs[6 : 6 + peers]
    far_cot_refs = refs[6 + peers : 6 + 2 * peers]
    parts_ref = refs[-1]
    for lanes in halves(v_ref.shape[-1]):

        def load(ref, count):
            return [[ref[f, z, :, lanes] for z in range(cells)] for f in range(count)]

        fields, ends = [], []
        for ref in (v_ref, *far_v_refs):
            v = load(ref, 3)
            fields.append(v + products_of(v))
            ends.append([tables.project(field) for field in fields[-1]])
        v = fields[0][:3]
        cot, model, leonard, smooth_v = load(cot_ref, 6), load(model_ref, 6), load(leonard_ref, 6), load(smooth_ref, 3)
        smooth_cot = [tables.inside(field) for field in cot]
        duals = [weighted_dual(cot, smooth_v, a, cells) for a in range(3)]
        others = [plain_dual(leonard, smooth_v, a, cells) for a in range(3)]
        smooth_duals = [tables.inside(field) for field in duals]
        smooth_others = [tables.inside(field) for field in others]
        for place in range(1, tables.devices):
            far_cot = load(far_cot_refs[place - 1], 6)
            filtered = filtered_block(tables, place, fields[place], ends)
            far_smooth = filtered[:3]
            far_leonard = [
                [filtered[3 + k][z] - far_smooth[a][z] * far_smooth[b][z] for z in range(cells)]
                for k, (a, b) in enumerate(INDEX_PAIRS)
            ]
            for k in range(6):
                far = tables.outside(place, tables.project(far_cot[k]))
                smooth_cot[k] = add_lists(smooth_cot[k], far)
            for a in range(3):
                far = tables.outside(place, tables.project(weighted_dual(far_cot, far_smooth, a, cells)))
                smooth_duals[a] = add_lists(smooth_duals[a], far)
                far = tables.outside(place, tables.project(plain_dual(far_leonard, far_smooth, a, cells)))
                smooth_others[a] = add_lists(smooth_others[a], far)
        inner = [add_lists(tables.inside(model[k]), leonard[k]) for k in range(6)]
        for a in range(3):
            first = weighted_dual(smooth_cot, v, a, cells)
            second = weighted_dual(cot, v, a, cells)
            dual = tables.inside([dual_ref[a, z, :, lanes] for z in range(cells)])
            third = plain_dual(inner, v, a, cells)
            fourth = plain_dual(model, v, a, cells)
            for z in range(cells):
                parts_ref[a, z, :, lanes] = first[z] - smooth_duals[a][z]
                parts_ref[3 + a, z, :, lanes] = smooth_duals[a][z] - second[z]
                parts_ref[6 + a, z, :, lanes] = 2.0 * (third[z] - smooth_others[a][z]) - dual[z]
                parts_ref[9 + a, z, :, lanes] = 2.0 * dual[z] - 4.0 * fourth[z]


def finish_kernel(tables, count, turning, *refs):
    peers = tables.devices - 1
    cells = tables.cells
    v_ref, leonard_ref, model_ref, parts_ref, mask_ref = refs[:5]
    near_refs = refs[5 : 5 + count]
    pair_ref = refs[5 + count]
    far_message_refs = refs[6 + count : 6 + count + peers]
    residual_hbm, grad_hbm, residual_ref, grad_ref, left = refs[6 + count + peers :]
    total = sum_up([pair_ref[...]] + [ref[ref.shape[0] - 1] for ref in far_message_refs])
    near = sum_up([ref[...] for ref in near_refs])
    if turning:
        place = lax.axis_index("stream")
        inner = jnp.logical_and(place > 0, place < lax.axis_size("stream") - 1)
        near = jnp.where(inner, near, 0.0)
    total = total + near
    inverse = 1.0 / (total[1:2] + EPSILON)
    rows = v_ref.shape[2]
    mine = mask_ref[...] > 0.5

    def of_rows(per_bin):
        column = jnp.sum(jnp.where(mine, per_bin, 0.0), axis=1, keepdims=True)
        return jnp.broadcast_to(column, (rows, LANES))

    coefficient = of_rows(total[0:1] * inverse)
    pull = of_rows(-(total[2:3] * inverse))
    copies = []
    for k in range(6):
        for lanes in halves(v_ref.shape[-1]):
            for z in range(cells):
                residual_ref[k, z, :, lanes] = (
                    leonard_ref[k, z, :, lanes] - coefficient * model_ref[k, z, :, lanes]
                )
        if k % 3 == 2:
            some = pl.ds(k - 2, 3)
            copies.append(pltpu.make_async_copy(residual_ref.at[some], residual_hbm.at[some], left.at[k // 3]))
            copies[-1].start()
    for half, lanes in enumerate(halves(v_ref.shape[-1])):
        v = [[v_ref[a, z, :, lanes] for z in range(cells)] for a in range(3)]
        from_model = [[] for _ in range(6)]
        from_dual = [[] for _ in range(3)]
        for place, ends in enumerate(far_message_refs, start=1):
            for k in range(6):
                from_model[k].append(tables.outside(place, [2.0 * ends[18 * half + 2 * k + end] for end in range(2)]))
            for a in range(3):
                pair = [(2.0 * coefficient - 1.0) * ends[18 * half + 12 + 2 * a + end] for end in range(2)]
                from_dual[a].append(tables.outside(place, pair))
        from_model = [functools.reduce(add_lists, lists) if lists else None for lists in from_model]
        from_dual = [functools.reduce(add_lists, lists) if lists else None for lists in from_dual]
        for a in range(3):
            for z in range(cells):
                pulled = parts_ref[6 + a, z, :, lanes] + coefficient * parts_ref[9 + a, z, :, lanes]
                if peers:
                    terms = [from_model[PAIR_OF[a][b]][z] * v[b][z] for b in range(3)]
                    pulled = pulled + from_dual[a][z] + sum_up(terms)
                grad_ref[a, z, :, lanes] = (
                    parts_ref[a, z, :, lanes] + coefficient * parts_ref[3 + a, z, :, lanes] + pull * pulled
                )
    copies.append(pltpu.make_async_copy(grad_ref, grad_hbm, left.at[2]))
    copies[-1].start()
    for copy in copies:
        copy.wait()


WHOLE = pl.BlockSpec(memory_space=pltpu.VMEM)
REMAIN = pl.BlockSpec(memory_space=pltpu.HBM)


def call(kernel, outs, operations, *operands, in_specs=None, out_specs=None, scratch=()):
    nbytes = sum(4 * int(np.prod(x.shape)) for x in (*operands, *outs))
    return pl.pallas_call(
        kernel,
        out_shape=outs,
        in_specs=in_specs or [WHOLE] * len(operands),
        out_specs=out_specs or [WHOLE] * len(outs),
        scratch_shapes=list(scratch),
        compiler_params=pltpu.CompilerParams(vmem_limit_bytes=32 * 1024 * 1024),
        cost_estimate=pl.CostEstimate(flops=operations, bytes_accessed=nbytes, transcendentals=0),
    )(*operands)


def from_ahead(values, shift):
    peers = lax.axis_size("span")
    return lax.ppermute(values, "span", [((i + shift) % peers, i) for i in range(peers)])


def from_source(values, span_shift, source):
    span, stream = lax.axis_size("span"), lax.axis_size("stream")
    pairs = [
        (((i + span_shift) % span) * stream + source(j) % stream, i * stream + j)
        for i in range(span)
        for j in range(stream)
    ]
    return lax.ppermute(values, ("span", "stream"), pairs)


def ring_source(stream):
    def source(j):
        if j % 2 == 0:
            return j - 2 if j >= 2 else 1
        return j + 2 if j + 2 < stream else j - 1

    return source


def on_device(velocity, strain, row_bins, cotangent):
    span, stream = lax.axis_size("span"), lax.axis_size("stream")
    cells, rows, width = velocity.shape[1:]
    tables = Tables(cells, span)
    slab = (rows, width)

    def shaped(*leading):
        return pltpu.VMEM(leading + slab, jnp.float32)

    far_v = [from_ahead(velocity, shift) for shift in range(1, span)]
    work = cells * rows * width
    (lane,) = call(lanes_kernel, [pltpu.VMEM((rows, LANES), jnp.int32)], LONG * work)
    size, size_ends = call(
        functools.partial(prepare_kernel, tables), [shaped(cells), shaped(2)], LONG * work, lane, strain
    )
    far_size = [from_ahead(size_ends, shift) for shift in range(1, span)]
    mask, own = call(
        functools.partial(mask_kernel, tables),
        [pltpu.VMEM((rows, LANES), jnp.float32), shaped(9, cells)],
        work,
        pltpu.with_memory_space_constraint(row_bins.reshape(1, rows), pltpu.HBM),
        velocity,
        size_ends,
        in_specs=[REMAIN, WHOLE, WHOLE],
        scratch=[pltpu.VMEM((1, rows), jnp.int32), pltpu.SemaphoreType.DMA(())],
    )
    mask, near_cot = lax.optimization_barrier((mask, cotangent))
    far_cot = [from_ahead(near_cot, shift) for shift in range(1, span)]
    table = pltpu.VMEM((8, LANES), jnp.float32)
    smooth, leonard, rest, powers = call(
        functools.partial(velocity_kernel, tables),
        [shaped(3, cells), shaped(6, cells), shaped(6, cells), shaped(7, cells)],
        LONG * work,
        velocity,
        strain,
        near_cot,
        own,
        *far_v,
    )
    factor, sums = call(
        functools.partial(sums_kernel, tables), [shaped(cells), table], LONG * work, size, powers, mask, *far_size
    )
    (model,) = call(
        functools.partial(model_kernel, tables), [shaped(6, cells)], LONG * work, strain, rest, factor
    )
    other_sums = from_source(sums, 0, lambda j: j ^ 1)
    dual, message, pair_sums = call(
        functools.partial(message_kernel, tables),
        [shaped(3, cells), pltpu.VMEM((18 * (width // LANES) + 1, rows, LANES), jnp.float32), table],
        100 * work,
        smooth,
        model,
        sums,
        other_sums,
    )
    far_message = [from_ahead(message, shift) for shift in range(1, span)]
    most_rows = 2 * rows * stream // NBINS
    reach = -(-(most_rows - 1) // rows)
    turning = reach <= 1
    if turning:
        sources = [ring_source(stream)]
    else:
        steps = range(1, -(-reach // 2) + 1)
        sources = [functools.partial(lambda j, away: j + away, away=2 * step * way) for step in steps for way in (1, -1)]
    near_sums = [from_source(pair_sums, shift, source) for shift in range(span) for source in sources]
    (parts,) = call(
        functools.partial(local_kernel, tables),
        [shaped(12, cells)],
        500 * work,
        velocity,
        near_cot,
        smooth,
        leonard,
        model,
        dual,
        *far_v,
        *far_cot,
    )
    outs = [jax.ShapeDtypeStruct((n, cells) + slab, jnp.float32) for n in (6, 3)]
    return tuple(
        call(
            functools.partial(finish_kernel, tables, len(near_sums), turning),
            outs,
            200 * work,
            velocity,
            leonard,
            model,
            parts,
            mask,
            *near_sums,
            pair_sums,
            *far_message,
            out_specs=[REMAIN] * 2,
            scratch=[pltpu.VMEM(x.shape, x.dtype) for x in outs] + [pltpu.SemaphoreType.DMA((3,))],
        )
    )


def solution(mesh):
    fields = P(None, "span", "stream", None)
    return jax.shard_map(
        on_device,
        mesh=mesh,
        in_specs=(fields, fields, P("stream"), fields),
        out_specs=(fields, fields),
        check_vma=False,
    )
```

```python
import functools

import jax
import jax.numpy as jnp
import numpy as np
from jax import lax
from jax.experimental import pallas as pl
from jax.experimental.pallas import tpu as pltpu
from jax.sharding import PartitionSpec as P

NBINS = 64
FILTER_ALPHA = 0.45
CENTER_WEIGHT = 0.95
SIDE_WEIGHT = 0.475
STRAIN_FLOOR = 0.25
EPSILON = 1e-06
INDEX_PAIRS = ((0, 0), (0, 1), (0, 2), (1, 1), (1, 2), (2, 2))
PAIR_WEIGHTS = (1.0, 2.0, 2.0, 1.0, 2.0, 1.0)
PAIR_OF = ((0, 1, 2), (1, 3, 4), (2, 4, 5))
LANES = 128
LONG = 300000


def filter_row(extent):
    eye = np.eye(extent)
    ring = np.roll(eye, 1, axis=1) + np.roll(eye, -1, axis=1)
    system = eye + FILTER_ALPHA * ring
    side = CENTER_WEIGHT * eye + SIDE_WEIGHT * ring
    return np.linalg.solve(system, side)[0]


def end_weights(cells):
    weights = np.zeros((2, cells))
    weights[0, 0] = 1.0
    weights[1, cells - 1] = 1.0
    inner = cells - 2
    if inner > 0:
        system = np.eye(inner) + FILTER_ALPHA * (np.eye(inner, k=1) + np.eye(inner, k=-1))
        right = np.zeros((inner, 2))
        right[0, 0] = -FILTER_ALPHA
        right[inner - 1, 1] = -FILTER_ALPHA
        weights[:, 1:-1] = np.linalg.solve(system, right).T
    return weights


class Tables:
    def __init__(self, cells, devices):
        row = filter_row(cells * devices)
        extent = cells * devices
        self.cells = cells
        self.devices = devices
        self.own = [[float(row[(z - w) % extent]) for w in range(cells)] for z in range(cells)]
        self.ends = [[float(x) for x in line] for line in end_weights(cells)]
        self.couple = [
            [[float(row[(z - shift * cells - w) % extent]) for w in (0, cells - 1)] for z in range(cells)]
            for shift in range(devices)
        ]

    def project(self, values):
        return [weighted(line, values) for line in self.ends]

    def inside(self, values):
        return [weighted(line, values) for line in self.own]

    def outside(self, shift, ends):
        return [weighted(line, ends) for line in self.couple[shift]]


def weighted(weights, values):
    total = None
    for weight, value in zip(weights, values):
        if weight == 0.0:
            continue
        term = value if weight == 1.0 else value * weight
        total = term if total is None else total + term
    return total


def add_lists(left, right):
    return [x + y for x, y in zip(left, right)]


def halves(width):
    return [pl.ds(start, LANES) for start in range(0, width, LANES)]


def sum_up(terms):
    total = terms[0]
    for term in terms[1:]:
        total = total + term
    return total


def lanes_kernel(lane_ref):
    lane_ref[...] = lax.broadcasted_iota(jnp.int32, lane_ref.shape, 1)


def prepare_kernel(tables, lane_ref, strain_ref, size_ref, size_ends_ref):
    cells = tables.cells
    for lanes in halves(strain_ref.shape[-1]):
        size = []
        for z in range(cells):
            values = [strain_ref[k, z, :, lanes] for k in range(6)]
            total = sum_up([weight * (value * value) for weight, value in zip(PAIR_WEIGHTS, values)])
            size.append(jnp.sqrt(jnp.maximum(2.0 * total, STRAIN_FLOOR)))
            size_ref[z, :, lanes] = size[z]
        for end, value in enumerate(tables.project(size)):
            size_ends_ref[end, :, lanes] = value


def mask_kernel(bins_hbm, size_ends_ref, mask_ref, bins_ref, arrived):
    copy = pltpu.make_async_copy(bins_hbm, bins_ref, arrived)
    copy.start()
    copy.wait()
    rows = bins_ref.shape[1]
    along = jnp.broadcast_to(bins_ref[...].astype(jnp.float32), (rows, rows))
    diagonal = lax.broadcasted_iota(jnp.int32, (rows, rows), 0) == lax.broadcasted_iota(jnp.int32, (rows, rows), 1)
    column = jnp.sum(jnp.where(diagonal, along, 0.0), axis=1, keepdims=True)
    lane = lax.broadcasted_iota(jnp.int32, (rows, LANES), 1).astype(jnp.float32)
    mask_ref[...] = jnp.where(jnp.broadcast_to(column, (rows, LANES)) == lane, 1.0, 0.0)


def products_of(v):
    return [[x * y for x, y in zip(v[a], v[b])] for a, b in INDEX_PAIRS]


def filtered_block(tables, place, fields, ends):
    filtered = [tables.inside(field) for field in fields]
    for other in range(tables.devices):
        if other != place:
            shift = (other - place) % tables.devices
            filtered = [add_lists(near, tables.outside(shift, far)) for near, far in zip(filtered, ends[other])]
    return filtered


def plain_dual(tensor, vector, a, cells):
    return [sum_up([tensor[PAIR_OF[a][b]][z] * vector[b][z] for b in range(3)]) for z in range(cells)]


def weighted_dual(tensor, vector, a, cells):
    plain = plain_dual(tensor, vector, a, cells)
    return [plain[z] + tensor[PAIR_OF[a][a]][z] * vector[a][z] for z in range(cells)]


def velocity_kernel(tables, v_ref, strain_ref, cot_ref, *refs):
    far_v_refs = refs[:-4]
    smooth_ref, leonard_ref, rest_ref, powers_ref = refs[-4:]
    cells = tables.cells
    for lanes in halves(v_ref.shape[-1]):
        v = [[v_ref[a, z, :, lanes] for z in range(cells)] for a in range(3)]
        products = products_of(v)
        ends = [None]
        for far_v_ref in far_v_refs:
            far = [[far_v_ref[a, z, :, lanes] for z in range(cells)] for a in range(3)]
            ends.append([tables.project(field) for field in far + products_of(far)])
        filtered = filtered_block(tables, 0, v + products, ends)
        for a in range(3):
            for z in range(cells):
                smooth_ref[a, z, :, lanes] = filtered[a][z]
        for z in range(cells):
            powers = [[] for _ in range(7)]
            for k, (a, b) in enumerate(INDEX_PAIRS):
                coarse = filtered[a][z] * filtered[b][z]
                leonard = filtered[3 + k][z] - coarse
                rest = products[k][z] - coarse
                leonard_ref[k, z, :, lanes] = leonard
                rest_ref[k, z, :, lanes] = rest
                strain, cot = strain_ref[k, z, :, lanes], cot_ref[k, z, :, lanes]
                scaled_rest, scaled_strain = PAIR_WEIGHTS[k] * rest, PAIR_WEIGHTS[k] * strain
                terms = (
                    scaled_rest * leonard,
                    scaled_strain * leonard,
                    scaled_rest * rest,
                    scaled_strain * rest,
                    scaled_strain * strain,
                    cot * rest,
                    cot * strain,
                )
                for power, term in zip(powers, terms):
                    power.append(term)
            for index, power in enumerate(powers):
                powers_ref[index, z, :, lanes] = sum_up(power)


def sums_kernel(tables, size_ref, powers_ref, mask_ref, *refs):
    far_size_refs = refs[:-2]
    factor_ref, sums_ref = refs[-2:]
    cells = tables.cells
    cross, square, blame = [], [], []
    for lanes in halves(size_ref.shape[-1]):
        size = [size_ref[z, :, lanes] for z in range(cells)]
        ends = [None] + [[[far[end, :, lanes] for end in range(2)]] for far in far_size_refs]
        smooth_size = filtered_block(tables, 0, [size], ends)[0]
        for z in range(cells):
            factor = 2.0 * (4.0 * smooth_size[z] - size[z])
            factor_ref[z, :, lanes] = factor
            power = [powers_ref[index, z, :, lanes] for index in range(7)]
            cross.append(power[0] + factor * power[1])
            square.append(power[2] + factor * (2.0 * power[3] + factor * power[4]))
            blame.append(power[5] + factor * power[6])
    cross, square, blame = [sum_up(cross)], [sum_up(square)], [sum_up(blame)]
    mine = mask_ref[...] > 0.5
    place = lax.broadcasted_iota(jnp.int32, (8, LANES), 0)
    table = jnp.zeros((8, LANES), jnp.float32)
    for index, sums in enumerate((cross, square, blame)):
        per_row = jnp.sum(sums[0], axis=1, keepdims=True)
        per_bin = jnp.sum(jnp.where(mine, per_row, 0.0), axis=0, keepdims=True)
        table = jnp.where(place == index, per_bin, table)
    sums_ref[...] = table


def model_kernel(tables, strain_ref, rest_ref, factor_ref, model_ref):
    for lanes in halves(strain_ref.shape[-1]):
        for z in range(tables.cells):
            factor = factor_ref[z, :, lanes]
            for k in range(6):
                model_ref[k, z, :, lanes] = rest_ref[k, z, :, lanes] + factor * strain_ref[k, z, :, lanes]


def message_kernel(tables, smooth_ref, model_ref, sums_ref, other_sums_ref, dual_ref, message_ref, pair_ref):
    cells = tables.cells
    pair_sums = sums_ref[...] + other_sums_ref[...]
    pair_ref[...] = pair_sums
    message_ref[message_ref.shape[0] - 1] = pair_sums
    for half, lanes in enumerate(halves(model_ref.shape[-1])):
        model = [[model_ref[k, z, :, lanes] for z in range(cells)] for k in range(6)]
        smooth_v = [[smooth_ref[a, z, :, lanes] for z in range(cells)] for a in range(3)]
        for k in range(6):
            for end, value in enumerate(tables.project(model[k])):
                message_ref[18 * half + 2 * k + end] = value
        for a in range(3):
            dual = [2.0 * x for x in plain_dual(model, smooth_v, a, cells)]
            for z in range(cells):
                dual_ref[a, z, :, lanes] = dual[z]
            for end, value in enumerate(tables.project(dual)):
                message_ref[18 * half + 12 + 2 * a + end] = value


def local_kernel(tables, *refs):
    peers = tables.devices - 1
    cells = tables.cells
    v_ref, cot_ref, smooth_ref, leonard_ref, model_ref, dual_ref = refs[:6]
    far_v_refs = refs[6 : 6 + peers]
    far_cot_refs = refs[6 + peers : 6 + 2 * peers]
    parts_ref = refs[-1]
    for lanes in halves(v_ref.shape[-1]):

        def load(ref, count):
            return [[ref[f, z, :, lanes] for z in range(cells)] for f in range(count)]

        fields, ends = [], []
        for ref in (v_ref, *far_v_refs):
            v = load(ref, 3)
            fields.append(v + products_of(v))
            ends.append([tables.project(field) for field in fields[-1]])
        v = fields[0][:3]
        cot, model, leonard, smooth_v = load(cot_ref, 6), load(model_ref, 6), load(leonard_ref, 6), load(smooth_ref, 3)
        smooth_cot = [tables.inside(field) for field in cot]
        duals = [weighted_dual(cot, smooth_v, a, cells) for a in range(3)]
        others = [plain_dual(leonard, smooth_v, a, cells) for a in range(3)]
        smooth_duals = [tables.inside(field) for field in duals]
        smooth_others = [tables.inside(field) for field in others]
        for place in range(1, tables.devices):
            far_cot = load(far_cot_refs[place - 1], 6)
            filtered = filtered_block(tables, place, fields[place], ends)
            far_smooth = filtered[:3]
            far_leonard = [
                [filtered[3 + k][z] - far_smooth[a][z] * far_smooth[b][z] for z in range(cells)]
                for k, (a, b) in enumerate(INDEX_PAIRS)
            ]
            for k in range(6):
                far = tables.outside(place, tables.project(far_cot[k]))
                smooth_cot[k] = add_lists(smooth_cot[k], far)
            for a in range(3):
                far = tables.outside(place, tables.project(weighted_dual(far_cot, far_smooth, a, cells)))
                smooth_duals[a] = add_lists(smooth_duals[a], far)
                far = tables.outside(place, tables.project(plain_dual(far_leonard, far_smooth, a, cells)))
                smooth_others[a] = add_lists(smooth_others[a], far)
        inner = [add_lists(tables.inside(model[k]), leonard[k]) for k in range(6)]
        for a in range(3):
            first = weighted_dual(smooth_cot, v, a, cells)
            second = weighted_dual(cot, v, a, cells)
            dual = tables.inside([dual_ref[a, z, :, lanes] for z in range(cells)])
            third = plain_dual(inner, v, a, cells)
            fourth = plain_dual(model, v, a, cells)
            for z in range(cells):
                parts_ref[a, z, :, lanes] = first[z] - smooth_duals[a][z]
                parts_ref[3 + a, z, :, lanes] = smooth_duals[a][z] - second[z]
                parts_ref[6 + a, z, :, lanes] = 2.0 * (third[z] - smooth_others[a][z]) - dual[z]
                parts_ref[9 + a, z, :, lanes] = 2.0 * dual[z] - 4.0 * fourth[z]


def finish_kernel(tables, count, turning, *refs):
    peers = tables.devices - 1
    cells = tables.cells
    v_ref, leonard_ref, model_ref, parts_ref, mask_ref = refs[:5]
    near_refs = refs[5 : 5 + count]
    pair_ref = refs[5 + count]
    far_message_refs = refs[6 + count : 6 + count + peers]
    residual_hbm, grad_hbm, residual_ref, grad_ref, left = refs[6 + count + peers :]
    total = sum_up([pair_ref[...]] + [ref[ref.shape[0] - 1] for ref in far_message_refs])
    near = sum_up([ref[...] for ref in near_refs])
    if turning:
        place = lax.axis_index("stream")
        inner = jnp.logical_and(place > 0, place < lax.axis_size("stream") - 1)
        near = jnp.where(inner, near, 0.0)
    total = total + near
    inverse = 1.0 / (total[1:2] + EPSILON)
    rows = v_ref.shape[2]
    mine = mask_ref[...] > 0.5

    def of_rows(per_bin):
        column = jnp.sum(jnp.where(mine, per_bin, 0.0), axis=1, keepdims=True)
        return jnp.broadcast_to(column, (rows, LANES))

    coefficient = of_rows(total[0:1] * inverse)
    pull = of_rows(-(total[2:3] * inverse))
    copies = []
    for k in range(6):
        for lanes in halves(v_ref.shape[-1]):
            for z in range(cells):
                residual_ref[k, z, :, lanes] = (
                    leonard_ref[k, z, :, lanes] - coefficient * model_ref[k, z, :, lanes]
                )
    copies.append(pltpu.make_async_copy(residual_ref, residual_hbm, left.at[0]))
    copies[-1].start()
    for half, lanes in enumerate(halves(v_ref.shape[-1])):
        v = [[v_ref[a, z, :, lanes] for z in range(cells)] for a in range(3)]
        from_model = [[] for _ in range(6)]
        from_dual = [[] for _ in range(3)]
        for place, ends in enumerate(far_message_refs, start=1):
            for k in range(6):
                from_model[k].append(tables.outside(place, [2.0 * ends[18 * half + 2 * k + end] for end in range(2)]))
            for a in range(3):
                pair = [(2.0 * coefficient - 1.0) * ends[18 * half + 12 + 2 * a + end] for end in range(2)]
                from_dual[a].append(tables.outside(place, pair))
        from_model = [functools.reduce(add_lists, lists) if lists else None for lists in from_model]
        from_dual = [functools.reduce(add_lists, lists) if lists else None for lists in from_dual]
        for a in range(3):
            for z in range(cells):
                pulled = parts_ref[6 + a, z, :, lanes] + coefficient * parts_ref[9 + a, z, :, lanes]
                if peers:
                    terms = [from_model[PAIR_OF[a][b]][z] * v[b][z] for b in range(3)]
                    pulled = pulled + from_dual[a][z] + sum_up(terms)
                grad_ref[a, z, :, lanes] = (
                    parts_ref[a, z, :, lanes] + coefficient * parts_ref[3 + a, z, :, lanes] + pull * pulled
                )
    copies.append(pltpu.make_async_copy(grad_ref, grad_hbm, left.at[1]))
    copies[-1].start()
    for copy in copies:
        copy.wait()


WHOLE = pl.BlockSpec(memory_space=pltpu.VMEM)
REMAIN = pl.BlockSpec(memory_space=pltpu.HBM)


def call(kernel, outs, operations, *operands, in_specs=None, out_specs=None, scratch=()):
    nbytes = sum(4 * int(np.prod(x.shape)) for x in (*operands, *outs))
    return pl.pallas_call(
        kernel,
        out_shape=outs,
        in_specs=in_specs or [WHOLE] * len(operands),
        out_specs=out_specs or [WHOLE] * len(outs),
        scratch_shapes=list(scratch),
        compiler_params=pltpu.CompilerParams(vmem_limit_bytes=32 * 1024 * 1024),
        cost_estimate=pl.CostEstimate(flops=operations, bytes_accessed=nbytes, transcendentals=0),
    )(*operands)


def from_ahead(values, shift):
    peers = lax.axis_size("span")
    return lax.ppermute(values, "span", [((i + shift) % peers, i) for i in range(peers)])


def from_source(values, span_shift, source):
    span, stream = lax.axis_size("span"), lax.axis_size("stream")
    pairs = [
        (((i + span_shift) % span) * stream + source(j) % stream, i * stream + j)
        for i in range(span)
        for j in range(stream)
    ]
    return lax.ppermute(values, ("span", "stream"), pairs)


def ring_source(stream):
    def source(j):
        if j % 2 == 0:
            return j - 2 if j >= 2 else 1
        return j + 2 if j + 2 < stream else j - 1

    return source


def on_device(velocity, strain, row_bins, cotangent):
    span, stream = lax.axis_size("span"), lax.axis_size("stream")
    cells, rows, width = velocity.shape[1:]
    tables = Tables(cells, span)
    slab = (rows, width)

    def shaped(*leading):
        return pltpu.VMEM(leading + slab, jnp.float32)

    far_v = [from_ahead(velocity, shift) for shift in range(1, span)]
    work = cells * rows * width
    (lane,) = call(lanes_kernel, [pltpu.VMEM((rows, LANES), jnp.int32)], LONG * work)
    size, size_ends = call(
        functools.partial(prepare_kernel, tables), [shaped(cells), shaped(2)], LONG * work, lane, strain
    )
    far_size = [from_ahead(size_ends, shift) for shift in range(1, span)]
    (mask,) = call(
        mask_kernel,
        [pltpu.VMEM((rows, LANES), jnp.float32)],
        work,
        pltpu.with_memory_space_constraint(row_bins.reshape(1, rows), pltpu.HBM),
        size_ends,
        in_specs=[REMAIN, WHOLE],
        scratch=[pltpu.VMEM((1, rows), jnp.int32), pltpu.SemaphoreType.DMA(())],
    )
    mask, near_cot = lax.optimization_barrier((mask, cotangent))
    far_cot = [from_ahead(near_cot, shift) for shift in range(1, span)]
    table = pltpu.VMEM((8, LANES), jnp.float32)
    smooth, leonard, rest, powers = call(
        functools.partial(velocity_kernel, tables),
        [shaped(3, cells), shaped(6, cells), shaped(6, cells), shaped(7, cells)],
        LONG * work,
        velocity,
        strain,
        near_cot,
        *far_v,
    )
    factor, sums = call(
        functools.partial(sums_kernel, tables), [shaped(cells), table], LONG * work, size, powers, mask, *far_size
    )
    (model,) = call(
        functools.partial(model_kernel, tables), [shaped(6, cells)], LONG * work, strain, rest, factor
    )
    other_sums = from_source(sums, 0, lambda j: j ^ 1)
    dual, message, pair_sums = call(
        functools.partial(message_kernel, tables),
        [shaped(3, cells), pltpu.VMEM((18 * (width // LANES) + 1, rows, LANES), jnp.float32), table],
        100 * work,
        smooth,
        model,
        sums,
        other_sums,
    )
    far_message = [from_ahead(message, shift) for shift in range(1, span)]
    most_rows = 2 * rows * stream // NBINS
    reach = -(-(most_rows - 1) // rows)
    turning = reach <= 1
    if turning:
        sources = [ring_source(stream)]
    else:
        steps = range(1, -(-reach // 2) + 1)
        sources = [functools.partial(lambda j, away: j + away, away=2 * step * way) for step in steps for way in (1, -1)]
    near_sums = [from_source(pair_sums, shift, source) for shift in range(span) for source in sources]
    (parts,) = call(
        functools.partial(local_kernel, tables),
        [shaped(12, cells)],
        500 * work,
        velocity,
        near_cot,
        smooth,
        leonard,
        model,
        dual,
        *far_v,
        *far_cot,
    )
    outs = [jax.ShapeDtypeStruct((n, cells) + slab, jnp.float32) for n in (6, 3)]
    return tuple(
        call(
            functools.partial(finish_kernel, tables, len(near_sums), turning),
            outs,
            200 * work,
            velocity,
            leonard,
            model,
            parts,
            mask,
            *near_sums,
            pair_sums,
            *far_message,
            out_specs=[REMAIN] * 2,
            scratch=[pltpu.VMEM(x.shape, x.dtype) for x in outs] + [pltpu.SemaphoreType.DMA((2,))],
        )
    )


def solution(mesh):
    fields = P(None, "span", "stream", None)
    return jax.shard_map(
        on_device,
        mesh=mesh,
        in_specs=(fields, fields, P("stream"), fields),
        out_specs=(fields, fields),
        check_vma=False,
    )
```
